32 devices in a mesh: dp: 8 (over z, x), tensor: 4 (over y, core).
Axes of the slice: x: 2, y: 2, z: 4, core: 2. Of those that a mesh axis runs over, the one named last changes fastest.
Arguments:
- tokens: bfloat16 [32768, 768], P(('dp', 'tensor')), may hold values from -6 to 6
- cotangent: bfloat16 [32768, 768], P(('dp', 'tensor')), may hold values from -6 to 6
- segment_ids: int32 [32768], P('dp'), may hold values from 0 to 255, never falling along the last dimension, each value on 1 to 1024 neighbouring positions
- buckets: int32 [2047], replicated, may hold values from 0 to 31
- owners: int32 [2304], replicated, may hold values from 0 to 7, as said below
- master: float32 [4, 4608, 768], P('tensor', 'dp'), may hold values from -2 to 2
- first_moment: float32 [4, 4608, 768], P('tensor', 'dp'), may hold values from -262144 to 262144
- second_moment: float32 [4, 4608, 768], P('tensor', 'dp'), may hold values from 0 to 2097152
- small_params: float32 [3616], replicated, may hold values from -5 to 5
- small_first: float32 [3616], replicated, may hold values from -524288 to 524288
- small_second: float32 [3616], replicated, may hold values from 0 to 2097152
- adapter_ema: float32 [1696], replicated, may hold values from -5 to 5
- step_count: int32 [1], replicated, may hold values from 2 to 20
Outputs:
- layer_out: bfloat16 [32768, 768], P(('dp', 'tensor'))
- input_grad: bfloat16 [32768, 768], P(('dp', 'tensor'))
- weight_grads: float32 [4, 4608, 768], P('tensor', 'dp')
- new_first: float32 [4, 4608, 768], P('tensor', 'dp')
- new_second: float32 [4, 4608, 768], P('tensor', 'dp')
- new_master: float32 [4, 4608, 768], P('tensor', 'dp')
- new_copies: bfloat16 [4, 4608, 768], P('tensor', 'dp')
- small_grads: float32 [3616], replicated
- small_first_new: float32 [3616], replicated
- small_second_new: float32 [3616], replicated
- small_new: float32 [3616], replicated
- ema_new: float32 [1696], replicated
The draws below stay inside these ranges and needn't reach their ends.
Inputs may be any that keep to these rules, and one draw needn't show every extreme that they name: `owners`: no owner holds more than 576 rows, and some owner holds exactly 576.
All inputs are finite; a program needn't handle non-finite values.
Results may differ from the reference program's by a relative error of at most 0.02.
Values may be sent and summed in bfloat16 or wider, within the bound.
A program may use at most 192 MiB of HBM per device.

```python
import math
import jax
import jax.numpy as jnp
import numpy as np
from jax import lax

D = 768
H = 12
HS = 64
FF = 3072
NB = 32
R = 48
PHM = 4
SEQ = 1024
SEQS_DP = 4
TOKENS = 32768
HDT = 192
FFT = 768
ROWS_T = 2304
CAP = 576
NSMALL = 3616
NADAPT = 1696
N_DP = 8
N_TENSOR = 4


def owner_list(key):
    base = jax.random.fold_in(key, 101)
    rows_key, owner_key = jax.random.split(base)
    row_order = jax.random.permutation(rows_key, ROWS_T)
    owner_order = jax.random.permutation(owner_key, N_DP)
    mean_rows = ROWS_T // N_DP
    places = jnp.arange(ROWS_T, dtype=jnp.int32)
    offset = places % (4 * mean_rows)
    within = (offset >= 2 * mean_rows).astype(jnp.int32) + (offset >= 2 * mean_rows + mean_rows // 2).astype(jnp.int32) + (offset >= 3 * mean_rows + mean_rows // 2).astype(jnp.int32)
    owner_place = 4 * (places // (4 * mean_rows)) + within
    by_place = owner_order[owner_place].astype(jnp.int32)
    return jnp.zeros((ROWS_T,), jnp.int32).at[row_order].set(by_place)


def slot_rows(key):
    owners = owner_list(key)
    onehot = (owners[:, None] == jnp.arange(N_DP, dtype=jnp.int32)[None, :]).astype(jnp.int32)
    within = jnp.sum(jnp.cumsum(onehot, axis=0) * onehot, axis=1) - 1
    slots = owners * CAP + within
    return jnp.full((N_DP * CAP,), -1, jnp.int32).at[slots].set(jnp.arange(ROWS_T, dtype=jnp.int32))


def role_values(rows, table):
    return jnp.where(rows < HDT, table[0], jnp.where(rows < 2 * HDT, table[1], jnp.where(rows < 3 * HDT, table[2], jnp.where(rows < 4 * HDT, table[3], jnp.where(rows < 4 * HDT + FFT, table[4], table[5]))))).astype(jnp.float32)


def noise(key, shape):
    return jnp.clip(jax.random.normal(key, shape, jnp.float32), -4.0, 4.0)


def ratio_draw(key, shape):
    return jnp.exp(jax.random.uniform(key, shape, jnp.float32, 0.0, math.log(4.0)))


def weight_grad_scale(key):
    rows = slot_rows(key)
    attend_scale = 0.5 * HS ** 0.25
    return role_values(rows, (attend_scale, attend_scale, 1.1, 0.6, 0.9, 0.8)) * TOKENS ** 0.5


def draw_owners(key, part):
    return owner_list(key)


def draw_master(key, part):
    rows = slot_rows(key)
    score_scale = D ** (-0.5) * HS ** (-0.25)
    scales = role_values(rows, (score_scale, score_scale, 3.0 * (H * HS) ** (-0.5), D ** (-0.5), D ** (-0.5), 2.0 * FF ** (-0.5)))
    return noise(jax.random.fold_in(key, 1), (N_TENSOR, N_DP * CAP, D)) * scales[None, :, None]


def draw_first_moment(key, part):
    scales = weight_grad_scale(key)
    return noise(jax.random.fold_in(key, 2), (N_TENSOR, N_DP * CAP, D)) * scales[None, :, None]


def draw_second_moment(key, part):
    scales = weight_grad_scale(key)
    return ratio_draw(jax.random.fold_in(key, 3), (N_TENSOR, N_DP * CAP, D)) * (scales * scales)[None, :, None]


def small_region():
    bounds = (D, 2 * D, 2 * D + PHM ** 3, 3 * D + PHM ** 3, 3 * D + PHM ** 3 + R, 3 * D + PHM ** 3 + 2 * R, 4 * D + PHM ** 3 + 2 * R)
    places = jnp.arange(NSMALL, dtype=jnp.int32)
    region = jnp.zeros((NSMALL,), jnp.int32)
    for bound in bounds:
        region = region + (places >= bound).astype(jnp.int32)
    return region


def small_lookup(values):
    return jnp.array(values, jnp.float32)[small_region()]


def draw_small_params(key, part):
    center = small_lookup((1.0, 1.0, 0.0, 0.0, 0.0, 0.0, 0.0, 0.0))
    spread = small_lookup((0.1, 0.1, 1.0, 0.15, 0.15, 0.2, 0.2, 1.0))
    return center + spread * noise(jax.random.fold_in(key, 4), (NSMALL,))


def draw_small_first(key, part):
    scales = small_lookup((1.0, 1.0, 3.0, 3.0, 3.0, 3.0, 3.0, 1.0)) * TOKENS ** 0.5
    return scales * noise(jax.random.fold_in(key, 5), (NSMALL,))


def draw_small_second(key, part):
    scales = small_lookup((1.0, 1.0, 3.0, 3.0, 3.0, 3.0, 3.0, 1.0)) * TOKENS ** 0.5
    return scales * scales * ratio_draw(jax.random.fold_in(key, 6), (NSMALL,))


def draw_adapter_ema(key, part):
    spread = small_lookup((0.1, 0.1, 1.0, 0.15, 0.15, 0.2, 0.2, 1.0))[2 * D:2 * D + NADAPT]
    return spread * noise(jax.random.fold_in(key, 7), (NADAPT,))


def place_ends(entries, stream_key, smallest, top_value):
    shape = entries.shape
    place = [jax.random.randint(jax.random.fold_in(stream_key, axis), (), 0, shape[axis]) for axis in range(len(shape))]
    entries = entries.at[tuple(place)].set(smallest)
    longest = shape.index(max(shape))
    place[longest] = (place[longest] + 1) % shape[longest]
    return entries.at[tuple(place)].set(top_value)


def steps_of(key, extent, shards, smallest, high):
    def one(axis_at, blocks):
        heights = jax.random.uniform(jax.random.fold_in(jax.random.fold_in(key, 6), axis_at), (blocks,), jnp.float32, smallest / len(shards), high / len(shards))
        return jnp.repeat(jnp.exp(heights), extent[axis_at] // blocks).reshape((-1,) + (1,) * (len(extent) - axis_at - 1))

    loudness = one(*shards[0])
    for cut in shards[1:]:
        loudness = loudness * one(*cut)
    return loudness


def profile(number_of, total, reach, skew):
    portions = [(1 << 20) // math.isqrt(rank ** skew) + 1 for rank in range(2, number_of + 1)]
    spare, holding = total - reach - (number_of - 1), [1] * (number_of - 1)
    while spare > 0:
        movable = [i for i in range(number_of - 1) if holding[i] < reach]
        whole, left = sum([portions[i] for i in movable]), spare
        for i in movable:
            extra = min(reach - holding[i], max(1, left * portions[i] // whole), spare)
            holding[i] = holding[i] + extra
            spare = spare - extra
    return np.array([reach] + holding)


def uneven(key, amount, total, most, skew):
    if amount == 2:
        one = jax.random.randint(key, (), max(1, total - most), min(most, total - 1) + 1)
        return jnp.stack([one, total - one])
    sizes = jnp.asarray(profile(amount, total, most, skew), jnp.int32)
    pairs = (amount - 1) // 2
    donor, taker = sizes[1:1 + 2 * pairs:2], sizes[2:2 + 2 * pairs:2]
    margin = jnp.minimum(donor - 1, most - taker)
    passed = jax.random.randint(jax.random.fold_in(key, 1), (pairs,), 0, 1 << 20) % (margin + 1)
    sizes = sizes.at[1:1 + 2 * pairs:2].set(donor - passed).at[2:2 + 2 * pairs:2].set(taker + passed)
    return sizes[jax.random.permutation(jax.random.fold_in(key, 2), amount)]


def bell_draw(rng, shape, scale, most, shards=(), kind=jnp.bfloat16):
    values = jax.random.normal(rng, shape, jnp.float32) * scale
    if len(shards) > 0:
        values = steps_of(rng, shape, shards, -0.22, 0.18) * values
    return jnp.clip(values, min=-most, max=most).astype(kind)


def setup_inputs(seed: int = 0) -> dict:
    streams_of = jax.random.split(jax.random.key(seed), 14)
    tokens = bell_draw(streams_of[0], (TOKENS, D), 1.0, 6.0, ((0, 32),))
    cotangent = bell_draw(streams_of[1], (TOKENS, D), 1.0, 6.0, ((0, 32),))
    segment_ids = jnp.searchsorted(jnp.cumsum(uneven(streams_of[2], TOKENS * 8 // SEQ, TOKENS, SEQ, 2)), jnp.arange(TOKENS), side="right").astype(jnp.int32)
    buckets = place_ends(jax.random.randint(streams_of[3], (2 * SEQ - 1,), 0, NB), jax.random.fold_in(streams_of[3], 1), 0, NB - 1).astype(jnp.int32)
    owners = draw_owners(jax.random.fold_in(streams_of[13], 71), 0)
    master = draw_master(jax.random.fold_in(streams_of[13], 71), 0)
    first_moment = draw_first_moment(jax.random.fold_in(streams_of[13], 71), 0)
    second_moment = draw_second_moment(jax.random.fold_in(streams_of[13], 71), 0)
    small_params = draw_small_params(jax.random.fold_in(streams_of[13], 71), 0)
    small_first = draw_small_first(jax.random.fold_in(streams_of[13], 71), 0)
    small_second = draw_small_second(jax.random.fold_in(streams_of[13], 71), 0)
    adapter_ema = draw_adapter_ema(jax.random.fold_in(streams_of[13], 71), 0)
    step_count = jax.random.randint(streams_of[12], (1,), 2, 21).astype(jnp.int32)
    return {"tokens": tokens, "cotangent": cotangent, "segment_ids": segment_ids, "buckets": buckets, "owners": owners, "master": master, "first_moment": first_moment, "second_moment": second_moment, "small_params": small_params, "small_first": small_first, "small_second": small_second, "adapter_ema": adapter_ema, "step_count": step_count}


highest = lax.Precision.HIGHEST
norm_epsilon = 1e-06
beta_first = 0.5
beta_second = 0.5
adam_epsilon = 1e-08
rate_per_step = 0.01
weight_decay = 0.1
average_keep = 0.75

@jax.custom_vjp
def low(v):
    return lax.optimization_barrier(v.astype(jnp.bfloat16)).astype(jnp.float32)

@jax.custom_vjp
def low_back(v):
    return v

def low_keep(v):
    return (low(v), None)

def low_pass(kept, grad):
    return (grad,)

def back_keep(v):
    return (v, None)

def back_low(kept, grad):
    return (low(grad),)
low.defvjp(low_keep, low_pass)
low_back.defvjp(back_keep, back_low)

def owner_slots(owners):
    onehot = (owners[:, None] == jnp.arange(N_DP, dtype=jnp.int32)[None, :]).astype(jnp.int32)
    within = lax.optimization_barrier(jnp.sum(jnp.cumsum(onehot, axis=0) * onehot, axis=1)) - 1
    return (owners * CAP + within).astype(jnp.int32)

def unpack(packed):
    widths = (D, D, PHM ** 3, D, R, R, D, NB * H)
    pieces = []
    offset = 0
    for width in widths:
        pieces.append(packed[offset:offset + width])
        offset = offset + width
    gain_one, gain_two, mix_flat, down_left, down_right, up_left, up_right, table_flat = pieces
    adapter = (mix_flat.reshape(PHM, PHM, PHM), down_left.reshape(PHM, D // PHM), down_right.reshape(PHM, R // PHM), up_left.reshape(PHM, R // PHM), up_right.reshape(PHM, D // PHM))
    return (gain_one, gain_two, adapter, table_flat.reshape(NB, H))

def adapter_apply(features, adapter):
    mix, down_left, down_right, up_left, up_right = adapter
    down_matrix = jnp.einsum('iab,ip,iq->apbq', mix, down_left, down_right, precision=highest).reshape(D, R)
    up_matrix = jnp.einsum('iab,iq,ip->aqbp', mix, up_left, up_right, precision=highest).reshape(R, D)
    hidden = jnp.dot(features, down_matrix, precision=highest)
    return features + jnp.dot(jax.nn.gelu(hidden, approximate=False), up_matrix, precision=highest)

def rms_norm(values, gain):
    return values * lax.rsqrt(lax.optimization_barrier(jnp.mean(values * values, axis=-1, keepdims=True)) + norm_epsilon) * gain

def matmul(left, right):
    return jnp.dot(left, right, precision=highest)

def attention(queries, key_rows, value_rows, segments, buckets, table):
    seq_count = queries.shape[0] // SEQ
    seq_shape = (seq_count, SEQ, H, HS)
    offsets = jnp.arange(SEQ, dtype=jnp.int32)[None, :] - jnp.arange(SEQ, dtype=jnp.int32)[:, None] + SEQ - 1
    bias = jnp.transpose(table[buckets[offsets]], (2, 0, 1))

    def one_sequence(inputs):
        query_seq, key_seq, value_seq, segment_seq = inputs
        raw_scores = jnp.einsum('ihd,lhd->hil', query_seq, key_seq, precision=highest) + bias
        raw_scores = low_back(raw_scores)
        same_doc = segment_seq[:, None] == segment_seq[None, :]
        scores = jnp.where(same_doc[None], raw_scores, -1000000000.0)
        soft_probs = low(jax.nn.softmax(scores, axis=-1))
        return jnp.einsum('hil,lhd->ihd', soft_probs, value_seq, precision=highest)
    attended = lax.map(jax.checkpoint(one_sequence), (queries.reshape(seq_shape), key_rows.reshape(seq_shape), value_rows.reshape(seq_shape), segments.reshape(seq_count, SEQ)))
    return attended.reshape(queries.shape[0], H * HS)

def group_forward(rows, bank, small, segments, buckets):
    gain_one, gain_two, adapter, table = unpack(small)
    normed_one = low(rms_norm(rows, gain_one))
    query_parts, key_parts, value_parts = ([], [], [])
    for group in range(N_TENSOR):
        projected = low(low_back(matmul(normed_one, bank[group, :3 * HDT].T)))
        query_parts.append(projected[:, :HDT])
        key_parts.append(projected[:, HDT:2 * HDT])
        value_parts.append(projected[:, 2 * HDT:])
    queries = jnp.concatenate(query_parts, axis=1)
    key_rows = jnp.concatenate(key_parts, axis=1)
    value_rows = jnp.concatenate(value_parts, axis=1)
    attended = low(low_back(attention(queries, key_rows, value_rows, segments, buckets, table)))
    attn = jnp.zeros(rows.shape, jnp.float32)
    for group in range(N_TENSOR):
        attn = attn + matmul(attended[:, group * HDT:(group + 1) * HDT], bank[group, 3 * HDT:4 * HDT])
    attn = low_back(attn)
    mid = rows + attn
    normed_two = low(rms_norm(mid, gain_two))
    ffn_out = jnp.zeros(rows.shape, jnp.float32)
    for group in range(N_TENSOR):
        pre_act = matmul(normed_two, bank[group, 4 * HDT:4 * HDT + FFT].T)
        activ = low(jax.nn.gelu(low_back(pre_act), approximate=False))
        ffn_out = ffn_out + matmul(activ, bank[group, 4 * HDT + FFT:])
    ffn_out = low_back(ffn_out)
    return mid + adapter_apply(ffn_out, adapter)

def adamw(weights, grads, first, second, step):
    first_new = beta_first * first + (1.0 - beta_first) * grads
    second_new = beta_second * second + (1.0 - beta_second) * grads * grads
    first_hat = first_new / (1.0 - beta_first ** step)
    second_hat = second_new / (1.0 - beta_second ** step)
    weights_new = weights - rate_per_step * step * (first_hat / (jnp.sqrt(second_hat) + adam_epsilon) + weight_decay * weights)
    return (weights_new, first_new, second_new)

def reference(tokens, cotangent, segment_ids, buckets, owners, master, first_moment, second_moment, small_params, small_first, small_second, adapter_ema, step_count):
    slots = owner_slots(owners)
    bank = master[:, slots, :].astype(jnp.bfloat16).astype(jnp.float32)
    group_rows = SEQS_DP * SEQ
    rows_all = tokens.astype(jnp.float32).reshape(N_DP, group_rows, D)
    grads_all = cotangent.astype(jnp.float32).reshape(N_DP, group_rows, D)
    segments_all = segment_ids.reshape(N_DP, group_rows)

    def scan_step(carry, inputs):
        bank_sum, small_sum = carry
        rows, grad_rows, segments = inputs

        def forward(rows_in, bank_in, small_in):
            return group_forward(rows_in, bank_in, small_in, segments, buckets)
        result, pull = jax.vjp(forward, rows, bank, small_params)
        row_grad, bank_grad, small_grad = pull(grad_rows)
        return ((bank_sum + bank_grad, small_sum + small_grad), (result.astype(jnp.bfloat16), row_grad.astype(jnp.bfloat16)))
    start = (jnp.zeros(bank.shape, jnp.float32), jnp.zeros(small_params.shape, jnp.float32))
    (bank_sum, small_sum), (outputs, input_grads) = lax.scan(scan_step, start, (rows_all, grads_all, segments_all))
    weight_grads = jnp.zeros(master.shape, jnp.float32).at[:, slots, :].set(bank_sum)
    filled = jnp.zeros((N_DP * CAP,), jnp.float32).at[slots].set(1.0)[None, :, None]
    step = step_count[0].astype(jnp.float32)
    new_master, new_first, new_second = adamw(master, weight_grads, first_moment, second_moment, step)
    new_master = new_master * filled
    new_first = new_first * filled
    new_second = new_second * filled
    small_new, small_first_new, small_second_new = adamw(small_params, small_sum, small_first, small_second, step)
    ema_new = average_keep * adapter_ema + (1.0 - average_keep) * small_new[2 * D:2 * D + NADAPT]
    return (outputs.reshape(TOKENS, D), input_grads.reshape(TOKENS, D), weight_grads, new_first, new_second, new_master, new_master.astype(jnp.bfloat16), small_sum, small_first_new, small_second_new, small_new, ema_new)
```

```python
import functools
import math

import jax
import jax.numpy as jnp
from jax import lax
from jax.experimental import pallas as pl
from jax.experimental.pallas import tpu as pltpu
from jax.sharding import PartitionSpec as P

D = 768
H = 12
HS = 64
FF = 3072
NB = 32
R = 48
PHM = 4
SEQ = 1024
NADAPT = 1696

highest = lax.Precision.HIGHEST
norm_epsilon = 1e-06
beta_first = 0.5
beta_second = 0.5
adam_epsilon = 1e-08
rate_per_step = 0.01
weight_decay = 0.1
average_keep = 0.75
masked_score = -1000000000.0

TILE = 128
WINDOW = 2 * SEQ - TILE
QUERY_TILE = 256
KEY_TILE = 256
VMEM_LIMIT = 48 * 1024 * 1024


def owner_slots(owners, devices, capacity):
    onehot = (owners[:, None] == jnp.arange(devices, dtype=jnp.int32)[None, :]).astype(jnp.int32)
    within = jnp.sum(jnp.cumsum(onehot, axis=0) * onehot, axis=1) - 1
    return owners * capacity + within


def unpack(packed):
    widths = (D, D, PHM**3, D, R, R, D, NB * H)
    pieces = []
    offset = 0
    for width in widths:
        pieces.append(packed[offset : offset + width])
        offset = offset + width
    gain_one, gain_two, mix_flat, down_left, down_right, up_left, up_right, table_flat = pieces
    adapter = (
        mix_flat.reshape(PHM, PHM, PHM),
        down_left.reshape(PHM, D // PHM),
        down_right.reshape(PHM, R // PHM),
        up_left.reshape(PHM, R // PHM),
        up_right.reshape(PHM, D // PHM),
    )
    return (gain_one, gain_two, adapter, table_flat.reshape(NB, H))


def adapter_apply(features, adapter):
    mix, down_left, down_right, up_left, up_right = adapter
    down_matrix = jnp.einsum(
        "iab,ip,iq->apbq", mix, down_left, down_right, precision=highest
    ).reshape(D, R)
    up_matrix = jnp.einsum("iab,iq,ip->aqbp", mix, up_left, up_right, precision=highest).reshape(
        R, D
    )
    hidden = jnp.dot(features, down_matrix, precision=highest)
    return features + jnp.dot(jax.nn.gelu(hidden, approximate=False), up_matrix, precision=highest)


def rms_norm(values, gain):
    return (
        values * lax.rsqrt(jnp.mean(values * values, axis=-1, keepdims=True) + norm_epsilon) * gain
    )


def contract(left, right, left_dim, right_dim):
    return lax.dot_general(
        left,
        right,
        (((left_dim,), (right_dim,)), ((), ())),
        preferred_element_type=jnp.float32,
    )


def attend_kernel(
    query_ref,
    key_ref,
    value_ref,
    bias_ref,
    segment_keys_ref,
    segment_queries_ref,
    exp_ref,
    out_ref,
    scale_ref,
    window,
    scores,
):
    for tile in range(WINDOW // TILE):
        base = WINDOW - TILE * tile
        row = jnp.broadcast_to(bias_ref[0, :, base - TILE : base + TILE], (TILE, 2 * TILE))
        rolled = pltpu.roll(row, TILE, 1, stride=1, stride_axis=0)
        window[TILE * tile : TILE * (tile + 1), :] = rolled[:, :TILE]
    keys = key_ref[...].T
    values = jnp.concatenate([value_ref[...], jnp.ones((16, SEQ), jnp.bfloat16)], axis=0)
    for q0 in range(0, SEQ, QUERY_TILE):
        queries = query_ref[:, q0 : q0 + QUERY_TILE]
        peak = jnp.full((8, QUERY_TILE), -jnp.inf, jnp.float32)
        for k0 in range(0, SEQ, KEY_TILE):
            raw = jnp.dot(keys[k0 : k0 + KEY_TILE], queries, preferred_element_type=jnp.float32)
            parts = []
            for l0 in range(0, QUERY_TILE, TILE):
                start = SEQ - TILE - (q0 + l0) + k0
                same_doc = (
                    segment_keys_ref[k0 : k0 + KEY_TILE, :]
                    == segment_queries_ref[:, q0 + l0 : q0 + l0 + TILE]
                )
                part = jnp.where(
                    same_doc,
                    raw[:, l0 : l0 + TILE] + window[start : start + KEY_TILE, :],
                    masked_score,
                )
                scores[k0 : k0 + KEY_TILE, l0 : l0 + TILE] = part
                parts.append(part)
            whole = jnp.concatenate(parts, axis=1)
            peak = jnp.maximum(peak, jnp.max(whole.reshape(KEY_TILE // 8, 8, QUERY_TILE), axis=0))
        peak = jnp.max(peak, axis=0, keepdims=True)
        total = jnp.zeros((HS + 16, QUERY_TILE), jnp.float32)
        for k0 in range(0, SEQ, KEY_TILE):
            exp_scores = jnp.exp(scores[k0 : k0 + KEY_TILE, :] - peak).astype(jnp.bfloat16)
            exp_ref[0, k0 : k0 + KEY_TILE, q0 : q0 + QUERY_TILE] = exp_scores
            total = total + jnp.dot(
                values[:, k0 : k0 + KEY_TILE], exp_scores, preferred_element_type=jnp.float32
            )
        scale = 1.0 / total[HS : HS + 1]
        scale_ref[0, :, q0 : q0 + QUERY_TILE] = scale
        out_ref[:, q0 : q0 + QUERY_TILE] = (total[:HS] * scale).astype(jnp.bfloat16)


def attend_back_kernel(
    query_ref,
    key_ref,
    value_ref,
    exp_ref,
    out_ref,
    scale_ref,
    out_grad_ref,
    query_grad_ref,
    key_grad_ref,
    value_grad_ref,
    offset_grad_ref,
    window,
    score_grads,
):
    scaled = out_grad_ref[...].astype(jnp.float32) * scale_ref[0]
    delta = jnp.sum(scaled * out_ref[...].astype(jnp.float32), axis=0, keepdims=True)
    scaled_low = scaled.astype(jnp.bfloat16)
    delta_high = delta.astype(jnp.bfloat16).astype(jnp.float32)
    delta_rest = delta - delta_high
    place = lax.broadcasted_iota(jnp.int32, (16, SEQ), 0)
    extra = jnp.where(
        place == 0,
        jnp.broadcast_to(-delta_high, (16, SEQ)),
        jnp.where(place == 1, jnp.broadcast_to(-delta_rest, (16, SEQ)), 0.0),
    ).astype(jnp.bfloat16)
    grads = jnp.concatenate([scaled_low, extra], axis=0)
    values = jnp.concatenate([value_ref[...], jnp.ones((16, SEQ), jnp.bfloat16)], axis=0).T
    window[...] = jnp.zeros_like(window)
    keys = key_ref[...]
    for q0 in range(0, SEQ, QUERY_TILE):
        total = jnp.zeros((HS, QUERY_TILE), jnp.float32)
        for k0 in range(0, SEQ, KEY_TILE):
            centered = jnp.dot(
                values[k0 : k0 + KEY_TILE],
                grads[:, q0 : q0 + QUERY_TILE],
                preferred_element_type=jnp.float32,
            )
            score_grad = centered * exp_ref[
                0, k0 : k0 + KEY_TILE, q0 : q0 + QUERY_TILE
            ].astype(jnp.float32)
            for l0 in range(0, QUERY_TILE, TILE):
                start = SEQ - TILE - (q0 + l0) + k0
                window[start : start + KEY_TILE, :] += score_grad[:, l0 : l0 + TILE]
            score_low = score_grad.astype(jnp.bfloat16)
            score_grads[k0 : k0 + KEY_TILE, q0 : q0 + QUERY_TILE] = score_low
            total = total + jnp.dot(
                keys[:, k0 : k0 + KEY_TILE], score_low, preferred_element_type=jnp.float32
            )
        query_grad_ref[:, q0 : q0 + QUERY_TILE] = total.astype(jnp.bfloat16)
    queries = query_ref[...].T
    scaled_rows = scaled_low.T
    for k0 in range(0, SEQ, KEY_TILE):
        key_grad = jnp.dot(
            score_grads[k0 : k0 + KEY_TILE, :], queries, preferred_element_type=jnp.float32
        )
        value_grad = jnp.dot(
            exp_ref[0, k0 : k0 + KEY_TILE, :], scaled_rows, preferred_element_type=jnp.float32
        )
        key_grad_ref[:, k0 : k0 + KEY_TILE] = key_grad.T.astype(jnp.bfloat16)
        value_grad_ref[:, k0 : k0 + KEY_TILE] = value_grad.T.astype(jnp.bfloat16)
    offset_grad_ref[...] = jnp.zeros_like(offset_grad_ref)
    for tile in range(WINDOW // TILE):
        base = WINDOW - TILE * tile
        block = window[TILE * tile : TILE * (tile + 1), :]
        folded = jnp.concatenate([jnp.zeros((TILE, TILE), jnp.float32), block], axis=1)
        rows = TILE // 2
        while rows >= 1:
            folded = folded[:rows] + pltpu.roll(folded[rows:], 2 * TILE - rows, 1)
            rows //= 2
        offset_grad_ref[0, :, base - TILE : base + TILE] += folded


def head_specs(group_heads):
    def rows(part):
        return pl.BlockSpec(
            (HS, SEQ),
            lambda h: ((h // group_heads) * 3 * group_heads + part * group_heads + h % group_heads, 0),
        )

    return [rows(0), rows(1), rows(2)]


def head_block():
    return pl.BlockSpec((HS, SEQ), lambda h: (h, 0))


def attend(projected, bias_rows, segment_keys, segment_queries, group_heads):
    return pl.pallas_call(
        attend_kernel,
        grid=(H,),
        in_specs=head_specs(group_heads)
        + [
            pl.BlockSpec((1, 1, 2 * SEQ), lambda h: (h, 0, 0)),
            pl.BlockSpec((SEQ, TILE), lambda h: (0, 0)),
            pl.BlockSpec((1, SEQ), lambda h: (0, 0)),
        ],
        out_specs=[
            pl.BlockSpec((1, SEQ, SEQ), lambda h: (h, 0, 0)),
            head_block(),
            pl.BlockSpec((1, 1, SEQ), lambda h: (h, 0, 0)),
        ],
        out_shape=[
            jax.ShapeDtypeStruct((H, SEQ, SEQ), jnp.bfloat16),
            jax.ShapeDtypeStruct((D, SEQ), jnp.bfloat16),
            jax.ShapeDtypeStruct((H, 1, SEQ), jnp.float32),
        ],
        scratch_shapes=[
            pltpu.VMEM((WINDOW, TILE), jnp.float32),
            pltpu.VMEM((SEQ, QUERY_TILE), jnp.float32),
        ],
        compiler_params=pltpu.CompilerParams(vmem_limit_bytes=VMEM_LIMIT),
        cost_estimate=pl.CostEstimate(
            flops=4 * H * SEQ * SEQ * 256, bytes_accessed=32 * 1024 * 1024, transcendentals=H * SEQ * SEQ
        ),
        name="attend",
    )(projected, projected, projected, bias_rows, segment_keys, segment_queries)


def attend_back(projected, exp_scores, attended, scale, attended_grad, group_heads):
    return pl.pallas_call(
        attend_back_kernel,
        grid=(H,),
        in_specs=head_specs(group_heads)
        + [
            pl.BlockSpec((1, SEQ, SEQ), lambda h: (h, 0, 0)),
            head_block(),
            pl.BlockSpec((1, 1, SEQ), lambda h: (h, 0, 0)),
            head_block(),
        ],
        out_specs=[
            head_block(),
            head_block(),
            head_block(),
            pl.BlockSpec((1, 1, 2 * SEQ), lambda h: (h, 0, 0)),
        ],
        out_shape=[jax.ShapeDtypeStruct((D, SEQ), jnp.bfloat16)] * 3
        + [jax.ShapeDtypeStruct((H, 1, 2 * SEQ), jnp.float32)],
        scratch_shapes=[
            pltpu.VMEM((WINDOW, TILE), jnp.float32),
            pltpu.VMEM((SEQ, SEQ), jnp.bfloat16),
        ],
        compiler_params=pltpu.CompilerParams(vmem_limit_bytes=VMEM_LIMIT),
        cost_estimate=pl.CostEstimate(
            flops=8 * H * SEQ * SEQ * 256, bytes_accessed=32 * 1024 * 1024, transcendentals=0
        ),
        name="attend_back",
    )(projected, projected, projected, exp_scores, attended, scale, attended_grad)


def feed_kernel(rows_ref, w_in_ref, w_down_ref, activ_ref, slope_ref, out_ref):
    step = pl.program_id(0)
    row_tile = 256

    @pl.when(step == 0)
    def _():
        out_ref[...] = jnp.zeros_like(out_ref)

    for r0 in range(0, SEQ, row_tile):
        pre = contract(rows_ref[r0 : r0 + row_tile, :], w_in_ref[...], 1, 1)
        cdf = 0.5 * (1.0 + lax.erf(pre * (1.0 / math.sqrt(2.0))))
        pdf = jnp.exp(-0.5 * pre * pre) * (1.0 / math.sqrt(2.0 * math.pi))
        activ = (pre * cdf).astype(jnp.bfloat16)
        activ_ref[r0 : r0 + row_tile, :] = activ
        slope_ref[r0 : r0 + row_tile, :] = (cdf + pre * pdf).astype(jnp.bfloat16)
        out_ref[r0 : r0 + row_tile, :] += jnp.dot(
            activ, w_down_ref[...], preferred_element_type=jnp.float32
        )


def feed(rows, w_in, w_down):
    width = 384
    tokens = rows.shape[0]
    return pl.pallas_call(
        feed_kernel,
        grid=(FF // width,),
        in_specs=[
            pl.BlockSpec((tokens, D), lambda j: (0, 0)),
            pl.BlockSpec((width, D), lambda j: (j, 0)),
            pl.BlockSpec((width, D), lambda j: (j, 0)),
        ],
        out_specs=[
            pl.BlockSpec((tokens, width), lambda j: (0, j)),
            pl.BlockSpec((tokens, width), lambda j: (0, j)),
            pl.BlockSpec((tokens, D), lambda j: (0, 0)),
        ],
        out_shape=[
            jax.ShapeDtypeStruct((tokens, FF), jnp.bfloat16),
            jax.ShapeDtypeStruct((tokens, FF), jnp.bfloat16),
            jax.ShapeDtypeStruct((tokens, D), jnp.float32),
        ],
        compiler_params=pltpu.CompilerParams(vmem_limit_bytes=VMEM_LIMIT),
        cost_estimate=pl.CostEstimate(
            flops=4 * tokens * FF * D,
            bytes_accessed=24 * 1024 * 1024,
            transcendentals=2 * tokens * FF,
        ),
        name="feed",
    )(rows, w_in, w_down)


def adamw(weights, grads, first, second, step):
    first_new = beta_first * first + (1.0 - beta_first) * grads
    second_new = beta_second * second + (1.0 - beta_second) * grads * grads
    first_hat = first_new / (1.0 - beta_first**step)
    second_hat = second_new / (1.0 - beta_second**step)
    weights_new = weights - rate_per_step * step * (
        first_hat / (jnp.sqrt(second_hat) + adam_epsilon) + weight_decay * weights
    )
    return (weights_new, first_new, second_new)


def per_device(
    tokens,
    cotangent,
    segment_ids,
    buckets,
    owners,
    master,
    first_moment,
    second_moment,
    small_params,
    small_first,
    small_second,
    adapter_ema,
    step_count,
):
    dp_count = lax.axis_size("dp")
    tensor_count = lax.axis_size("tensor")
    capacity = master.shape[1]
    group_heads = H // tensor_count
    head_rows = group_heads * HS
    hidden_rows = FF // tensor_count
    dp_pos = lax.axis_index("dp")
    tensor_pos = lax.axis_index("tensor")

    slots = owner_slots(owners, dp_count, capacity)
    gathered = lax.all_gather(master[0].astype(jnp.bfloat16), "dp", axis=0, tiled=True)
    ends = (0, 3 * head_rows, 4 * head_rows, 4 * head_rows + hidden_rows, owners.shape[0])
    w_qkv, w_out, w_in, w_down = [
        lax.all_gather(jnp.take(gathered, slots[low:high], axis=0), "tensor", axis=0, tiled=True)
        for low, high in zip(ends[:-1], ends[1:])
    ]

    gain_one, gain_two, adapter, table = unpack(small_params)
    bucket_onehot = (buckets[:, None] == jnp.arange(NB, dtype=jnp.int32)[None, :]).astype(
        jnp.float32
    )
    per_offset = contract(table, bucket_onehot, 0, 1)
    bias_rows = jnp.concatenate([jnp.zeros((H, 1), jnp.float32), per_offset[:, ::-1]], axis=1)
    segments = lax.dynamic_slice_in_dim(segment_ids, tensor_pos * SEQ, SEQ, 0)
    segment_keys = jnp.broadcast_to(segments[:, None], (SEQ, TILE))

    inputs_f = tokens.astype(jnp.float32)
    normed_one = rms_norm(inputs_f, gain_one).astype(jnp.bfloat16)
    projected = contract(w_qkv, normed_one, 1, 1).astype(jnp.bfloat16)
    exp_scores, attended, scale = attend(
        projected, bias_rows[:, None, :], segment_keys, segments[None, :], group_heads
    )
    mid = inputs_f + contract(attended, w_out, 0, 0)
    normed_two = rms_norm(mid, gain_two).astype(jnp.bfloat16)
    activ, slope, ffn_out = feed(normed_two, w_in, w_down)
    final, adapter_pull = jax.vjp(adapter_apply, ffn_out, adapter)
    layer_out = (mid + final).astype(jnp.bfloat16)

    out_grad = cotangent.astype(jnp.float32)
    ffn_grad, adapter_grad = adapter_pull(out_grad)
    ffn_grad = ffn_grad.astype(jnp.bfloat16)

    def reduce_rows(part):
        part = lax.psum_scatter(
            part.astype(jnp.bfloat16), "tensor", scatter_dimension=0, tiled=True
        )
        return lax.psum(part, "dp")

    pre_grad = (contract(ffn_grad, w_down, 1, 1) * slope.astype(jnp.float32)).astype(jnp.bfloat16)
    down_grad = reduce_rows(contract(activ, ffn_grad, 0, 0))
    in_grad = reduce_rows(contract(pre_grad, normed_two, 0, 0))
    normed_two_grad = jnp.dot(pre_grad, w_in, preferred_element_type=jnp.float32)
    _, norm_two_pull = jax.vjp(rms_norm, mid, gain_two)
    mid_extra, gain_two_grad = norm_two_pull(normed_two_grad)
    mid_grad = out_grad + mid_extra
    mid_grad_low = mid_grad.astype(jnp.bfloat16)
    attended_grad = contract(w_out, mid_grad_low, 1, 1).astype(jnp.bfloat16)
    out_weight_grad = reduce_rows(jnp.dot(attended, mid_grad_low, preferred_element_type=jnp.float32))
    query_grad, key_grad, value_grad, offset_grad = attend_back(
        projected, exp_scores, attended, scale, attended_grad, group_heads
    )
    proj_grad = jnp.stack(
        [
            part.reshape(tensor_count, head_rows, SEQ)
            for part in (query_grad, key_grad, value_grad)
        ],
        axis=1,
    ).reshape(3 * D, SEQ)
    qkv_grad = reduce_rows(jnp.dot(proj_grad, normed_one, preferred_element_type=jnp.float32))
    normed_one_grad = contract(proj_grad, w_qkv, 0, 0)
    _, norm_one_pull = jax.vjp(rms_norm, inputs_f, gain_one)
    input_extra, gain_one_grad = norm_one_pull(normed_one_grad)
    input_grad = (mid_grad + input_extra).astype(jnp.bfloat16)
    table_grad = jnp.dot(
        bucket_onehot.T, offset_grad[:, 0, 1:][:, ::-1].T, precision=highest
    )
    small_local = jnp.concatenate(
        [gain_one_grad, gain_two_grad]
        + [piece.reshape(-1) for piece in adapter_grad]
        + [table_grad.reshape(-1)]
    )
    small_total = lax.psum(small_local, ("dp", "tensor"))

    bank_grad = jnp.concatenate([qkv_grad, out_weight_grad, in_grad, down_grad], axis=0)
    own_slots = dp_pos * capacity + jnp.arange(capacity, dtype=jnp.int32)
    match = slots[None, :] == own_slots[:, None]
    own_filled = jnp.any(match, axis=1)
    own_rows = jnp.sum(
        jnp.where(match, jnp.arange(owners.shape[0], dtype=jnp.int32)[None, :], 0), axis=1
    )
    own_filled = own_filled.astype(jnp.float32)[:, None]
    owned_grad = jnp.take(bank_grad, own_rows, axis=0).astype(jnp.float32) * own_filled
    step = step_count[0].astype(jnp.float32)
    new_master, new_first, new_second = adamw(
        master[0], owned_grad, first_moment[0], second_moment[0], step
    )
    new_master = new_master * own_filled
    new_first = new_first * own_filled
    new_second = new_second * own_filled
    small_new, small_first_new, small_second_new = adamw(
        small_params, small_total, small_first, small_second, step
    )
    ema_new = average_keep * adapter_ema + (1.0 - average_keep) * small_new[2 * D : 2 * D + NADAPT]
    return (
        layer_out,
        input_grad,
        owned_grad[None],
        new_first[None],
        new_second[None],
        new_master[None],
        new_master.astype(jnp.bfloat16)[None],
        small_total,
        small_first_new,
        small_second_new,
        small_new,
        ema_new,
    )


def solution(mesh):
    token_spec = P(("dp", "tensor"), None)
    owner_spec = P("tensor", "dp", None)
    return jax.shard_map(
        per_device,
        mesh=mesh,
        in_specs=(token_spec, token_spec, P("dp"), P(), P())
        + (owner_spec,) * 3
        + (P(),) * 5,
        out_specs=(token_spec,) * 2 + (owner_spec,) * 5 + (P(),) * 5,
        check_vma=False,
    )
```

```python
import functools
import math

import jax
import jax.numpy as jnp
from jax import lax
from jax.experimental import pallas as pl
from jax.experimental.pallas import tpu as pltpu
from jax.sharding import PartitionSpec as P

D = 768
H = 12
HS = 64
FF = 3072
NB = 32
R = 48
PHM = 4
SEQ = 1024
NADAPT = 1696

highest = lax.Precision.HIGHEST
norm_epsilon = 1e-06
beta_first = 0.5
beta_second = 0.5
adam_epsilon = 1e-08
rate_per_step = 0.01
weight_decay = 0.1
average_keep = 0.75
masked_score = -1000000000.0

TILE = 128
WINDOW = 2 * SEQ - TILE
QUERY_TILE = 256
KEY_TILE = 256
VMEM_LIMIT = 48 * 1024 * 1024
MESH = pl.DeviceIdType.MESH


def unpack(packed):
    widths = (D, D, PHM**3, D, R, R, D, NB * H)
    pieces = []
    offset = 0
    for width in widths:
        pieces.append(packed[offset : offset + width])
        offset = offset + width
    gain_one, gain_two, mix_flat, down_left, down_right, up_left, up_right, table_flat = pieces
    adapter = (
        mix_flat.reshape(PHM, PHM, PHM),
        down_left.reshape(PHM, D // PHM),
        down_right.reshape(PHM, R // PHM),
        up_left.reshape(PHM, R // PHM),
        up_right.reshape(PHM, D // PHM),
    )
    return (gain_one, gain_two, adapter, table_flat.reshape(NB, H))


def adapter_apply(features, adapter):
    mix, down_left, down_right, up_left, up_right = adapter
    down_matrix = jnp.einsum(
        "iab,ip,iq->apbq", mix, down_left, down_right, precision=highest
    ).reshape(D, R)
    up_matrix = jnp.einsum("iab,iq,ip->aqbp", mix, up_left, up_right, precision=highest).reshape(
        R, D
    )
    hidden = jnp.dot(features, down_matrix, precision=highest)
    return features + jnp.dot(jax.nn.gelu(hidden, approximate=False), up_matrix, precision=highest)


def rms_norm(values, gain):
    return (
        values * lax.rsqrt(jnp.mean(values * values, axis=-1, keepdims=True) + norm_epsilon) * gain
    )


def contract(left, right, left_dim, right_dim):
    return lax.dot_general(
        left,
        right,
        (((left_dim,), (right_dim,)), ((), ())),
        preferred_element_type=jnp.float32,
    )


def bias_window(bias, window):
    for tile in range(WINDOW // TILE):
        base = WINDOW - TILE * tile
        row = jnp.broadcast_to(bias[:, base - TILE : base + TILE], (TILE, 2 * TILE))
        rolled = pltpu.roll(row, TILE, 1, stride=1, stride_axis=0)
        window[TILE * tile : TILE * (tile + 1), :] = rolled[:, :TILE]


def attend_head(
    query_rows, key_rows, value_rows, segment_keys_ref, segment_queries_ref, window, scores, exp_ref
):
    keys = key_rows.T
    values = jnp.concatenate([value_rows, jnp.ones((16, SEQ), jnp.bfloat16)], axis=0)
    outs, scales = [], []
    for q0 in range(0, SEQ, QUERY_TILE):
        queries = query_rows[:, q0 : q0 + QUERY_TILE]
        peak = jnp.full((8, QUERY_TILE), -jnp.inf, jnp.float32)
        for k0 in range(0, SEQ, KEY_TILE):
            raw = jnp.dot(keys[k0 : k0 + KEY_TILE], queries, preferred_element_type=jnp.float32)
            parts = []
            for l0 in range(0, QUERY_TILE, TILE):
                start = SEQ - TILE - (q0 + l0) + k0
                same_doc = (
                    segment_keys_ref[k0 : k0 + KEY_TILE, :]
                    == segment_queries_ref[:, q0 + l0 : q0 + l0 + TILE]
                )
                part = jnp.where(
                    same_doc,
                    raw[:, l0 : l0 + TILE] + window[start : start + KEY_TILE, :],
                    masked_score,
                )
                scores[k0 : k0 + KEY_TILE, l0 : l0 + TILE] = part
                parts.append(part)
            whole = jnp.concatenate(parts, axis=1)
            peak = jnp.maximum(peak, jnp.max(whole.reshape(KEY_TILE // 8, 8, QUERY_TILE), axis=0))
        peak = jnp.max(peak, axis=0, keepdims=True)
        total = jnp.zeros((HS + 16, QUERY_TILE), jnp.float32)
        for k0 in range(0, SEQ, KEY_TILE):
            exp_scores = jnp.exp(scores[k0 : k0 + KEY_TILE, :] - peak).astype(jnp.bfloat16)
            exp_ref[k0 : k0 + KEY_TILE, q0 : q0 + QUERY_TILE] = exp_scores
            total = total + jnp.dot(
                values[:, k0 : k0 + KEY_TILE], exp_scores, preferred_element_type=jnp.float32
            )
        scale = 1.0 / total[HS : HS + 1]
        scales.append(scale)
        outs.append((total[:HS] * scale).astype(jnp.bfloat16))
    return jnp.concatenate(outs, axis=1), jnp.concatenate(scales, axis=1)


def one_hot(place, shape, dim):
    hit = lax.broadcasted_iota(jnp.int32, shape, dim) == place
    return jnp.where(hit, 1.0, 0.0).astype(jnp.bfloat16)


def front_kernel(
    sizes,
    mine_ref,
    slot_place_ref,
    spread_place_ref,
    order_qkv_ref,
    order_out_ref,
    order_in_ref,
    order_down_ref,
    normed_ref,
    bias_ref,
    segment_keys_ref,
    segment_queries_ref,
    w_qkv_ref,
    w_out_ref,
    w_in_ref,
    w_down_ref,
    projected_ref,
    attended_ref,
    scale_ref,
    exp_ref,
    sent,
    received,
    spread,
    buf_qkv,
    buf_out,
    buf_in,
    buf_down,
    stage_out,
    stage_in,
    stage_down,
    window,
    scores,
    exp_stage,
    deal_send,
    deal_recv,
    gather_send,
    gather_recv,
    group_send,
    group_recv,
    local_sem,
    exp_sem,
):
    dp_count, pair_rows = sent.shape[0], sent.shape[1]
    tensor_count = w_qkv_ref.shape[0]
    heads = bias_ref.shape[0]
    group_heads = heads // tensor_count
    head_rows = group_heads * HS
    dp_pos, tensor_pos = lax.axis_index("dp"), lax.axis_index("tensor")
    core_peer = (dp_pos, tensor_pos + 1 - 2 * lax.rem(tensor_pos, 2))
    far_peer = (dp_pos, lax.rem(tensor_pos + 2, tensor_count))

    def dp_peer(m):
        return (lax.rem(dp_pos + m, dp_count), tensor_pos)

    def each_peer(run):
        def step(m, carry):
            run(m)
            return carry

        lax.fori_loop(1, dp_count, step, 0)

    barrier = pltpu.get_barrier_semaphore()

    def greet(m):
        pl.semaphore_signal(barrier, inc=1, device_id=dp_peer(m), device_id_type=MESH)

    each_peer(greet)
    for peer in (core_peer, far_peer):
        pl.semaphore_signal(barrier, inc=1, device_id=peer, device_id_type=MESH)

    place = slot_place_ref[...]
    mine = mine_ref[...]
    for m in range(dp_count):
        hot = one_hot(place - m * pair_rows, (pair_rows, mine.shape[0]), 0)
        sent[m] = jnp.dot(hot, mine, preferred_element_type=jnp.float32).astype(jnp.bfloat16)
    pl.semaphore_wait(barrier, dp_count + 1)

    def deal(m):
        return pltpu.make_async_remote_copy(
            sent.at[m],
            received.at[m],
            deal_send.at[m],
            deal_recv.at[m],
            device_id=dp_peer(m),
            device_id_type=MESH,
        )

    each_peer(lambda m: deal(m).start())
    received[0] = sent[0]
    each_peer(lambda m: deal(m).wait())
    rows = spread.shape[0]
    hot = one_hot(spread_place_ref[...], (rows, dp_count * pair_rows), 0)
    spread[...] = jnp.dot(
        hot, received[...].reshape(dp_count * pair_rows, D), preferred_element_type=jnp.float32
    ).astype(jnp.bfloat16)

    bufs = (buf_qkv, buf_out, buf_in, buf_down)
    orders = (order_qkv_ref, order_out_ref, order_in_ref, order_down_ref)
    stages = (w_qkv_ref.at[0], stage_out, stage_in, stage_down)
    finals = (w_qkv_ref, w_out_ref, w_in_ref, w_down_ref)
    offsets = [sum(buf.shape[1] for buf in bufs[:role]) for role in range(len(bufs))]

    def gather(role, m):
        count = bufs[role].shape[1]
        return pltpu.make_async_remote_copy(
            spread.at[pl.ds(offsets[role], count)],
            bufs[role].at[m],
            gather_send.at[role, m],
            gather_recv.at[role, m],
            device_id=dp_peer(m),
            device_id_type=MESH,
        )

    def start_gather(role):
        each_peer(lambda m: gather(role, m).start())
        bufs[role][0] = spread[offsets[role] : offsets[role] + bufs[role].shape[1], :]

    def order(role):
        each_peer(lambda m: gather(role, m).wait())
        count = bufs[role].shape[1]
        source = bufs[role][...].reshape(dp_count * count, D)
        step = 192
        for r0 in range(0, sizes[role], step):
            hot = one_hot(orders[role][r0 : r0 + step, :], (step, dp_count * count), 1)
            stages[role][r0 : r0 + step, :] = jnp.dot(
                hot, source, preferred_element_type=jnp.float32
            ).astype(jnp.bfloat16)

    def share(role, part):
        src, slot, peer = (
            (stages[role], 1, core_peer),
            (stages[role], 2, far_peer),
            (finals[role].at[2], 3, core_peer),
        )[part]
        return pltpu.make_async_remote_copy(
            src,
            finals[role].at[slot],
            group_send.at[role, part],
            group_recv.at[role, part],
            device_id=peer,
            device_id_type=MESH,
        )

    def keep(role):
        return pltpu.make_async_copy(stages[role], finals[role].at[0], local_sem.at[role])

    def start_share(role):
        order(role)
        share(role, 0).start()
        share(role, 1).start()
        if role > 0:
            keep(role).start()

    def forward(role):
        share(role, 1).wait_recv()
        share(role, 2).start()

    start_gather(0)
    start_share(0)
    start_gather(1)
    start_gather(2)

    def head_step(i, carry):
        group, head = lax.div(i, group_heads), lax.rem(i, group_heads)

        @pl.when(i == 1)
        def _():
            start_share(1)

        @pl.when(i == group_heads)
        def _():
            share(0, 0).wait_recv()

        @pl.when(i == 2 * group_heads)
        def _():
            forward(0)

        @pl.when(i == 3 * group_heads)
        def _():
            share(0, 2).wait_recv()
            forward(1)
            start_gather(3)

        @pl.when(head == 0)
        def _():
            projected_ref[group] = contract(w_qkv_ref[group], normed_ref[...], 1, 1).astype(
                jnp.bfloat16
            )

        def head_part(part):
            start = pl.multiple_of(part * head_rows + head * HS, HS)
            return projected_ref[group, pl.ds(start, HS), :]

        slot = lax.rem(i, 2)

        def save(head_index, slot):
            return pltpu.make_async_copy(
                exp_stage.at[slot], exp_ref.at[head_index], exp_sem.at[slot]
            )

        @pl.when(i >= 2)
        def _():
            save(i - 2, slot).wait()

        bias_window(bias_ref[i], window)
        attended, scale = attend_head(
            head_part(0),
            head_part(1),
            head_part(2),
            segment_keys_ref,
            segment_queries_ref,
            window,
            scores,
            exp_stage.at[slot],
        )
        attended_ref[pl.ds(pl.multiple_of(i * HS, HS), HS), :] = attended
        scale_ref[i] = scale
        save(i, slot).start()
        return carry

    lax.fori_loop(0, heads, head_step, 0)
    for i in (heads - 2, heads - 1):
        pltpu.make_async_copy(exp_stage.at[i % 2], exp_ref.at[i], exp_sem.at[i % 2]).wait()
    start_share(2)
    start_share(3)
    forward(2)
    forward(3)
    for role in range(len(bufs)):
        share(role, 0).wait_send()
        share(role, 1).wait_send()
        share(role, 2).wait_send()
        if role > 0:
            share(role, 0).wait_recv()
            share(role, 2).wait_recv()
            keep(role).wait()


def front(mine, slot_place, spread_place, orders, local_sizes, pair_rows, normed, bias, segments):
    dp_count, tensor_count = lax.axis_size("dp"), lax.axis_size("tensor")
    sizes = [order.shape[0] for order in orders]
    heads = bias.shape[0]
    low = jnp.bfloat16
    dma = pltpu.SemaphoreType.DMA
    roles = len(sizes)
    whole = pl.BlockSpec(memory_space=pltpu.VMEM)
    away = pl.BlockSpec(memory_space=pl.ANY)
    return pl.pallas_call(
        functools.partial(front_kernel, sizes),
        in_specs=[whole] * 11,
        out_specs=[whole, away, away, away, whole, whole, whole, away],
        out_shape=[jax.ShapeDtypeStruct((tensor_count, size, D), low) for size in sizes]
        + [
            jax.ShapeDtypeStruct((tensor_count, sizes[0], SEQ), low),
            jax.ShapeDtypeStruct((heads * HS, SEQ), low),
            jax.ShapeDtypeStruct((heads, 1, SEQ), jnp.float32),
            jax.ShapeDtypeStruct((heads, SEQ, SEQ), low),
        ],
        scratch_shapes=[
            pltpu.VMEM((dp_count, pair_rows, D), low),
            pltpu.VMEM((dp_count, pair_rows, D), low),
            pltpu.VMEM((sum(local_sizes), D), low),
        ]
        + [pltpu.VMEM((dp_count, size, D), low) for size in local_sizes]
        + [pltpu.VMEM((size, D), low) for size in sizes[1:]]
        + [
            pltpu.VMEM((WINDOW, TILE), jnp.float32),
            pltpu.VMEM((SEQ, QUERY_TILE), jnp.float32),
            pltpu.VMEM((2, SEQ, SEQ), low),
            dma((dp_count,)),
            dma((dp_count,)),
            dma((roles, dp_count)),
            dma((roles, dp_count)),
            dma((roles, 3)),
            dma((roles, 3)),
            dma((roles,)),
            dma((2,)),
        ],
        compiler_params=pltpu.CompilerParams(
            collective_id=1, has_side_effects=True, vmem_limit_bytes=56 * 1024 * 1024
        ),
        cost_estimate=pl.CostEstimate(
            flops=10 * heads * SEQ * SEQ * 256,
            bytes_accessed=64 * 1024 * 1024,
            transcendentals=heads * SEQ * SEQ,
        ),
        name="front",
    )(
        mine,
        slot_place[None, :],
        spread_place[None, :],
        *[order[:, None] for order in orders],
        normed,
        bias,
        jnp.broadcast_to(segments[:, None], (SEQ, TILE)),
        segments[None, :],
    )


def attend_back_kernel(
    query_ref,
    key_ref,
    value_ref,
    exp_ref,
    out_ref,
    scale_ref,
    out_grad_ref,
    proj_grad_ref,
    offset_grad_ref,
    window,
    score_grads,
):
    scaled = out_grad_ref[...].astype(jnp.float32) * scale_ref[0]
    delta = jnp.sum(scaled * out_ref[0].astype(jnp.float32), axis=0, keepdims=True)
    scaled_low = scaled.astype(jnp.bfloat16)
    delta_high = delta.astype(jnp.bfloat16).astype(jnp.float32)
    delta_rest = delta - delta_high
    place = lax.broadcasted_iota(jnp.int32, (16, SEQ), 0)
    extra = jnp.where(
        place == 0,
        jnp.broadcast_to(-delta_high, (16, SEQ)),
        jnp.where(place == 1, jnp.broadcast_to(-delta_rest, (16, SEQ)), 0.0),
    ).astype(jnp.bfloat16)
    grads = jnp.concatenate([scaled_low, extra], axis=0)
    values = jnp.concatenate([value_ref[0], jnp.ones((16, SEQ), jnp.bfloat16)], axis=0).T
    window[...] = jnp.zeros_like(window)
    keys = key_ref[0]
    for q0 in range(0, SEQ, QUERY_TILE):
        total = jnp.zeros((HS, QUERY_TILE), jnp.float32)
        for k0 in range(0, SEQ, KEY_TILE):
            centered = jnp.dot(
                values[k0 : k0 + KEY_TILE],
                grads[:, q0 : q0 + QUERY_TILE],
                preferred_element_type=jnp.float32,
            )
            score_grad = centered * exp_ref[
                0, k0 : k0 + KEY_TILE, q0 : q0 + QUERY_TILE
            ].astype(jnp.float32)
            for l0 in range(0, QUERY_TILE, TILE):
                start = SEQ - TILE - (q0 + l0) + k0
                window[start : start + KEY_TILE, :] += score_grad[:, l0 : l0 + TILE]
            score_low = score_grad.astype(jnp.bfloat16)
            score_grads[k0 : k0 + KEY_TILE, q0 : q0 + QUERY_TILE] = score_low
            total = total + jnp.dot(
                keys[:, k0 : k0 + KEY_TILE], score_low, preferred_element_type=jnp.float32
            )
        proj_grad_ref[0, 0, :, q0 : q0 + QUERY_TILE] = total.astype(jnp.bfloat16)
    queries = query_ref[0].T
    scaled_rows = scaled_low.T
    for k0 in range(0, SEQ, KEY_TILE):
        key_grad = jnp.dot(
            score_grads[k0 : k0 + KEY_TILE, :], queries, preferred_element_type=jnp.float32
        )
        value_grad = jnp.dot(
            exp_ref[0, k0 : k0 + KEY_TILE, :], scaled_rows, preferred_element_type=jnp.float32
        )
        proj_grad_ref[1, 0, :, k0 : k0 + KEY_TILE] = key_grad.T.astype(jnp.bfloat16)
        proj_grad_ref[2, 0, :, k0 : k0 + KEY_TILE] = value_grad.T.astype(jnp.bfloat16)
    offset_grad_ref[...] = jnp.zeros_like(offset_grad_ref)
    for tile in range(WINDOW // TILE):
        base = WINDOW - TILE * tile
        block = window[TILE * tile : TILE * (tile + 1), :]
        folded = jnp.concatenate([jnp.zeros((TILE, TILE), jnp.float32), block], axis=1)
        rows = TILE // 2
        while rows >= 1:
            folded = folded[:rows] + pltpu.roll(folded[rows:], 2 * TILE - rows, 1)
            rows //= 2
        offset_grad_ref[0, :, base - TILE : base + TILE] += folded


def attend_back(group, projected, exp_scores, attended, scale, attended_grad):
    heads = H // projected.shape[0]
    first = group * heads
    return pl.pallas_call(
        attend_back_kernel,
        grid=(heads,),
        in_specs=[
            pl.BlockSpec((1, HS, SEQ), lambda h, part=part: (group, part * heads + h, 0))
            for part in range(3)
        ]
        + [
            pl.BlockSpec((1, SEQ, SEQ), lambda h: (first + h, 0, 0)),
            pl.BlockSpec((1, HS, SEQ), lambda h: (group, h, 0)),
            pl.BlockSpec((1, 1, SEQ), lambda h: (first + h, 0, 0)),
            pl.BlockSpec((HS, SEQ), lambda h: (h, 0)),
        ],
        out_specs=[
            pl.BlockSpec((3, 1, HS, SEQ), lambda h: (0, h, 0, 0)),
            pl.BlockSpec((1, 1, 2 * SEQ), lambda h: (h, 0, 0)),
        ],
        out_shape=[
            jax.ShapeDtypeStruct((3, heads, HS, SEQ), jnp.bfloat16),
            jax.ShapeDtypeStruct((heads, 1, 2 * SEQ), jnp.float32),
        ],
        scratch_shapes=[
            pltpu.VMEM((WINDOW, TILE), jnp.float32),
            pltpu.VMEM((SEQ, SEQ), jnp.bfloat16),
        ],
        compiler_params=pltpu.CompilerParams(vmem_limit_bytes=VMEM_LIMIT),
        cost_estimate=pl.CostEstimate(
            flops=12 * heads * SEQ * SEQ * 256, bytes_accessed=3 * heads * SEQ * SEQ, transcendentals=0
        ),
        name="attend_back",
    )(projected, projected, projected, exp_scores, attended, scale, attended_grad)


def feed_kernel(rows_ref, w_in_ref, w_down_ref, before_ref, activ_ref, slope_ref, out_ref):
    row_tile = 256

    @pl.when(pl.program_id(0) == 0)
    def _():
        out_ref[...] = before_ref[...]

    for r0 in range(0, SEQ, row_tile):
        pre = contract(rows_ref[r0 : r0 + row_tile, :], w_in_ref[...], 1, 1)
        cdf = 0.5 * (1.0 + lax.erf(pre * (1.0 / math.sqrt(2.0))))
        pdf = jnp.exp(-0.5 * pre * pre) * (1.0 / math.sqrt(2.0 * math.pi))
        activ = (pre * cdf).astype(jnp.bfloat16)
        activ_ref[r0 : r0 + row_tile, :] = activ
        slope_ref[r0 : r0 + row_tile, :] = (cdf + pre * pdf).astype(jnp.bfloat16)
        out_ref[r0 : r0 + row_tile, :] += jnp.dot(
            activ, w_down_ref[...], preferred_element_type=jnp.float32
        )


def feed(rows, w_in, w_down, before):
    width = 384
    tokens = rows.shape[0]
    hidden = w_in.shape[0]
    return pl.pallas_call(
        feed_kernel,
        grid=(hidden // width,),
        in_specs=[
            pl.BlockSpec((tokens, D), lambda j: (0, 0)),
            pl.BlockSpec((width, D), lambda j: (j, 0)),
            pl.BlockSpec((width, D), lambda j: (j, 0)),
            pl.BlockSpec((tokens, D), lambda j: (0, 0)),
        ],
        out_specs=[
            pl.BlockSpec((tokens, width), lambda j: (0, j)),
            pl.BlockSpec((tokens, width), lambda j: (0, j)),
            pl.BlockSpec((tokens, D), lambda j: (0, 0)),
        ],
        out_shape=[
            jax.ShapeDtypeStruct((tokens, hidden), jnp.bfloat16),
            jax.ShapeDtypeStruct((tokens, hidden), jnp.bfloat16),
            jax.ShapeDtypeStruct((tokens, D), jnp.float32),
        ],
        compiler_params=pltpu.CompilerParams(vmem_limit_bytes=VMEM_LIMIT),
        cost_estimate=pl.CostEstimate(
            flops=8 * tokens * hidden * D,
            bytes_accessed=10 * 1024 * 1024,
            transcendentals=2 * tokens * hidden,
        ),
        name="feed",
    )(rows, w_in, w_down, before)


def select_kernel(by_row, count, place_ref, *refs):
    blocks, out_ref = refs[:-1], refs[-1]
    total = jnp.zeros(out_ref.shape, jnp.float32)
    offset = 0
    for block in blocks:
        rows = block.shape[0]
        shape = (count, rows)
        if by_row:
            hit = lax.broadcasted_iota(jnp.int32, shape, 1) + offset == place_ref[...]
        else:
            hit = lax.broadcasted_iota(jnp.int32, shape, 0) == place_ref[...]
        hit = jnp.where(hit, 1.0, 0.0).astype(jnp.bfloat16)
        total = total + jnp.dot(hit, block[...], preferred_element_type=jnp.float32)
        offset += rows
    out_ref[...] = total.astype(out_ref.dtype)


def select_rows(blocks, count, source=None, target=None, dtype=jnp.bfloat16):
    if len(blocks) > 16:
        blocks = [jnp.concatenate(blocks, axis=0)]
    place = source[:, None] if target is None else target[None, :]
    total = sum(block.shape[0] for block in blocks)
    return pl.pallas_call(
        functools.partial(select_kernel, target is None, count),
        out_shape=jax.ShapeDtypeStruct((count, D), dtype),
        compiler_params=pltpu.CompilerParams(vmem_limit_bytes=VMEM_LIMIT),
        cost_estimate=pl.CostEstimate(
            flops=2 * count * total * D, bytes_accessed=2 * (count + total) * D, transcendentals=0
        ),
        name="select_rows",
    )(place, *blocks)


def adamw(weights, grads, first, second, step):
    first_new = beta_first * first + (1.0 - beta_first) * grads
    second_new = beta_second * second + (1.0 - beta_second) * grads * grads
    first_hat = first_new / (1.0 - beta_first**step)
    second_hat = second_new / (1.0 - beta_second**step)
    weights_new = weights - rate_per_step * step * (
        first_hat / (jnp.sqrt(second_hat) + adam_epsilon) + weight_decay * weights
    )
    return (weights_new, first_new, second_new)


def per_device(
    tokens,
    cotangent,
    segment_ids,
    buckets,
    owners,
    master,
    first_moment,
    second_moment,
    small_params,
    small_first,
    small_second,
    adapter_ema,
    step_count,
):
    dp_count = lax.axis_size("dp")
    tensor_count = lax.axis_size("tensor")
    capacity = master.shape[1]
    group_heads = H // tensor_count
    head_rows = group_heads * HS
    hidden_rows = FF // tensor_count
    dp_pos = lax.axis_index("dp")
    tensor_pos = lax.axis_index("tensor")

    ends = (0, 3 * head_rows, 4 * head_rows, 4 * head_rows + hidden_rows, owners.shape[0])
    sizes = [high - low for low, high in zip(ends[:-1], ends[1:])]
    roles = len(sizes)

    pair_rows = -(-((capacity + roles * (dp_count - 1)) // dp_count) // 16) * 16
    owner_hot = (owners[:, None] == jnp.arange(dp_count, dtype=jnp.int32)[None, :]).astype(jnp.int32)
    counts = jnp.stack(
        [jnp.sum(owner_hot[low:high], axis=0) for low, high in zip(ends[:-1], ends[1:])]
    )
    dps = jnp.arange(dp_count, dtype=jnp.int32)
    starts = jnp.sum(
        jnp.where(dps[None, :] < dps[:, None], counts[:, None, :], 0), axis=2, dtype=jnp.int32
    )
    role_ids = jnp.arange(roles, dtype=jnp.int32)
    earlier = role_ids[None, :] < role_ids[:, None]
    role_starts = jnp.sum(jnp.where(earlier[:, :, None], counts[None], 0), axis=1, dtype=jnp.int32)

    def hits(first, number, target):
        return (first + number - 1 - target) // dp_count - (first - 1 - target) // dp_count

    def own(values):
        return lax.dynamic_index_in_dim(values, dp_pos, values.ndim - 1, keepdims=False)

    slot = jnp.arange(capacity, dtype=jnp.int32)
    slot_place = jnp.full((capacity,), -1, jnp.int32)
    own_counts, own_starts, own_role_starts = own(counts), own(starts), own(role_starts)
    for role in range(roles):
        inside = (slot >= own_role_starts[role]) & (
            slot < own_role_starts[role] + own_counts[role]
        )
        rank = slot - own_role_starts[role]
        target = (own_starts[role] + rank) % dp_count
        place = rank // dp_count
        for other in range(role):
            place = place + hits(own_starts[other], own_counts[other], target)
        slot_place = jnp.where(
            inside, ((target - dp_pos) % dp_count) * pair_rows + place, slot_place
        )
    local_sizes = [-(-size // dp_count // 16) * 16 for size in sizes]
    local_starts = [sum(local_sizes[:role]) for role in range(roles)]
    source_dp = (dp_pos - dps) % dp_count
    sent_counts, sent_starts = counts[:, source_dp], starts[:, source_dp]
    pair_place = jnp.arange(pair_rows, dtype=jnp.int32)[None, :]
    spread_place = jnp.full((dp_count, pair_rows), -1, jnp.int32)
    passed = jnp.zeros((dp_count, 1), jnp.int32)
    for role in range(roles):
        number = hits(sent_starts[role], sent_counts[role], dp_pos)[:, None]
        first = sent_starts[role] + (dp_pos - sent_starts[role]) % dp_count
        rank = pair_place - passed
        local = local_starts[role] + first[:, None] // dp_count + rank
        spread_place = jnp.where((rank >= 0) & (rank < number), local, spread_place)
        passed = passed + number
    spread_place = spread_place.reshape(-1)
    below = jnp.cumsum(owner_hot, axis=0) - 1
    row_target = []
    row_rank = []
    for role, (low, high) in enumerate(zip(ends[:-1], ends[1:])):
        number = jnp.sum(
            owner_hot[low:high] * (below[low:high] - role_starts[role] + starts[role]), axis=1
        )
        row_target.append(number % dp_count)
        row_rank.append(number // dp_count)

    def swap(values, axis, bit):
        count = lax.axis_size(axis)
        return lax.ppermute(values, axis, [(i, i ^ bit) for i in range(count)])

    orders = [
        ((dp_pos - row_target[role]) % dp_count) * local_sizes[role] + row_rank[role]
        for role in range(roles)
    ]

    gain_one, gain_two, adapter, table = unpack(small_params)
    bucket_onehot = (buckets[:, None] == jnp.arange(NB, dtype=jnp.int32)[None, :]).astype(
        jnp.float32
    )
    per_offset = lax.dot_general(
        table, bucket_onehot, (((0,), (1,)), ((), ())), precision=highest
    )
    bias_rows = jnp.concatenate([jnp.zeros((H, 1), jnp.float32), per_offset[:, ::-1]], axis=1)
    group_order = jnp.arange(tensor_count, dtype=jnp.int32) ^ tensor_pos
    bias_rows = bias_rows.reshape(tensor_count, group_heads, 2 * SEQ)[group_order]
    bias_rows = bias_rows.reshape(H, 1, 2 * SEQ)
    segments = lax.dynamic_slice_in_dim(segment_ids, tensor_pos * SEQ, SEQ, 0)

    inputs_f = tokens.astype(jnp.float32)
    normed_one = rms_norm(inputs_f, gain_one).astype(jnp.bfloat16)
    groups = range(tensor_count)
    w_qkv, w_out, w_in, w_down, projected, attended, scale, exp_scores = front(
        master[0].astype(jnp.bfloat16),
        slot_place,
        spread_place,
        orders,
        local_sizes,
        pair_rows,
        normed_one,
        bias_rows,
        segments,
    )
    attended = attended.reshape(tensor_count, head_rows, SEQ)
    mid = inputs_f
    for k in groups:
        mid = mid + contract(attended[k], w_out[k], 0, 0)
    normed_two = rms_norm(mid, gain_two).astype(jnp.bfloat16)
    activ, slope = [], []
    ffn_out = jnp.zeros(mid.shape, jnp.float32)
    for k in groups:
        part, part_slope, ffn_out = feed(normed_two, w_in[k], w_down[k], ffn_out)
        activ.append(part)
        slope.append(part_slope)
    final, adapter_pull = jax.vjp(adapter_apply, ffn_out, adapter)
    layer_out = (mid + final).astype(jnp.bfloat16)

    out_grad = cotangent.astype(jnp.float32)
    ffn_grad, adapter_grad = adapter_pull(out_grad)
    ffn_grad = ffn_grad.astype(jnp.bfloat16)

    def low_add(left, right):
        return (left.astype(jnp.float32) + right.astype(jnp.float32)).astype(jnp.bfloat16)

    def to_own(parts):
        total = low_add(parts[0], swap(parts[1], "tensor", 1))
        for bit in range(2, tensor_count, 2):
            pair = low_add(parts[bit], swap(parts[bit + 1], "tensor", 1))
            total = low_add(total, swap(pair, "tensor", bit))
        return total

    def to_spread(role, parts):
        total = to_own(parts)
        place = row_target[role] * local_sizes[role] + row_rank[role]
        total = select_rows([total], dp_count * local_sizes[role], target=place)
        total = lax.all_to_all(
            total.reshape(dp_count, local_sizes[role], D),
            "dp",
            split_axis=0,
            concat_axis=0,
            tiled=True,
        )
        return jnp.sum(total.astype(jnp.float32), axis=0).astype(jnp.bfloat16)

    back = list(groups)[::-1]
    normed_two_grad = jnp.zeros(mid.shape, jnp.float32)
    down_grad, in_grad = [None] * tensor_count, [None] * tensor_count
    for k in back:
        pre_grad = (contract(ffn_grad, w_down[k], 1, 1) * slope[k].astype(jnp.float32)).astype(
            jnp.bfloat16
        )
        down_grad[k] = contract(activ[k], ffn_grad, 0, 0).astype(jnp.bfloat16)
        in_grad[k] = contract(pre_grad, normed_two, 0, 0).astype(jnp.bfloat16)
        normed_two_grad = normed_two_grad + jnp.dot(
            pre_grad, w_in[k], preferred_element_type=jnp.float32
        )
    down_grad = to_spread(3, down_grad)
    in_grad = to_spread(2, in_grad)
    _, norm_two_pull = jax.vjp(rms_norm, mid, gain_two)
    mid_extra, gain_two_grad = norm_two_pull(normed_two_grad)
    mid_grad = out_grad + mid_extra
    mid_grad_low = mid_grad.astype(jnp.bfloat16)
    out_weight_grad = to_spread(
        1,
        [
            jnp.dot(attended[k], mid_grad_low, preferred_element_type=jnp.float32).astype(
                jnp.bfloat16
            )
            for k in groups
        ],
    )
    normed_one_grad = jnp.zeros(mid.shape, jnp.float32)
    qkv_grad, offset_grad = [None] * tensor_count, [None] * tensor_count
    for k in back:
        attended_grad = contract(w_out[k], mid_grad_low, 1, 1).astype(jnp.bfloat16)
        proj_grad, offset_grad[k] = attend_back(
            k, projected, exp_scores, attended, scale, attended_grad
        )
        proj_grad = proj_grad.reshape(3 * head_rows, SEQ)
        qkv_grad[k] = jnp.dot(proj_grad, normed_one, preferred_element_type=jnp.float32).astype(
            jnp.bfloat16
        )
        normed_one_grad = normed_one_grad + contract(proj_grad, w_qkv[k], 0, 0)
    qkv_grad = to_spread(0, qkv_grad)
    _, norm_one_pull = jax.vjp(rms_norm, inputs_f, gain_one)
    input_extra, gain_one_grad = norm_one_pull(normed_one_grad)
    input_grad = (mid_grad + input_extra).astype(jnp.bfloat16)
    offset_all = jnp.stack(offset_grad)
    offset_all = offset_all[group_order].reshape(H, 2 * SEQ)
    table_grad = jnp.dot(bucket_onehot.T, offset_all[:, 1:][:, ::-1].T, precision=highest)
    small_total = jnp.concatenate(
        [gain_one_grad, gain_two_grad]
        + [piece.reshape(-1) for piece in adapter_grad]
        + [table_grad.reshape(-1)]
    )
    for axis, count in (("tensor", tensor_count), ("dp", dp_count)):
        bit = 1
        while bit < count:
            small_total = small_total + swap(small_total, axis, bit)
            bit *= 2

    bank_grad = jnp.concatenate([qkv_grad, out_weight_grad, in_grad, down_grad], axis=0)
    sent = select_rows(
        [bank_grad],
        dp_count * pair_rows,
        source=spread_place.reshape(dp_count, pair_rows)[source_dp].reshape(-1),
    )
    received = lax.all_to_all(
        sent.reshape(dp_count, pair_rows, D), "dp", split_axis=0, concat_axis=0, tiled=True
    )
    back_place = jnp.where(
        slot_place >= 0,
        (slot_place // pair_rows + dp_pos) % dp_count * pair_rows + slot_place % pair_rows,
        -1,
    )
    owned_grad = select_rows(
        [received.reshape(-1, D)], capacity, source=back_place, dtype=jnp.float32
    )
    own_filled = (slot_place >= 0).astype(jnp.float32)[:, None]
    step = step_count[0].astype(jnp.float32)
    new_master, new_first, new_second = adamw(
        master[0], owned_grad, first_moment[0], second_moment[0], step
    )
    new_master = new_master * own_filled
    new_first = new_first * own_filled
    new_second = new_second * own_filled
    small_new, small_first_new, small_second_new = adamw(
        small_params, small_total, small_first, small_second, step
    )
    ema_new = average_keep * adapter_ema + (1.0 - average_keep) * small_new[2 * D : 2 * D + NADAPT]
    return (
        layer_out,
        input_grad,
        owned_grad[None],
        new_first[None],
        new_second[None],
        new_master[None],
        new_master.astype(jnp.bfloat16)[None],
        small_total,
        small_first_new,
        small_second_new,
        small_new,
        ema_new,
    )


def solution(mesh):
    token_spec = P(("dp", "tensor"), None)
    owner_spec = P("tensor", "dp", None)
    return jax.shard_map(
        per_device,
        mesh=mesh,
        in_specs=(token_spec, token_spec, P("dp"), P(), P())
        + (owner_spec,) * 3
        + (P(),) * 5,
        out_specs=(token_spec,) * 2 + (owner_spec,) * 5 + (P(),) * 5,
        check_vma=False,
    )
```

```python
import functools
import math

import jax
import jax.numpy as jnp
from jax import lax
from jax.experimental import pallas as pl
from jax.experimental.pallas import tpu as pltpu
from jax.sharding import PartitionSpec as P

D = 768
H = 12
HS = 64
FF = 3072
NB = 32
R = 48
PHM = 4
SEQ = 1024
NADAPT = 1696

highest = lax.Precision.HIGHEST
norm_epsilon = 1e-06
beta_first = 0.5
beta_second = 0.5
adam_epsilon = 1e-08
rate_per_step = 0.01
weight_decay = 0.1
average_keep = 0.75
masked_score = -1000000000.0

TILE = 128
WINDOW = 2 * SEQ - TILE
QUERY_TILE = 256
KEY_TILE = 256
VMEM_LIMIT = 48 * 1024 * 1024
MESH = pl.DeviceIdType.MESH


def unpack(packed):
    widths = (D, D, PHM**3, D, R, R, D, NB * H)
    pieces = []
    offset = 0
    for width in widths:
        pieces.append(packed[offset : offset + width])
        offset = offset + width
    gain_one, gain_two, mix_flat, down_left, down_right, up_left, up_right, table_flat = pieces
    adapter = (
        mix_flat.reshape(PHM, PHM, PHM),
        down_left.reshape(PHM, D // PHM),
        down_right.reshape(PHM, R // PHM),
        up_left.reshape(PHM, R // PHM),
        up_right.reshape(PHM, D // PHM),
    )
    return (gain_one, gain_two, adapter, table_flat.reshape(NB, H))


def adapter_apply(features, adapter):
    mix, down_left, down_right, up_left, up_right = adapter
    down_matrix = jnp.einsum(
        "iab,ip,iq->apbq", mix, down_left, down_right, precision=highest
    ).reshape(D, R)
    up_matrix = jnp.einsum("iab,iq,ip->aqbp", mix, up_left, up_right, precision=highest).reshape(
        R, D
    )
    hidden = jnp.dot(features, down_matrix, precision=highest)
    return features + jnp.dot(jax.nn.gelu(hidden, approximate=False), up_matrix, precision=highest)


def rms_norm(values, gain):
    return (
        values * lax.rsqrt(jnp.mean(values * values, axis=-1, keepdims=True) + norm_epsilon) * gain
    )


def contract(left, right, left_dim, right_dim):
    return lax.dot_general(
        left,
        right,
        (((left_dim,), (right_dim,)), ((), ())),
        preferred_element_type=jnp.float32,
    )


def bias_window(bias, window):
    for tile in range(WINDOW // TILE):
        base = WINDOW - TILE * tile
        row = jnp.broadcast_to(bias[:, base - TILE : base + TILE], (TILE, 2 * TILE))
        rolled = pltpu.roll(row, TILE, 1, stride=1, stride_axis=0)
        window[TILE * tile : TILE * (tile + 1), :] = rolled[:, :TILE]


def attend_head(
    query_rows, key_rows, value_rows, segment_keys_ref, segment_queries_ref, window, scores, exp_ref
):
    keys = key_rows.T
    values = jnp.concatenate([value_rows, jnp.ones((16, SEQ), jnp.bfloat16)], axis=0)
    outs, scales = [], []
    for q0 in range(0, SEQ, QUERY_TILE):
        queries = query_rows[:, q0 : q0 + QUERY_TILE]
        peak = jnp.full((8, QUERY_TILE), -jnp.inf, jnp.float32)
        for k0 in range(0, SEQ, KEY_TILE):
            raw = jnp.dot(keys[k0 : k0 + KEY_TILE], queries, preferred_element_type=jnp.float32)
            parts = []
            for l0 in range(0, QUERY_TILE, TILE):
                start = SEQ - TILE - (q0 + l0) + k0
                same_doc = (
                    segment_keys_ref[k0 : k0 + KEY_TILE, :]
                    == segment_queries_ref[:, q0 + l0 : q0 + l0 + TILE]
                )
                part = jnp.where(
                    same_doc,
                    raw[:, l0 : l0 + TILE] + window[start : start + KEY_TILE, :],
                    masked_score,
                )
                scores[k0 : k0 + KEY_TILE, l0 : l0 + TILE] = part
                parts.append(part)
            whole = jnp.concatenate(parts, axis=1)
            peak = jnp.maximum(peak, jnp.max(whole.reshape(KEY_TILE // 8, 8, QUERY_TILE), axis=0))
        peak = jnp.max(peak, axis=0, keepdims=True)
        total = jnp.zeros((HS + 16, QUERY_TILE), jnp.float32)
        for k0 in range(0, SEQ, KEY_TILE):
            exp_scores = jnp.exp(scores[k0 : k0 + KEY_TILE, :] - peak).astype(jnp.bfloat16)
            exp_ref[k0 : k0 + KEY_TILE, q0 : q0 + QUERY_TILE] = exp_scores
            total = total + jnp.dot(
                values[:, k0 : k0 + KEY_TILE], exp_scores, preferred_element_type=jnp.float32
            )
        scale = 1.0 / total[HS : HS + 1]
        scales.append(scale)
        outs.append((total[:HS] * scale).astype(jnp.bfloat16))
    return jnp.concatenate(outs, axis=1), jnp.concatenate(scales, axis=1)


def one_hot(place, shape, dim):
    hit = lax.broadcasted_iota(jnp.int32, shape, dim) == place
    return jnp.where(hit, 1.0, 0.0).astype(jnp.bfloat16)


def front_kernel(
    sizes,
    mine_ref,
    slot_place_ref,
    spread_place_ref,
    order_qkv_ref,
    order_out_ref,
    order_in_ref,
    order_down_ref,
    normed_ref,
    bias_ref,
    segment_keys_ref,
    segment_queries_ref,
    w_qkv_ref,
    w_out_ref,
    w_in_ref,
    w_down_ref,
    projected_ref,
    attended_ref,
    scale_ref,
    exp_ref,
    sent,
    received,
    spread,
    buf_qkv,
    buf_out,
    buf_in,
    buf_down,
    stage_out,
    stage_in,
    stage_down,
    window,
    scores,
    exp_stage,
    deal_send,
    deal_recv,
    gather_send,
    gather_recv,
    group_send,
    group_recv,
    local_sem,
    exp_sem,
):
    dp_count, pair_rows = sent.shape[0], sent.shape[1]
    tensor_count = w_qkv_ref.shape[0]
    heads = bias_ref.shape[0]
    group_heads = heads // tensor_count
    head_rows = group_heads * HS
    dp_pos, tensor_pos = lax.axis_index("dp"), lax.axis_index("tensor")
    core_peer = (dp_pos, tensor_pos + 1 - 2 * lax.rem(tensor_pos, 2))
    far_peer = (dp_pos, lax.rem(tensor_pos + 2, tensor_count))

    def dp_peer(m):
        return (lax.rem(dp_pos + m, dp_count), tensor_pos)

    def each_peer(run):
        def step(m, carry):
            run(m)
            return carry

        lax.fori_loop(1, dp_count, step, 0)

    barrier = pltpu.get_barrier_semaphore()

    def greet(m):
        pl.semaphore_signal(barrier, inc=1, device_id=dp_peer(m), device_id_type=MESH)

    each_peer(greet)
    for peer in (core_peer, far_peer):
        pl.semaphore_signal(barrier, inc=1, device_id=peer, device_id_type=MESH)

    place = slot_place_ref[...]
    mine = mine_ref[...]
    for m in range(dp_count):
        hot = one_hot(place - m * pair_rows, (pair_rows, mine.shape[0]), 0)
        sent[m] = jnp.dot(hot, mine, preferred_element_type=jnp.float32).astype(jnp.bfloat16)
    pl.semaphore_wait(barrier, dp_count + 1)

    def deal(m):
        return pltpu.make_async_remote_copy(
            sent.at[m],
            received.at[m],
            deal_send.at[m],
            deal_recv.at[m],
            device_id=dp_peer(m),
            device_id_type=MESH,
        )

    each_peer(lambda m: deal(m).start())
    received[0] = sent[0]
    each_peer(lambda m: deal(m).wait())
    rows = spread.shape[0]
    hot = one_hot(spread_place_ref[...], (rows, dp_count * pair_rows), 0)
    spread[...] = jnp.dot(
        hot, received[...].reshape(dp_count * pair_rows, D), preferred_element_type=jnp.float32
    ).astype(jnp.bfloat16)

    bufs = (buf_qkv, buf_out, buf_in, buf_down)
    orders = (order_qkv_ref, order_out_ref, order_in_ref, order_down_ref)
    stages = (w_qkv_ref.at[0], stage_out, stage_in, stage_down)
    finals = (w_qkv_ref, w_out_ref, w_in_ref, w_down_ref)
    offsets = [sum(buf.shape[1] for buf in bufs[:role]) for role in range(len(bufs))]

    def gather(role, m):
        count = bufs[role].shape[1]
        return pltpu.make_async_remote_copy(
            spread.at[pl.ds(offsets[role], count)],
            bufs[role].at[m],
            gather_send.at[role, m],
            gather_recv.at[role, m],
            device_id=dp_peer(m),
            device_id_type=MESH,
        )

    def start_gather(role):
        each_peer(lambda m: gather(role, m).start())
        bufs[role][0] = spread[offsets[role] : offsets[role] + bufs[role].shape[1], :]

    def order(role):
        each_peer(lambda m: gather(role, m).wait())
        count = bufs[role].shape[1]
        source = bufs[role][...].reshape(dp_count * count, D)
        step = 192
        for r0 in range(0, sizes[role], step):
            hot = one_hot(orders[role][r0 : r0 + step, :], (step, dp_count * count), 1)
            stages[role][r0 : r0 + step, :] = jnp.dot(
                hot, source, preferred_element_type=jnp.float32
            ).astype(jnp.bfloat16)

    def share(role, part):
        src, slot, peer = (
            (stages[role], 1, core_peer),
            (stages[role], 2, far_peer),
            (finals[role].at[2], 3, core_peer),
        )[part]
        return pltpu.make_async_remote_copy(
            src,
            finals[role].at[slot],
            group_send.at[role, part],
            group_recv.at[role, part],
            device_id=peer,
            device_id_type=MESH,
        )

    def keep(role):
        return pltpu.make_async_copy(stages[role], finals[role].at[0], local_sem.at[role])

    def start_share(role):
        order(role)
        share(role, 0).start()
        share(role, 1).start()
        if role > 0:
            keep(role).start()

    def forward(role):
        share(role, 1).wait_recv()
        share(role, 2).start()

    start_gather(0)
    start_share(0)
    start_gather(1)
    start_gather(2)

    def head_step(i, carry):
        group, head = lax.div(i, group_heads), lax.rem(i, group_heads)

        @pl.when(i == 1)
        def _():
            start_share(1)

        @pl.when(i == group_heads)
        def _():
            share(0, 0).wait_recv()

        @pl.when(i == 2 * group_heads)
        def _():
            forward(0)

        @pl.when(i == 3 * group_heads)
        def _():
            share(0, 2).wait_recv()
            forward(1)
            start_gather(3)

        @pl.when(head == 0)
        def _():
            projected_ref[group] = contract(w_qkv_ref[group], normed_ref[...], 1, 1).astype(
                jnp.bfloat16
            )

        def head_part(part):
            start = pl.multiple_of(part * head_rows + head * HS, HS)
            return projected_ref[group, pl.ds(start, HS), :]

        slot = lax.rem(i, 2)

        def save(head_index, slot):
            return pltpu.make_async_copy(
                exp_stage.at[slot], exp_ref.at[head_index], exp_sem.at[slot]
            )

        @pl.when(i >= 2)
        def _():
            save(i - 2, slot).wait()

        bias_window(bias_ref[i], window)
        attended, scale = attend_head(
            head_part(0),
            head_part(1),
            head_part(2),
            segment_keys_ref,
            segment_queries_ref,
            window,
            scores,
            exp_stage.at[slot],
        )
        attended_ref[pl.ds(pl.multiple_of(i * HS, HS), HS), :] = attended
        scale_ref[i] = scale
        save(i, slot).start()
        return carry

    lax.fori_loop(0, heads, head_step, 0)
    for i in (heads - 2, heads - 1):
        pltpu.make_async_copy(exp_stage.at[i % 2], exp_ref.at[i], exp_sem.at[i % 2]).wait()
    start_share(2)
    start_share(3)
    forward(2)
    forward(3)
    for role in range(len(bufs)):
        share(role, 0).wait_send()
        share(role, 1).wait_send()
        share(role, 2).wait_send()
        if role > 0:
            share(role, 0).wait_recv()
            share(role, 2).wait_recv()
            keep(role).wait()


def front(mine, slot_place, spread_place, orders, local_sizes, pair_rows, normed, bias, segments):
    dp_count, tensor_count = lax.axis_size("dp"), lax.axis_size("tensor")
    sizes = [order.shape[0] for order in orders]
    heads = bias.shape[0]
    low = jnp.bfloat16
    dma = pltpu.SemaphoreType.DMA
    roles = len(sizes)
    whole = pl.BlockSpec(memory_space=pltpu.VMEM)
    away = pl.BlockSpec(memory_space=pl.ANY)
    return pl.pallas_call(
        functools.partial(front_kernel, sizes),
        in_specs=[whole] * 11,
        out_specs=[whole, away, away, away, whole, whole, whole, away],
        out_shape=[jax.ShapeDtypeStruct((tensor_count, size, D), low) for size in sizes]
        + [
            jax.ShapeDtypeStruct((tensor_count, sizes[0], SEQ), low),
            jax.ShapeDtypeStruct((heads * HS, SEQ), low),
            jax.ShapeDtypeStruct((heads, 1, SEQ), jnp.float32),
            jax.ShapeDtypeStruct((heads, SEQ, SEQ), low),
        ],
        scratch_shapes=[
            pltpu.VMEM((dp_count, pair_rows, D), low),
            pltpu.VMEM((dp_count, pair_rows, D), low),
            pltpu.VMEM((sum(local_sizes), D), low),
        ]
        + [pltpu.VMEM((dp_count, size, D), low) for size in local_sizes]
        + [pltpu.VMEM((size, D), low) for size in sizes[1:]]
        + [
            pltpu.VMEM((WINDOW, TILE), jnp.float32),
            pltpu.VMEM((SEQ, QUERY_TILE), jnp.float32),
            pltpu.VMEM((2, SEQ, SEQ), low),
            dma((dp_count,)),
            dma((dp_count,)),
            dma((roles, dp_count)),
            dma((roles, dp_count)),
            dma((roles, 3)),
            dma((roles, 3)),
            dma((roles,)),
            dma((2,)),
        ],
        compiler_params=pltpu.CompilerParams(
            collective_id=1, has_side_effects=True, vmem_limit_bytes=56 * 1024 * 1024
        ),
        cost_estimate=pl.CostEstimate(
            flops=10 * heads * SEQ * SEQ * 256,
            bytes_accessed=64 * 1024 * 1024,
            transcendentals=heads * SEQ * SEQ,
        ),
        name="front",
    )(
        mine,
        slot_place[None, :],
        spread_place[None, :],
        *[order[:, None] for order in orders],
        normed,
        bias,
        jnp.broadcast_to(segments[:, None], (SEQ, TILE)),
        segments[None, :],
    )


def attend_head_back(
    query_rows,
    key_rows,
    value_rows,
    exp_ref,
    attended,
    scale,
    attended_grad,
    window,
    score_grads,
    store,
):
    scaled = attended_grad.astype(jnp.float32) * scale
    delta = jnp.sum(scaled * attended.astype(jnp.float32), axis=0, keepdims=True)
    scaled_low = scaled.astype(jnp.bfloat16)
    delta_high = delta.astype(jnp.bfloat16).astype(jnp.float32)
    delta_rest = delta - delta_high
    place = lax.broadcasted_iota(jnp.int32, (16, SEQ), 0)
    extra = jnp.where(
        place == 0,
        jnp.broadcast_to(-delta_high, (16, SEQ)),
        jnp.where(place == 1, jnp.broadcast_to(-delta_rest, (16, SEQ)), 0.0),
    ).astype(jnp.bfloat16)
    grads = jnp.concatenate([scaled_low, extra], axis=0)
    values = jnp.concatenate([value_rows, jnp.ones((16, SEQ), jnp.bfloat16)], axis=0).T
    window[...] = jnp.zeros_like(window)
    for q0 in range(0, SEQ, QUERY_TILE):
        total = jnp.zeros((HS, QUERY_TILE), jnp.float32)
        for k0 in range(0, SEQ, KEY_TILE):
            centered = jnp.dot(
                values[k0 : k0 + KEY_TILE],
                grads[:, q0 : q0 + QUERY_TILE],
                preferred_element_type=jnp.float32,
            )
            score_grad = centered * exp_ref[
                k0 : k0 + KEY_TILE, q0 : q0 + QUERY_TILE
            ].astype(jnp.float32)
            for l0 in range(0, QUERY_TILE, TILE):
                start = SEQ - TILE - (q0 + l0) + k0
                window[start : start + KEY_TILE, :] += score_grad[:, l0 : l0 + TILE]
            score_low = score_grad.astype(jnp.bfloat16)
            score_grads[k0 : k0 + KEY_TILE, q0 : q0 + QUERY_TILE] = score_low
            total = total + jnp.dot(
                key_rows[:, k0 : k0 + KEY_TILE], score_low, preferred_element_type=jnp.float32
            )
        store(0, q0, total.astype(jnp.bfloat16))
    queries = query_rows.T
    scaled_rows = scaled_low.T
    for k0 in range(0, SEQ, KEY_TILE):
        key_grad = jnp.dot(
            score_grads[k0 : k0 + KEY_TILE, :], queries, preferred_element_type=jnp.float32
        )
        value_grad = jnp.dot(
            exp_ref[k0 : k0 + KEY_TILE, :], scaled_rows, preferred_element_type=jnp.float32
        )
        store(1, k0, key_grad.T.astype(jnp.bfloat16))
        store(2, k0, value_grad.T.astype(jnp.bfloat16))
    pieces = [jnp.zeros((1, TILE), jnp.float32)] * (2 * SEQ // TILE)
    for tile in range(WINDOW // TILE):
        base = WINDOW - TILE * tile
        block = window[TILE * tile : TILE * (tile + 1), :]
        folded = jnp.concatenate([jnp.zeros((TILE, TILE), jnp.float32), block], axis=1)
        rows = TILE // 2
        while rows >= 1:
            folded = folded[:rows] + pltpu.roll(folded[rows:], 2 * TILE - rows, 1)
            rows //= 2
        pieces[base // TILE - 1] += folded[:, :TILE]
        pieces[base // TILE] += folded[:, TILE:]
    return jnp.concatenate(pieces, axis=1)


SMALL_ROWS = 48
TABLE_ROW = 32


def back_kernel(
    sizes,
    grad_out_ref,
    grad_in_ref,
    grad_down_ref,
    projected_ref,
    exp_ref,
    attended_ref,
    scale_ref,
    attended_grad_ref,
    normed_ref,
    w_qkv_ref,
    tokens_ref,
    mid_grad_ref,
    gain_ref,
    small_ref,
    bucket_ref,
    place_qkv_ref,
    place_out_ref,
    place_in_ref,
    place_down_ref,
    spread_place_ref,
    slot_place_ref,
    owned_ref,
    input_grad_ref,
    small_total_ref,
    proj,
    proj_grad,
    normed_grad,
    window,
    score_grads,
    exp_stage,
    qkv_odd,
    zero_qkv,
    zero_out,
    zero_in,
    zero_down,
    two_qkv,
    two_out,
    two_in,
    two_down,
    core_one_qkv,
    core_one_out,
    core_one_in,
    core_one_down,
    core_three_qkv,
    core_three_out,
    core_three_in,
    core_three_down,
    far_qkv,
    far_out,
    far_in,
    far_down,
    got_qkv,
    got_out,
    got_in,
    got_down,
    spread,
    sent,
    received,
    small_own,
    small_tensor,
    small_dp,
    core_send,
    core_recv,
    far_send,
    far_recv,
    deal_send,
    deal_recv,
    back_send,
    back_recv,
    small_send,
    small_recv,
    load_sem,
    exp_sem,
    proj_sem,
):
    dp_count, pair_rows = sent.shape[0], sent.shape[1]
    tensor_count = w_qkv_ref.shape[0]
    heads = scale_ref.shape[0]
    group_heads = heads // tensor_count
    head_rows = group_heads * HS
    dp_pos, tensor_pos = lax.axis_index("dp"), lax.axis_index("tensor")
    core_pos = tensor_pos + 1 - 2 * lax.rem(tensor_pos, 2)
    far_pos = lax.rem(tensor_pos + 2, tensor_count)
    core_peer, far_peer = (dp_pos, core_pos), (dp_pos, far_pos)
    grad_refs = (None, grad_out_ref, grad_in_ref, grad_down_ref)
    zeros = (zero_qkv, zero_out, zero_in, zero_down)
    twos = (two_qkv, two_out, two_in, two_down)
    core_ones = (core_one_qkv, core_one_out, core_one_in, core_one_down)
    core_threes = (core_three_qkv, core_three_out, core_three_in, core_three_down)
    fars = (far_qkv, far_out, far_in, far_down)
    gots = (got_qkv, got_out, got_in, got_down)
    places = (place_qkv_ref, place_out_ref, place_in_ref, place_down_ref)
    offsets = [sum(got.shape[1] for got in gots[:role]) for role in range(len(gots))]
    low = jnp.bfloat16

    def up(m):
        return lax.rem(dp_pos + m, dp_count)

    def down(m):
        return lax.rem(dp_pos + dp_count - m, dp_count)

    def each_peer(run):
        def step(m, carry):
            run(m)
            return carry

        lax.fori_loop(1, dp_count, step, 0)

    def tensor_peer(m):
        return (dp_pos, lax.rem(tensor_pos + m, tensor_count))

    barrier = pltpu.get_barrier_semaphore()

    def greet(m):
        pl.semaphore_signal(barrier, inc=1, device_id=(up(m), tensor_pos), device_id_type=MESH)

    each_peer(greet)
    for m in range(1, tensor_count):
        pl.semaphore_signal(barrier, inc=1, device_id=tensor_peer(m), device_id_type=MESH)

    def load_exp(head, slot):
        return pltpu.make_async_copy(exp_ref.at[head], exp_stage.at[slot], exp_sem.at[slot])

    def load_proj(group):
        return pltpu.make_async_copy(projected_ref.at[group], proj, proj_sem)

    def load(role, which):
        target = zeros[role] if which == 0 else twos[role]
        return pltpu.make_async_copy(
            grad_refs[role].at[which], target, load_sem.at[role, which // 2]
        )

    def core_copy(role, which):
        if role == 0:
            src = qkv_odd.at[which // 2]
        else:
            src = grad_refs[role].at[which]
        target = core_ones[role] if which == 1 else core_threes[role].at[pl.ds(0, sizes[role])]
        return pltpu.make_async_remote_copy(
            src,
            target,
            core_send.at[role, which // 2],
            core_recv.at[role, which // 2],
            device_id=core_peer,
            device_id_type=MESH,
        )

    def far_copy(role):
        return pltpu.make_async_remote_copy(
            twos[role],
            fars[role],
            far_send.at[role],
            far_recv.at[role],
            device_id=far_peer,
            device_id_type=MESH,
        )

    def deal_copy(role, m):
        count = gots[role].shape[1]
        start = pl.multiple_of(m * count, 16)
        return pltpu.make_async_remote_copy(
            core_threes[role].at[pl.ds(start, count)],
            gots[role].at[m],
            deal_send.at[role, m],
            deal_recv.at[role, m],
            device_id=(up(m), tensor_pos),
            device_id_type=MESH,
        )

    def send_far(role):
        core_copy(role, 3).wait_recv()
        if role > 0:
            load(role, 2).wait()
        count = twos[role].shape[0]
        twos[role][...] = (
            twos[role][...].astype(jnp.float32)
            + core_threes[role][0:count, :].astype(jnp.float32)
        ).astype(low)
        far_copy(role).start()

    def send_deal(role):
        core_copy(role, 1).wait_recv()
        if role > 0:
            load(role, 0).wait()
        far_copy(role).wait_recv()
        total = (
            zeros[role][...].astype(jnp.float32)
            + core_ones[role][...].astype(jnp.float32)
            + fars[role][...].astype(jnp.float32)
        ).astype(low)
        count = gots[role].shape[1]
        for m in range(dp_count):
            hot = one_hot(places[role][...] - m * count, (count, sizes[role]), 0)
            core_threes[role][m * count : (m + 1) * count, :] = jnp.dot(
                hot, total, preferred_element_type=jnp.float32
            ).astype(low)
        each_peer(lambda m: deal_copy(role, m).start())

    def finish_deal(role):
        each_peer(lambda m: deal_copy(role, m).wait())
        count = gots[role].shape[1]
        total = core_threes[role][0:count, :].astype(jnp.float32)
        for m in range(1, dp_count):
            total = total + gots[role][m].astype(jnp.float32)
        spread[offsets[role] : offsets[role] + count, :] = total.astype(low)

    load_exp(heads - group_heads, 0).start()
    load_proj(tensor_count - 1).start()
    for role in (3, 2, 1):
        load(role, 2).start()
        load(role, 0).start()
    normed_grad[...] = jnp.zeros_like(normed_grad)
    small_own[0:TABLE_ROW, :] = small_ref[...]
    small_own[TABLE_ROW:SMALL_ROWS, :] = jnp.zeros((SMALL_ROWS - TABLE_ROW, TILE), jnp.float32)
    pl.semaphore_wait(barrier, dp_count + tensor_count - 2)
    for role in (3, 2, 1):
        core_copy(role, 3).start()
        core_copy(role, 1).start()

    def head_step(i, carry):
        group = tensor_count - 1 - lax.div(i, group_heads)
        part_head = lax.rem(i, group_heads)
        head = group * group_heads + part_head
        slot = lax.rem(i, 2)

        @pl.when(i == 1)
        def _():
            send_far(3)

        @pl.when(i == 7)
        def _():
            send_far(2)

        @pl.when(i == 9)
        def _():
            send_deal(3)

        @pl.when(part_head == 0)
        def _():
            load_proj(group).wait()

        @pl.when(i + 1 < heads)
        def _():
            later = i + 1
            later_group = tensor_count - 1 - lax.div(later, group_heads)
            later_head = later_group * group_heads + lax.rem(later, group_heads)
            load_exp(later_head, lax.rem(later, 2)).start()

        load_exp(head, slot).wait()

        def rows(part):
            return pl.ds(pl.multiple_of(part * head_rows + part_head * HS, HS), HS)

        def store(part, column, value):
            proj_grad[rows(part), column : column + value.shape[1]] = value

        here = pl.ds(pl.multiple_of(head * HS, HS), HS)
        offset_grad = attend_head_back(
            proj[rows(0), :],
            proj[rows(1), :],
            proj[rows(2), :],
            exp_stage.at[slot],
            attended_ref[here, :],
            scale_ref[head],
            attended_grad_ref[here, :],
            window,
            score_grads,
            store,
        )
        flips = (tensor_pos, core_pos, far_pos, tensor_count - 1 - tensor_pos)
        true_group = flips[0]
        for g in range(1, tensor_count):
            true_group = true_group + (flips[g] - flips[0]) * (
                lax.div(group + tensor_count - g, tensor_count)
                - lax.div(group + tensor_count - g - 1, tensor_count)
            )
        high = offset_grad.astype(low)
        rest = (offset_grad - high.astype(jnp.float32)).astype(low)
        both = jnp.concatenate([high, rest] + [jnp.zeros_like(high)] * 6, axis=0)
        sums = jnp.dot(both, bucket_ref[...], preferred_element_type=jnp.float32)
        line = lax.broadcasted_iota(jnp.int32, (SMALL_ROWS - TABLE_ROW, TILE), 0)
        small_own[TABLE_ROW:SMALL_ROWS, :] += jnp.where(
            line == true_group * group_heads + part_head,
            jnp.broadcast_to(sums[0:1] + sums[1:2], (SMALL_ROWS - TABLE_ROW, TILE)),
            0.0,
        )

        @pl.when(part_head == group_heads - 1)
        def _():
            @pl.when(group > 0)
            def _():
                load_proj(group - 1).start()

            def weight_grad(target):
                for r0 in range(0, 3 * head_rows, head_rows):
                    target[r0 : r0 + head_rows, :] = jnp.dot(
                        proj_grad[r0 : r0 + head_rows, :],
                        normed_ref[...],
                        preferred_element_type=jnp.float32,
                    ).astype(low)

            @pl.when(group == 3)
            def _():
                weight_grad(qkv_odd.at[1])
                core_copy(0, 3).start()

            @pl.when(group == 2)
            def _():
                weight_grad(two_qkv)

            @pl.when(group == 1)
            def _():
                weight_grad(qkv_odd.at[0])
                core_copy(0, 1).start()

            @pl.when(group == 0)
            def _():
                weight_grad(zero_qkv)

            for r0 in range(0, SEQ, 256):
                normed_grad[r0 : r0 + 256, :] += jnp.dot(
                    proj_grad[:, r0 : r0 + 256].T,
                    w_qkv_ref[group],
                    preferred_element_type=jnp.float32,
                )

        return carry

    lax.fori_loop(0, heads, head_step, 0)
    send_far(1)
    send_far(0)

    gain_grad = jnp.zeros((1, D), jnp.float32)
    for r0 in range(0, SEQ, 128):
        values = tokens_ref[r0 : r0 + 128, :].astype(jnp.float32)
        grads = normed_grad[r0 : r0 + 128, :]
        inverse = lax.rsqrt(jnp.mean(values * values, axis=1, keepdims=True) + norm_epsilon)
        scaled = values * inverse
        gain_grad = gain_grad + jnp.sum(grads * scaled, axis=0, keepdims=True)
        grads = grads * gain_ref[...]
        inner = jnp.mean(grads * scaled, axis=1, keepdims=True)
        input_grad_ref[r0 : r0 + 128, :] = (
            mid_grad_ref[r0 : r0 + 128, :].astype(jnp.float32) + inverse * (grads - scaled * inner)
        ).astype(low)
    for part in range(D // TILE):
        small_own[part : part + 1, :] = gain_grad[:, TILE * part : TILE * (part + 1)]

    def small_copy(stage, m):
        if stage == 0:
            src, target, peer = small_own, small_tensor.at[tensor_pos], tensor_peer(m)
        else:
            src, target, peer = small_total_ref, small_dp.at[dp_pos], (up(m), tensor_pos)
        return pltpu.make_async_remote_copy(
            src,
            target,
            small_send.at[stage, m],
            small_recv.at[stage, m],
            device_id=peer,
            device_id_type=MESH,
        )

    for m in range(1, tensor_count):
        small_copy(0, m).start()
    send_deal(2)
    small_tensor[tensor_pos] = small_own[...]
    for m in range(1, tensor_count):
        small_copy(0, m).wait()
    total = small_tensor[0]
    for m in range(1, tensor_count):
        total = total + small_tensor[m]
    small_total_ref[...] = total
    each_peer(lambda m: small_copy(1, m).start())
    send_deal(1)
    finish_deal(3)
    send_deal(0)
    small_dp[dp_pos] = small_total_ref[...]
    each_peer(lambda m: small_copy(1, m).wait())
    total = small_dp[0]
    for m in range(1, dp_count):
        total = total + small_dp[m]
    small_total_ref[...] = total
    for role in (2, 1, 0):
        finish_deal(role)

    values = spread[...]
    for m in range(dp_count):
        hot = one_hot(
            spread_place_ref[m * pair_rows : (m + 1) * pair_rows, :],
            (pair_rows, values.shape[0]),
            1,
        )
        sent[m] = jnp.dot(hot, values, preferred_element_type=jnp.float32).astype(low)

    def back_copy(m):
        return pltpu.make_async_remote_copy(
            sent.at[m],
            received.at[m],
            back_send.at[m],
            back_recv.at[m],
            device_id=(down(m), tensor_pos),
            device_id_type=MESH,
        )

    each_peer(lambda m: back_copy(m).start())
    received[0] = sent[0]
    each_peer(lambda m: back_copy(m).wait())
    capacity = owned_ref.shape[0]
    hot = one_hot(slot_place_ref[...], (capacity, dp_count * pair_rows), 1)
    owned_ref[...] = jnp.dot(
        hot, received[...].reshape(dp_count * pair_rows, D), preferred_element_type=jnp.float32
    )
    for role in range(len(gots)):
        core_copy(role, 1).wait_send()
        core_copy(role, 3).wait_send()
        far_copy(role).wait_send()


def back(
    weight_grads,
    projected,
    exp_scores,
    attended,
    scale,
    attended_grad,
    normed,
    w_qkv,
    tokens,
    mid_grad,
    gain,
    small,
    buckets,
    places,
    local_sizes,
    pair_rows,
    spread_place,
    slot_place,
):
    dp_count, tensor_count = lax.axis_size("dp"), lax.axis_size("tensor")
    sizes = [place.shape[0] for place in places]
    capacity = slot_place.shape[0]
    low = jnp.bfloat16
    dma = pltpu.SemaphoreType.DMA
    roles = len(sizes)
    whole = pl.BlockSpec(memory_space=pltpu.VMEM)
    away = pl.BlockSpec(memory_space=pl.ANY)
    parts = [pltpu.VMEM((size, D), low) for size in sizes]
    padded = [pltpu.VMEM((dp_count * size, D), low) for size in local_sizes]
    padded = [
        pltpu.VMEM((max(dp_count * size, full), D), low) for size, full in zip(local_sizes, sizes)
    ]
    bucket_place = jnp.concatenate([jnp.full((1,), -1, jnp.int32), buckets[::-1]])
    bucket_hot = (
        bucket_place[:, None] == jnp.arange(TILE, dtype=jnp.int32)[None, :]
    ).astype(low)
    return pl.pallas_call(
        functools.partial(back_kernel, sizes),
        in_specs=[away] * 5 + [whole] * 16,
        out_specs=[whole] * 3,
        out_shape=[
            jax.ShapeDtypeStruct((capacity, D), jnp.float32),
            jax.ShapeDtypeStruct((SEQ, D), low),
            jax.ShapeDtypeStruct((SMALL_ROWS, TILE), jnp.float32),
        ],
        scratch_shapes=[
            pltpu.VMEM((sizes[0], SEQ), low),
            pltpu.VMEM((sizes[0], SEQ), low),
            pltpu.VMEM((SEQ, D), jnp.float32),
            pltpu.VMEM((WINDOW, TILE), jnp.float32),
            pltpu.VMEM((SEQ, SEQ), low),
            pltpu.VMEM((2, SEQ, SEQ), low),
            pltpu.VMEM((2, sizes[0], D), low),
        ]
        + parts
        + parts
        + parts
        + padded
        + parts
        + [pltpu.VMEM((dp_count, size, D), low) for size in local_sizes]
        + [
            pltpu.VMEM((sum(local_sizes), D), low),
            pltpu.VMEM((dp_count, pair_rows, D), low),
            pltpu.VMEM((dp_count, pair_rows, D), low),
            pltpu.VMEM((SMALL_ROWS, TILE), jnp.float32),
            pltpu.VMEM((tensor_count, SMALL_ROWS, TILE), jnp.float32),
            pltpu.VMEM((dp_count, SMALL_ROWS, TILE), jnp.float32),
            dma((roles, 2)),
            dma((roles, 2)),
            dma((roles,)),
            dma((roles,)),
            dma((roles, dp_count)),
            dma((roles, dp_count)),
            dma((dp_count,)),
            dma((dp_count,)),
            dma((2, max(dp_count, tensor_count))),
            dma((2, max(dp_count, tensor_count))),
            dma((roles, 2)),
            dma((2,)),
            dma,
        ],
        compiler_params=pltpu.CompilerParams(
            collective_id=2, has_side_effects=True, vmem_limit_bytes=62 * 1024 * 1024
        ),
        cost_estimate=pl.CostEstimate(
            flops=16 * H * SEQ * SEQ * 256,
            bytes_accessed=64 * 1024 * 1024,
            transcendentals=0,
        ),
        name="back",
    )(
        *weight_grads,
        projected,
        exp_scores,
        attended,
        scale,
        attended_grad,
        normed,
        w_qkv,
        tokens,
        mid_grad,
        gain[None, :],
        small,
        bucket_hot,
        *[place[None, :] for place in places],
        spread_place[:, None],
        slot_place[:, None],
    )


def feed_kernel(rows_ref, w_in_ref, w_down_ref, before_ref, activ_ref, slope_ref, out_ref):
    row_tile = 256

    @pl.when(pl.program_id(0) == 0)
    def _():
        out_ref[...] = before_ref[...]

    for r0 in range(0, SEQ, row_tile):
        pre = contract(rows_ref[r0 : r0 + row_tile, :], w_in_ref[...], 1, 1)
        cdf = 0.5 * (1.0 + lax.erf(pre * (1.0 / math.sqrt(2.0))))
        pdf = jnp.exp(-0.5 * pre * pre) * (1.0 / math.sqrt(2.0 * math.pi))
        activ = (pre * cdf).astype(jnp.bfloat16)
        activ_ref[r0 : r0 + row_tile, :] = activ
        slope_ref[r0 : r0 + row_tile, :] = (cdf + pre * pdf).astype(jnp.bfloat16)
        out_ref[r0 : r0 + row_tile, :] += jnp.dot(
            activ, w_down_ref[...], preferred_element_type=jnp.float32
        )


def feed(rows, w_in, w_down, before):
    width = 384
    tokens = rows.shape[0]
    hidden = w_in.shape[0]
    return pl.pallas_call(
        feed_kernel,
        grid=(hidden // width,),
        in_specs=[
            pl.BlockSpec((tokens, D), lambda j: (0, 0)),
            pl.BlockSpec((width, D), lambda j: (j, 0)),
            pl.BlockSpec((width, D), lambda j: (j, 0)),
            pl.BlockSpec((tokens, D), lambda j: (0, 0)),
        ],
        out_specs=[
            pl.BlockSpec((tokens, width), lambda j: (0, j)),
            pl.BlockSpec((tokens, width), lambda j: (0, j)),
            pl.BlockSpec((tokens, D), lambda j: (0, 0)),
        ],
        out_shape=[
            jax.ShapeDtypeStruct((tokens, hidden), jnp.bfloat16),
            jax.ShapeDtypeStruct((tokens, hidden), jnp.bfloat16),
            jax.ShapeDtypeStruct((tokens, D), jnp.float32),
        ],
        compiler_params=pltpu.CompilerParams(vmem_limit_bytes=VMEM_LIMIT),
        cost_estimate=pl.CostEstimate(
            flops=8 * tokens * hidden * D,
            bytes_accessed=10 * 1024 * 1024,
            transcendentals=2 * tokens * hidden,
        ),
        name="feed",
    )(rows, w_in, w_down, before)


def adamw(weights, grads, first, second, step):
    first_new = beta_first * first + (1.0 - beta_first) * grads
    second_new = beta_second * second + (1.0 - beta_second) * grads * grads
    first_hat = first_new / (1.0 - beta_first**step)
    second_hat = second_new / (1.0 - beta_second**step)
    weights_new = weights - rate_per_step * step * (
        first_hat / (jnp.sqrt(second_hat) + adam_epsilon) + weight_decay * weights
    )
    return (weights_new, first_new, second_new)


def per_device(
    tokens,
    cotangent,
    segment_ids,
    buckets,
    owners,
    master,
    first_moment,
    second_moment,
    small_params,
    small_first,
    small_second,
    adapter_ema,
    step_count,
):
    dp_count = lax.axis_size("dp")
    tensor_count = lax.axis_size("tensor")
    capacity = master.shape[1]
    group_heads = H // tensor_count
    head_rows = group_heads * HS
    hidden_rows = FF // tensor_count
    dp_pos = lax.axis_index("dp")
    tensor_pos = lax.axis_index("tensor")

    ends = (0, 3 * head_rows, 4 * head_rows, 4 * head_rows + hidden_rows, owners.shape[0])
    sizes = [high - low for low, high in zip(ends[:-1], ends[1:])]
    roles = len(sizes)

    pair_rows = -(-((capacity + roles * (dp_count - 1)) // dp_count) // 16) * 16
    owner_hot = (owners[:, None] == jnp.arange(dp_count, dtype=jnp.int32)[None, :]).astype(jnp.int32)
    counts = jnp.stack(
        [jnp.sum(owner_hot[low:high], axis=0) for low, high in zip(ends[:-1], ends[1:])]
    )
    dps = jnp.arange(dp_count, dtype=jnp.int32)
    starts = jnp.sum(
        jnp.where(dps[None, :] < dps[:, None], counts[:, None, :], 0), axis=2, dtype=jnp.int32
    )
    role_ids = jnp.arange(roles, dtype=jnp.int32)
    earlier = role_ids[None, :] < role_ids[:, None]
    role_starts = jnp.sum(jnp.where(earlier[:, :, None], counts[None], 0), axis=1, dtype=jnp.int32)

    def hits(first, number, target):
        return (first + number - 1 - target) // dp_count - (first - 1 - target) // dp_count

    def own(values):
        return lax.dynamic_index_in_dim(values, dp_pos, values.ndim - 1, keepdims=False)

    slot = jnp.arange(capacity, dtype=jnp.int32)
    slot_place = jnp.full((capacity,), -1, jnp.int32)
    own_counts, own_starts, own_role_starts = own(counts), own(starts), own(role_starts)
    for role in range(roles):
        inside = (slot >= own_role_starts[role]) & (
            slot < own_role_starts[role] + own_counts[role]
        )
        rank = slot - own_role_starts[role]
        target = (own_starts[role] + rank) % dp_count
        place = rank // dp_count
        for other in range(role):
            place = place + hits(own_starts[other], own_counts[other], target)
        slot_place = jnp.where(
            inside, ((target - dp_pos) % dp_count) * pair_rows + place, slot_place
        )
    local_sizes = [-(-size // dp_count // 16) * 16 for size in sizes]
    local_starts = [sum(local_sizes[:role]) for role in range(roles)]
    source_dp = (dp_pos - dps) % dp_count
    sent_counts, sent_starts = counts[:, source_dp], starts[:, source_dp]
    pair_place = jnp.arange(pair_rows, dtype=jnp.int32)[None, :]
    spread_place = jnp.full((dp_count, pair_rows), -1, jnp.int32)
    passed = jnp.zeros((dp_count, 1), jnp.int32)
    for role in range(roles):
        number = hits(sent_starts[role], sent_counts[role], dp_pos)[:, None]
        first = sent_starts[role] + (dp_pos - sent_starts[role]) % dp_count
        rank = pair_place - passed
        local = local_starts[role] + first[:, None] // dp_count + rank
        spread_place = jnp.where((rank >= 0) & (rank < number), local, spread_place)
        passed = passed + number
    spread_place = spread_place.reshape(-1)
    below = jnp.cumsum(owner_hot, axis=0) - 1
    row_target = []
    row_rank = []
    for role, (low, high) in enumerate(zip(ends[:-1], ends[1:])):
        number = jnp.sum(
            owner_hot[low:high] * (below[low:high] - role_starts[role] + starts[role]), axis=1
        )
        row_target.append(number % dp_count)
        row_rank.append(number // dp_count)

    orders = [
        ((dp_pos - row_target[role]) % dp_count) * local_sizes[role] + row_rank[role]
        for role in range(roles)
    ]

    gain_one, gain_two, adapter, table = unpack(small_params)
    bucket_onehot = (buckets[:, None] == jnp.arange(NB, dtype=jnp.int32)[None, :]).astype(
        jnp.float32
    )
    per_offset = lax.dot_general(
        table, bucket_onehot, (((0,), (1,)), ((), ())), precision=highest
    )
    bias_rows = jnp.concatenate([jnp.zeros((H, 1), jnp.float32), per_offset[:, ::-1]], axis=1)
    group_order = jnp.arange(tensor_count, dtype=jnp.int32) ^ tensor_pos
    bias_rows = bias_rows.reshape(tensor_count, group_heads, 2 * SEQ)[group_order]
    bias_rows = bias_rows.reshape(H, 1, 2 * SEQ)
    segments = lax.dynamic_slice_in_dim(segment_ids, tensor_pos * SEQ, SEQ, 0)

    inputs_f = tokens.astype(jnp.float32)
    normed_one = rms_norm(inputs_f, gain_one).astype(jnp.bfloat16)
    groups = range(tensor_count)
    w_qkv, w_out, w_in, w_down, projected, attended, scale, exp_scores = front(
        master[0].astype(jnp.bfloat16),
        slot_place,
        spread_place,
        orders,
        local_sizes,
        pair_rows,
        normed_one,
        bias_rows,
        segments,
    )
    attended = attended.reshape(tensor_count, head_rows, SEQ)
    mid = inputs_f
    for k in groups:
        mid = mid + contract(attended[k], w_out[k], 0, 0)
    normed_two = rms_norm(mid, gain_two).astype(jnp.bfloat16)
    activ, slope = [], []
    ffn_out = jnp.zeros(mid.shape, jnp.float32)
    for k in groups:
        part, part_slope, ffn_out = feed(normed_two, w_in[k], w_down[k], ffn_out)
        activ.append(part)
        slope.append(part_slope)
    final, adapter_pull = jax.vjp(adapter_apply, ffn_out, adapter)
    layer_out = (mid + final).astype(jnp.bfloat16)

    out_grad = cotangent.astype(jnp.float32)
    ffn_grad, adapter_grad = adapter_pull(out_grad)
    ffn_grad = ffn_grad.astype(jnp.bfloat16)

    normed_two_grad = jnp.zeros(mid.shape, jnp.float32)
    down_grad, in_grad = [None] * tensor_count, [None] * tensor_count
    for k in reversed(groups):
        pre_grad = (contract(ffn_grad, w_down[k], 1, 1) * slope[k].astype(jnp.float32)).astype(
            jnp.bfloat16
        )
        down_grad[k] = contract(activ[k], ffn_grad, 0, 0).astype(jnp.bfloat16)
        in_grad[k] = contract(pre_grad, normed_two, 0, 0).astype(jnp.bfloat16)
        normed_two_grad = normed_two_grad + jnp.dot(
            pre_grad, w_in[k], preferred_element_type=jnp.float32
        )
    _, norm_two_pull = jax.vjp(rms_norm, mid, gain_two)
    mid_extra, gain_two_grad = norm_two_pull(normed_two_grad)
    mid_grad = out_grad + mid_extra
    mid_grad_low = mid_grad.astype(jnp.bfloat16)
    attended_all = attended.reshape(D, SEQ)
    out_weight_grad = jnp.dot(
        attended_all, mid_grad_low, preferred_element_type=jnp.float32
    ).astype(jnp.bfloat16)
    attended_grad = contract(w_out.reshape(D, D), mid_grad_low, 1, 1).astype(jnp.bfloat16)
    small_local = jnp.concatenate(
        [jnp.zeros((D,), jnp.float32), gain_two_grad]
        + [piece.reshape(-1) for piece in adapter_grad]
        + [jnp.zeros((TABLE_ROW * TILE - 2 * D - NADAPT,), jnp.float32)]
    ).reshape(TABLE_ROW, TILE)
    owned_grad, input_grad, small_total = back(
        (
            out_weight_grad.reshape(tensor_count, head_rows, D),
            jnp.stack(in_grad),
            jnp.stack(down_grad),
        ),
        projected,
        exp_scores,
        attended_all,
        scale,
        attended_grad,
        normed_one,
        w_qkv,
        tokens,
        mid_grad_low,
        gain_one,
        small_local,
        buckets,
        [
            ((row_target[role] - dp_pos) % dp_count) * local_sizes[role] + row_rank[role]
            for role in range(roles)
        ],
        local_sizes,
        pair_rows,
        spread_place,
        slot_place,
    )
    small_total = jnp.concatenate(
        [
            small_total[:TABLE_ROW].reshape(-1)[: 2 * D + NADAPT],
            small_total[TABLE_ROW : TABLE_ROW + H, :NB].T.reshape(-1),
        ]
    )
    own_filled = (slot_place >= 0).astype(jnp.float32)[:, None]
    step = step_count[0].astype(jnp.float32)
    new_master, new_first, new_second = adamw(
        master[0], owned_grad, first_moment[0], second_moment[0], step
    )
    new_master = new_master * own_filled
    new_first = new_first * own_filled
    new_second = new_second * own_filled
    small_new, small_first_new, small_second_new = adamw(
        small_params, small_total, small_first, small_second, step
    )
    ema_new = average_keep * adapter_ema + (1.0 - average_keep) * small_new[2 * D : 2 * D + NADAPT]
    return (
        layer_out,
        input_grad,
        owned_grad[None],
        new_first[None],
        new_second[None],
        new_master[None],
        new_master.astype(jnp.bfloat16)[None],
        small_total,
        small_first_new,
        small_second_new,
        small_new,
        ema_new,
    )


def solution(mesh):
    token_spec = P(("dp", "tensor"), None)
    owner_spec = P("tensor", "dp", None)
    return jax.shard_map(
        per_device,
        mesh=mesh,
        in_specs=(token_spec, token_spec, P("dp"), P(), P())
        + (owner_spec,) * 3
        + (P(),) * 5,
        out_specs=(token_spec,) * 2 + (owner_spec,) * 5 + (P(),) * 5,
        check_vma=False,
    )
```

```python
import functools
import math

import jax
import jax.numpy as jnp
from jax import lax
from jax.experimental import pallas as pl
from jax.experimental.pallas import tpu as pltpu
from jax.sharding import PartitionSpec as P

D = 768
H = 12
HS = 64
FF = 3072
NB = 32
R = 48
PHM = 4
SEQ = 1024
NADAPT = 1696

highest = lax.Precision.HIGHEST
norm_epsilon = 1e-06
beta_first = 0.5
beta_second = 0.5
adam_epsilon = 1e-08
rate_per_step = 0.01
weight_decay = 0.1
average_keep = 0.75
masked_score = -1000000000.0

TILE = 128
WINDOW = 2 * SEQ - TILE
QUERY_TILE = 256
KEY_TILE = 256
VMEM_LIMIT = 48 * 1024 * 1024
MESH = pl.DeviceIdType.MESH


def unpack(packed):
    widths = (D, D, PHM**3, D, R, R, D, NB * H)
    pieces = []
    offset = 0
    for width in widths:
        pieces.append(packed[offset : offset + width])
        offset = offset + width
    gain_one, gain_two, mix_flat, down_left, down_right, up_left, up_right, table_flat = pieces
    adapter = (
        mix_flat.reshape(PHM, PHM, PHM),
        down_left.reshape(PHM, D // PHM),
        down_right.reshape(PHM, R // PHM),
        up_left.reshape(PHM, R // PHM),
        up_right.reshape(PHM, D // PHM),
    )
    return (gain_one, gain_two, adapter, table_flat.reshape(NB, H))


def adapter_factors(adapter):
    mix, down_left, down_right, up_left, up_right = adapter
    eye = jnp.eye(PHM, dtype=jnp.float32)
    left = mix.transpose(2, 0, 1)[:, None] * down_right.T[None, :, :, None]
    right = (eye[None, :, :, None] * down_left[:, None, None, :]).reshape(PHM * PHM, D)
    wide = mix.transpose(1, 0, 2)[:, None] * up_left.T[None, :, :, None]
    tall = (eye[None, :, :, None] * up_right[:, None, None, :]).reshape(PHM * PHM, D)
    return (left.reshape(R, PHM * PHM), right, wide.reshape(R, PHM * PHM), tall)


def normal_parts(values):
    size = jnp.abs(values)
    shrink = 1.0 / (1.0 + (0.3275911 * math.sqrt(0.5)) * size)
    bell = jnp.exp(-0.5 * values * values)
    series = 0.5 * 1.061405429
    for term in (-1.453152027, 1.421413741, -0.284496736, 0.254829592):
        series = series * shrink + 0.5 * term
    tail = series * shrink * bell
    return jnp.where(values >= 0.0, 1.0 - tail, tail), bell * (1.0 / math.sqrt(2.0 * math.pi))


def contract(left, right, left_dim, right_dim):
    return lax.dot_general(
        left,
        right,
        (((left_dim,), (right_dim,)), ((), ())),
        preferred_element_type=jnp.float32,
    )


def bias_window(bias, window):
    for tile in range(WINDOW // TILE):
        base = WINDOW - TILE * tile
        row = jnp.broadcast_to(bias[:, base - TILE : base + TILE], (TILE, 2 * TILE))
        rolled = pltpu.roll(row, TILE, 1, stride=1, stride_axis=0)
        window[TILE * tile : TILE * (tile + 1), :] = rolled[:, :TILE]


def attend_head(
    query_rows, key_rows, value_rows, segment_keys_ref, segment_queries_ref, window, scores, exp_ref
):
    keys = key_rows.T
    values = jnp.concatenate([value_rows, jnp.ones((16, SEQ), jnp.bfloat16)], axis=0)
    outs, scales = [], []
    for q0 in range(0, SEQ, QUERY_TILE):
        queries = query_rows[:, q0 : q0 + QUERY_TILE]
        peak = jnp.full((8, QUERY_TILE), -jnp.inf, jnp.float32)
        for k0 in range(0, SEQ, KEY_TILE):
            raw = jnp.dot(keys[k0 : k0 + KEY_TILE], queries, preferred_element_type=jnp.float32)
            parts = []
            for l0 in range(0, QUERY_TILE, TILE):
                start = SEQ - TILE - (q0 + l0) + k0
                same_doc = (
                    segment_keys_ref[k0 : k0 + KEY_TILE, :]
                    == segment_queries_ref[:, q0 + l0 : q0 + l0 + TILE]
                )
                part = jnp.where(
                    same_doc,
                    raw[:, l0 : l0 + TILE] + window[start : start + KEY_TILE, :],
                    masked_score,
                )
                scores[k0 : k0 + KEY_TILE, l0 : l0 + TILE] = part
                parts.append(part)
            whole = jnp.concatenate(parts, axis=1)
            peak = jnp.maximum(peak, jnp.max(whole.reshape(KEY_TILE // 8, 8, QUERY_TILE), axis=0))
        peak = jnp.max(peak, axis=0, keepdims=True)
        total = jnp.zeros((HS + 16, QUERY_TILE), jnp.float32)
        for k0 in range(0, SEQ, KEY_TILE):
            exp_scores = jnp.exp(scores[k0 : k0 + KEY_TILE, :] - peak).astype(jnp.bfloat16)
            exp_ref[k0 : k0 + KEY_TILE, q0 : q0 + QUERY_TILE] = exp_scores
            total = total + jnp.dot(
                values[:, k0 : k0 + KEY_TILE], exp_scores, preferred_element_type=jnp.float32
            )
        scale = 1.0 / total[HS : HS + 1]
        scales.append(scale)
        outs.append((total[:HS] * scale).astype(jnp.bfloat16))
    return jnp.concatenate(outs, axis=1), jnp.concatenate(scales, axis=1)


def one_hot(place, shape, dim):
    hit = lax.broadcasted_iota(jnp.int32, shape, dim) == place
    return jnp.where(hit, 1.0, 0.0).astype(jnp.bfloat16)


def plan_kernel(dp_count, pair_rows, local_sizes, *refs):
    roles = len(local_sizes)
    owner_refs, slot_ref, spread_ref = refs[:roles], refs[roles], refs[roles + 1]
    order_refs, place_refs = refs[roles + 2 : 2 * roles + 2], refs[2 * roles + 2 :]
    dp_pos = lax.axis_index("dp").astype(jnp.float32)

    def quotient(values):
        return jnp.floor((values + 0.5) * (1.0 / dp_count))

    def remainder(values):
        return values - dp_count * quotient(values)

    owners = [ref[...].astype(jnp.float32) for ref in owner_refs]

    def stats(who):
        counts = [
            jnp.sum(jnp.where(row == who, 1.0, 0.0), axis=1, keepdims=True) for row in owners
        ]
        starts = [jnp.sum(jnp.where(row < who, 1.0, 0.0), axis=1, keepdims=True) for row in owners]
        return counts, starts

    def hits(first, number, target):
        return quotient(first + number - 1.0 - target) - quotient(first - 1.0 - target)

    counts, starts = stats(jnp.full((1, 1), dp_pos))
    slot = lax.broadcasted_iota(jnp.int32, slot_ref.shape, 1).astype(jnp.float32)
    found = jnp.full(slot_ref.shape, -1.0)
    low = jnp.zeros((1, 1), jnp.float32)
    for role in range(roles):
        rank = slot - low
        target = remainder(starts[role] + rank)
        place = quotient(rank)
        for other in range(role):
            place = place + hits(starts[other], counts[other], target)
        found = jnp.where(
            (rank >= 0.0) & (rank < counts[role]),
            remainder(target - dp_pos) * pair_rows + place,
            found,
        )
        low = low + counts[role]
    slot_ref[...] = found.astype(jnp.int32)

    column = lax.broadcasted_iota(jnp.int32, (dp_count, 1), 0).astype(jnp.float32)
    counts, starts = stats(remainder(dp_pos - column))
    pair = lax.broadcasted_iota(jnp.int32, spread_ref.shape, 1).astype(jnp.float32)
    found = jnp.full(spread_ref.shape, -1.0)
    passed = jnp.zeros((dp_count, 1), jnp.float32)
    for role in range(roles):
        number = hits(starts[role], counts[role], dp_pos)
        first = starts[role] + remainder(dp_pos - starts[role])
        rank = pair - passed
        local = sum(local_sizes[:role]) + quotient(first) + rank
        found = jnp.where((rank >= 0.0) & (rank < number), local, found)
        passed = passed + number
    spread_ref[...] = found.astype(jnp.int32)

    counts, starts = stats(column)
    for role in range(roles):
        width = owners[role].shape[1]
        before = starts[role]
        for c0 in range(0, width, TILE):
            c1 = min(c0 + TILE, width)
            hot = jnp.where(owners[role][:, c0:c1] == column, 1.0, 0.0)
            shape = (c1 - c0, c1 - c0)
            above = lax.broadcasted_iota(jnp.int32, shape, 0) < lax.broadcasted_iota(
                jnp.int32, shape, 1
            )
            rank = jnp.dot(
                hot.astype(jnp.bfloat16),
                jnp.where(above, 1.0, 0.0).astype(jnp.bfloat16),
                preferred_element_type=jnp.float32,
            )
            number = jnp.sum(hot * (rank + before), axis=0, keepdims=True)
            before = before + jnp.sum(hot, axis=1, keepdims=True)
            target, row = remainder(number), quotient(number)
            order = remainder(dp_pos - target) * local_sizes[role] + row
            place = remainder(target - dp_pos) * local_sizes[role] + row
            order_refs[role][:, c0:c1] = order.astype(jnp.int32)
            place_refs[role][:, c0:c1] = place.astype(jnp.int32)


def plan(owners, sizes, local_sizes, capacity, pair_rows):
    dp_count = lax.axis_size("dp")
    rows, start = [], 0
    for size in sizes:
        rows.append(owners[start : start + size][None, :])
        start += size
    outs = pl.pallas_call(
        functools.partial(plan_kernel, dp_count, pair_rows, local_sizes),
        out_shape=[
            jax.ShapeDtypeStruct((1, capacity), jnp.int32),
            jax.ShapeDtypeStruct((dp_count, pair_rows), jnp.int32),
        ]
        + [jax.ShapeDtypeStruct((1, size), jnp.int32) for size in sizes] * 2,
        name="plan",
    )(*rows)
    return outs[0], outs[1], outs[2 : 2 + len(sizes)], outs[2 + len(sizes) :]


def true_group(positions, group, tensor_count):
    flips = positions + (tensor_count - 1 - positions[0],)
    found = flips[0]
    for g in range(1, tensor_count):
        found = found + (flips[g] - flips[0]) * (
            lax.div(group + tensor_count - g, tensor_count)
            - lax.div(group + tensor_count - g - 1, tensor_count)
        )
    return found


def front_kernel(
    sizes,
    mine_ref,
    slot_place_ref,
    spread_place_ref,
    order_qkv_ref,
    order_out_ref,
    order_in_ref,
    order_down_ref,
    tokens_ref,
    gain_ref,
    table_ref,
    bucket_ref,
    segment_ref,
    w_qkv_ref,
    w_out_ref,
    w_in_ref,
    w_down_ref,
    projected_ref,
    attended_ref,
    scale_ref,
    normed_ref,
    exp_ref,
    sent,
    received,
    spread,
    bias,
    segment_keys,
    buf_qkv,
    buf_out,
    buf_in,
    buf_down,
    stage_out,
    stage_in,
    stage_down,
    window,
    scores,
    exp_stage,
    deal_send,
    deal_recv,
    gather_send,
    gather_recv,
    group_send,
    group_recv,
    local_sem,
    exp_sem,
):
    dp_count, pair_rows = sent.shape[0], sent.shape[1]
    tensor_count = w_qkv_ref.shape[0]
    heads = scale_ref.shape[0]
    group_heads = heads // tensor_count
    head_rows = group_heads * HS
    dp_pos, tensor_pos = lax.axis_index("dp"), lax.axis_index("tensor")
    core_pos = tensor_pos + 1 - 2 * lax.rem(tensor_pos, 2)
    far_pos = lax.rem(tensor_pos + 2, tensor_count)
    core_peer, far_peer = (dp_pos, core_pos), (dp_pos, far_pos)

    def dp_peer(m):
        return (lax.rem(dp_pos + m, dp_count), tensor_pos)

    def each_peer(run):
        def step(m, carry):
            run(m)
            return carry

        lax.fori_loop(1, dp_count, step, 0)

    barrier = pltpu.get_barrier_semaphore()

    def greet(m):
        pl.semaphore_signal(barrier, inc=1, device_id=dp_peer(m), device_id_type=MESH)

    each_peer(greet)
    for peer in (core_peer, far_peer):
        pl.semaphore_signal(barrier, inc=1, device_id=peer, device_id_type=MESH)

    place = slot_place_ref[...]
    mine = mine_ref[...].astype(jnp.bfloat16)
    for m in range(dp_count):
        hot = one_hot(place - m * pair_rows, (pair_rows, mine.shape[0]), 0)
        sent[m] = jnp.dot(hot, mine, preferred_element_type=jnp.float32).astype(jnp.bfloat16)
    pl.semaphore_wait(barrier, dp_count + 1)

    def deal(m):
        return pltpu.make_async_remote_copy(
            sent.at[m],
            received.at[m],
            deal_send.at[m],
            deal_recv.at[m],
            device_id=dp_peer(m),
            device_id_type=MESH,
        )

    each_peer(lambda m: deal(m).start())
    received[0] = sent[0]

    for r0 in range(0, SEQ, 128):
        values = tokens_ref[r0 : r0 + 128, :].astype(jnp.float32)
        inverse = lax.rsqrt(jnp.mean(values * values, axis=1, keepdims=True) + norm_epsilon)
        normed_ref[r0 : r0 + 128, :] = (values * inverse * gain_ref[...]).astype(jnp.bfloat16)
    rest = table_ref[...]
    hot = one_hot(bucket_ref[...], (NB, 2 * SEQ), 0)
    biases = jnp.zeros((rest.shape[0], 2 * SEQ), jnp.float32)
    for _ in range(3):
        part = rest.astype(jnp.bfloat16)
        rest = rest - part.astype(jnp.float32)
        biases = biases + jnp.dot(part, hot, preferred_element_type=jnp.float32)
    for head in range(heads):
        bias[head] = biases[head : head + 1, :]
    segment_keys[...] = jnp.broadcast_to(segment_ref[...], (TILE, SEQ)).T

    each_peer(lambda m: deal(m).wait())
    rows = spread.shape[0]
    total = jnp.zeros((rows, D), jnp.float32)
    for m in range(dp_count):
        hot = one_hot(spread_place_ref[m : m + 1, :], (rows, pair_rows), 0)
        total = total + jnp.dot(hot, received[m], preferred_element_type=jnp.float32)
    spread[...] = total.astype(jnp.bfloat16)

    bufs = (buf_qkv, buf_out, buf_in, buf_down)
    orders = (order_qkv_ref, order_out_ref, order_in_ref, order_down_ref)
    stages = (w_qkv_ref.at[0], stage_out, stage_in, stage_down)
    finals = (w_qkv_ref, w_out_ref, w_in_ref, w_down_ref)
    offsets = [sum(buf.shape[1] for buf in bufs[:role]) for role in range(len(bufs))]

    def gather(role, m):
        count = bufs[role].shape[1]
        return pltpu.make_async_remote_copy(
            spread.at[pl.ds(offsets[role], count)],
            bufs[role].at[m],
            gather_send.at[role, m],
            gather_recv.at[role, m],
            device_id=dp_peer(m),
            device_id_type=MESH,
        )

    def start_gather(role):
        each_peer(lambda m: gather(role, m).start())
        bufs[role][0] = spread[offsets[role] : offsets[role] + bufs[role].shape[1], :]

    def order(role):
        each_peer(lambda m: gather(role, m).wait())
        count = bufs[role].shape[1]
        source = bufs[role][...].reshape(dp_count * count, D)
        step = 256
        for r0 in range(0, sizes[role], step):
            r1 = min(r0 + step, sizes[role])
            hot = one_hot(orders[role][:, r0:r1], (dp_count * count, r1 - r0), 0)
            stages[role][r0:r1, :] = contract(hot, source, 0, 0).astype(jnp.bfloat16)

    def share(role, part):
        src, slot, peer = (
            (stages[role], 1, core_peer),
            (stages[role], 2, far_peer),
            (finals[role].at[2], 3, core_peer),
        )[part]
        return pltpu.make_async_remote_copy(
            src,
            finals[role].at[slot],
            group_send.at[role, part],
            group_recv.at[role, part],
            device_id=peer,
            device_id_type=MESH,
        )

    def keep(role):
        return pltpu.make_async_copy(stages[role], finals[role].at[0], local_sem.at[role])

    def start_share(role):
        order(role)
        share(role, 0).start()
        share(role, 1).start()
        if role > 0:
            keep(role).start()

    def forward(role):
        share(role, 1).wait_recv()
        share(role, 2).start()

    start_gather(0)
    start_share(0)
    start_gather(1)
    start_gather(2)

    def true_head(group, head):
        return true_group((tensor_pos, core_pos, far_pos), group, tensor_count) * group_heads + head

    def head_step(i, carry):
        group, head = lax.div(i, group_heads), lax.rem(i, group_heads)

        @pl.when(i == 1)
        def _():
            start_share(1)

        @pl.when(i == group_heads)
        def _():
            share(0, 0).wait_recv()

        @pl.when(i == 2 * group_heads)
        def _():
            forward(0)

        @pl.when(i == 3 * group_heads)
        def _():
            share(0, 2).wait_recv()
            forward(1)
            start_gather(3)

        @pl.when(head == 0)
        def _():
            projected_ref[group] = contract(w_qkv_ref[group], normed_ref[...], 1, 1).astype(
                jnp.bfloat16
            )

        def head_part(part):
            start = pl.multiple_of(part * head_rows + head * HS, HS)
            return projected_ref[group, pl.ds(start, HS), :]

        slot = lax.rem(i, 2)

        def save(head_index, slot):
            return pltpu.make_async_copy(
                exp_stage.at[slot], exp_ref.at[head_index], exp_sem.at[slot]
            )

        @pl.when(i >= 2)
        def _():
            save(i - 2, slot).wait()

        bias_window(bias[true_head(group, head)], window)
        attended, scale = attend_head(
            head_part(0),
            head_part(1),
            head_part(2),
            segment_keys,
            segment_ref,
            window,
            scores,
            exp_stage.at[slot],
        )
        attended_ref[pl.ds(pl.multiple_of(i * HS, HS), HS), :] = attended
        scale_ref[i] = scale
        save(i, slot).start()
        return carry

    lax.fori_loop(0, heads, head_step, 0)
    for i in (heads - 2, heads - 1):
        pltpu.make_async_copy(exp_stage.at[i % 2], exp_ref.at[i], exp_sem.at[i % 2]).wait()
    start_share(2)
    start_share(3)
    forward(2)
    forward(3)
    for role in range(len(bufs)):
        share(role, 0).wait_send()
        share(role, 1).wait_send()
        share(role, 2).wait_send()
        if role > 0:
            share(role, 0).wait_recv()
            share(role, 2).wait_recv()
            keep(role).wait()


def front(
    mine,
    slot_place,
    spread_place,
    orders,
    local_sizes,
    tokens,
    gain,
    table,
    bucket_place,
    segments,
):
    dp_count, tensor_count = lax.axis_size("dp"), lax.axis_size("tensor")
    sizes = [order.shape[1] for order in orders]
    pair_rows = spread_place.shape[1]
    low = jnp.bfloat16
    dma = pltpu.SemaphoreType.DMA
    roles = len(sizes)
    whole = pl.BlockSpec(memory_space=pltpu.VMEM)
    away = pl.BlockSpec(memory_space=pl.ANY)
    return pl.pallas_call(
        functools.partial(front_kernel, sizes),
        in_specs=[whole] * 12,
        out_specs=[whole, away, away, away, whole, whole, whole, whole, away],
        out_shape=[jax.ShapeDtypeStruct((tensor_count, size, D), low) for size in sizes]
        + [
            jax.ShapeDtypeStruct((tensor_count, sizes[0], SEQ), low),
            jax.ShapeDtypeStruct((H * HS, SEQ), low),
            jax.ShapeDtypeStruct((H, 1, SEQ), jnp.float32),
            jax.ShapeDtypeStruct((SEQ, D), low),
            jax.ShapeDtypeStruct((H, SEQ, SEQ), low),
        ],
        scratch_shapes=[
            pltpu.VMEM((dp_count, pair_rows, D), low),
            pltpu.VMEM((dp_count, pair_rows, D), low),
            pltpu.VMEM((sum(local_sizes), D), low),
            pltpu.VMEM((H, 1, 2 * SEQ), jnp.float32),
            pltpu.VMEM((SEQ, TILE), jnp.float32),
        ]
        + [pltpu.VMEM((dp_count, size, D), low) for size in local_sizes]
        + [pltpu.VMEM((size, D), low) for size in sizes[1:]]
        + [
            pltpu.VMEM((WINDOW, TILE), jnp.float32),
            pltpu.VMEM((SEQ, QUERY_TILE), jnp.float32),
            pltpu.VMEM((2, SEQ, SEQ), low),
            dma((dp_count,)),
            dma((dp_count,)),
            dma((roles, dp_count)),
            dma((roles, dp_count)),
            dma((roles, 3)),
            dma((roles, 3)),
            dma((roles,)),
            dma((2,)),
        ],
        compiler_params=pltpu.CompilerParams(
            collective_id=1, has_side_effects=True, vmem_limit_bytes=56 * 1024 * 1024
        ),
        cost_estimate=pl.CostEstimate(
            flops=10 * H * SEQ * SEQ * 256,
            bytes_accessed=64 * 1024 * 1024,
            transcendentals=H * SEQ * SEQ,
        ),
        name="front",
    )(
        mine,
        slot_place,
        spread_place,
        *orders,
        tokens,
        gain[None, :],
        table,
        bucket_place,
        segments.astype(jnp.float32)[None, :],
    )


def attend_head_back(
    query_rows,
    key_rows,
    value_rows,
    exp_ref,
    attended,
    scale,
    attended_grad,
    window,
    score_grads,
    store,
):
    scaled = attended_grad.astype(jnp.float32) * scale
    delta = jnp.sum(scaled * attended.astype(jnp.float32), axis=0, keepdims=True)
    scaled_low = scaled.astype(jnp.bfloat16)
    delta_high = delta.astype(jnp.bfloat16).astype(jnp.float32)
    delta_rest = delta - delta_high
    place = lax.broadcasted_iota(jnp.int32, (16, SEQ), 0)
    extra = jnp.where(
        place == 0,
        jnp.broadcast_to(-delta_high, (16, SEQ)),
        jnp.where(place == 1, jnp.broadcast_to(-delta_rest, (16, SEQ)), 0.0),
    ).astype(jnp.bfloat16)
    grads = jnp.concatenate([scaled_low, extra], axis=0)
    values = jnp.concatenate([value_rows, jnp.ones((16, SEQ), jnp.bfloat16)], axis=0).T
    window[...] = jnp.zeros_like(window)
    for q0 in range(0, SEQ, QUERY_TILE):
        total = jnp.zeros((HS, QUERY_TILE), jnp.float32)
        for k0 in range(0, SEQ, KEY_TILE):
            centered = jnp.dot(
                values[k0 : k0 + KEY_TILE],
                grads[:, q0 : q0 + QUERY_TILE],
                preferred_element_type=jnp.float32,
            )
            score_grad = centered * exp_ref[
                k0 : k0 + KEY_TILE, q0 : q0 + QUERY_TILE
            ].astype(jnp.float32)
            for l0 in range(0, QUERY_TILE, TILE):
                start = SEQ - TILE - (q0 + l0) + k0
                window[start : start + KEY_TILE, :] += score_grad[:, l0 : l0 + TILE]
            score_low = score_grad.astype(jnp.bfloat16)
            score_grads[k0 : k0 + KEY_TILE, q0 : q0 + QUERY_TILE] = score_low
            total = total + jnp.dot(
                key_rows[:, k0 : k0 + KEY_TILE], score_low, preferred_element_type=jnp.float32
            )
        store(0, q0, total.astype(jnp.bfloat16))
    queries = query_rows.T
    scaled_rows = scaled_low.T
    for k0 in range(0, SEQ, KEY_TILE):
        key_grad = jnp.dot(
            score_grads[k0 : k0 + KEY_TILE, :], queries, preferred_element_type=jnp.float32
        )
        value_grad = jnp.dot(
            exp_ref[k0 : k0 + KEY_TILE, :], scaled_rows, preferred_element_type=jnp.float32
        )
        store(1, k0, key_grad.T.astype(jnp.bfloat16))
        store(2, k0, value_grad.T.astype(jnp.bfloat16))
    pieces = [jnp.zeros((1, TILE), jnp.float32)] * (2 * SEQ // TILE)
    for tile in range(WINDOW // TILE):
        base = WINDOW - TILE * tile
        block = window[TILE * tile : TILE * (tile + 1), :]
        folded = jnp.concatenate([jnp.zeros((TILE, TILE), jnp.float32), block], axis=1)
        rows = TILE // 2
        while rows >= 1:
            folded = folded[:rows] + pltpu.roll(folded[rows:], 2 * TILE - rows, 1)
            rows //= 2
        pieces[base // TILE - 1] += folded[:, :TILE]
        pieces[base // TILE] += folded[:, TILE:]
    return jnp.concatenate(pieces, axis=1)


SMALL_ROWS = 48
TABLE_ROW = 32


def back_kernel(
    sizes,
    grad_out_ref,
    grad_in_ref,
    grad_down_ref,
    projected_ref,
    exp_ref,
    attended_ref,
    scale_ref,
    attended_grad_ref,
    normed_ref,
    w_qkv_ref,
    tokens_ref,
    mid_grad_ref,
    gain_ref,
    small_ref,
    bucket_ref,
    place_qkv_ref,
    place_out_ref,
    place_in_ref,
    place_down_ref,
    spread_place_ref,
    slot_place_ref,
    owned_ref,
    input_grad_ref,
    small_total_ref,
    bucket_hot,
    proj,
    proj_grad,
    normed_grad,
    window,
    score_grads,
    exp_stage,
    qkv_odd,
    zero_qkv,
    zero_out,
    zero_in,
    zero_down,
    two_qkv,
    two_out,
    two_in,
    two_down,
    core_one_qkv,
    core_one_out,
    core_one_in,
    core_one_down,
    core_three_qkv,
    core_three_out,
    core_three_in,
    core_three_down,
    far_qkv,
    far_out,
    far_in,
    far_down,
    got_qkv,
    got_out,
    got_in,
    got_down,
    spread,
    sent,
    received,
    small_own,
    small_tensor,
    small_dp,
    core_send,
    core_recv,
    far_send,
    far_recv,
    deal_send,
    deal_recv,
    back_send,
    back_recv,
    small_send,
    small_recv,
    load_sem,
    exp_sem,
    proj_sem,
):
    dp_count, pair_rows = sent.shape[0], sent.shape[1]
    tensor_count = w_qkv_ref.shape[0]
    heads = scale_ref.shape[0]
    group_heads = heads // tensor_count
    head_rows = group_heads * HS
    dp_pos, tensor_pos = lax.axis_index("dp"), lax.axis_index("tensor")
    core_pos = tensor_pos + 1 - 2 * lax.rem(tensor_pos, 2)
    far_pos = lax.rem(tensor_pos + 2, tensor_count)
    core_peer, far_peer = (dp_pos, core_pos), (dp_pos, far_pos)
    grad_refs = (None, grad_out_ref, grad_in_ref, grad_down_ref)
    zeros = (zero_qkv, zero_out, zero_in, zero_down)
    twos = (two_qkv, two_out, two_in, two_down)
    core_ones = (core_one_qkv, core_one_out, core_one_in, core_one_down)
    core_threes = (core_three_qkv, core_three_out, core_three_in, core_three_down)
    fars = (far_qkv, far_out, far_in, far_down)
    gots = (got_qkv, got_out, got_in, got_down)
    places = (place_qkv_ref, place_out_ref, place_in_ref, place_down_ref)
    offsets = [sum(got.shape[1] for got in gots[:role]) for role in range(len(gots))]
    low = jnp.bfloat16

    def up(m):
        return lax.rem(dp_pos + m, dp_count)

    def down(m):
        return lax.rem(dp_pos + dp_count - m, dp_count)

    def each_peer(run):
        def step(m, carry):
            run(m)
            return carry

        lax.fori_loop(1, dp_count, step, 0)

    def tensor_peer(m):
        return (dp_pos, lax.rem(tensor_pos + m, tensor_count))

    barrier = pltpu.get_barrier_semaphore()

    def greet(m):
        pl.semaphore_signal(barrier, inc=1, device_id=(up(m), tensor_pos), device_id_type=MESH)

    each_peer(greet)
    for m in range(1, tensor_count):
        pl.semaphore_signal(barrier, inc=1, device_id=tensor_peer(m), device_id_type=MESH)

    def load_exp(head, slot):
        return pltpu.make_async_copy(exp_ref.at[head], exp_stage.at[slot], exp_sem.at[slot])

    def load_proj(group):
        return pltpu.make_async_copy(projected_ref.at[group], proj, proj_sem)

    def load(role, which):
        target = zeros[role] if which == 0 else twos[role]
        return pltpu.make_async_copy(
            grad_refs[role].at[which], target, load_sem.at[role, which // 2]
        )

    def core_copy(role, which):
        if role == 0:
            src = qkv_odd.at[which // 2]
        else:
            src = grad_refs[role].at[which]
        target = core_ones[role] if which == 1 else core_threes[role].at[pl.ds(0, sizes[role])]
        return pltpu.make_async_remote_copy(
            src,
            target,
            core_send.at[role, which // 2],
            core_recv.at[role, which // 2],
            device_id=core_peer,
            device_id_type=MESH,
        )

    def far_copy(role):
        return pltpu.make_async_remote_copy(
            twos[role],
            fars[role],
            far_send.at[role],
            far_recv.at[role],
            device_id=far_peer,
            device_id_type=MESH,
        )

    def deal_copy(role, m):
        count = gots[role].shape[1]
        start = pl.multiple_of(m * count, 16)
        return pltpu.make_async_remote_copy(
            core_threes[role].at[pl.ds(start, count)],
            gots[role].at[m],
            deal_send.at[role, m],
            deal_recv.at[role, m],
            device_id=(up(m), tensor_pos),
            device_id_type=MESH,
        )

    def send_far(role):
        core_copy(role, 3).wait_recv()
        if role > 0:
            load(role, 2).wait()
        count = twos[role].shape[0]
        twos[role][...] = (
            twos[role][...].astype(jnp.float32)
            + core_threes[role][0:count, :].astype(jnp.float32)
        ).astype(low)
        far_copy(role).start()

    def send_deal(role):
        core_copy(role, 1).wait_recv()
        if role > 0:
            load(role, 0).wait()
        far_copy(role).wait_recv()
        total = (
            zeros[role][...].astype(jnp.float32)
            + core_ones[role][...].astype(jnp.float32)
            + fars[role][...].astype(jnp.float32)
        ).astype(low)
        count = gots[role].shape[1]
        for m in range(dp_count):
            hot = one_hot(places[role][...] - m * count, (count, sizes[role]), 0)
            core_threes[role][m * count : (m + 1) * count, :] = jnp.dot(
                hot, total, preferred_element_type=jnp.float32
            ).astype(low)
        each_peer(lambda m: deal_copy(role, m).start())

    def finish_deal(role):
        each_peer(lambda m: deal_copy(role, m).wait())
        count = gots[role].shape[1]
        total = core_threes[role][0:count, :].astype(jnp.float32)
        for m in range(1, dp_count):
            total = total + gots[role][m].astype(jnp.float32)
        spread[offsets[role] : offsets[role] + count, :] = total.astype(low)

    load_exp(heads - group_heads, 0).start()
    load_proj(tensor_count - 1).start()
    for role in (3, 2, 1):
        load(role, 2).start()
        load(role, 0).start()
    bucket_hot[...] = one_hot(bucket_ref[...], (TILE, 2 * SEQ), 0)
    normed_grad[...] = jnp.zeros_like(normed_grad)
    small_own[0:TABLE_ROW, :] = small_ref[...]
    small_own[TABLE_ROW:SMALL_ROWS, :] = jnp.zeros((SMALL_ROWS - TABLE_ROW, TILE), jnp.float32)
    pl.semaphore_wait(barrier, dp_count + tensor_count - 2)
    for role in (3, 2, 1):
        core_copy(role, 3).start()
        core_copy(role, 1).start()

    def head_step(i, carry):
        group = tensor_count - 1 - lax.div(i, group_heads)
        part_head = lax.rem(i, group_heads)
        head = group * group_heads + part_head
        slot = lax.rem(i, 2)

        @pl.when(i == 1)
        def _():
            send_far(3)

        @pl.when(i == 7)
        def _():
            send_far(2)

        @pl.when(i == 9)
        def _():
            send_deal(3)

        @pl.when(part_head == 0)
        def _():
            load_proj(group).wait()

        @pl.when(i + 1 < heads)
        def _():
            later = i + 1
            later_group = tensor_count - 1 - lax.div(later, group_heads)
            later_head = later_group * group_heads + lax.rem(later, group_heads)
            load_exp(later_head, lax.rem(later, 2)).start()

        load_exp(head, slot).wait()

        def rows(part):
            return pl.ds(pl.multiple_of(part * head_rows + part_head * HS, HS), HS)

        def store(part, column, value):
            proj_grad[rows(part), column : column + value.shape[1]] = value

        here = pl.ds(pl.multiple_of(head * HS, HS), HS)
        offset_grad = attend_head_back(
            proj[rows(0), :],
            proj[rows(1), :],
            proj[rows(2), :],
            exp_stage.at[slot],
            attended_ref[here, :],
            scale_ref[head],
            attended_grad_ref[here, :],
            window,
            score_grads,
            store,
        )
        place = (
            true_group((tensor_pos, core_pos, far_pos), group, tensor_count) * group_heads + part_head
        )
        high = offset_grad.astype(low)
        rest = (offset_grad - high.astype(jnp.float32)).astype(low)
        both = jnp.concatenate([high, rest] + [jnp.zeros_like(high)] * 6, axis=0)
        sums = contract(both, bucket_hot[...], 1, 1)
        line = lax.broadcasted_iota(jnp.int32, (SMALL_ROWS - TABLE_ROW, TILE), 0)
        small_own[TABLE_ROW:SMALL_ROWS, :] += jnp.where(
            line == place,
            jnp.broadcast_to(sums[0:1] + sums[1:2], (SMALL_ROWS - TABLE_ROW, TILE)),
            0.0,
        )

        @pl.when(part_head == group_heads - 1)
        def _():
            @pl.when(group > 0)
            def _():
                load_proj(group - 1).start()

            def weight_grad(target):
                for r0 in range(0, 3 * head_rows, head_rows):
                    target[r0 : r0 + head_rows, :] = jnp.dot(
                        proj_grad[r0 : r0 + head_rows, :],
                        normed_ref[...],
                        preferred_element_type=jnp.float32,
                    ).astype(low)

            @pl.when(group == 3)
            def _():
                weight_grad(qkv_odd.at[1])
                core_copy(0, 3).start()

            @pl.when(group == 2)
            def _():
                weight_grad(two_qkv)

            @pl.when(group == 1)
            def _():
                weight_grad(qkv_odd.at[0])
                core_copy(0, 1).start()

            @pl.when(group == 0)
            def _():
                weight_grad(zero_qkv)

            for r0 in range(0, SEQ, 256):
                normed_grad[r0 : r0 + 256, :] += jnp.dot(
                    proj_grad[:, r0 : r0 + 256].T,
                    w_qkv_ref[group],
                    preferred_element_type=jnp.float32,
                )

        return carry

    lax.fori_loop(0, heads, head_step, 0)
    send_far(1)
    send_far(0)

    gain_grad = jnp.zeros((1, D), jnp.float32)
    for r0 in range(0, SEQ, 128):
        values = tokens_ref[r0 : r0 + 128, :].astype(jnp.float32)
        grads = normed_grad[r0 : r0 + 128, :]
        inverse = lax.rsqrt(jnp.mean(values * values, axis=1, keepdims=True) + norm_epsilon)
        scaled = values * inverse
        gain_grad = gain_grad + jnp.sum(grads * scaled, axis=0, keepdims=True)
        grads = grads * gain_ref[...]
        inner = jnp.mean(grads * scaled, axis=1, keepdims=True)
        input_grad_ref[r0 : r0 + 128, :] = (
            mid_grad_ref[r0 : r0 + 128, :].astype(jnp.float32) + inverse * (grads - scaled * inner)
        ).astype(low)
    for part in range(D // TILE):
        small_own[part : part + 1, :] = gain_grad[:, TILE * part : TILE * (part + 1)]

    def small_copy(stage, m):
        if stage == 0:
            src, target, peer = small_own, small_tensor.at[tensor_pos], tensor_peer(m)
        else:
            src, target, peer = small_total_ref, small_dp.at[dp_pos], (up(m), tensor_pos)
        return pltpu.make_async_remote_copy(
            src,
            target,
            small_send.at[stage, m],
            small_recv.at[stage, m],
            device_id=peer,
            device_id_type=MESH,
        )

    for m in range(1, tensor_count):
        small_copy(0, m).start()
    send_deal(2)
    small_tensor[tensor_pos] = small_own[...]
    for m in range(1, tensor_count):
        small_copy(0, m).wait()
    total = small_tensor[0]
    for m in range(1, tensor_count):
        total = total + small_tensor[m]
    small_total_ref[...] = total
    each_peer(lambda m: small_copy(1, m).start())
    send_deal(1)
    finish_deal(3)
    send_deal(0)
    small_dp[dp_pos] = small_total_ref[...]
    each_peer(lambda m: small_copy(1, m).wait())
    total = small_dp[0]
    for m in range(1, dp_count):
        total = total + small_dp[m]
    small_total_ref[...] = total
    for role in (2, 1, 0):
        finish_deal(role)

    values = spread[...]
    for m in range(dp_count):
        hot = one_hot(spread_place_ref[m : m + 1, :], (values.shape[0], pair_rows), 0)
        sent[m] = contract(hot, values, 0, 0).astype(low)

    def back_copy(m):
        return pltpu.make_async_remote_copy(
            sent.at[m],
            received.at[m],
            back_send.at[m],
            back_recv.at[m],
            device_id=(down(m), tensor_pos),
            device_id_type=MESH,
        )

    each_peer(lambda m: back_copy(m).start())
    received[0] = sent[0]
    each_peer(lambda m: back_copy(m).wait())
    hot = one_hot(slot_place_ref[...], (dp_count * pair_rows, owned_ref.shape[0]), 0)
    owned_ref[...] = contract(hot, received[...].reshape(dp_count * pair_rows, D), 0, 0)
    for role in range(len(gots)):
        core_copy(role, 1).wait_send()
        core_copy(role, 3).wait_send()
        far_copy(role).wait_send()


def back(
    weight_grads,
    projected,
    exp_scores,
    attended,
    scale,
    attended_grad,
    normed,
    w_qkv,
    tokens,
    mid_grad,
    gain,
    small,
    bucket_place,
    places,
    local_sizes,
    spread_place,
    slot_place,
):
    dp_count, tensor_count = lax.axis_size("dp"), lax.axis_size("tensor")
    sizes = [place.shape[1] for place in places]
    capacity, pair_rows = slot_place.shape[1], spread_place.shape[1]
    low = jnp.bfloat16
    dma = pltpu.SemaphoreType.DMA
    roles = len(sizes)
    whole = pl.BlockSpec(memory_space=pltpu.VMEM)
    away = pl.BlockSpec(memory_space=pl.ANY)
    parts = [pltpu.VMEM((size, D), low) for size in sizes]
    padded = [
        pltpu.VMEM((max(dp_count * size, full), D), low) for size, full in zip(local_sizes, sizes)
    ]
    return pl.pallas_call(
        functools.partial(back_kernel, sizes),
        in_specs=[away] * 5 + [whole] * 16,
        out_specs=[whole] * 3,
        out_shape=[
            jax.ShapeDtypeStruct((capacity, D), jnp.float32),
            jax.ShapeDtypeStruct((SEQ, D), low),
            jax.ShapeDtypeStruct((SMALL_ROWS, TILE), jnp.float32),
        ],
        scratch_shapes=[
            pltpu.VMEM((TILE, 2 * SEQ), low),
            pltpu.VMEM((sizes[0], SEQ), low),
            pltpu.VMEM((sizes[0], SEQ), low),
            pltpu.VMEM((SEQ, D), jnp.float32),
            pltpu.VMEM((WINDOW, TILE), jnp.float32),
            pltpu.VMEM((SEQ, SEQ), low),
            pltpu.VMEM((2, SEQ, SEQ), low),
            pltpu.VMEM((2, sizes[0], D), low),
        ]
        + parts
        + parts
        + parts
        + padded
        + parts
        + [pltpu.VMEM((dp_count, size, D), low) for size in local_sizes]
        + [
            pltpu.VMEM((sum(local_sizes), D), low),
            pltpu.VMEM((dp_count, pair_rows, D), low),
            pltpu.VMEM((dp_count, pair_rows, D), low),
            pltpu.VMEM((SMALL_ROWS, TILE), jnp.float32),
            pltpu.VMEM((tensor_count, SMALL_ROWS, TILE), jnp.float32),
            pltpu.VMEM((dp_count, SMALL_ROWS, TILE), jnp.float32),
            dma((roles, 2)),
            dma((roles, 2)),
            dma((roles,)),
            dma((roles,)),
            dma((roles, dp_count)),
            dma((roles, dp_count)),
            dma((dp_count,)),
            dma((dp_count,)),
            dma((2, max(dp_count, tensor_count))),
            dma((2, max(dp_count, tensor_count))),
            dma((roles, 2)),
            dma((2,)),
            dma,
        ],
        compiler_params=pltpu.CompilerParams(
            collective_id=2, has_side_effects=True, vmem_limit_bytes=62 * 1024 * 1024
        ),
        cost_estimate=pl.CostEstimate(
            flops=16 * H * SEQ * SEQ * 256,
            bytes_accessed=64 * 1024 * 1024,
            transcendentals=0,
        ),
        name="back",
    )(
        *weight_grads,
        projected,
        exp_scores,
        attended,
        scale,
        attended_grad,
        normed,
        w_qkv,
        tokens,
        mid_grad,
        gain[None, :],
        small,
        bucket_place,
        *places,
        spread_place,
        slot_place,
    )


FEED_WIDTH = 384


def feed_kernel(
    attended_ref,
    w_out_ref,
    tokens_ref,
    gain_ref,
    cotangent_ref,
    left_ref,
    right_ref,
    wide_ref,
    tall_ref,
    w_in_ref,
    w_down_ref,
    activ_ref,
    slope_ref,
    normed_ref,
    mid_ref,
    layer_out_ref,
    ffn_grad_ref,
    left_grad_ref,
    right_grad_ref,
    wide_grad_ref,
    tall_grad_ref,
    ffn_out,
):
    low = jnp.bfloat16
    row_tile = 256
    tiles = range(0, SEQ, row_tile)

    @pl.when(pl.program_id(0) == 0)
    def _():
        for r0 in tiles:
            rows = slice(r0, r0 + row_tile)
            attn = jnp.dot(
                attended_ref[:, rows].T, w_out_ref[...], preferred_element_type=jnp.float32
            )
            mid = tokens_ref[rows, :].astype(jnp.float32) + attn
            mid_ref[rows, :] = mid
            inverse = lax.rsqrt(jnp.mean(mid * mid, axis=1, keepdims=True) + norm_epsilon)
            normed_ref[rows, :] = (mid * inverse * gain_ref[...]).astype(low)
            ffn_out[rows, :] = jnp.zeros((row_tile, D), jnp.float32)

    for r0 in tiles:
        rows = slice(r0, r0 + row_tile)
        pre = contract(normed_ref[rows, :], w_in_ref[...], 1, 1)
        cdf, density = normal_parts(pre)
        activ = (pre * cdf).astype(low)
        activ_ref[rows, :] = activ
        slope_ref[rows, :] = (cdf + pre * density).astype(low)
        ffn_out[rows, :] += jnp.dot(activ, w_down_ref[...], preferred_element_type=jnp.float32)

    @pl.when(pl.program_id(0) == pl.num_programs(0) - 1)
    def _():
        down = jnp.dot(
            left_ref[...], right_ref[...], precision=highest, preferred_element_type=jnp.float32
        ).astype(low)
        up = jnp.dot(
            wide_ref[...], tall_ref[...], precision=highest, preferred_element_type=jnp.float32
        ).astype(low)
        down_grad = jnp.zeros((R, D), jnp.float32)
        up_grad = jnp.zeros((R, D), jnp.float32)
        for r0 in tiles:
            rows = slice(r0, r0 + row_tile)
            ffn = ffn_out[rows, :]
            ffn_low = ffn.astype(low)
            grad_low = cotangent_ref[rows, :]
            zed = contract(ffn_low, down, 1, 1)
            cdf, density = normal_parts(zed)
            hidden = (zed * cdf).astype(low)
            added = jnp.dot(hidden, up, preferred_element_type=jnp.float32)
            layer_out_ref[rows, :] = (mid_ref[rows, :] + ffn + added).astype(low)
            zed_grad = contract(grad_low, up, 1, 1) * (cdf + zed * density)
            zed_low = zed_grad.astype(low)
            ffn_grad_ref[rows, :] = (
                grad_low.astype(jnp.float32)
                + jnp.dot(zed_low, down, preferred_element_type=jnp.float32)
            ).astype(low)
            up_grad = up_grad + contract(hidden, grad_low, 0, 0)
            down_grad = down_grad + contract(zed_low, ffn_low, 0, 0)

        def exact(left, right, left_dim, right_dim):
            return lax.dot_general(
                left,
                right,
                (((left_dim,), (right_dim,)), ((), ())),
                precision=highest,
                preferred_element_type=jnp.float32,
            )

        left_grad_ref[...] = exact(down_grad, right_ref[...], 1, 1)
        right_grad_ref[...] = exact(left_ref[...], down_grad, 0, 0)
        wide_grad_ref[...] = exact(up_grad, tall_ref[...], 1, 1)
        tall_grad_ref[...] = exact(wide_ref[...], up_grad, 0, 0)


def feed(attended, w_out, tokens, gain, cotangent, factors, w_in, w_down):
    def fixed(*shape):
        return pl.BlockSpec(shape, lambda j: (0,) * len(shape))

    def stripe():
        return pl.BlockSpec((FEED_WIDTH, D), lambda j: (j, 0))

    low = jnp.bfloat16
    factor_specs = [fixed(*factor.shape) for factor in factors]
    outs = pl.pallas_call(
        feed_kernel,
        grid=(FF // FEED_WIDTH,),
        in_specs=[
            fixed(D, SEQ),
            fixed(D, D),
            fixed(SEQ, D),
            fixed(1, D),
            fixed(SEQ, D),
            *factor_specs,
            stripe(),
            stripe(),
        ],
        out_specs=[
            pl.BlockSpec((SEQ, FEED_WIDTH), lambda j: (0, j)),
            pl.BlockSpec((SEQ, FEED_WIDTH), lambda j: (0, j)),
            fixed(SEQ, D),
            fixed(SEQ, D),
            fixed(SEQ, D),
            fixed(SEQ, D),
            *factor_specs,
        ],
        out_shape=[
            jax.ShapeDtypeStruct((SEQ, FF), low),
            jax.ShapeDtypeStruct((SEQ, FF), low),
            jax.ShapeDtypeStruct((SEQ, D), low),
            jax.ShapeDtypeStruct((SEQ, D), jnp.float32),
            jax.ShapeDtypeStruct((SEQ, D), low),
            jax.ShapeDtypeStruct((SEQ, D), low),
            *[jax.ShapeDtypeStruct(factor.shape, jnp.float32) for factor in factors],
        ],
        scratch_shapes=[pltpu.VMEM((SEQ, D), jnp.float32)],
        compiler_params=pltpu.CompilerParams(vmem_limit_bytes=VMEM_LIMIT),
        cost_estimate=pl.CostEstimate(
            flops=6 * SEQ * FF * D, bytes_accessed=32 * 1024 * 1024, transcendentals=2 * SEQ * FF
        ),
        name="feed",
    )(attended, w_out, tokens, gain[None, :], cotangent, *factors, w_in, w_down)
    return outs[:6], tuple(outs[6:])


def feed_back_kernel(
    ffn_grad_ref,
    normed_ref,
    mid_ref,
    gain_ref,
    cotangent_ref,
    attended_ref,
    w_out_ref,
    activ_ref,
    slope_ref,
    w_in_ref,
    w_down_ref,
    in_grad_ref,
    down_grad_ref,
    mid_grad_ref,
    gain_grad_ref,
    out_grad_ref,
    attended_grad_ref,
    normed_grad,
    pre_grad,
):
    low = jnp.bfloat16
    row_tile = 256
    tiles = range(0, SEQ, row_tile)

    @pl.when(pl.program_id(0) == 0)
    def _():
        normed_grad[...] = jnp.zeros_like(normed_grad)

    for r0 in tiles:
        rows = slice(r0, r0 + row_tile)
        grad = contract(ffn_grad_ref[rows, :], w_down_ref[...], 1, 1)
        grad = (grad * slope_ref[rows, :].astype(jnp.float32)).astype(low)
        pre_grad[rows, :] = grad
        normed_grad[rows, :] += jnp.dot(grad, w_in_ref[...], preferred_element_type=jnp.float32)
    for c0 in range(0, FEED_WIDTH, TILE):
        columns = slice(c0, c0 + TILE)
        down_grad_ref[columns, :] = jnp.dot(
            activ_ref[:, columns].T, ffn_grad_ref[...], preferred_element_type=jnp.float32
        ).astype(low)
        in_grad_ref[columns, :] = jnp.dot(
            pre_grad[:, columns].T, normed_ref[...], preferred_element_type=jnp.float32
        ).astype(low)

    @pl.when(pl.program_id(0) == pl.num_programs(0) - 1)
    def _():
        gain_grad = jnp.zeros((1, D), jnp.float32)
        for r0 in tiles:
            rows = slice(r0, r0 + row_tile)
            mid = mid_ref[rows, :]
            grads = normed_grad[rows, :]
            inverse = lax.rsqrt(jnp.mean(mid * mid, axis=1, keepdims=True) + norm_epsilon)
            scaled = mid * inverse
            gain_grad = gain_grad + jnp.sum(grads * scaled, axis=0, keepdims=True)
            grads = grads * gain_ref[...]
            inner = jnp.mean(grads * scaled, axis=1, keepdims=True)
            mid_grad_ref[rows, :] = (
                cotangent_ref[rows, :].astype(jnp.float32) + inverse * (grads - scaled * inner)
            ).astype(low)
        gain_grad_ref[...] = gain_grad
        for r0 in range(0, D, 256):
            rows = slice(r0, r0 + 256)
            out_grad_ref[rows, :] = jnp.dot(
                attended_ref[rows, :], mid_grad_ref[...], preferred_element_type=jnp.float32
            ).astype(low)
            attended_grad_ref[rows, :] = contract(
                w_out_ref[rows, :], mid_grad_ref[...], 1, 1
            ).astype(low)


def feed_back(ffn_grad, normed, mid, gain, cotangent, attended, w_out, activ, slope, w_in, w_down):
    def fixed(*shape):
        return pl.BlockSpec(shape, lambda j: (0,) * len(shape))

    def stripe():
        return pl.BlockSpec((FEED_WIDTH, D), lambda j: (j, 0))

    def column():
        return pl.BlockSpec((SEQ, FEED_WIDTH), lambda j: (0, j))

    low = jnp.bfloat16
    return pl.pallas_call(
        feed_back_kernel,
        grid=(FF // FEED_WIDTH,),
        in_specs=[
            fixed(SEQ, D),
            fixed(SEQ, D),
            fixed(SEQ, D),
            fixed(1, D),
            fixed(SEQ, D),
            fixed(D, SEQ),
            fixed(D, D),
            column(),
            column(),
            stripe(),
            stripe(),
        ],
        out_specs=[
            stripe(),
            stripe(),
            fixed(SEQ, D),
            fixed(1, D),
            fixed(D, D),
            fixed(D, SEQ),
        ],
        out_shape=[
            jax.ShapeDtypeStruct((FF, D), low),
            jax.ShapeDtypeStruct((FF, D), low),
            jax.ShapeDtypeStruct((SEQ, D), low),
            jax.ShapeDtypeStruct((1, D), jnp.float32),
            jax.ShapeDtypeStruct((D, D), low),
            jax.ShapeDtypeStruct((D, SEQ), low),
        ],
        scratch_shapes=[pltpu.VMEM((SEQ, D), jnp.float32), pltpu.VMEM((SEQ, FEED_WIDTH), low)],
        compiler_params=pltpu.CompilerParams(vmem_limit_bytes=VMEM_LIMIT),
        cost_estimate=pl.CostEstimate(
            flops=10 * SEQ * FF * D, bytes_accessed=32 * 1024 * 1024, transcendentals=0
        ),
        name="feed_back",
    )(ffn_grad, normed, mid, gain[None, :], cotangent, attended, w_out, activ, slope, w_in, w_down)


def adamw(weights, grads, first, second, step):
    first_new = beta_first * first + (1.0 - beta_first) * grads
    second_new = beta_second * second + (1.0 - beta_second) * grads * grads
    first_hat = first_new / (1.0 - beta_first**step)
    second_hat = second_new / (1.0 - beta_second**step)
    weights_new = weights - rate_per_step * step * (
        first_hat / (jnp.sqrt(second_hat) + adam_epsilon) + weight_decay * weights
    )
    return (weights_new, first_new, second_new)


def per_device(
    tokens,
    cotangent,
    segment_ids,
    buckets,
    owners,
    master,
    first_moment,
    second_moment,
    small_params,
    small_first,
    small_second,
    adapter_ema,
    step_count,
):
    dp_count = lax.axis_size("dp")
    tensor_count = lax.axis_size("tensor")
    capacity = master.shape[1]
    group_heads = H // tensor_count
    head_rows = group_heads * HS
    hidden_rows = FF // tensor_count
    tensor_pos = lax.axis_index("tensor")
    sizes = [3 * head_rows, head_rows, hidden_rows, hidden_rows]
    local_sizes = [-(-size // dp_count // 16) * 16 for size in sizes]
    pair_rows = -(-((capacity + len(sizes) * (dp_count - 1)) // dp_count) // 16) * 16
    slot_place, spread_place, orders, places = plan(
        owners, sizes, local_sizes, capacity, pair_rows
    )

    gain_one, gain_two, adapter, table = unpack(small_params)
    table_rows = jnp.pad(table.T, ((0, 16 - H), (0, 0)))
    bucket_place = jnp.concatenate([jnp.full((1,), -1, jnp.int32), buckets[::-1]])[None, :]
    segments = lax.dynamic_slice_in_dim(segment_ids, tensor_pos * SEQ, SEQ, 0)
    w_qkv, w_out, w_in, w_down, projected, attended, scale, normed_one, exp_scores = front(
        master[0],
        slot_place,
        spread_place,
        orders,
        local_sizes,
        tokens,
        gain_one,
        table_rows,
        bucket_place,
        segments,
    )
    w_out, w_in, w_down = [part.reshape(-1, D) for part in (w_out, w_in, w_down)]
    factors, factors_pull = jax.vjp(adapter_factors, adapter)
    (activ, slope, normed_two, mid, layer_out, ffn_grad), factor_grads = feed(
        attended, w_out, tokens, gain_two, cotangent, factors, w_in, w_down
    )
    in_grad, down_grad, mid_grad, gain_two_grad, out_weight_grad, attended_grad = feed_back(
        ffn_grad,
        normed_two,
        mid,
        gain_two,
        cotangent,
        attended,
        w_out,
        activ,
        slope,
        w_in,
        w_down,
    )
    (adapter_grad,) = factors_pull(factor_grads)
    small_local = jnp.concatenate(
        [jnp.zeros((D,), jnp.float32), gain_two_grad[0]]
        + [piece.reshape(-1) for piece in adapter_grad]
        + [jnp.zeros((TABLE_ROW * TILE - 2 * D - NADAPT,), jnp.float32)]
    ).reshape(TABLE_ROW, TILE)
    owned_grad, input_grad, small_total = back(
        [
            grad.reshape(tensor_count, -1, D) for grad in (out_weight_grad, in_grad, down_grad)
        ],
        projected,
        exp_scores,
        attended,
        scale,
        attended_grad,
        normed_one,
        w_qkv,
        tokens,
        mid_grad,
        gain_one,
        small_local,
        bucket_place,
        places,
        local_sizes,
        spread_place,
        slot_place,
    )
    small_total = jnp.concatenate(
        [
            small_total[:TABLE_ROW].reshape(-1)[: 2 * D + NADAPT],
            small_total[TABLE_ROW : TABLE_ROW + H, :NB].T.reshape(-1),
        ]
    )
    own_filled = (slot_place[0] >= 0).astype(jnp.float32)[:, None]
    step = step_count[0].astype(jnp.float32)
    new_master, new_first, new_second = adamw(
        master[0], owned_grad, first_moment[0], second_moment[0], step
    )
    new_master = new_master * own_filled
    new_first = new_first * own_filled
    new_second = new_second * own_filled
    small_new, small_first_new, small_second_new = adamw(
        small_params, small_total, small_first, small_second, step
    )
    ema_new = average_keep * adapter_ema + (1.0 - average_keep) * small_new[2 * D : 2 * D + NADAPT]
    return (
        layer_out,
        input_grad,
        owned_grad[None],
        new_first[None],
        new_second[None],
        new_master[None],
        new_master.astype(jnp.bfloat16)[None],
        small_total,
        small_first_new,
        small_second_new,
        small_new,
        ema_new,
    )


def solution(mesh):
    token_spec = P(("dp", "tensor"), None)
    owner_spec = P("tensor", "dp", None)
    return jax.shard_map(
        per_device,
        mesh=mesh,
        in_specs=(token_spec, token_spec, P("dp"), P(), P())
        + (owner_spec,) * 3
        + (P(),) * 5,
        out_specs=(token_spec,) * 2 + (owner_spec,) * 5 + (P(),) * 5,
        check_vma=False,
    )
```

```python
import functools
import math

import jax
import jax.numpy as jnp
from jax import lax
from jax.experimental import pallas as pl
from jax.experimental.pallas import tpu as pltpu
from jax.sharding import PartitionSpec as P

D = 768
H = 12
HS = 64
FF = 3072
NB = 32
R = 48
PHM = 4
SEQ = 1024
NADAPT = 1696

highest = lax.Precision.HIGHEST
norm_epsilon = 1e-06
beta_first = 0.5
beta_second = 0.5
adam_epsilon = 1e-08
rate_per_step = 0.01
weight_decay = 0.1
average_keep = 0.75
masked_score = -1000000000.0

TILE = 128
WINDOW = 2 * SEQ - TILE
QUERY_TILE = 256
KEY_TILE = 256
VMEM_LIMIT = 48 * 1024 * 1024
MESH = pl.DeviceIdType.MESH


def unpack(packed):
    widths = (D, D, PHM**3, D, R, R, D, NB * H)
    pieces = []
    offset = 0
    for width in widths:
        pieces.append(packed[offset : offset + width])
        offset = offset + width
    gain_one, gain_two, mix_flat, down_left, down_right, up_left, up_right, table_flat = pieces
    adapter = (
        mix_flat.reshape(PHM, PHM, PHM),
        down_left.reshape(PHM, D // PHM),
        down_right.reshape(PHM, R // PHM),
        up_left.reshape(PHM, R // PHM),
        up_right.reshape(PHM, D // PHM),
    )
    return (gain_one, gain_two, adapter, table_flat.reshape(NB, H))


def adapter_factors(adapter):
    mix, down_left, down_right, up_left, up_right = adapter
    eye = jnp.eye(PHM, dtype=jnp.float32)
    left = mix.transpose(2, 0, 1)[:, None] * down_right.T[None, :, :, None]
    right = (eye[None, :, :, None] * down_left[:, None, None, :]).reshape(PHM * PHM, D)
    wide = mix.transpose(1, 0, 2)[:, None] * up_left.T[None, :, :, None]
    tall = (eye[None, :, :, None] * up_right[:, None, None, :]).reshape(PHM * PHM, D)
    return (left.reshape(R, PHM * PHM), right, wide.reshape(R, PHM * PHM), tall)


def normal_parts(values):
    size = jnp.abs(values)
    shrink = 1.0 / (1.0 + (0.3275911 * math.sqrt(0.5)) * size)
    bell = jnp.exp(-0.5 * values * values)
    series = 0.5 * 1.061405429
    for term in (-1.453152027, 1.421413741, -0.284496736, 0.254829592):
        series = series * shrink + 0.5 * term
    tail = series * shrink * bell
    return jnp.where(values >= 0.0, 1.0 - tail, tail), bell * (1.0 / math.sqrt(2.0 * math.pi))


def contract(left, right, left_dim, right_dim):
    return lax.dot_general(
        left,
        right,
        (((left_dim,), (right_dim,)), ((), ())),
        preferred_element_type=jnp.float32,
    )


def bias_window(bias, window):
    for tile in range(WINDOW // TILE):
        base = WINDOW - TILE * tile
        row = jnp.broadcast_to(bias[:, base - TILE : base + TILE], (TILE, 2 * TILE))
        rolled = pltpu.roll(row, TILE, 1, stride=1, stride_axis=0)
        window[TILE * tile : TILE * (tile + 1), :] = rolled[:, :TILE]


def attend_head(
    query_rows, key_rows, value_rows, segment_keys_ref, segment_queries_ref, window, scores, exp_ref
):
    keys = key_rows.T
    values = jnp.concatenate([value_rows, jnp.ones((16, SEQ), jnp.bfloat16)], axis=0)
    outs, scales = [], []
    for q0 in range(0, SEQ, QUERY_TILE):
        queries = query_rows[:, q0 : q0 + QUERY_TILE]
        peak = jnp.full((8, QUERY_TILE), -jnp.inf, jnp.float32)
        for k0 in range(0, SEQ, KEY_TILE):
            raw = jnp.dot(keys[k0 : k0 + KEY_TILE], queries, preferred_element_type=jnp.float32)
            parts = []
            for l0 in range(0, QUERY_TILE, TILE):
                start = SEQ - TILE - (q0 + l0) + k0
                same_doc = (
                    segment_keys_ref[k0 : k0 + KEY_TILE, :]
                    == segment_queries_ref[:, q0 + l0 : q0 + l0 + TILE]
                )
                part = jnp.where(
                    same_doc,
                    raw[:, l0 : l0 + TILE] + window[start : start + KEY_TILE, :],
                    masked_score,
                )
                scores[k0 : k0 + KEY_TILE, l0 : l0 + TILE] = part
                parts.append(part)
            whole = jnp.concatenate(parts, axis=1)
            peak = jnp.maximum(peak, jnp.max(whole.reshape(KEY_TILE // 8, 8, QUERY_TILE), axis=0))
        peak = jnp.max(peak, axis=0, keepdims=True)
        total = jnp.zeros((HS + 16, QUERY_TILE), jnp.float32)
        for k0 in range(0, SEQ, KEY_TILE):
            exp_scores = jnp.exp(scores[k0 : k0 + KEY_TILE, :] - peak).astype(jnp.bfloat16)
            exp_ref[k0 : k0 + KEY_TILE, q0 : q0 + QUERY_TILE] = exp_scores
            total = total + jnp.dot(
                values[:, k0 : k0 + KEY_TILE], exp_scores, preferred_element_type=jnp.float32
            )
        scale = 1.0 / total[HS : HS + 1]
        scales.append(scale)
        outs.append((total[:HS] * scale).astype(jnp.bfloat16))
    return jnp.concatenate(outs, axis=1), jnp.concatenate(scales, axis=1)


def one_hot(place, shape, dim):
    hit = lax.broadcasted_iota(jnp.int32, shape, dim) == place
    return jnp.where(hit, 1.0, 0.0).astype(jnp.bfloat16)


def plan_kernel(dp_count, pair_rows, local_sizes, *refs):
    roles = len(local_sizes)
    owner_refs, slot_ref, spread_ref = refs[:roles], refs[roles], refs[roles + 1]
    order_refs, place_refs = refs[roles + 2 : 2 * roles + 2], refs[2 * roles + 2 :]
    dp_pos = lax.axis_index("dp").astype(jnp.float32)

    def quotient(values):
        return jnp.floor((values + 0.5) * (1.0 / dp_count))

    def remainder(values):
        return values - dp_count * quotient(values)

    line = dp_count // 2

    def halve(values):
        return jnp.floor((values + 0.5) * 0.5)

    def around(values):
        return values - line * jnp.floor((values + 0.5) * (1.0 / line))

    owners = [ref[...].astype(jnp.float32) for ref in owner_refs]

    def stats(who):
        counts = [
            jnp.sum(jnp.where(row == who, 1.0, 0.0), axis=1, keepdims=True) for row in owners
        ]
        starts = [jnp.sum(jnp.where(row < who, 1.0, 0.0), axis=1, keepdims=True) for row in owners]
        return counts, starts

    def hits(first, number, target):
        return quotient(first + number - 1.0 - target) - quotient(first - 1.0 - target)

    counts, starts = stats(jnp.full((1, 1), dp_pos))
    slot = lax.broadcasted_iota(jnp.int32, slot_ref.shape, 1).astype(jnp.float32)
    found = jnp.full(slot_ref.shape, -1.0)
    low = jnp.zeros((1, 1), jnp.float32)
    for role in range(roles):
        rank = slot - low
        target = remainder(starts[role] + rank)
        place = quotient(rank)
        for other in range(role):
            place = place + hits(starts[other], counts[other], target)
        found = jnp.where(
            (rank >= 0.0) & (rank < counts[role]),
            remainder(target - dp_pos) * pair_rows + place,
            found,
        )
        low = low + counts[role]
    slot_ref[...] = found.astype(jnp.int32)

    column = lax.broadcasted_iota(jnp.int32, (dp_count, 1), 0).astype(jnp.float32)
    counts, starts = stats(remainder(dp_pos - column))
    pair = lax.broadcasted_iota(jnp.int32, spread_ref.shape, 1).astype(jnp.float32)
    found = jnp.full(spread_ref.shape, -1.0)
    passed = jnp.zeros((dp_count, 1), jnp.float32)
    for role in range(roles):
        number = hits(starts[role], counts[role], dp_pos)
        first = starts[role] + remainder(dp_pos - starts[role])
        rank = pair - passed
        local = sum(local_sizes[:role]) + quotient(first) + rank
        found = jnp.where((rank >= 0.0) & (rank < number), local, found)
        passed = passed + number
    spread_ref[...] = found.astype(jnp.int32)

    counts, starts = stats(column)
    for role in range(roles):
        width = owners[role].shape[1]
        before = starts[role]
        for c0 in range(0, width, TILE):
            c1 = min(c0 + TILE, width)
            hot = jnp.where(owners[role][:, c0:c1] == column, 1.0, 0.0)
            shape = (c1 - c0, c1 - c0)
            above = lax.broadcasted_iota(jnp.int32, shape, 0) < lax.broadcasted_iota(
                jnp.int32, shape, 1
            )
            rank = jnp.dot(
                hot.astype(jnp.bfloat16),
                jnp.where(above, 1.0, 0.0).astype(jnp.bfloat16),
                preferred_element_type=jnp.float32,
            )
            number = jnp.sum(hot * (rank + before), axis=0, keepdims=True)
            before = before + jnp.sum(hot, axis=1, keepdims=True)
            target, row = remainder(number), quotient(number)
            side = jnp.abs(target - 2.0 * halve(target) - dp_pos + 2.0 * halve(dp_pos)) * line
            ahead = halve(target) - halve(dp_pos)
            order = (around(0.0 - ahead) + side) * local_sizes[role] + row
            place = (around(ahead) + side) * local_sizes[role] + row
            order_refs[role][:, c0:c1] = order.astype(jnp.int32)
            place_refs[role][:, c0:c1] = place.astype(jnp.int32)


def plan(owners, sizes, local_sizes, capacity, pair_rows):
    dp_count = lax.axis_size("dp")
    rows, start = [], 0
    for size in sizes:
        rows.append(owners[start : start + size][None, :])
        start += size
    outs = pl.pallas_call(
        functools.partial(plan_kernel, dp_count, pair_rows, local_sizes),
        out_shape=[
            jax.ShapeDtypeStruct((1, capacity), jnp.int32),
            jax.ShapeDtypeStruct((dp_count, pair_rows), jnp.int32),
        ]
        + [jax.ShapeDtypeStruct((1, size), jnp.int32) for size in sizes] * 2,
        name="plan",
    )(*rows)
    return outs[0], outs[1], outs[2 : 2 + len(sizes)], outs[2 + len(sizes) :]


def true_group(positions, group, tensor_count):
    flips = positions + (tensor_count - 1 - positions[0],)
    found = flips[0]
    for g in range(1, tensor_count):
        found = found + (flips[g] - flips[0]) * (
            lax.div(group + tensor_count - g, tensor_count)
            - lax.div(group + tensor_count - g - 1, tensor_count)
        )
    return found


def front_kernel(
    sizes,
    mine_ref,
    slot_place_ref,
    spread_place_ref,
    order_qkv_ref,
    order_out_ref,
    order_in_ref,
    order_down_ref,
    tokens_ref,
    gain_ref,
    table_ref,
    bucket_ref,
    segment_ref,
    w_qkv_ref,
    w_out_ref,
    w_in_ref,
    w_down_ref,
    projected_ref,
    attended_ref,
    scale_ref,
    normed_ref,
    exp_ref,
    sent,
    received,
    spread,
    bias,
    segment_keys,
    buf_qkv,
    buf_out,
    buf_in,
    buf_down,
    buf_far,
    far_spread,
    stage_out,
    stage_in,
    stage_down,
    stage_far,
    window,
    scores,
    exp_stage,
    deal_send,
    deal_recv,
    far_send,
    far_recv,
    line_send,
    line_recv,
    side_send,
    side_recv,
    group_send,
    group_recv,
    local_sem,
    exp_sem,
):
    dp_count, pair_rows = sent.shape[0], sent.shape[1]
    tensor_count = w_qkv_ref.shape[0]
    heads = scale_ref.shape[0]
    group_heads = heads // tensor_count
    head_rows = group_heads * HS
    dp_pos, tensor_pos = lax.axis_index("dp"), lax.axis_index("tensor")
    core_pos = tensor_pos + 1 - 2 * lax.rem(tensor_pos, 2)
    far_pos = lax.rem(tensor_pos + 2, tensor_count)
    core_peer, far_peer = (dp_pos, core_pos), (dp_pos, far_pos)

    def dp_peer(m):
        return (lax.rem(dp_pos + m, dp_count), tensor_pos)

    def each_peer(run):
        def step(m, carry):
            run(m)
            return carry

        lax.fori_loop(1, dp_count, step, 0)

    barrier = pltpu.get_barrier_semaphore()

    def greet(m):
        pl.semaphore_signal(barrier, inc=1, device_id=dp_peer(m), device_id_type=MESH)

    each_peer(greet)
    for peer in (core_peer, far_peer):
        pl.semaphore_signal(barrier, inc=1, device_id=peer, device_id_type=MESH)

    place = slot_place_ref[...]
    mine = mine_ref[...].astype(jnp.bfloat16)
    for m in range(dp_count):
        hot = one_hot(place - m * pair_rows, (pair_rows, mine.shape[0]), 0)
        sent[m] = jnp.dot(hot, mine, preferred_element_type=jnp.float32).astype(jnp.bfloat16)
    pl.semaphore_wait(barrier, dp_count + 1)

    def deal(m):
        return pltpu.make_async_remote_copy(
            sent.at[m],
            received.at[m],
            deal_send.at[m],
            deal_recv.at[m],
            device_id=dp_peer(m),
            device_id_type=MESH,
        )

    each_peer(lambda m: deal(m).start())
    received[0] = sent[0]

    for r0 in range(0, SEQ, 128):
        values = tokens_ref[r0 : r0 + 128, :].astype(jnp.float32)
        inverse = lax.rsqrt(jnp.mean(values * values, axis=1, keepdims=True) + norm_epsilon)
        normed_ref[r0 : r0 + 128, :] = (values * inverse * gain_ref[...]).astype(jnp.bfloat16)
    rest = table_ref[...]
    hot = one_hot(bucket_ref[...], (NB, 2 * SEQ), 0)
    biases = jnp.zeros((rest.shape[0], 2 * SEQ), jnp.float32)
    for _ in range(3):
        part = rest.astype(jnp.bfloat16)
        rest = rest - part.astype(jnp.float32)
        biases = biases + jnp.dot(part, hot, preferred_element_type=jnp.float32)
    for head in range(heads):
        bias[head] = biases[head : head + 1, :]
    segment_keys[...] = jnp.broadcast_to(segment_ref[...], (TILE, SEQ)).T

    each_peer(lambda m: deal(m).wait())
    rows = spread.shape[0]
    total = jnp.zeros((rows, D), jnp.float32)
    for m in range(dp_count):
        hot = one_hot(spread_place_ref[m : m + 1, :], (rows, pair_rows), 0)
        total = total + jnp.dot(hot, received[m], preferred_element_type=jnp.float32)
    spread[...] = total.astype(jnp.bfloat16)

    bufs = (buf_qkv, buf_out, buf_in, buf_down, buf_far)
    orders = (order_qkv_ref, order_out_ref, order_in_ref, order_down_ref, order_down_ref)
    stages = (w_qkv_ref.at[0], stage_out, stage_in, stage_down, stage_far)
    finals = (w_qkv_ref, w_out_ref, w_in_ref, w_down_ref, w_down_ref)
    sizes = tuple(sizes) + (sizes[3],)
    offsets = [sum(buf.shape[1] for buf in bufs[:role]) for role in range(4)]
    line = dp_count // 2
    line_pos, side = lax.div(dp_pos, 2), lax.rem(dp_pos, 2)
    side_peer = (dp_pos + 1 - 2 * side, tensor_pos)

    def far_exchange():
        return pltpu.make_async_remote_copy(
            spread.at[pl.ds(offsets[3], far_spread.shape[0])],
            far_spread,
            far_send,
            far_recv,
            device_id=far_peer,
            device_id_type=MESH,
        )

    def block(role):
        if role == 4:
            return far_spread
        return spread.at[pl.ds(offsets[role], bufs[role].shape[1])]

    def along_line(role, m):
        return pltpu.make_async_remote_copy(
            block(role),
            bufs[role].at[m],
            line_send.at[role, m],
            line_recv.at[role, m],
            device_id=(lax.rem(line_pos + m, line) * 2 + side, tensor_pos),
            device_id_type=MESH,
        )

    def to_side(role, m):
        return pltpu.make_async_remote_copy(
            bufs[role].at[m],
            bufs[role].at[line + m],
            side_send.at[role, m],
            side_recv.at[role, m],
            device_id=side_peer,
            device_id_type=MESH,
        )

    def each_line(first, run):
        def step(m, carry):
            run(m)
            return carry

        lax.fori_loop(first, line, step, 0)

    def start_line(role):
        if role == 4:
            far_exchange().wait()
        each_line(1, lambda m: along_line(role, m).start())
        bufs[role][0] = block(role)[...]
        to_side(role, 0).start()

    def start_side(role):
        def step(m):
            along_line(role, m).wait()
            to_side(role, m).start()

        each_line(1, step)

    def order(role):
        each_line(0, lambda m: to_side(role, m).wait())
        count = bufs[role].shape[1]
        source = bufs[role][...].reshape(dp_count * count, D)
        step = 256
        for r0 in range(0, sizes[role], step):
            r1 = min(r0 + step, sizes[role])
            hot = one_hot(orders[role][:, r0:r1], (dp_count * count, r1 - r0), 0)
            stages[role][r0:r1, :] = contract(hot, source, 0, 0).astype(jnp.bfloat16)

    def share(role, part):
        if role == 4:
            src, slot, peer = stages[role], 3, core_peer
        else:
            src, slot, peer = (
                (stages[role], 1, core_peer),
                (stages[role], 2, far_peer),
                (finals[role].at[2], 3, core_peer),
            )[part]
        return pltpu.make_async_remote_copy(
            src,
            finals[role].at[slot],
            group_send.at[role, part],
            group_recv.at[role, part],
            device_id=peer,
            device_id_type=MESH,
        )

    def keep(role):
        slot = 2 if role == 4 else 0
        return pltpu.make_async_copy(stages[role], finals[role].at[slot], local_sem.at[role])

    def start_share(role):
        order(role)
        share(role, 0).start()
        if role < 3:
            share(role, 1).start()
        if role > 0:
            keep(role).start()

    def forward(role):
        share(role, 1).wait_recv()
        share(role, 2).start()

    far_exchange().start()
    start_line(0)
    start_side(0)
    start_share(0)
    start_line(1)
    start_line(2)

    def true_head(group, head):
        return true_group((tensor_pos, core_pos, far_pos), group, tensor_count) * group_heads + head

    def head_step(i, carry):
        group, head = lax.div(i, group_heads), lax.rem(i, group_heads)

        @pl.when(i == 1)
        def _():
            start_side(1)

        @pl.when(i == 3)
        def _():
            start_share(1)

        @pl.when(i == 5)
        def _():
            start_side(2)
            start_line(3)
            start_line(4)

        @pl.when(i == 10)
        def _():
            start_share(2)

        @pl.when(i == group_heads)
        def _():
            share(0, 0).wait_recv()

        @pl.when(i == 2 * group_heads)
        def _():
            forward(0)

        @pl.when(i == 3 * group_heads)
        def _():
            share(0, 2).wait_recv()
            forward(1)

        @pl.when(i == 11)
        def _():
            start_side(3)

        @pl.when(head == 0)
        def _():
            projected_ref[group] = contract(w_qkv_ref[group], normed_ref[...], 1, 1).astype(
                jnp.bfloat16
            )

        def head_part(part):
            start = pl.multiple_of(part * head_rows + head * HS, HS)
            return projected_ref[group, pl.ds(start, HS), :]

        slot = lax.rem(i, 2)

        def save(head_index, slot):
            return pltpu.make_async_copy(
                exp_stage.at[slot], exp_ref.at[head_index], exp_sem.at[slot]
            )

        @pl.when(i >= 2)
        def _():
            save(i - 2, slot).wait()

        bias_window(bias[true_head(group, head)], window)
        attended, scale = attend_head(
            head_part(0),
            head_part(1),
            head_part(2),
            segment_keys,
            segment_ref,
            window,
            scores,
            exp_stage.at[slot],
        )
        attended_ref[pl.ds(pl.multiple_of(i * HS, HS), HS), :] = attended
        scale_ref[i] = scale
        save(i, slot).start()
        return carry

    lax.fori_loop(0, heads, head_step, 0)
    for i in (heads - 2, heads - 1):
        pltpu.make_async_copy(exp_stage.at[i % 2], exp_ref.at[i], exp_sem.at[i % 2]).wait()
    start_side(4)
    start_share(3)
    start_share(4)
    forward(2)
    for role in range(len(bufs)):
        share(role, 0).wait_send()
        if role < 3:
            share(role, 1).wait_send()
            share(role, 2).wait_send()
        if role > 0:
            share(role, 0).wait_recv()
            keep(role).wait()
        if role in (1, 2):
            share(role, 2).wait_recv()


def front(
    mine,
    slot_place,
    spread_place,
    orders,
    local_sizes,
    tokens,
    gain,
    table,
    bucket_place,
    segments,
):
    dp_count, tensor_count = lax.axis_size("dp"), lax.axis_size("tensor")
    sizes = [order.shape[1] for order in orders]
    pair_rows = spread_place.shape[1]
    low = jnp.bfloat16
    dma = pltpu.SemaphoreType.DMA
    roles = len(sizes)
    whole = pl.BlockSpec(memory_space=pltpu.VMEM)
    away = pl.BlockSpec(memory_space=pl.ANY)
    return pl.pallas_call(
        functools.partial(front_kernel, sizes),
        in_specs=[whole] * 12,
        out_specs=[whole, away, away, away, whole, whole, whole, whole, away],
        out_shape=[jax.ShapeDtypeStruct((tensor_count, size, D), low) for size in sizes]
        + [
            jax.ShapeDtypeStruct((tensor_count, sizes[0], SEQ), low),
            jax.ShapeDtypeStruct((H * HS, SEQ), low),
            jax.ShapeDtypeStruct((H, 1, SEQ), jnp.float32),
            jax.ShapeDtypeStruct((SEQ, D), low),
            jax.ShapeDtypeStruct((H, SEQ, SEQ), low),
        ],
        scratch_shapes=[
            pltpu.VMEM((dp_count, pair_rows, D), low),
            pltpu.VMEM((dp_count, pair_rows, D), low),
            pltpu.VMEM((sum(local_sizes), D), low),
            pltpu.VMEM((H, 1, 2 * SEQ), jnp.float32),
            pltpu.VMEM((SEQ, TILE), jnp.float32),
        ]
        + [pltpu.VMEM((dp_count, size, D), low) for size in local_sizes + local_sizes[3:]]
        + [pltpu.VMEM((local_sizes[3], D), low)]
        + [pltpu.VMEM((size, D), low) for size in sizes[1:] + sizes[3:]]
        + [
            pltpu.VMEM((WINDOW, TILE), jnp.float32),
            pltpu.VMEM((SEQ, QUERY_TILE), jnp.float32),
            pltpu.VMEM((2, SEQ, SEQ), low),
            dma((dp_count,)),
            dma((dp_count,)),
            dma,
            dma,
            dma((roles + 1, dp_count // 2)),
            dma((roles + 1, dp_count // 2)),
            dma((roles + 1, dp_count // 2)),
            dma((roles + 1, dp_count // 2)),
            dma((roles + 1, 3)),
            dma((roles + 1, 3)),
            dma((roles + 1,)),
            dma((2,)),
        ],
        compiler_params=pltpu.CompilerParams(
            collective_id=1, has_side_effects=True, vmem_limit_bytes=56 * 1024 * 1024
        ),
        cost_estimate=pl.CostEstimate(
            flops=10 * H * SEQ * SEQ * 256,
            bytes_accessed=64 * 1024 * 1024,
            transcendentals=H * SEQ * SEQ,
        ),
        name="front",
    )(
        mine,
        slot_place,
        spread_place,
        *orders,
        tokens,
        gain[None, :],
        table,
        bucket_place,
        segments.astype(jnp.float32)[None, :],
    )


def attend_head_back(
    query_rows,
    key_rows,
    value_rows,
    exp_ref,
    attended,
    scale,
    attended_grad,
    window,
    score_grads,
    store,
):
    scaled = attended_grad.astype(jnp.float32) * scale
    delta = jnp.sum(scaled * attended.astype(jnp.float32), axis=0, keepdims=True)
    scaled_low = scaled.astype(jnp.bfloat16)
    delta_high = delta.astype(jnp.bfloat16).astype(jnp.float32)
    delta_rest = delta - delta_high
    place = lax.broadcasted_iota(jnp.int32, (16, SEQ), 0)
    extra = jnp.where(
        place == 0,
        jnp.broadcast_to(-delta_high, (16, SEQ)),
        jnp.where(place == 1, jnp.broadcast_to(-delta_rest, (16, SEQ)), 0.0),
    ).astype(jnp.bfloat16)
    grads = jnp.concatenate([scaled_low, extra], axis=0)
    values = jnp.concatenate([value_rows, jnp.ones((16, SEQ), jnp.bfloat16)], axis=0).T
    window[...] = jnp.zeros_like(window)
    for q0 in range(0, SEQ, QUERY_TILE):
        total = jnp.zeros((HS, QUERY_TILE), jnp.float32)
        for k0 in range(0, SEQ, KEY_TILE):
            centered = jnp.dot(
                values[k0 : k0 + KEY_TILE],
                grads[:, q0 : q0 + QUERY_TILE],
                preferred_element_type=jnp.float32,
            )
            score_grad = centered * exp_ref[
                k0 : k0 + KEY_TILE, q0 : q0 + QUERY_TILE
            ].astype(jnp.float32)
            for l0 in range(0, QUERY_TILE, TILE):
                start = SEQ - TILE - (q0 + l0) + k0
                window[start : start + KEY_TILE, :] += score_grad[:, l0 : l0 + TILE]
            score_low = score_grad.astype(jnp.bfloat16)
            score_grads[k0 : k0 + KEY_TILE, q0 : q0 + QUERY_TILE] = score_low
            total = total + jnp.dot(
                key_rows[:, k0 : k0 + KEY_TILE], score_low, preferred_element_type=jnp.float32
            )
        store(0, q0, total.astype(jnp.bfloat16))
    queries = query_rows.T
    scaled_rows = scaled_low.T
    for k0 in range(0, SEQ, KEY_TILE):
        key_grad = jnp.dot(
            score_grads[k0 : k0 + KEY_TILE, :], queries, preferred_element_type=jnp.float32
        )
        value_grad = jnp.dot(
            exp_ref[k0 : k0 + KEY_TILE, :], scaled_rows, preferred_element_type=jnp.float32
        )
        store(1, k0, key_grad.T.astype(jnp.bfloat16))
        store(2, k0, value_grad.T.astype(jnp.bfloat16))
    pieces = [jnp.zeros((1, TILE), jnp.float32)] * (2 * SEQ // TILE)
    for tile in range(WINDOW // TILE):
        base = WINDOW - TILE * tile
        block = window[TILE * tile : TILE * (tile + 1), :]
        folded = jnp.concatenate([jnp.zeros((TILE, TILE), jnp.float32), block], axis=1)
        rows = TILE // 2
        while rows >= 1:
            folded = folded[:rows] + pltpu.roll(folded[rows:], 2 * TILE - rows, 1)
            rows //= 2
        pieces[base // TILE - 1] += folded[:, :TILE]
        pieces[base // TILE] += folded[:, TILE:]
    return jnp.concatenate(pieces, axis=1)


SMALL_ROWS = 48
TABLE_ROW = 32


def back_kernel(
    sizes,
    grad_out_ref,
    grad_in_ref,
    grad_down_ref,
    projected_ref,
    exp_ref,
    attended_ref,
    scale_ref,
    attended_grad_ref,
    normed_ref,
    w_qkv_ref,
    tokens_ref,
    mid_grad_ref,
    gain_ref,
    small_ref,
    bucket_ref,
    place_qkv_ref,
    place_out_ref,
    place_in_ref,
    place_down_ref,
    spread_place_ref,
    slot_place_ref,
    owned_ref,
    input_grad_ref,
    small_total_ref,
    bucket_hot,
    weights,
    proj,
    proj_grad,
    normed_grad,
    window,
    score_grads,
    exp_stage,
    qkv_odd,
    zero_qkv,
    zero_out,
    zero_in,
    zero_down,
    two_qkv,
    two_out,
    two_in,
    two_down,
    core_one_qkv,
    core_one_out,
    core_one_in,
    core_one_down,
    core_three_qkv,
    core_three_out,
    core_three_in,
    core_three_down,
    far_qkv,
    far_out,
    far_in,
    far_down,
    got_qkv,
    got_out,
    got_in,
    got_down,
    side_qkv,
    side_out,
    side_down,
    end_mine,
    end_far,
    spread,
    sent,
    received,
    small_own,
    small_tensor,
    small_dp,
    core_send,
    core_recv,
    far_send,
    far_recv,
    side_send,
    side_recv,
    line_send,
    line_recv,
    end_send,
    end_recv,
    back_send,
    back_recv,
    small_send,
    small_recv,
    load_sem,
    exp_sem,
    proj_sem,
):
    dp_count, pair_rows = sent.shape[0], sent.shape[1]
    tensor_count = w_qkv_ref.shape[0]
    heads = scale_ref.shape[0]
    group_heads = heads // tensor_count
    head_rows = group_heads * HS
    dp_pos, tensor_pos = lax.axis_index("dp"), lax.axis_index("tensor")
    core_pos = tensor_pos + 1 - 2 * lax.rem(tensor_pos, 2)
    far_pos = lax.rem(tensor_pos + 2, tensor_count)
    core_peer, far_peer = (dp_pos, core_pos), (dp_pos, far_pos)
    grad_refs = (None, grad_out_ref, grad_in_ref, grad_down_ref)
    zeros = (zero_qkv, zero_out, zero_in, zero_down)
    twos = (two_qkv, two_out, two_in, two_down)
    core_ones = (core_one_qkv, core_one_out, core_one_in, core_one_down)
    core_threes = (core_three_qkv, core_three_out, core_three_in, core_three_down)
    fars = (far_qkv, far_out, far_in, far_down)
    gots = (got_qkv, got_out, got_in, got_down)
    side_got = (side_qkv, side_out, far_in, side_down)
    places = (place_qkv_ref, place_out_ref, place_in_ref, place_down_ref)
    offsets = [sum(got.shape[1] for got in gots[:role]) for role in range(len(gots))]
    low = jnp.bfloat16

    def up(m):
        return lax.rem(dp_pos + m, dp_count)

    def down(m):
        return lax.rem(dp_pos + dp_count - m, dp_count)

    def each_peer(run):
        def step(m, carry):
            run(m)
            return carry

        lax.fori_loop(1, dp_count, step, 0)

    def tensor_peer(m):
        return (dp_pos, lax.rem(tensor_pos + m, tensor_count))

    barrier = pltpu.get_barrier_semaphore()

    def greet(m):
        pl.semaphore_signal(barrier, inc=1, device_id=(up(m), tensor_pos), device_id_type=MESH)

    each_peer(greet)
    for m in range(1, tensor_count):
        pl.semaphore_signal(barrier, inc=1, device_id=tensor_peer(m), device_id_type=MESH)

    def load_exp(head, slot):
        return pltpu.make_async_copy(exp_ref.at[head], exp_stage.at[slot], exp_sem.at[slot])

    def load_proj(group):
        return pltpu.make_async_copy(projected_ref.at[group], proj, proj_sem.at[0])

    def load_weights(group):
        return pltpu.make_async_copy(w_qkv_ref.at[group], weights, proj_sem.at[1])

    def load(role, which):
        target = zeros[role] if which == 0 else twos[role]
        return pltpu.make_async_copy(
            grad_refs[role].at[which], target, load_sem.at[role, which // 2]
        )

    def core_copy(role, which):
        if role == 0:
            src = qkv_odd.at[which // 2]
        else:
            src = grad_refs[role].at[which]
        target = (core_ones if which == 1 else core_threes)[role].at[pl.ds(0, sizes[role])]
        return pltpu.make_async_remote_copy(
            src,
            target,
            core_send.at[role, which // 2],
            core_recv.at[role, which // 2],
            device_id=core_peer,
            device_id_type=MESH,
        )

    def far_copy(role):
        return pltpu.make_async_remote_copy(
            twos[role],
            fars[role],
            far_send.at[role],
            far_recv.at[role],
            device_id=far_peer,
            device_id_type=MESH,
        )

    line = dp_count // 2
    line_pos, side = lax.div(dp_pos, 2), lax.rem(dp_pos, 2)
    side_peer = (dp_pos + 1 - 2 * side, tensor_pos)

    def each_line(run):
        def step(m, carry):
            run(m)
            return carry

        lax.fori_loop(1, line, step, 0)

    def leaving(role, far):
        return core_ones[role] if far else core_threes[role]

    def side_copy(role, far=0):
        count = gots[role].shape[1] * line
        return pltpu.make_async_remote_copy(
            leaving(role, far).at[pl.ds(count, count)],
            side_got[role].at[pl.ds(count * far, count)],
            side_send.at[role, far],
            side_recv.at[role, far],
            device_id=side_peer,
            device_id_type=MESH,
        )

    def line_copy(role, m, far=0):
        count = gots[role].shape[1]
        return pltpu.make_async_remote_copy(
            leaving(role, far).at[pl.ds(pl.multiple_of(m * count, 16), count)],
            gots[role].at[far * line + m],
            line_send.at[role, far * line + m],
            line_recv.at[role, far * line + m],
            device_id=(lax.rem(line_pos + m, line) * 2 + side, tensor_pos),
            device_id_type=MESH,
        )

    def end_copy():
        return pltpu.make_async_remote_copy(
            end_mine, end_far, end_send, end_recv, device_id=far_peer, device_id_type=MESH
        )

    def send_far(role):
        core_copy(role, 3).wait_recv()
        if role > 0:
            load(role, 2).wait()
        count = twos[role].shape[0]
        twos[role][...] = (
            twos[role][...].astype(jnp.float32)
            + core_threes[role][0:count, :].astype(jnp.float32)
        ).astype(low)
        far_copy(role).start()

    def scatter(role, far, total):
        count = gots[role].shape[1]
        for m in range(dp_count):
            hot = one_hot(places[role][...] - m * count, (count, sizes[role]), 0)
            leaving(role, far)[m * count : (m + 1) * count, :] = jnp.dot(
                hot, total, preferred_element_type=jnp.float32
            ).astype(low)
        side_copy(role, far).start()

    def send_deal(role):
        core_copy(role, 1).wait_recv()
        if role > 0:
            load(role, 0).wait()
        far_copy(role).wait_recv()
        total = (
            zeros[role][...].astype(jnp.float32)
            + core_ones[role][...].astype(jnp.float32)
            + fars[role][...].astype(jnp.float32)
        ).astype(low)
        scatter(role, 0, total)

    def send_both(role):
        core_copy(role, 1).wait_recv()
        core_copy(role, 3).wait_recv()
        load(role, 0).wait()
        load(role, 2).wait()
        count = sizes[role]
        near = (
            zeros[role][...].astype(jnp.float32)
            + core_ones[role][0:count, :].astype(jnp.float32)
        ).astype(low)
        far = (
            twos[role][...].astype(jnp.float32)
            + core_threes[role][0:count, :].astype(jnp.float32)
        ).astype(low)
        scatter(role, 0, near)
        scatter(role, 1, far)

    def pass_line(role, far=0):
        side_copy(role, far).wait()
        count = gots[role].shape[1] * line
        leaving(role, far)[0:count, :] = (
            leaving(role, far)[0:count, :].astype(jnp.float32)
            + side_got[role][count * far : count * (far + 1), :].astype(jnp.float32)
        ).astype(low)
        each_line(lambda m: line_copy(role, m, far).start())

    def line_sum(role, far=0):
        each_line(lambda m: line_copy(role, m, far).wait())
        total = leaving(role, far)[0 : gots[role].shape[1], :].astype(jnp.float32)
        for m in range(1, line):
            total = total + gots[role][far * line + m].astype(jnp.float32)
        return total

    def finish_deal(role):
        count = gots[role].shape[1]
        spread[offsets[role] : offsets[role] + count, :] = line_sum(role).astype(low)

    def finish_far():
        end_mine[...] = line_sum(2, 1).astype(low)
        end_copy().start()

    def finish_near():
        total = line_sum(2)
        end_copy().wait()
        count = gots[2].shape[1]
        spread[offsets[2] : offsets[2] + count, :] = (
            total + end_far[...].astype(jnp.float32)
        ).astype(low)

    load_exp(heads - group_heads, 0).start()
    load_proj(tensor_count - 1).start()
    load_weights(tensor_count - 1).start()
    for role in (3, 2, 1):
        load(role, 2).start()
        load(role, 0).start()
    bucket_hot[...] = one_hot(bucket_ref[...], (TILE, 2 * SEQ), 0)
    normed_grad[...] = jnp.zeros_like(normed_grad)
    small_own[0:TABLE_ROW, :] = small_ref[...]
    small_own[TABLE_ROW:SMALL_ROWS, :] = jnp.zeros((SMALL_ROWS - TABLE_ROW, TILE), jnp.float32)
    pl.semaphore_wait(barrier, dp_count + tensor_count - 2)
    for role in (3, 2, 1):
        core_copy(role, 3).start()
        core_copy(role, 1).start()

    def head_step(i, carry):
        group = tensor_count - 1 - lax.div(i, group_heads)
        part_head = lax.rem(i, group_heads)
        head = group * group_heads + part_head
        slot = lax.rem(i, 2)

        @pl.when(i == 1)
        def _():
            send_far(3)

        @pl.when(i == 2)
        def _():
            send_both(2)

        @pl.when(i == 6)
        def _():
            send_far(0)

        @pl.when(i == 7)
        def _():
            send_far(1)

        @pl.when(i == 8)
        def _():
            send_deal(3)

        @pl.when(i == 9)
        def _():
            pass_line(2, 1)
            pass_line(2, 0)

        @pl.when(i == 11)
        def _():
            pass_line(3)

        @pl.when(part_head == 0)
        def _():
            load_proj(group).wait()

        @pl.when(i + 1 < heads)
        def _():
            later = i + 1
            later_group = tensor_count - 1 - lax.div(later, group_heads)
            later_head = later_group * group_heads + lax.rem(later, group_heads)
            load_exp(later_head, lax.rem(later, 2)).start()

        load_exp(head, slot).wait()

        def rows(part):
            return pl.ds(pl.multiple_of(part * head_rows + part_head * HS, HS), HS)

        def store(part, column, value):
            proj_grad[rows(part), column : column + value.shape[1]] = value

        here = pl.ds(pl.multiple_of(head * HS, HS), HS)
        offset_grad = attend_head_back(
            proj[rows(0), :],
            proj[rows(1), :],
            proj[rows(2), :],
            exp_stage.at[slot],
            attended_ref[here, :],
            scale_ref[head],
            attended_grad_ref[here, :],
            window,
            score_grads,
            store,
        )
        place = (
            true_group((tensor_pos, core_pos, far_pos), group, tensor_count) * group_heads + part_head
        )
        high = offset_grad.astype(low)
        rest = (offset_grad - high.astype(jnp.float32)).astype(low)
        both = jnp.concatenate([high, rest] + [jnp.zeros_like(high)] * 6, axis=0)
        sums = contract(both, bucket_hot[...], 1, 1)
        line = lax.broadcasted_iota(jnp.int32, (SMALL_ROWS - TABLE_ROW, TILE), 0)
        small_own[TABLE_ROW:SMALL_ROWS, :] += jnp.where(
            line == place,
            jnp.broadcast_to(sums[0:1] + sums[1:2], (SMALL_ROWS - TABLE_ROW, TILE)),
            0.0,
        )

        @pl.when(part_head == group_heads - 1)
        def _():
            @pl.when(group > 0)
            def _():
                load_proj(group - 1).start()

            def weight_grad(target):
                for r0 in range(0, 3 * head_rows, head_rows):
                    target[r0 : r0 + head_rows, :] = jnp.dot(
                        proj_grad[r0 : r0 + head_rows, :],
                        normed_ref[...],
                        preferred_element_type=jnp.float32,
                    ).astype(low)

            @pl.when(group == 3)
            def _():
                weight_grad(qkv_odd.at[1])
                core_copy(0, 3).start()

            @pl.when(group == 2)
            def _():
                weight_grad(two_qkv)

            @pl.when(group == 1)
            def _():
                weight_grad(qkv_odd.at[0])
                core_copy(0, 1).start()

            @pl.when(group == 0)
            def _():
                weight_grad(zero_qkv)

            load_weights(group).wait()
            for r0 in range(0, SEQ, 256):
                normed_grad[r0 : r0 + 256, :] += jnp.dot(
                    proj_grad[:, r0 : r0 + 256].T,
                    weights[...],
                    preferred_element_type=jnp.float32,
                )

            @pl.when(group > 0)
            def _():
                load_weights(group - 1).start()

        return carry

    lax.fori_loop(0, heads, head_step, 0)

    def load_rows(which):
        source = (tokens_ref, mid_grad_ref)[which]
        return pltpu.make_async_copy(
            source, exp_stage.at[which, :, pl.ds(0, D)], exp_sem.at[which]
        )

    load_rows(0).start()
    load_rows(1).start()
    send_deal(1)
    send_deal(0)
    load_rows(0).wait()
    load_rows(1).wait()

    gain_grad = jnp.zeros((1, D), jnp.float32)
    for r0 in range(0, SEQ, 128):
        values = exp_stage[0, r0 : r0 + 128, 0:D].astype(jnp.float32)
        grads = normed_grad[r0 : r0 + 128, :]
        inverse = lax.rsqrt(jnp.mean(values * values, axis=1, keepdims=True) + norm_epsilon)
        scaled = values * inverse
        gain_grad = gain_grad + jnp.sum(grads * scaled, axis=0, keepdims=True)
        grads = grads * gain_ref[...]
        inner = jnp.mean(grads * scaled, axis=1, keepdims=True)
        input_grad_ref[r0 : r0 + 128, :] = (
            exp_stage[1, r0 : r0 + 128, 0:D].astype(jnp.float32) + inverse * (grads - scaled * inner)
        ).astype(low)
    for part in range(D // TILE):
        small_own[part : part + 1, :] = gain_grad[:, TILE * part : TILE * (part + 1)]

    def small_copy(stage, m):
        if stage == 0:
            src, target, peer = small_own, small_tensor.at[tensor_pos], tensor_peer(m)
        else:
            src, target, peer = small_total_ref, small_dp.at[dp_pos], (up(m), tensor_pos)
        return pltpu.make_async_remote_copy(
            src,
            target,
            small_send.at[stage, m],
            small_recv.at[stage, m],
            device_id=peer,
            device_id_type=MESH,
        )

    for m in range(1, tensor_count):
        small_copy(0, m).start()
    small_tensor[tensor_pos] = small_own[...]
    for m in range(1, tensor_count):
        small_copy(0, m).wait()
    total = small_tensor[0]
    for m in range(1, tensor_count):
        total = total + small_tensor[m]
    small_total_ref[...] = total
    each_peer(lambda m: small_copy(1, m).start())
    finish_far()
    pass_line(1)
    pass_line(0)
    finish_near()
    finish_deal(3)
    small_dp[dp_pos] = small_total_ref[...]
    each_peer(lambda m: small_copy(1, m).wait())
    total = small_dp[0]
    for m in range(1, dp_count):
        total = total + small_dp[m]
    small_total_ref[...] = total
    finish_deal(1)
    finish_deal(0)

    values = spread[...]
    for m in range(dp_count):
        hot = one_hot(spread_place_ref[m : m + 1, :], (values.shape[0], pair_rows), 0)
        sent[m] = contract(hot, values, 0, 0).astype(low)

    def back_copy(m):
        return pltpu.make_async_remote_copy(
            sent.at[m],
            received.at[m],
            back_send.at[m],
            back_recv.at[m],
            device_id=(down(m), tensor_pos),
            device_id_type=MESH,
        )

    each_peer(lambda m: back_copy(m).start())
    received[0] = sent[0]
    each_peer(lambda m: back_copy(m).wait())
    hot = one_hot(slot_place_ref[...], (dp_count * pair_rows, owned_ref.shape[0]), 0)
    owned_ref[...] = contract(hot, received[...].reshape(dp_count * pair_rows, D), 0, 0)
    for role in range(len(gots)):
        core_copy(role, 1).wait_send()
        core_copy(role, 3).wait_send()
        if role != 2:
            far_copy(role).wait_send()


def back(
    weight_grads,
    projected,
    exp_scores,
    attended,
    scale,
    attended_grad,
    normed,
    w_qkv,
    tokens,
    mid_grad,
    gain,
    small,
    bucket_place,
    places,
    local_sizes,
    spread_place,
    slot_place,
):
    dp_count, tensor_count = lax.axis_size("dp"), lax.axis_size("tensor")
    sizes = [place.shape[1] for place in places]
    capacity, pair_rows = slot_place.shape[1], spread_place.shape[1]
    low = jnp.bfloat16
    dma = pltpu.SemaphoreType.DMA
    roles = len(sizes)
    whole = pl.BlockSpec(memory_space=pltpu.VMEM)
    away = pl.BlockSpec(memory_space=pl.ANY)
    parts = [pltpu.VMEM((size, D), low) for size in sizes]
    padded = [
        pltpu.VMEM((max(dp_count * size, full), D), low) for size, full in zip(local_sizes, sizes)
    ]
    return pl.pallas_call(
        functools.partial(back_kernel, sizes),
        in_specs=[away] * 5 + [whole] * 4 + [away] * 3 + [whole] * 9,
        out_specs=[whole] * 3,
        out_shape=[
            jax.ShapeDtypeStruct((capacity, D), jnp.float32),
            jax.ShapeDtypeStruct((SEQ, D), low),
            jax.ShapeDtypeStruct((SMALL_ROWS, TILE), jnp.float32),
        ],
        scratch_shapes=[
            pltpu.VMEM((TILE, 2 * SEQ), low),
            pltpu.VMEM((sizes[0], D), low),
            pltpu.VMEM((sizes[0], SEQ), low),
            pltpu.VMEM((sizes[0], SEQ), low),
            pltpu.VMEM((SEQ, D), jnp.float32),
            pltpu.VMEM((WINDOW, TILE), jnp.float32),
            pltpu.VMEM((SEQ, SEQ), low),
            pltpu.VMEM((2, SEQ, SEQ), low),
            pltpu.VMEM((2, sizes[0], D), low),
        ]
        + parts
        + parts
        + parts[:2]
        + padded[2:3]
        + parts[3:]
        + padded
        + parts[:2]
        + [pltpu.VMEM((dp_count * local_sizes[2], D), low)]
        + parts[3:]
        + [
            pltpu.VMEM((dp_count if role == 2 else dp_count // 2, size, D), low)
            for role, size in enumerate(local_sizes)
        ]
        + [pltpu.VMEM((dp_count // 2 * local_sizes[role], D), low) for role in (0, 1, 3)]
        + [
            pltpu.VMEM((local_sizes[2], D), low),
            pltpu.VMEM((local_sizes[2], D), low),
            pltpu.VMEM((sum(local_sizes), D), low),
            pltpu.VMEM((dp_count, pair_rows, D), low),
            pltpu.VMEM((dp_count, pair_rows, D), low),
            pltpu.VMEM((SMALL_ROWS, TILE), jnp.float32),
            pltpu.VMEM((tensor_count, SMALL_ROWS, TILE), jnp.float32),
            pltpu.VMEM((dp_count, SMALL_ROWS, TILE), jnp.float32),
            dma((roles, 2)),
            dma((roles, 2)),
            dma((roles,)),
            dma((roles,)),
            dma((roles, 2)),
            dma((roles, 2)),
            dma((roles, dp_count)),
            dma((roles, dp_count)),
            dma,
            dma,
            dma((dp_count,)),
            dma((dp_count,)),
            dma((2, max(dp_count, tensor_count))),
            dma((2, max(dp_count, tensor_count))),
            dma((roles, 2)),
            dma((2,)),
            dma((2,)),
        ],
        compiler_params=pltpu.CompilerParams(
            collective_id=2, has_side_effects=True, vmem_limit_bytes=62 * 1024 * 1024
        ),
        cost_estimate=pl.CostEstimate(
            flops=16 * H * SEQ * SEQ * 256,
            bytes_accessed=64 * 1024 * 1024,
            transcendentals=0,
        ),
        name="back",
    )(
        *weight_grads,
        projected,
        exp_scores,
        attended,
        scale,
        attended_grad,
        normed,
        w_qkv,
        tokens,
        mid_grad,
        gain[None, :],
        small,
        bucket_place,
        *places,
        spread_place,
        slot_place,
    )


FEED_WIDTH = 384


def feed_kernel(
    attended_ref,
    w_out_ref,
    tokens_ref,
    gain_ref,
    cotangent_ref,
    left_ref,
    right_ref,
    wide_ref,
    tall_ref,
    w_in_ref,
    w_down_ref,
    activ_ref,
    slope_ref,
    normed_ref,
    mid_ref,
    layer_out_ref,
    ffn_grad_ref,
    left_grad_ref,
    right_grad_ref,
    wide_grad_ref,
    tall_grad_ref,
    ffn_out,
):
    low = jnp.bfloat16
    row_tile = 256
    tiles = range(0, SEQ, row_tile)

    @pl.when(pl.program_id(0) == 0)
    def _():
        for r0 in tiles:
            rows = slice(r0, r0 + row_tile)
            attn = jnp.dot(
                attended_ref[:, rows].T, w_out_ref[...], preferred_element_type=jnp.float32
            )
            mid = tokens_ref[rows, :].astype(jnp.float32) + attn
            mid_ref[rows, :] = mid
            inverse = lax.rsqrt(jnp.mean(mid * mid, axis=1, keepdims=True) + norm_epsilon)
            normed_ref[rows, :] = (mid * inverse * gain_ref[...]).astype(low)
            ffn_out[rows, :] = jnp.zeros((row_tile, D), jnp.float32)

    for r0 in tiles:
        rows = slice(r0, r0 + row_tile)
        pre = contract(normed_ref[rows, :], w_in_ref[...], 1, 1)
        cdf, density = normal_parts(pre)
        activ = (pre * cdf).astype(low)
        activ_ref[rows, :] = activ
        slope_ref[rows, :] = (cdf + pre * density).astype(low)
        ffn_out[rows, :] += jnp.dot(activ, w_down_ref[...], preferred_element_type=jnp.float32)

    @pl.when(pl.program_id(0) == pl.num_programs(0) - 1)
    def _():
        down = jnp.dot(
            left_ref[...], right_ref[...], precision=highest, preferred_element_type=jnp.float32
        ).astype(low)
        up = jnp.dot(
            wide_ref[...], tall_ref[...], precision=highest, preferred_element_type=jnp.float32
        ).astype(low)
        down_grad = jnp.zeros((R, D), jnp.float32)
        up_grad = jnp.zeros((R, D), jnp.float32)
        for r0 in tiles:
            rows = slice(r0, r0 + row_tile)
            ffn = ffn_out[rows, :]
            ffn_low = ffn.astype(low)
            grad_low = cotangent_ref[rows, :]
            zed = contract(ffn_low, down, 1, 1)
            cdf, density = normal_parts(zed)
            hidden = (zed * cdf).astype(low)
            added = jnp.dot(hidden, up, preferred_element_type=jnp.float32)
            layer_out_ref[rows, :] = (mid_ref[rows, :] + ffn + added).astype(low)
            zed_grad = contract(grad_low, up, 1, 1) * (cdf + zed * density)
            zed_low = zed_grad.astype(low)
            ffn_grad_ref[rows, :] = (
                grad_low.astype(jnp.float32)
                + jnp.dot(zed_low, down, preferred_element_type=jnp.float32)
            ).astype(low)
            up_grad = up_grad + contract(hidden, grad_low, 0, 0)
            down_grad = down_grad + contract(zed_low, ffn_low, 0, 0)

        def exact(left, right, left_dim, right_dim):
            return lax.dot_general(
                left,
                right,
                (((left_dim,), (right_dim,)), ((), ())),
                precision=highest,
                preferred_element_type=jnp.float32,
            )

        left_grad_ref[...] = exact(down_grad, right_ref[...], 1, 1)
        right_grad_ref[...] = exact(left_ref[...], down_grad, 0, 0)
        wide_grad_ref[...] = exact(up_grad, tall_ref[...], 1, 1)
        tall_grad_ref[...] = exact(wide_ref[...], up_grad, 0, 0)


def feed(attended, w_out, tokens, gain, cotangent, factors, w_in, w_down):
    def fixed(*shape):
        return pl.BlockSpec(shape, lambda j: (0,) * len(shape))

    def stripe():
        return pl.BlockSpec((FEED_WIDTH, D), lambda j: (j, 0))

    low = jnp.bfloat16
    factor_specs = [fixed(*factor.shape) for factor in factors]
    outs = pl.pallas_call(
        feed_kernel,
        grid=(FF // FEED_WIDTH,),
        in_specs=[
            fixed(D, SEQ),
            fixed(D, D),
            fixed(SEQ, D),
            fixed(1, D),
            fixed(SEQ, D),
            *factor_specs,
            stripe(),
            stripe(),
        ],
        out_specs=[
            pl.BlockSpec((SEQ, FEED_WIDTH), lambda j: (0, j)),
            pl.BlockSpec((SEQ, FEED_WIDTH), lambda j: (0, j)),
            fixed(SEQ, D),
            fixed(SEQ, D),
            fixed(SEQ, D),
            fixed(SEQ, D),
            *factor_specs,
        ],
        out_shape=[
            jax.ShapeDtypeStruct((SEQ, FF), low),
            jax.ShapeDtypeStruct((SEQ, FF), low),
            jax.ShapeDtypeStruct((SEQ, D), low),
            jax.ShapeDtypeStruct((SEQ, D), jnp.float32),
            jax.ShapeDtypeStruct((SEQ, D), low),
            jax.ShapeDtypeStruct((SEQ, D), low),
            *[jax.ShapeDtypeStruct(factor.shape, jnp.float32) for factor in factors],
        ],
        scratch_shapes=[pltpu.VMEM((SEQ, D), jnp.float32)],
        compiler_params=pltpu.CompilerParams(vmem_limit_bytes=VMEM_LIMIT),
        cost_estimate=pl.CostEstimate(
            flops=6 * SEQ * FF * D, bytes_accessed=32 * 1024 * 1024, transcendentals=2 * SEQ * FF
        ),
        name="feed",
    )(attended, w_out, tokens, gain[None, :], cotangent, *factors, w_in, w_down)
    return outs[:6], tuple(outs[6:])


def feed_back_kernel(
    ffn_grad_ref,
    normed_ref,
    mid_ref,
    gain_ref,
    cotangent_ref,
    attended_ref,
    w_out_ref,
    activ_ref,
    slope_ref,
    w_in_ref,
    w_down_ref,
    in_grad_ref,
    down_grad_ref,
    mid_grad_ref,
    gain_grad_ref,
    out_grad_ref,
    attended_grad_ref,
    normed_grad,
    pre_grad,
):
    low = jnp.bfloat16
    row_tile = 256
    tiles = range(0, SEQ, row_tile)

    @pl.when(pl.program_id(0) == 0)
    def _():
        normed_grad[...] = jnp.zeros_like(normed_grad)

    for r0 in tiles:
        rows = slice(r0, r0 + row_tile)
        grad = contract(ffn_grad_ref[rows, :], w_down_ref[...], 1, 1)
        grad = (grad * slope_ref[rows, :].astype(jnp.float32)).astype(low)
        pre_grad[rows, :] = grad
        normed_grad[rows, :] += jnp.dot(grad, w_in_ref[...], preferred_element_type=jnp.float32)
    for c0 in range(0, FEED_WIDTH, TILE):
        columns = slice(c0, c0 + TILE)
        down_grad_ref[columns, :] = jnp.dot(
            activ_ref[:, columns].T, ffn_grad_ref[...], preferred_element_type=jnp.float32
        ).astype(low)
        in_grad_ref[columns, :] = jnp.dot(
            pre_grad[:, columns].T, normed_ref[...], preferred_element_type=jnp.float32
        ).astype(low)

    @pl.when(pl.program_id(0) == pl.num_programs(0) - 1)
    def _():
        gain_grad = jnp.zeros((1, D), jnp.float32)
        for r0 in tiles:
            rows = slice(r0, r0 + row_tile)
            mid = mid_ref[rows, :]
            grads = normed_grad[rows, :]
            inverse = lax.rsqrt(jnp.mean(mid * mid, axis=1, keepdims=True) + norm_epsilon)
            scaled = mid * inverse
            gain_grad = gain_grad + jnp.sum(grads * scaled, axis=0, keepdims=True)
            grads = grads * gain_ref[...]
            inner = jnp.mean(grads * scaled, axis=1, keepdims=True)
            mid_grad_ref[rows, :] = (
                cotangent_ref[rows, :].astype(jnp.float32) + inverse * (grads - scaled * inner)
            ).astype(low)
        gain_grad_ref[...] = gain_grad
        for r0 in range(0, D, 256):
            rows = slice(r0, r0 + 256)
            out_grad_ref[rows, :] = jnp.dot(
                attended_ref[rows, :], mid_grad_ref[...], preferred_element_type=jnp.float32
            ).astype(low)
            attended_grad_ref[rows, :] = contract(
                w_out_ref[rows, :], mid_grad_ref[...], 1, 1
            ).astype(low)


def feed_back(ffn_grad, normed, mid, gain, cotangent, attended, w_out, activ, slope, w_in, w_down):
    def fixed(*shape):
        return pl.BlockSpec(shape, lambda j: (0,) * len(shape))

    def stripe():
        return pl.BlockSpec((FEED_WIDTH, D), lambda j: (j, 0))

    def column():
        return pl.BlockSpec((SEQ, FEED_WIDTH), lambda j: (0, j))

    low = jnp.bfloat16
    return pl.pallas_call(
        feed_back_kernel,
        grid=(FF // FEED_WIDTH,),
        in_specs=[
            fixed(SEQ, D),
            fixed(SEQ, D),
            fixed(SEQ, D),
            fixed(1, D),
            fixed(SEQ, D),
            fixed(D, SEQ),
            fixed(D, D),
            column(),
            column(),
            stripe(),
            stripe(),
        ],
        out_specs=[
            stripe(),
            stripe(),
            fixed(SEQ, D),
            fixed(1, D),
            fixed(D, D),
            fixed(D, SEQ),
        ],
        out_shape=[
            jax.ShapeDtypeStruct((FF, D), low),
            jax.ShapeDtypeStruct((FF, D), low),
            jax.ShapeDtypeStruct((SEQ, D), low),
            jax.ShapeDtypeStruct((1, D), jnp.float32),
            jax.ShapeDtypeStruct((D, D), low),
            jax.ShapeDtypeStruct((D, SEQ), low),
        ],
        scratch_shapes=[pltpu.VMEM((SEQ, D), jnp.float32), pltpu.VMEM((SEQ, FEED_WIDTH), low)],
        compiler_params=pltpu.CompilerParams(vmem_limit_bytes=VMEM_LIMIT),
        cost_estimate=pl.CostEstimate(
            flops=10 * SEQ * FF * D, bytes_accessed=32 * 1024 * 1024, transcendentals=0
        ),
        name="feed_back",
    )(ffn_grad, normed, mid, gain[None, :], cotangent, attended, w_out, activ, slope, w_in, w_down)


def adamw(weights, grads, first, second, step):
    first_new = beta_first * first + (1.0 - beta_first) * grads
    second_new = beta_second * second + (1.0 - beta_second) * grads * grads
    first_hat = first_new / (1.0 - beta_first**step)
    second_hat = second_new / (1.0 - beta_second**step)
    weights_new = weights - rate_per_step * step * (
        first_hat / (jnp.sqrt(second_hat) + adam_epsilon) + weight_decay * weights
    )
    return (weights_new, first_new, second_new)


def per_device(
    tokens,
    cotangent,
    segment_ids,
    buckets,
    owners,
    master,
    first_moment,
    second_moment,
    small_params,
    small_first,
    small_second,
    adapter_ema,
    step_count,
):
    dp_count = lax.axis_size("dp")
    tensor_count = lax.axis_size("tensor")
    capacity = master.shape[1]
    group_heads = H // tensor_count
    head_rows = group_heads * HS
    hidden_rows = FF // tensor_count
    tensor_pos = lax.axis_index("tensor")
    sizes = [3 * head_rows, head_rows, hidden_rows, hidden_rows]
    local_sizes = [-(-size // dp_count // 16) * 16 for size in sizes]
    pair_rows = -(-((capacity + len(sizes) * (dp_count - 1)) // dp_count) // 16) * 16
    slot_place, spread_place, orders, places = plan(
        owners, sizes, local_sizes, capacity, pair_rows
    )

    gain_one, gain_two, adapter, table = unpack(small_params)
    table_rows = jnp.pad(table.T, ((0, 16 - H), (0, 0)))
    bucket_place = jnp.concatenate([jnp.full((1,), -1, jnp.int32), buckets[::-1]])[None, :]
    segments = lax.dynamic_slice_in_dim(segment_ids, tensor_pos * SEQ, SEQ, 0)
    w_qkv, w_out, w_in, w_down, projected, attended, scale, normed_one, exp_scores = front(
        master[0],
        slot_place,
        spread_place,
        orders,
        local_sizes,
        tokens,
        gain_one,
        table_rows,
        bucket_place,
        segments,
    )
    w_out, w_in, w_down = [part.reshape(-1, D) for part in (w_out, w_in, w_down)]
    factors, factors_pull = jax.vjp(adapter_factors, adapter)
    (activ, slope, normed_two, mid, layer_out, ffn_grad), factor_grads = feed(
        attended, w_out, tokens, gain_two, cotangent, factors, w_in, w_down
    )
    in_grad, down_grad, mid_grad, gain_two_grad, out_weight_grad, attended_grad = feed_back(
        ffn_grad,
        normed_two,
        mid,
        gain_two,
        cotangent,
        attended,
        w_out,
        activ,
        slope,
        w_in,
        w_down,
    )
    (adapter_grad,) = factors_pull(factor_grads)
    small_local = jnp.concatenate(
        [jnp.zeros((D,), jnp.float32), gain_two_grad[0]]
        + [piece.reshape(-1) for piece in adapter_grad]
        + [jnp.zeros((TABLE_ROW * TILE - 2 * D - NADAPT,), jnp.float32)]
    ).reshape(TABLE_ROW, TILE)
    owned_grad, input_grad, small_total = back(
        [
            grad.reshape(tensor_count, -1, D) for grad in (out_weight_grad, in_grad, down_grad)
        ],
        projected,
        exp_scores,
        attended,
        scale,
        attended_grad,
        normed_one,
        w_qkv,
        tokens,
        mid_grad,
        gain_one,
        small_local,
        bucket_place,
        places,
        local_sizes,
        spread_place,
        slot_place,
    )
    small_total = jnp.concatenate(
        [
            small_total[:TABLE_ROW].reshape(-1)[: 2 * D + NADAPT],
            small_total[TABLE_ROW : TABLE_ROW + H, :NB].T.reshape(-1),
        ]
    )
    own_filled = (slot_place[0] >= 0).astype(jnp.float32)[:, None]
    step = step_count[0].astype(jnp.float32)
    new_master, new_first, new_second = adamw(
        master[0], owned_grad, first_moment[0], second_moment[0], step
    )
    new_master = new_master * own_filled
    new_first = new_first * own_filled
    new_second = new_second * own_filled
    small_new, small_first_new, small_second_new = adamw(
        small_params, small_total, small_first, small_second, step
    )
    ema_new = average_keep * adapter_ema + (1.0 - average_keep) * small_new[2 * D : 2 * D + NADAPT]
    return (
        layer_out,
        input_grad,
        owned_grad[None],
        new_first[None],
        new_second[None],
        new_master[None],
        new_master.astype(jnp.bfloat16)[None],
        small_total,
        small_first_new,
        small_second_new,
        small_new,
        ema_new,
    )


def solution(mesh):
    token_spec = P(("dp", "tensor"), None)
    owner_spec = P("tensor", "dp", None)
    return jax.shard_map(
        per_device,
        mesh=mesh,
        in_specs=(token_spec, token_spec, P("dp"), P(), P())
        + (owner_spec,) * 3
        + (P(),) * 5,
        out_specs=(token_spec,) * 2 + (owner_spec,) * 5 + (P(),) * 5,
        check_vma=False,
    )
```

```python
import functools
import math

import jax
import jax.numpy as jnp
from jax import lax
from jax.experimental import pallas as pl
from jax.experimental.pallas import tpu as pltpu
from jax.sharding import PartitionSpec as P

D = 768
H = 12
HS = 64
FF = 3072
NB = 32
R = 48
PHM = 4
SEQ = 1024
NADAPT = 1696

highest = lax.Precision.HIGHEST
norm_epsilon = 1e-06
beta_first = 0.5
beta_second = 0.5
adam_epsilon = 1e-08
rate_per_step = 0.01
weight_decay = 0.1
average_keep = 0.75
masked_score = -1000000000.0

TILE = 128
WINDOW = 2 * SEQ - TILE
QUERY_TILE = 512
KEY_TILE = 512
BACK_QUERY_TILE = 512
BACK_KEY_TILE = 1024
VMEM_LIMIT = 48 * 1024 * 1024
MESH = pl.DeviceIdType.MESH


def unpack(packed):
    widths = (D, D, PHM**3, D, R, R, D, NB * H)
    pieces = []
    offset = 0
    for width in widths:
        pieces.append(packed[offset : offset + width])
        offset = offset + width
    gain_one, gain_two, mix_flat, down_left, down_right, up_left, up_right, table_flat = pieces
    adapter = (
        mix_flat.reshape(PHM, PHM, PHM),
        down_left.reshape(PHM, D // PHM),
        down_right.reshape(PHM, R // PHM),
        up_left.reshape(PHM, R // PHM),
        up_right.reshape(PHM, D // PHM),
    )
    return (gain_one, gain_two, adapter, table_flat.reshape(NB, H))


def adapter_factors(adapter):
    mix, down_left, down_right, up_left, up_right = adapter
    eye = jnp.eye(PHM, dtype=jnp.float32)
    left = mix.transpose(2, 0, 1)[:, None] * down_right.T[None, :, :, None]
    right = (eye[None, :, :, None] * down_left[:, None, None, :]).reshape(PHM * PHM, D)
    wide = mix.transpose(1, 0, 2)[:, None] * up_left.T[None, :, :, None]
    tall = (eye[None, :, :, None] * up_right[:, None, None, :]).reshape(PHM * PHM, D)
    return (left.reshape(R, PHM * PHM), right, wide.reshape(R, PHM * PHM), tall)


def normal_parts(values):
    size = jnp.abs(values)
    shrink = 1.0 / (1.0 + (0.3275911 * math.sqrt(0.5)) * size)
    bell = jnp.exp(-0.5 * values * values)
    series = 0.5 * 1.061405429
    for term in (-1.453152027, 1.421413741, -0.284496736, 0.254829592):
        series = series * shrink + 0.5 * term
    tail = series * shrink * bell
    return jnp.where(values >= 0.0, 1.0 - tail, tail), bell * (1.0 / math.sqrt(2.0 * math.pi))


def contract(left, right, left_dim, right_dim):
    return lax.dot_general(
        left,
        right,
        (((left_dim,), (right_dim,)), ((), ())),
        preferred_element_type=jnp.float32,
    )


def bias_window(bias, window):
    for tile in range(WINDOW // TILE):
        base = WINDOW - TILE * tile
        row = jnp.broadcast_to(bias[:, base - TILE : base + TILE], (TILE, 2 * TILE))
        rolled = pltpu.roll(row, TILE, 1, stride=1, stride_axis=0)
        window[TILE * tile : TILE * (tile + 1), :] = rolled[:, :TILE]


def attend_head(
    query_rows, key_rows, value_rows, segment_keys_ref, segment_queries_ref, window, scores, exp_ref
):
    keys = key_rows.T
    values = jnp.concatenate([value_rows, jnp.ones((16, SEQ), jnp.bfloat16)], axis=0)
    outs, scales = [], []
    for q0 in range(0, SEQ, QUERY_TILE):
        queries = query_rows[:, q0 : q0 + QUERY_TILE]
        peak = jnp.full((8, QUERY_TILE), -jnp.inf, jnp.float32)
        for k0 in range(0, SEQ, KEY_TILE):
            raw = jnp.dot(keys[k0 : k0 + KEY_TILE], queries, preferred_element_type=jnp.float32)
            parts = []
            for l0 in range(0, QUERY_TILE, TILE):
                start = SEQ - TILE - (q0 + l0) + k0
                same_doc = (
                    segment_keys_ref[k0 : k0 + KEY_TILE, :]
                    == segment_queries_ref[:, q0 + l0 : q0 + l0 + TILE]
                )
                part = jnp.where(
                    same_doc,
                    raw[:, l0 : l0 + TILE] + window[start : start + KEY_TILE, :],
                    masked_score,
                )
                scores[k0 : k0 + KEY_TILE, l0 : l0 + TILE] = part
                parts.append(part)
            whole = jnp.concatenate(parts, axis=1)
            peak = jnp.maximum(peak, jnp.max(whole.reshape(KEY_TILE // 8, 8, QUERY_TILE), axis=0))
        peak = jnp.max(peak, axis=0, keepdims=True)
        total = jnp.zeros((HS + 16, QUERY_TILE), jnp.float32)
        for k0 in range(0, SEQ, KEY_TILE):
            exp_scores = jnp.exp(scores[k0 : k0 + KEY_TILE, :] - peak).astype(jnp.bfloat16)
            exp_ref[k0 : k0 + KEY_TILE, q0 : q0 + QUERY_TILE] = exp_scores
            total = total + jnp.dot(
                values[:, k0 : k0 + KEY_TILE], exp_scores, preferred_element_type=jnp.float32
            )
        scale = 1.0 / total[HS : HS + 1]
        scales.append(scale)
        outs.append((total[:HS] * scale).astype(jnp.bfloat16))
    return jnp.concatenate(outs, axis=1), jnp.concatenate(scales, axis=1)


def one_hot(place, shape, dim):
    hit = lax.broadcasted_iota(jnp.int32, shape, dim) == place
    return jnp.where(hit, 1.0, 0.0).astype(jnp.bfloat16)


def plan_kernel(dp_count, pair_rows, local_sizes, *refs):
    roles = len(local_sizes)
    owner_refs, slot_ref, spread_ref = refs[:roles], refs[roles], refs[roles + 1]
    order_refs, place_refs = refs[roles + 2 : 2 * roles + 2], refs[2 * roles + 2 :]
    dp_pos = lax.axis_index("dp").astype(jnp.float32)

    def quotient(values):
        return jnp.floor((values + 0.5) * (1.0 / dp_count))

    def remainder(values):
        return values - dp_count * quotient(values)

    line = dp_count // 2

    def halve(values):
        return jnp.floor((values + 0.5) * 0.5)

    def around(values):
        return values - line * jnp.floor((values + 0.5) * (1.0 / line))

    owners = [ref[...].astype(jnp.float32) for ref in owner_refs]

    def stats(who):
        counts = [
            jnp.sum(jnp.where(row == who, 1.0, 0.0), axis=1, keepdims=True) for row in owners
        ]
        starts = [jnp.sum(jnp.where(row < who, 1.0, 0.0), axis=1, keepdims=True) for row in owners]
        return counts, starts

    def hits(first, number, target):
        return quotient(first + number - 1.0 - target) - quotient(first - 1.0 - target)

    counts, starts = stats(jnp.full((1, 1), dp_pos))
    slot = lax.broadcasted_iota(jnp.int32, slot_ref.shape, 1).astype(jnp.float32)
    found = jnp.full(slot_ref.shape, -1.0)
    low = jnp.zeros((1, 1), jnp.float32)
    for role in range(roles):
        rank = slot - low
        target = remainder(starts[role] + rank)
        place = quotient(rank)
        for other in range(role):
            place = place + hits(starts[other], counts[other], target)
        found = jnp.where(
            (rank >= 0.0) & (rank < counts[role]),
            remainder(target - dp_pos) * pair_rows + place,
            found,
        )
        low = low + counts[role]
    slot_ref[...] = found.astype(jnp.int32)

    column = lax.broadcasted_iota(jnp.int32, (dp_count, 1), 0).astype(jnp.float32)
    counts, starts = stats(remainder(dp_pos - column))
    pair = lax.broadcasted_iota(jnp.int32, spread_ref.shape, 1).astype(jnp.float32)
    found = jnp.full(spread_ref.shape, -1.0)
    passed = jnp.zeros((dp_count, 1), jnp.float32)
    for role in range(roles):
        number = hits(starts[role], counts[role], dp_pos)
        first = starts[role] + remainder(dp_pos - starts[role])
        rank = pair - passed
        local = sum(local_sizes[:role]) + quotient(first) + rank
        found = jnp.where((rank >= 0.0) & (rank < number), local, found)
        passed = passed + number
    spread_ref[...] = found.astype(jnp.int32)

    counts, starts = stats(column)
    for role in range(roles):
        width = owners[role].shape[1]
        before = starts[role]
        for c0 in range(0, width, TILE):
            c1 = min(c0 + TILE, width)
            hot = jnp.where(owners[role][:, c0:c1] == column, 1.0, 0.0)
            shape = (c1 - c0, c1 - c0)
            above = lax.broadcasted_iota(jnp.int32, shape, 0) < lax.broadcasted_iota(
                jnp.int32, shape, 1
            )
            rank = jnp.dot(
                hot.astype(jnp.bfloat16),
                jnp.where(above, 1.0, 0.0).astype(jnp.bfloat16),
                preferred_element_type=jnp.float32,
            )
            number = jnp.sum(hot * (rank + before), axis=0, keepdims=True)
            before = before + jnp.sum(hot, axis=1, keepdims=True)
            target, row = remainder(number), quotient(number)
            side = jnp.abs(target - 2.0 * halve(target) - dp_pos + 2.0 * halve(dp_pos)) * line
            ahead = halve(target) - halve(dp_pos)
            order = (around(0.0 - ahead) + side) * local_sizes[role] + row
            place = (around(ahead) + side) * local_sizes[role] + row
            order_refs[role][:, c0:c1] = order.astype(jnp.int32)
            place_refs[role][:, c0:c1] = place.astype(jnp.int32)


def plan(owners, sizes, local_sizes, capacity, pair_rows):
    dp_count = lax.axis_size("dp")
    rows, start = [], 0
    for size in sizes:
        rows.append(owners[start : start + size][None, :])
        start += size
    outs = pl.pallas_call(
        functools.partial(plan_kernel, dp_count, pair_rows, local_sizes),
        out_shape=[
            jax.ShapeDtypeStruct((1, capacity), jnp.int32),
            jax.ShapeDtypeStruct((dp_count, pair_rows), jnp.int32),
        ]
        + [jax.ShapeDtypeStruct((1, size), jnp.int32) for size in sizes] * 2,
        name="plan",
    )(*rows)
    return outs[0], outs[1], outs[2 : 2 + len(sizes)], outs[2 + len(sizes) :]


def true_group(positions, group, tensor_count):
    flips = positions + (tensor_count - 1 - positions[0],)
    found = flips[0]
    for g in range(1, tensor_count):
        found = found + (flips[g] - flips[0]) * (
            lax.div(group + tensor_count - g, tensor_count)
            - lax.div(group + tensor_count - g - 1, tensor_count)
        )
    return found


def front_kernel(
    sizes,
    mine_ref,
    slot_place_ref,
    spread_place_ref,
    order_qkv_ref,
    order_out_ref,
    order_in_ref,
    order_down_ref,
    tokens_ref,
    gain_ref,
    table_ref,
    bucket_ref,
    segment_ref,
    w_qkv_ref,
    w_out_ref,
    w_in_ref,
    w_down_ref,
    projected_ref,
    attended_ref,
    scale_ref,
    normed_ref,
    exp_ref,
    sent,
    received,
    spread,
    bias,
    segment_keys,
    buf_qkv,
    buf_out,
    buf_in,
    buf_down,
    buf_far,
    far_spread,
    stage_out,
    stage_in,
    stage_down,
    stage_far,
    window,
    scores,
    exp_stage,
    deal_send,
    deal_recv,
    far_send,
    far_recv,
    line_send,
    line_recv,
    side_send,
    side_recv,
    group_send,
    group_recv,
    local_sem,
    exp_sem,
):
    dp_count, pair_rows = sent.shape[0], sent.shape[1]
    tensor_count = w_qkv_ref.shape[0]
    heads = scale_ref.shape[0]
    group_heads = heads // tensor_count
    head_rows = group_heads * HS
    dp_pos, tensor_pos = lax.axis_index("dp"), lax.axis_index("tensor")
    core_pos = tensor_pos + 1 - 2 * lax.rem(tensor_pos, 2)
    far_pos = lax.rem(tensor_pos + 2, tensor_count)
    core_peer, far_peer = (dp_pos, core_pos), (dp_pos, far_pos)

    def dp_peer(m):
        return (lax.rem(dp_pos + m, dp_count), tensor_pos)

    def each_peer(run):
        def step(m, carry):
            run(m)
            return carry

        lax.fori_loop(1, dp_count, step, 0)

    barrier = pltpu.get_barrier_semaphore()

    def greet(m):
        pl.semaphore_signal(barrier, inc=1, device_id=dp_peer(m), device_id_type=MESH)

    each_peer(greet)
    for peer in (core_peer, far_peer):
        pl.semaphore_signal(barrier, inc=1, device_id=peer, device_id_type=MESH)

    mine = mine_ref[...].astype(jnp.bfloat16)
    hot = one_hot(slot_place_ref[...], (dp_count * pair_rows, mine.shape[0]), 0)
    sent[...] = (
        jnp.dot(hot, mine, preferred_element_type=jnp.float32)
        .astype(jnp.bfloat16)
        .reshape(dp_count, pair_rows, D)
    )
    pl.semaphore_wait(barrier, dp_count + 1)

    def deal(m):
        return pltpu.make_async_remote_copy(
            sent.at[m],
            received.at[m],
            deal_send.at[m],
            deal_recv.at[m],
            device_id=dp_peer(m),
            device_id_type=MESH,
        )

    each_peer(lambda m: deal(m).start())
    received[0] = sent[0]

    for r0 in range(0, SEQ, 128):
        values = tokens_ref[r0 : r0 + 128, :].astype(jnp.float32)
        inverse = lax.rsqrt(jnp.mean(values * values, axis=1, keepdims=True) + norm_epsilon)
        normed_ref[r0 : r0 + 128, :] = (values * inverse * gain_ref[...]).astype(jnp.bfloat16)
    rest = table_ref[...]
    hot = one_hot(bucket_ref[...], (NB, 2 * SEQ), 0)
    biases = jnp.zeros((rest.shape[0], 2 * SEQ), jnp.float32)
    for _ in range(3):
        part = rest.astype(jnp.bfloat16)
        rest = rest - part.astype(jnp.float32)
        biases = biases + jnp.dot(part, hot, preferred_element_type=jnp.float32)
    for head in range(heads):
        bias[head] = biases[head : head + 1, :]
    segment_keys[...] = jnp.broadcast_to(segment_ref[...], (TILE, SEQ)).T

    each_peer(lambda m: deal(m).wait())
    rows = spread.shape[0]
    place = jnp.concatenate([spread_place_ref[m : m + 1, :] for m in range(dp_count)], axis=1)
    hot = one_hot(place, (rows, dp_count * pair_rows), 0)
    spread[...] = jnp.dot(
        hot, received[...].reshape(dp_count * pair_rows, D), preferred_element_type=jnp.float32
    ).astype(jnp.bfloat16)

    bufs = (buf_qkv, buf_out, buf_in, buf_down, buf_far)
    orders = (order_qkv_ref, order_out_ref, order_in_ref, order_down_ref, order_down_ref)
    stages = (w_qkv_ref.at[0], stage_out, stage_in, stage_down, stage_far)
    finals = (w_qkv_ref, w_out_ref, w_in_ref, w_down_ref, w_down_ref)
    sizes = tuple(sizes) + (sizes[3],)
    offsets = [sum(buf.shape[1] for buf in bufs[:role]) for role in range(4)]
    line = dp_count // 2
    line_pos, side = lax.div(dp_pos, 2), lax.rem(dp_pos, 2)
    side_peer = (dp_pos + 1 - 2 * side, tensor_pos)

    def far_exchange():
        return pltpu.make_async_remote_copy(
            spread.at[pl.ds(offsets[3], far_spread.shape[0])],
            far_spread,
            far_send,
            far_recv,
            device_id=far_peer,
            device_id_type=MESH,
        )

    def block(role):
        if role == 4:
            return far_spread
        return spread.at[pl.ds(offsets[role], bufs[role].shape[1])]

    def along_line(role, m):
        return pltpu.make_async_remote_copy(
            block(role),
            bufs[role].at[m],
            line_send.at[role, m],
            line_recv.at[role, m],
            device_id=(lax.rem(line_pos + m, line) * 2 + side, tensor_pos),
            device_id_type=MESH,
        )

    def to_side(role, m):
        return pltpu.make_async_remote_copy(
            bufs[role].at[m],
            bufs[role].at[line + m],
            side_send.at[role, m],
            side_recv.at[role, m],
            device_id=side_peer,
            device_id_type=MESH,
        )

    def each_line(first, run):
        def step(m, carry):
            run(m)
            return carry

        lax.fori_loop(first, line, step, 0)

    def start_line(role):
        if role == 4:
            far_exchange().wait()
        each_line(1, lambda m: along_line(role, m).start())
        bufs[role][0] = block(role)[...]
        to_side(role, 0).start()

    def start_side(role):
        def step(m):
            along_line(role, m).wait()
            to_side(role, m).start()

        each_line(1, step)

    def order(role):
        each_line(0, lambda m: to_side(role, m).wait())
        count = bufs[role].shape[1]
        source = bufs[role][...].reshape(dp_count * count, D)
        step = 384 if sizes[role] > 576 else sizes[role]
        for r0 in range(0, sizes[role], step):
            r1 = min(r0 + step, sizes[role])
            hot = one_hot(orders[role][:, r0:r1], (dp_count * count, r1 - r0), 0)
            stages[role][r0:r1, :] = contract(hot, source, 0, 0).astype(jnp.bfloat16)

    def share(role, part):
        if role == 4:
            src, slot, peer = stages[role], 3, core_peer
        else:
            src, slot, peer = (
                (stages[role], 1, core_peer),
                (stages[role], 2, far_peer),
                (finals[role].at[2], 3, core_peer),
            )[part]
        return pltpu.make_async_remote_copy(
            src,
            finals[role].at[slot],
            group_send.at[role, part],
            group_recv.at[role, part],
            device_id=peer,
            device_id_type=MESH,
        )

    def keep(role):
        slot = 2 if role == 4 else 0
        return pltpu.make_async_copy(stages[role], finals[role].at[slot], local_sem.at[role])

    def start_share(role):
        order(role)
        share(role, 0).start()
        if role < 3:
            share(role, 1).start()
        if role > 0:
            keep(role).start()

    def forward(role):
        share(role, 1).wait_recv()
        share(role, 2).start()

    far_exchange().start()
    start_line(0)
    start_side(0)
    start_share(0)
    start_line(1)
    start_line(2)

    def true_head(group, head):
        return true_group((tensor_pos, core_pos, far_pos), group, tensor_count) * group_heads + head

    def head_step(i, carry):
        group, head = lax.div(i, group_heads), lax.rem(i, group_heads)

        @pl.when(i == 1)
        def _():
            start_side(1)

        @pl.when(i == 3)
        def _():
            start_share(1)

        @pl.when(i == 5)
        def _():
            start_side(2)
            start_line(3)
            start_line(4)

        @pl.when(i == 10)
        def _():
            start_share(2)

        @pl.when(i == group_heads)
        def _():
            share(0, 0).wait_recv()

        @pl.when(i == 2 * group_heads)
        def _():
            forward(0)

        @pl.when(i == 3 * group_heads)
        def _():
            share(0, 2).wait_recv()
            forward(1)

        @pl.when(i == 11)
        def _():
            start_side(3)

        @pl.when(head == 0)
        def _():
            projected_ref[group] = contract(w_qkv_ref[group], normed_ref[...], 1, 1).astype(
                jnp.bfloat16
            )

        def head_part(part):
            start = pl.multiple_of(part * head_rows + head * HS, HS)
            return projected_ref[group, pl.ds(start, HS), :]

        slot = lax.rem(i, 2)

        def save(head_index, slot):
            return pltpu.make_async_copy(
                exp_stage.at[slot], exp_ref.at[head_index], exp_sem.at[slot]
            )

        @pl.when(i >= 2)
        def _():
            save(i - 2, slot).wait()

        bias_window(bias[true_head(group, head)], window)
        attended, scale = attend_head(
            head_part(0),
            head_part(1),
            head_part(2),
            segment_keys,
            segment_ref,
            window,
            scores,
            exp_stage.at[slot],
        )
        attended_ref[pl.ds(pl.multiple_of(i * HS, HS), HS), :] = attended
        scale_ref[i] = scale
        save(i, slot).start()
        return carry

    lax.fori_loop(0, heads, head_step, 0)
    for i in (heads - 2, heads - 1):
        pltpu.make_async_copy(exp_stage.at[i % 2], exp_ref.at[i], exp_sem.at[i % 2]).wait()
    start_side(4)
    start_share(3)
    start_share(4)
    forward(2)
    for role in range(len(bufs)):
        share(role, 0).wait_send()
        if role < 3:
            share(role, 1).wait_send()
            share(role, 2).wait_send()
        if role > 0:
            share(role, 0).wait_recv()
            keep(role).wait()
        if role in (1, 2):
            share(role, 2).wait_recv()


def front(
    mine,
    slot_place,
    spread_place,
    orders,
    local_sizes,
    tokens,
    gain,
    table,
    bucket_place,
    segments,
):
    dp_count, tensor_count = lax.axis_size("dp"), lax.axis_size("tensor")
    sizes = [order.shape[1] for order in orders]
    pair_rows = spread_place.shape[1]
    low = jnp.bfloat16
    dma = pltpu.SemaphoreType.DMA
    roles = len(sizes)
    whole = pl.BlockSpec(memory_space=pltpu.VMEM)
    away = pl.BlockSpec(memory_space=pl.ANY)
    return pl.pallas_call(
        functools.partial(front_kernel, sizes),
        in_specs=[whole] * 12,
        out_specs=[whole, away, away, away, whole, whole, whole, whole, away],
        out_shape=[jax.ShapeDtypeStruct((tensor_count, size, D), low) for size in sizes]
        + [
            jax.ShapeDtypeStruct((tensor_count, sizes[0], SEQ), low),
            jax.ShapeDtypeStruct((H * HS, SEQ), low),
            jax.ShapeDtypeStruct((H, 1, SEQ), jnp.float32),
            jax.ShapeDtypeStruct((SEQ, D), low),
            jax.ShapeDtypeStruct((H, SEQ, SEQ), low),
        ],
        scratch_shapes=[
            pltpu.VMEM((dp_count, pair_rows, D), low),
            pltpu.VMEM((dp_count, pair_rows, D), low),
            pltpu.VMEM((sum(local_sizes), D), low),
            pltpu.VMEM((H, 1, 2 * SEQ), jnp.float32),
            pltpu.VMEM((SEQ, TILE), jnp.float32),
        ]
        + [pltpu.VMEM((dp_count, size, D), low) for size in local_sizes + local_sizes[3:]]
        + [pltpu.VMEM((local_sizes[3], D), low)]
        + [pltpu.VMEM((size, D), low) for size in sizes[1:] + sizes[3:]]
        + [
            pltpu.VMEM((WINDOW, TILE), jnp.float32),
            pltpu.VMEM((SEQ, QUERY_TILE), jnp.float32),
            pltpu.VMEM((2, SEQ, SEQ), low),
            dma((dp_count,)),
            dma((dp_count,)),
            dma,
            dma,
            dma((roles + 1, dp_count // 2)),
            dma((roles + 1, dp_count // 2)),
            dma((roles + 1, dp_count // 2)),
            dma((roles + 1, dp_count // 2)),
            dma((roles + 1, 3)),
            dma((roles + 1, 3)),
            dma((roles + 1,)),
            dma((2,)),
        ],
        compiler_params=pltpu.CompilerParams(
            collective_id=1, has_side_effects=True, vmem_limit_bytes=56 * 1024 * 1024
        ),
        cost_estimate=pl.CostEstimate(
            flops=10 * H * SEQ * SEQ * 256,
            bytes_accessed=64 * 1024 * 1024,
            transcendentals=H * SEQ * SEQ,
        ),
        name="front",
    )(
        mine,
        slot_place,
        spread_place,
        *orders,
        tokens,
        gain[None, :],
        table,
        bucket_place,
        segments.astype(jnp.float32)[None, :],
    )


def attend_head_back(
    query_rows,
    key_rows,
    value_rows,
    exp_ref,
    attended,
    scale,
    attended_grad,
    window,
    score_grads,
    store,
):
    scaled = attended_grad.astype(jnp.float32) * scale
    delta = jnp.sum(scaled * attended.astype(jnp.float32), axis=0, keepdims=True)
    scaled_low = scaled.astype(jnp.bfloat16)
    delta_high = delta.astype(jnp.bfloat16).astype(jnp.float32)
    delta_rest = delta - delta_high
    place = lax.broadcasted_iota(jnp.int32, (16, SEQ), 0)
    extra = jnp.where(
        place == 0,
        jnp.broadcast_to(-delta_high, (16, SEQ)),
        jnp.where(place == 1, jnp.broadcast_to(-delta_rest, (16, SEQ)), 0.0),
    ).astype(jnp.bfloat16)
    grads = jnp.concatenate([scaled_low, extra], axis=0)
    values = jnp.concatenate([value_rows, jnp.ones((16, SEQ), jnp.bfloat16)], axis=0).T
    window[...] = jnp.zeros_like(window)
    for q0 in range(0, SEQ, BACK_QUERY_TILE):
        total = jnp.zeros((HS, BACK_QUERY_TILE), jnp.float32)
        for k0 in range(0, SEQ, BACK_KEY_TILE):
            centered = jnp.dot(
                values[k0 : k0 + BACK_KEY_TILE],
                grads[:, q0 : q0 + BACK_QUERY_TILE],
                preferred_element_type=jnp.float32,
            )
            score_grad = centered * exp_ref[
                k0 : k0 + BACK_KEY_TILE, q0 : q0 + BACK_QUERY_TILE
            ].astype(jnp.float32)
            for l0 in range(0, BACK_QUERY_TILE, TILE):
                start = SEQ - TILE - (q0 + l0) + k0
                window[start : start + BACK_KEY_TILE, :] += score_grad[:, l0 : l0 + TILE]
            score_low = score_grad.astype(jnp.bfloat16)
            score_grads[k0 : k0 + BACK_KEY_TILE, q0 : q0 + BACK_QUERY_TILE] = score_low
            total = total + jnp.dot(
                key_rows[:, k0 : k0 + BACK_KEY_TILE], score_low, preferred_element_type=jnp.float32
            )
        store(0, q0, total.astype(jnp.bfloat16))
    queries = query_rows.T
    scaled_rows = scaled_low.T
    for k0 in range(0, SEQ, BACK_KEY_TILE):
        key_grad = jnp.dot(
            score_grads[k0 : k0 + BACK_KEY_TILE, :], queries, preferred_element_type=jnp.float32
        )
        value_grad = jnp.dot(
            exp_ref[k0 : k0 + BACK_KEY_TILE, :], scaled_rows, preferred_element_type=jnp.float32
        )
        store(1, k0, key_grad.T.astype(jnp.bfloat16))
        store(2, k0, value_grad.T.astype(jnp.bfloat16))
    pieces = [jnp.zeros((1, TILE), jnp.float32)] * (2 * SEQ // TILE)
    for tile in range(WINDOW // TILE):
        base = WINDOW - TILE * tile
        block = window[TILE * tile : TILE * (tile + 1), :]
        folded = jnp.concatenate([jnp.zeros((TILE, TILE), jnp.float32), block], axis=1)
        rows = TILE // 2
        while rows >= 1:
            folded = folded[:rows] + pltpu.roll(folded[rows:], 2 * TILE - rows, 1)
            rows //= 2
        pieces[base // TILE - 1] += folded[:, :TILE]
        pieces[base // TILE] += folded[:, TILE:]
    return jnp.concatenate(pieces, axis=1)


SMALL_ROWS = 48
TABLE_ROW = 32


def back_kernel(
    sizes,
    ffn_grad_ref,
    normed_two_ref,
    mid_ref,
    cotangent_ref,
    w_out_ref,
    activ_ref,
    slope_ref,
    w_in_ref,
    w_down_ref,
    projected_ref,
    exp_ref,
    w_qkv_ref,
    tokens_ref,
    normed_one_ref,
    attended_ref,
    scale_ref,
    gain_one_ref,
    gain_two_ref,
    small_ref,
    bucket_ref,
    place_qkv_ref,
    place_out_ref,
    place_in_ref,
    place_down_ref,
    spread_place_ref,
    slot_place_ref,
    owned_ref,
    input_grad_ref,
    small_total_ref,
    bucket_hot,
    weights,
    proj,
    proj_grad,
    normed_grad,
    window,
    score_grads,
    exp_stage,
    row_grads,
    normed,
    attended_grad,
    odd_out,
    odd_in,
    odd_down,
    zero_qkv,
    zero_out,
    zero_in,
    zero_down,
    two_qkv,
    two_out,
    two_in,
    two_down,
    core_one_qkv,
    core_one_out,
    core_one_in,
    core_one_down,
    core_three_qkv,
    core_three_out,
    core_three_in,
    core_three_down,
    far_qkv,
    far_out,
    far_in,
    far_down,
    got_qkv,
    got_out,
    got_in,
    got_down,
    side_qkv,
    side_out,
    side_down,
    end_mine,
    end_far,
    spread,
    sent,
    received,
    small_own,
    small_tensor,
    small_dp,
    core_send,
    core_recv,
    far_send,
    far_recv,
    side_send,
    side_recv,
    line_send,
    line_recv,
    end_send,
    end_recv,
    back_send,
    back_recv,
    small_send,
    small_recv,
    load_sem,
    exp_sem,
    proj_sem,
):
    dp_count, pair_rows = spread_place_ref.shape
    hidden_rows = w_in_ref.shape[1]
    tensor_count = w_qkv_ref.shape[0]
    heads = scale_ref.shape[0]
    group_heads = heads // tensor_count
    head_rows = group_heads * HS
    dp_pos, tensor_pos = lax.axis_index("dp"), lax.axis_index("tensor")
    core_pos = tensor_pos + 1 - 2 * lax.rem(tensor_pos, 2)
    far_pos = lax.rem(tensor_pos + 2, tensor_count)
    core_peer, far_peer = (dp_pos, core_pos), (dp_pos, far_pos)
    zeros = (zero_qkv, zero_out, zero_in, zero_down)
    twos = (two_qkv, two_out, two_in, two_down)
    core_ones = (core_one_qkv, core_one_out, core_one_in, core_one_down)
    core_threes = (core_three_qkv, core_three_out, core_three_in, core_three_down)
    fars = (far_qkv, far_out, far_in, far_down)
    gots = (got_qkv, got_out, got_in, got_down)
    side_got = (side_qkv, side_out, far_in, side_down)
    places = (place_qkv_ref, place_out_ref, place_in_ref, place_down_ref)
    offsets = [sum(got.shape[1] for got in gots[:role]) for role in range(len(gots))]
    low = jnp.bfloat16

    def up(m):
        return lax.rem(dp_pos + m, dp_count)

    def down(m):
        return lax.rem(dp_pos + dp_count - m, dp_count)

    def each_peer(run):
        def step(m, carry):
            run(m)
            return carry

        lax.fori_loop(1, dp_count, step, 0)

    def tensor_peer(m):
        return (dp_pos, lax.rem(tensor_pos + m, tensor_count))

    barrier = pltpu.get_barrier_semaphore()

    def greet(m):
        pl.semaphore_signal(barrier, inc=1, device_id=(up(m), tensor_pos), device_id_type=MESH)

    each_peer(greet)
    for m in range(1, tensor_count):
        pl.semaphore_signal(barrier, inc=1, device_id=tensor_peer(m), device_id_type=MESH)

    def load_exp(head, slot):
        return pltpu.make_async_copy(exp_ref.at[head], exp_stage.at[slot], exp_sem.at[slot])

    def load_proj(group):
        return pltpu.make_async_copy(projected_ref.at[group], proj, proj_sem.at[0])

    def load_weights(group):
        return pltpu.make_async_copy(w_qkv_ref.at[group], weights, proj_sem.at[1])

    def load(which, group=0):
        columns = pl.ds(pl.multiple_of(group * hidden_rows, TILE), hidden_rows)
        source, target = (
            (lambda: activ_ref.at[:, columns], lambda: exp_stage.at[0, :, pl.ds(0, hidden_rows)]),
            (lambda: slope_ref.at[:, columns], lambda: exp_stage.at[1, :, pl.ds(0, hidden_rows)]),
            (lambda: w_in_ref.at[group], lambda: received.at[pl.ds(0, hidden_rows)]),
            (lambda: w_down_ref.at[group], lambda: sent.at[pl.ds(0, hidden_rows)]),
            (lambda: ffn_grad_ref, lambda: row_grads),
            (lambda: normed_two_ref, lambda: normed),
            (lambda: mid_ref, lambda: exp_stage.at[0, :, pl.ds(0, D)]),
            (lambda: cotangent_ref, lambda: exp_stage.at[1, :, pl.ds(0, D)]),
            (lambda: w_out_ref, lambda: sent.at[pl.ds(0, D)]),
            (lambda: normed_one_ref, lambda: normed),
            (lambda: tokens_ref, lambda: exp_stage.at[0, :, pl.ds(0, D)]),
        )[which]
        return pltpu.make_async_copy(source(), target(), load_sem.at[which])

    def core_copy(role, which):
        half = which // 2
        if role == 0:
            src = (odd_in, odd_down)[half].at[pl.ds(0, sizes[0])]
        else:
            src = (None, odd_out.at[half], odd_in, odd_down)[role]
        target = (core_ones if which == 1 else core_threes)[role].at[pl.ds(0, sizes[role])]
        return pltpu.make_async_remote_copy(
            src,
            target,
            core_send.at[role, half],
            core_recv.at[role, half],
            device_id=core_peer,
            device_id_type=MESH,
        )

    def far_copy(role):
        return pltpu.make_async_remote_copy(
            twos[role],
            fars[role],
            far_send.at[role],
            far_recv.at[role],
            device_id=far_peer,
            device_id_type=MESH,
        )

    line = dp_count // 2
    line_pos, side = lax.div(dp_pos, 2), lax.rem(dp_pos, 2)
    side_peer = (dp_pos + 1 - 2 * side, tensor_pos)

    def each_line(run):
        def step(m, carry):
            run(m)
            return carry

        lax.fori_loop(1, line, step, 0)

    def leaving(role, far):
        return core_ones[role] if far else core_threes[role]

    def side_copy(role, far=0):
        count = gots[role].shape[1] * line
        return pltpu.make_async_remote_copy(
            leaving(role, far).at[pl.ds(count, count)],
            side_got[role].at[pl.ds(count * far, count)],
            side_send.at[role, far],
            side_recv.at[role, far],
            device_id=side_peer,
            device_id_type=MESH,
        )

    def line_copy(role, m, far=0):
        count = gots[role].shape[1]
        return pltpu.make_async_remote_copy(
            leaving(role, far).at[pl.ds(pl.multiple_of(m * count, 16), count)],
            gots[role].at[far * line + m],
            line_send.at[role, far * line + m],
            line_recv.at[role, far * line + m],
            device_id=(lax.rem(line_pos + m, line) * 2 + side, tensor_pos),
            device_id_type=MESH,
        )

    def end_copy():
        return pltpu.make_async_remote_copy(
            end_mine, end_far, end_send, end_recv, device_id=far_peer, device_id_type=MESH
        )

    def send_far(role):
        core_copy(role, 3).wait_recv()
        count = twos[role].shape[0]
        twos[role][...] = (
            twos[role][...].astype(jnp.float32)
            + core_threes[role][0:count, :].astype(jnp.float32)
        ).astype(low)
        far_copy(role).start()

    def scatter(role, far, total):
        count = gots[role].shape[1]
        for r0 in range(0, dp_count * count, 384):
            r1 = min(r0 + 384, dp_count * count)
            hot = one_hot(places[role][...] - r0, (r1 - r0, sizes[role]), 0)
            leaving(role, far)[r0:r1, :] = jnp.dot(
                hot, total, preferred_element_type=jnp.float32
            ).astype(low)
        side_copy(role, far).start()

    def send_deal(role):
        core_copy(role, 1).wait_recv()
        far_copy(role).wait_recv()
        total = (
            zeros[role][...].astype(jnp.float32)
            + core_ones[role][...].astype(jnp.float32)
            + fars[role][...].astype(jnp.float32)
        ).astype(low)
        scatter(role, 0, total)

    def send_both(role):
        core_copy(role, 1).wait_recv()
        core_copy(role, 3).wait_recv()
        count = sizes[role]
        near = (
            zeros[role][...].astype(jnp.float32)
            + core_ones[role][0:count, :].astype(jnp.float32)
        ).astype(low)
        far = (
            twos[role][...].astype(jnp.float32)
            + core_threes[role][0:count, :].astype(jnp.float32)
        ).astype(low)
        scatter(role, 0, near)
        scatter(role, 1, far)

    def pass_line(role, far=0):
        side_copy(role, far).wait()
        count = gots[role].shape[1] * line
        leaving(role, far)[0:count, :] = (
            leaving(role, far)[0:count, :].astype(jnp.float32)
            + side_got[role][count * far : count * (far + 1), :].astype(jnp.float32)
        ).astype(low)
        each_line(lambda m: line_copy(role, m, far).start())

    def line_sum(role, far=0):
        each_line(lambda m: line_copy(role, m, far).wait())
        total = leaving(role, far)[0 : gots[role].shape[1], :].astype(jnp.float32)
        for m in range(1, line):
            total = total + gots[role][far * line + m].astype(jnp.float32)
        return total

    def finish_deal(role):
        count = gots[role].shape[1]
        spread[offsets[role] : offsets[role] + count, :] = line_sum(role).astype(low)

    def finish_far():
        end_mine[...] = line_sum(2, 1).astype(low)
        end_copy().start()

    def finish_near():
        total = line_sum(2)
        end_copy().wait()
        count = gots[2].shape[1]
        spread[offsets[2] : offsets[2] + count, :] = (
            total + end_far[...].astype(jnp.float32)
        ).astype(low)

    for which in (4, 5):
        load(which).start()
    for which in range(4):
        load(which, tensor_count - 1).start()
    bucket_hot[...] = one_hot(bucket_ref[...], (NB, 2 * SEQ), 0)
    normed_grad[...] = jnp.zeros_like(normed_grad)
    small_own[0:TABLE_ROW, :] = small_ref[...]
    small_own[TABLE_ROW:SMALL_ROWS, :] = jnp.zeros((SMALL_ROWS - TABLE_ROW, TILE), jnp.float32)
    pl.semaphore_wait(barrier, dp_count + tensor_count - 2)
    for which in (4, 5):
        load(which).wait()
    row_tiles = [slice(r0, r0 + 256) for r0 in range(0, SEQ, 256)]
    pre_grad = score_grads

    def feed_step(i, carry):
        group = tensor_count - 1 - i

        def load_next(which):
            @pl.when(group > 0)
            def _():
                load(which, group - 1).start()

        load(3, group).wait()
        load(1, group).wait()
        for rows in row_tiles:
            grad = contract(row_grads[rows, :], sent[0:hidden_rows, :], 1, 1)
            grad = grad * exp_stage[1, rows, 0:hidden_rows].astype(jnp.float32)
            pre_grad[rows, 0:hidden_rows] = grad.astype(low)
        load_next(3)
        load_next(1)
        load(2, group).wait()
        for rows in row_tiles:
            normed_grad[rows, :] += jnp.dot(
                pre_grad[rows, 0:hidden_rows],
                received[0:hidden_rows, :],
                preferred_element_type=jnp.float32,
            )
        load_next(2)

        @pl.when(group == 2)
        def _():
            for role in (3, 2):
                core_copy(role, 3).wait_send()

        @pl.when(group == 0)
        def _():
            for role in (3, 2):
                core_copy(role, 1).wait_send()

        load(0, group).wait()
        for c0 in range(0, hidden_rows, 256):
            columns = slice(c0, c0 + 256)
            odd_down[columns, :] = jnp.dot(
                exp_stage[0, :, columns].T, row_grads[...], preferred_element_type=jnp.float32
            ).astype(low)
        load_next(0)

        @pl.when(group == 3)
        def _():
            core_copy(3, 3).start()

        @pl.when(group == 2)
        def _():
            two_down[...] = odd_down[...]
            send_far(3)

        @pl.when(group == 1)
        def _():
            core_copy(3, 1).start()

        @pl.when(group == 0)
        def _():
            zero_down[...] = odd_down[...]

        for c0 in range(0, hidden_rows, 256):
            columns = slice(c0, c0 + 256)
            odd_in[columns, :] = jnp.dot(
                pre_grad[:, columns].T, normed[...], preferred_element_type=jnp.float32
            ).astype(low)

        @pl.when(group == 3)
        def _():
            core_copy(2, 3).start()

        @pl.when(group == 2)
        def _():
            two_in[...] = odd_in[...]

        @pl.when(group == 1)
        def _():
            core_copy(2, 1).start()

        @pl.when(group == 0)
        def _():
            zero_in[...] = odd_in[...]

        return carry

    lax.fori_loop(0, tensor_count, feed_step, 0)
    for which in (6, 7, 8, 9):
        load(which).start()
    send_both(2)
    for which in (6, 7, 8):
        load(which).wait()
    gain_grad = jnp.zeros((1, D), jnp.float32)
    for r0 in range(0, SEQ, 128):
        rows = slice(r0, r0 + 128)
        mid = exp_stage[0, rows, 0:D].astype(jnp.float32)
        grads = normed_grad[rows, :]
        inverse = lax.rsqrt(jnp.mean(mid * mid, axis=1, keepdims=True) + norm_epsilon)
        scaled = mid * inverse
        gain_grad = gain_grad + jnp.sum(grads * scaled, axis=0, keepdims=True)
        grads = grads * gain_two_ref[...]
        inner = jnp.mean(grads * scaled, axis=1, keepdims=True)
        row_grads[rows, :] = (
            exp_stage[1, rows, 0:D].astype(jnp.float32) + inverse * (grads - scaled * inner)
        ).astype(low)
    for part in range(D // TILE):
        line_at = D // TILE + part
        small_own[line_at : line_at + 1, :] = gain_grad[:, TILE * part : TILE * (part + 1)]
    normed_grad[...] = jnp.zeros_like(normed_grad)
    load_exp(heads - group_heads, 0).start()
    load_proj(tensor_count - 1).start()
    load_weights(tensor_count - 1).start()
    for group, target in enumerate((zero_out, odd_out.at[0], two_out, odd_out.at[1])):
        rows = slice(group * head_rows, (group + 1) * head_rows)
        target[...] = jnp.dot(
            attended_ref[rows, :], row_grads[...], preferred_element_type=jnp.float32
        ).astype(low)
    core_copy(1, 3).start()
    core_copy(1, 1).start()
    for r0 in range(0, D, 256):
        rows = slice(r0, r0 + 256)
        attended_grad[rows, :] = contract(sent[rows, :], row_grads[...], 1, 1).astype(low)
    load(9).wait()

    def head_step(i, carry):
        group = tensor_count - 1 - lax.div(i, group_heads)
        part_head = lax.rem(i, group_heads)
        head = group * group_heads + part_head
        slot = lax.rem(i, 2)

        @pl.when(i == 1)
        def _():
            send_deal(3)

        @pl.when(i == 2)
        def _():
            send_far(1)

        @pl.when(i == 5)
        def _():
            send_deal(1)

        @pl.when(i == 6)
        def _():
            send_far(0)
            pass_line(2, 1)
            pass_line(2, 0)

        @pl.when(i == 9)
        def _():
            pass_line(3)

        @pl.when(i == 10)
        def _():
            pass_line(1)

        @pl.when(part_head == 0)
        def _():
            load_proj(group).wait()

        @pl.when(i + 1 < heads)
        def _():
            later = i + 1
            later_group = tensor_count - 1 - lax.div(later, group_heads)
            later_head = later_group * group_heads + lax.rem(later, group_heads)
            load_exp(later_head, lax.rem(later, 2)).start()

        load_exp(head, slot).wait()

        def rows(part):
            return pl.ds(pl.multiple_of(part * head_rows + part_head * HS, HS), HS)

        def store(part, column, value):
            proj_grad[rows(part), column : column + value.shape[1]] = value

        here = pl.ds(pl.multiple_of(head * HS, HS), HS)
        offset_grad = attend_head_back(
            proj[rows(0), :],
            proj[rows(1), :],
            proj[rows(2), :],
            exp_stage.at[slot],
            attended_ref[here, :],
            scale_ref[head],
            attended_grad[here, :],
            window,
            score_grads,
            store,
        )
        place = (
            true_group((tensor_pos, core_pos, far_pos), group, tensor_count) * group_heads + part_head
        )
        high = offset_grad.astype(low)
        rest = (offset_grad - high.astype(jnp.float32)).astype(low)
        both = jnp.concatenate([high, rest] + [jnp.zeros_like(high)] * 6, axis=0)
        sums = contract(both, bucket_hot[...], 1, 1)
        row = lax.broadcasted_iota(jnp.int32, (SMALL_ROWS - TABLE_ROW, TILE), 0)
        found = jnp.concatenate(
            [sums[0:1] + sums[1:2], jnp.zeros((1, TILE - NB), jnp.float32)], axis=1
        )
        small_own[TABLE_ROW:SMALL_ROWS, :] += jnp.where(
            row == place,
            jnp.broadcast_to(found, (SMALL_ROWS - TABLE_ROW, TILE)),
            0.0,
        )

        @pl.when(part_head == group_heads - 1)
        def _():
            @pl.when(group > 0)
            def _():
                load_proj(group - 1).start()

            def weight_grad(target):
                for r0 in range(0, 3 * head_rows, head_rows):
                    target[r0 : r0 + head_rows, :] = jnp.dot(
                        proj_grad[r0 : r0 + head_rows, :],
                        normed[...],
                        preferred_element_type=jnp.float32,
                    ).astype(low)

            @pl.when(group == 3)
            def _():
                weight_grad(odd_down)
                core_copy(0, 3).start()

            @pl.when(group == 2)
            def _():
                weight_grad(two_qkv)

            @pl.when(group == 1)
            def _():
                weight_grad(odd_in)
                core_copy(0, 1).start()

            @pl.when(group == 0)
            def _():
                weight_grad(zero_qkv)

            load_weights(group).wait()
            for r0 in range(0, SEQ, 256):
                normed_grad[r0 : r0 + 256, :] += jnp.dot(
                    proj_grad[:, r0 : r0 + 256].T,
                    weights[...],
                    preferred_element_type=jnp.float32,
                )

            @pl.when(group > 0)
            def _():
                load_weights(group - 1).start()

        return carry

    lax.fori_loop(0, heads, head_step, 0)

    load(10).start()
    send_deal(0)
    load(10).wait()

    gain_grad = jnp.zeros((1, D), jnp.float32)
    for r0 in range(0, SEQ, 128):
        values = exp_stage[0, r0 : r0 + 128, 0:D].astype(jnp.float32)
        grads = normed_grad[r0 : r0 + 128, :]
        inverse = lax.rsqrt(jnp.mean(values * values, axis=1, keepdims=True) + norm_epsilon)
        scaled = values * inverse
        gain_grad = gain_grad + jnp.sum(grads * scaled, axis=0, keepdims=True)
        grads = grads * gain_one_ref[...]
        inner = jnp.mean(grads * scaled, axis=1, keepdims=True)
        row_grads[r0 : r0 + 128, :] = (
            row_grads[r0 : r0 + 128, :].astype(jnp.float32) + inverse * (grads - scaled * inner)
        ).astype(low)
    for part in range(D // TILE):
        small_own[part : part + 1, :] = gain_grad[:, TILE * part : TILE * (part + 1)]

    save_rows = pltpu.make_async_copy(row_grads, input_grad_ref, exp_sem.at[1])
    save_rows.start()

    def small_copy(stage, m):
        if stage == 0:
            src, target, peer = small_own, small_tensor.at[tensor_pos], tensor_peer(m)
        else:
            src, target, peer = small_total_ref, small_dp.at[dp_pos], (up(m), tensor_pos)
        return pltpu.make_async_remote_copy(
            src,
            target,
            small_send.at[stage, m],
            small_recv.at[stage, m],
            device_id=peer,
            device_id_type=MESH,
        )

    for m in range(1, tensor_count):
        small_copy(0, m).start()
    small_tensor[tensor_pos] = small_own[...]
    for m in range(1, tensor_count):
        small_copy(0, m).wait()
    total = small_tensor[0]
    for m in range(1, tensor_count):
        total = total + small_tensor[m]
    small_total_ref[...] = total
    each_peer(lambda m: small_copy(1, m).start())
    finish_far()
    pass_line(0)
    finish_near()
    finish_deal(3)
    small_dp[dp_pos] = small_total_ref[...]
    each_peer(lambda m: small_copy(1, m).wait())
    total = small_dp[0]
    for m in range(1, dp_count):
        total = total + small_dp[m]
    small_total_ref[...] = total
    finish_deal(1)
    finish_deal(0)

    place = jnp.concatenate([spread_place_ref[m : m + 1, :] for m in range(dp_count)], axis=1)
    hot = one_hot(place, (spread.shape[0], dp_count * pair_rows), 0)
    sent[0 : dp_count * pair_rows, :] = contract(hot, spread[...], 0, 0).astype(low)

    def back_copy(m):
        here = pl.ds(pl.multiple_of(m * pair_rows, 16), pair_rows)
        return pltpu.make_async_remote_copy(
            sent.at[here],
            received.at[here],
            back_send.at[m],
            back_recv.at[m],
            device_id=(down(m), tensor_pos),
            device_id_type=MESH,
        )

    each_peer(lambda m: back_copy(m).start())
    received[0:pair_rows, :] = sent[0:pair_rows, :]
    each_peer(lambda m: back_copy(m).wait())
    hot = one_hot(slot_place_ref[...], (dp_count * pair_rows, owned_ref.shape[0]), 0)
    owned_ref[...] = contract(hot, received[0 : dp_count * pair_rows, :], 0, 0)
    save_rows.wait()
    for role in range(len(gots)):
        if role < 2:
            core_copy(role, 1).wait_send()
            core_copy(role, 3).wait_send()
        if role != 2:
            far_copy(role).wait_send()


def back(
    feed_parts,
    projected,
    exp_scores,
    w_qkv,
    tokens,
    normed_one,
    attended,
    scale,
    gain_one,
    gain_two,
    small,
    bucket_place,
    places,
    local_sizes,
    spread_place,
    slot_place,
):
    dp_count, tensor_count = lax.axis_size("dp"), lax.axis_size("tensor")
    sizes = [place.shape[1] for place in places]
    capacity, pair_rows = slot_place.shape[1], spread_place.shape[1]
    low = jnp.bfloat16
    dma = pltpu.SemaphoreType.DMA
    roles = len(sizes)
    whole = pl.BlockSpec(memory_space=pltpu.VMEM)
    away = pl.BlockSpec(memory_space=pl.ANY)
    parts = [pltpu.VMEM((size, D), low) for size in sizes]
    padded = [
        pltpu.VMEM((max(dp_count * size, full), D), low) for size, full in zip(local_sizes, sizes)
    ]
    return pl.pallas_call(
        functools.partial(back_kernel, sizes),
        in_specs=[away] * 14 + [whole] * 12,
        out_specs=[whole, away, whole],
        out_shape=[
            jax.ShapeDtypeStruct((capacity, D), jnp.float32),
            jax.ShapeDtypeStruct((SEQ, D), low),
            jax.ShapeDtypeStruct((SMALL_ROWS, TILE), jnp.float32),
        ],
        scratch_shapes=[
            pltpu.VMEM((NB, 2 * SEQ), low),
            pltpu.VMEM((sizes[0], D), low),
            pltpu.VMEM((sizes[0], SEQ), low),
            pltpu.VMEM((sizes[0], SEQ), low),
            pltpu.VMEM((SEQ, D), jnp.float32),
            pltpu.VMEM((WINDOW, TILE), jnp.float32),
            pltpu.VMEM((SEQ, SEQ), low),
            pltpu.VMEM((2, SEQ, SEQ), low),
            pltpu.VMEM((SEQ, D), low),
            pltpu.VMEM((SEQ, D), low),
            pltpu.VMEM((D, SEQ), low),
            pltpu.VMEM((2, sizes[1], D), low),
            pltpu.VMEM((sizes[2], D), low),
            pltpu.VMEM((sizes[3], D), low),
        ]
        + parts
        + parts
        + parts[:2]
        + padded[2:3]
        + parts[3:]
        + padded
        + parts[:2]
        + [pltpu.VMEM((dp_count * local_sizes[2], D), low)]
        + parts[3:]
        + [
            pltpu.VMEM((dp_count if role == 2 else dp_count // 2, size, D), low)
            for role, size in enumerate(local_sizes)
        ]
        + [pltpu.VMEM((dp_count // 2 * local_sizes[role], D), low) for role in (0, 1, 3)]
        + [
            pltpu.VMEM((local_sizes[2], D), low),
            pltpu.VMEM((local_sizes[2], D), low),
            pltpu.VMEM((sum(local_sizes), D), low),
            pltpu.VMEM((max(dp_count * pair_rows, D), D), low),
            pltpu.VMEM((max(dp_count * pair_rows, D), D), low),
            pltpu.VMEM((SMALL_ROWS, TILE), jnp.float32),
            pltpu.VMEM((tensor_count, SMALL_ROWS, TILE), jnp.float32),
            pltpu.VMEM((dp_count, SMALL_ROWS, TILE), jnp.float32),
            dma((roles, 2)),
            dma((roles, 2)),
            dma((roles,)),
            dma((roles,)),
            dma((roles, 2)),
            dma((roles, 2)),
            dma((roles, dp_count)),
            dma((roles, dp_count)),
            dma,
            dma,
            dma((dp_count,)),
            dma((dp_count,)),
            dma((2, max(dp_count, tensor_count))),
            dma((2, max(dp_count, tensor_count))),
            dma((11,)),
            dma((2,)),
            dma((2,)),
        ],
        compiler_params=pltpu.CompilerParams(
            collective_id=2, has_side_effects=True, vmem_limit_bytes=63 * 1024 * 1024
        ),
        cost_estimate=pl.CostEstimate(
            flops=16 * H * SEQ * SEQ * 256 + 8 * SEQ * FF * D,
            bytes_accessed=96 * 1024 * 1024,
            transcendentals=0,
        ),
        name="back",
    )(
        *feed_parts,
        projected,
        exp_scores,
        w_qkv,
        tokens,
        normed_one,
        attended,
        scale,
        gain_one[None, :],
        gain_two[None, :],
        small,
        bucket_place,
        *places,
        spread_place,
        slot_place,
    )


FEED_WIDTH = 768


def feed_kernel(
    attended_ref,
    w_out_ref,
    tokens_ref,
    gain_ref,
    cotangent_ref,
    left_ref,
    right_ref,
    wide_ref,
    tall_ref,
    w_in_ref,
    w_down_ref,
    activ_ref,
    slope_ref,
    normed_ref,
    mid_ref,
    layer_out_ref,
    ffn_grad_ref,
    left_grad_ref,
    right_grad_ref,
    wide_grad_ref,
    tall_grad_ref,
    ffn_out,
    mid_rows,
):
    low = jnp.bfloat16
    row_tile = 256
    tiles = range(0, SEQ, row_tile)

    @pl.when(pl.program_id(0) == 0)
    def _():
        for r0 in tiles:
            rows = slice(r0, r0 + row_tile)
            attn = jnp.dot(
                attended_ref[:, rows].T, w_out_ref[...], preferred_element_type=jnp.float32
            )
            mid = tokens_ref[rows, :].astype(jnp.float32) + attn
            mid_rows[rows, :] = mid
            mid_ref[rows, :] = mid.astype(low)
            inverse = lax.rsqrt(jnp.mean(mid * mid, axis=1, keepdims=True) + norm_epsilon)
            normed_ref[rows, :] = (mid * inverse * gain_ref[...]).astype(low)
            ffn_out[rows, :] = jnp.zeros((row_tile, D), jnp.float32)

    for r0 in tiles:
        rows = slice(r0, r0 + row_tile)
        pre = contract(normed_ref[rows, :], w_in_ref[...], 1, 1)
        cdf, density = normal_parts(pre)
        activ = (pre * cdf).astype(low)
        activ_ref[rows, :] = activ
        slope_ref[rows, :] = (cdf + pre * density).astype(low)
        ffn_out[rows, :] += jnp.dot(activ, w_down_ref[...], preferred_element_type=jnp.float32)

    @pl.when(pl.program_id(0) == pl.num_programs(0) - 1)
    def _():
        down = jnp.dot(
            left_ref[...], right_ref[...], precision=highest, preferred_element_type=jnp.float32
        ).astype(low)
        up = jnp.dot(
            wide_ref[...], tall_ref[...], precision=highest, preferred_element_type=jnp.float32
        ).astype(low)
        down_grad = jnp.zeros((R, D), jnp.float32)
        up_grad = jnp.zeros((R, D), jnp.float32)
        for r0 in tiles:
            rows = slice(r0, r0 + row_tile)
            ffn = ffn_out[rows, :]
            ffn_low = ffn.astype(low)
            grad_low = cotangent_ref[rows, :]
            zed = contract(ffn_low, down, 1, 1)
            cdf, density = normal_parts(zed)
            hidden = (zed * cdf).astype(low)
            added = jnp.dot(hidden, up, preferred_element_type=jnp.float32)
            layer_out_ref[rows, :] = (mid_rows[rows, :] + ffn + added).astype(low)
            zed_grad = contract(grad_low, up, 1, 1) * (cdf + zed * density)
            zed_low = zed_grad.astype(low)
            ffn_grad_ref[rows, :] = (
                grad_low.astype(jnp.float32)
                + jnp.dot(zed_low, down, preferred_element_type=jnp.float32)
            ).astype(low)
            up_grad = up_grad + contract(hidden, grad_low, 0, 0)
            down_grad = down_grad + contract(zed_low, ffn_low, 0, 0)

        def exact(left, right, left_dim, right_dim):
            return lax.dot_general(
                left,
                right,
                (((left_dim,), (right_dim,)), ((), ())),
                precision=highest,
                preferred_element_type=jnp.float32,
            )

        left_grad_ref[...] = exact(down_grad, right_ref[...], 1, 1)
        right_grad_ref[...] = exact(left_ref[...], down_grad, 0, 0)
        wide_grad_ref[...] = exact(up_grad, tall_ref[...], 1, 1)
        tall_grad_ref[...] = exact(wide_ref[...], up_grad, 0, 0)


def feed(attended, w_out, tokens, gain, cotangent, factors, w_in, w_down):
    def fixed(*shape):
        return pl.BlockSpec(shape, lambda j: (0,) * len(shape))

    def stripe():
        return pl.BlockSpec((FEED_WIDTH, D), lambda j: (j, 0))

    low = jnp.bfloat16
    factor_specs = [fixed(*factor.shape) for factor in factors]
    outs = pl.pallas_call(
        feed_kernel,
        grid=(FF // FEED_WIDTH,),
        in_specs=[
            fixed(D, SEQ),
            fixed(D, D),
            fixed(SEQ, D),
            fixed(1, D),
            fixed(SEQ, D),
            *factor_specs,
            stripe(),
            stripe(),
        ],
        out_specs=[
            pl.BlockSpec((SEQ, FEED_WIDTH), lambda j: (0, j)),
            pl.BlockSpec((SEQ, FEED_WIDTH), lambda j: (0, j)),
            fixed(SEQ, D),
            fixed(SEQ, D),
            fixed(SEQ, D),
            fixed(SEQ, D),
            *factor_specs,
        ],
        out_shape=[
            jax.ShapeDtypeStruct((SEQ, FF), low),
            jax.ShapeDtypeStruct((SEQ, FF), low),
            jax.ShapeDtypeStruct((SEQ, D), low),
            jax.ShapeDtypeStruct((SEQ, D), low),
            jax.ShapeDtypeStruct((SEQ, D), low),
            jax.ShapeDtypeStruct((SEQ, D), low),
            *[jax.ShapeDtypeStruct(factor.shape, jnp.float32) for factor in factors],
        ],
        scratch_shapes=[pltpu.VMEM((SEQ, D), jnp.float32)] * 2,
        compiler_params=pltpu.CompilerParams(vmem_limit_bytes=VMEM_LIMIT),
        cost_estimate=pl.CostEstimate(
            flops=6 * SEQ * FF * D, bytes_accessed=32 * 1024 * 1024, transcendentals=2 * SEQ * FF
        ),
        name="feed",
    )(attended, w_out, tokens, gain[None, :], cotangent, *factors, w_in, w_down)
    return outs[:6], tuple(outs[6:])


def adamw(weights, grads, first, second, step):
    first_new = beta_first * first + (1.0 - beta_first) * grads
    second_new = beta_second * second + (1.0 - beta_second) * grads * grads
    first_hat = first_new / (1.0 - beta_first**step)
    second_hat = second_new / (1.0 - beta_second**step)
    weights_new = weights - rate_per_step * step * (
        first_hat / (jnp.sqrt(second_hat) + adam_epsilon) + weight_decay * weights
    )
    return (weights_new, first_new, second_new)


def per_device(
    tokens,
    cotangent,
    segment_ids,
    buckets,
    owners,
    master,
    first_moment,
    second_moment,
    small_params,
    small_first,
    small_second,
    adapter_ema,
    step_count,
):
    dp_count = lax.axis_size("dp")
    tensor_count = lax.axis_size("tensor")
    capacity = master.shape[1]
    group_heads = H // tensor_count
    head_rows = group_heads * HS
    hidden_rows = FF // tensor_count
    tensor_pos = lax.axis_index("tensor")
    sizes = [3 * head_rows, head_rows, hidden_rows, hidden_rows]
    local_sizes = [-(-size // dp_count // 16) * 16 for size in sizes]
    pair_rows = -(-((capacity + len(sizes) * (dp_count - 1)) // dp_count) // 16) * 16
    slot_place, spread_place, orders, places = plan(
        owners, sizes, local_sizes, capacity, pair_rows
    )

    gain_one, gain_two, adapter, table = unpack(small_params)
    table_rows = jnp.pad(table.T, ((0, 16 - H), (0, 0)))
    bucket_place = jnp.concatenate([jnp.full((1,), -1, jnp.int32), buckets[::-1]])[None, :]
    segments = lax.dynamic_slice_in_dim(segment_ids, tensor_pos * SEQ, SEQ, 0)
    w_qkv, w_out, w_in, w_down, projected, attended, scale, normed_one, exp_scores = front(
        master[0],
        slot_place,
        spread_place,
        orders,
        local_sizes,
        tokens,
        gain_one,
        table_rows,
        bucket_place,
        segments,
    )
    w_out, w_in, w_down = [part.reshape(-1, D) for part in (w_out, w_in, w_down)]
    factors, factors_pull = jax.vjp(adapter_factors, adapter)
    (activ, slope, normed_two, mid, layer_out, ffn_grad), factor_grads = feed(
        attended, w_out, tokens, gain_two, cotangent, factors, w_in, w_down
    )
    (adapter_grad,) = factors_pull(factor_grads)
    small_local = jnp.concatenate(
        [jnp.zeros((2 * D,), jnp.float32)]
        + [piece.reshape(-1) for piece in adapter_grad]
        + [jnp.zeros((TABLE_ROW * TILE - 2 * D - NADAPT,), jnp.float32)]
    ).reshape(TABLE_ROW, TILE)
    owned_grad, input_grad, small_total = back(
        (
            ffn_grad,
            normed_two,
            mid,
            cotangent,
            w_out,
            activ,
            slope,
            w_in.reshape(tensor_count, hidden_rows, D),
            w_down.reshape(tensor_count, hidden_rows, D),
        ),
        projected,
        exp_scores,
        w_qkv,
        tokens,
        normed_one,
        attended,
        scale,
        gain_one,
        gain_two,
        small_local,
        bucket_place,
        places,
        local_sizes,
        spread_place,
        slot_place,
    )
    small_total = jnp.concatenate(
        [
            small_total[:TABLE_ROW].reshape(-1)[: 2 * D + NADAPT],
            small_total[TABLE_ROW : TABLE_ROW + H, :NB].T.reshape(-1),
        ]
    )
    own_filled = (slot_place[0] >= 0).astype(jnp.float32)[:, None]
    step = step_count[0].astype(jnp.float32)
    new_master, new_first, new_second = adamw(
        master[0], owned_grad, first_moment[0], second_moment[0], step
    )
    new_master = new_master * own_filled
    new_first = new_first * own_filled
    new_second = new_second * own_filled
    small_new, small_first_new, small_second_new = adamw(
        small_params, small_total, small_first, small_second, step
    )
    ema_new = average_keep * adapter_ema + (1.0 - average_keep) * small_new[2 * D : 2 * D + NADAPT]
    return (
        layer_out,
        input_grad,
        owned_grad[None],
        new_first[None],
        new_second[None],
        new_master[None],
        new_master.astype(jnp.bfloat16)[None],
        small_total,
        small_first_new,
        small_second_new,
        small_new,
        ema_new,
    )


def solution(mesh):
    token_spec = P(("dp", "tensor"), None)
    owner_spec = P("tensor", "dp", None)
    return jax.shard_map(
        per_device,
        mesh=mesh,
        in_specs=(token_spec, token_spec, P("dp"), P(), P())
        + (owner_spec,) * 3
        + (P(),) * 5,
        out_specs=(token_spec,) * 2 + (owner_spec,) * 5 + (P(),) * 5,
        check_vma=False,
    )
```

```python
import functools
import math

import jax
import jax.numpy as jnp
from jax import lax
from jax.experimental import pallas as pl
from jax.experimental.pallas import tpu as pltpu
from jax.sharding import PartitionSpec as P

D = 768
H = 12
HS = 64
FF = 3072
NB = 32
R = 48
PHM = 4
SEQ = 1024
NADAPT = 1696

highest = lax.Precision.HIGHEST
norm_epsilon = 1e-06
beta_first = 0.5
beta_second = 0.5
adam_epsilon = 1e-08
rate_per_step = 0.01
weight_decay = 0.1
average_keep = 0.75
masked_score = -1000000000.0

TILE = 128
WINDOW = 2 * SEQ - TILE
QUERY_TILE = 512
KEY_TILE = 512
BACK_QUERY_TILE = 512
BACK_KEY_TILE = 1024
VMEM_LIMIT = 48 * 1024 * 1024
MESH = pl.DeviceIdType.MESH


def unpack(packed):
    widths = (D, D, PHM**3, D, R, R, D, NB * H)
    pieces = []
    offset = 0
    for width in widths:
        pieces.append(packed[offset : offset + width])
        offset = offset + width
    mix_flat, down_left, down_right, up_left, up_right = pieces[2:7]
    adapter = (
        mix_flat.reshape(PHM, PHM, PHM),
        down_left.reshape(PHM, D // PHM),
        down_right.reshape(PHM, R // PHM),
        up_left.reshape(PHM, R // PHM),
        up_right.reshape(PHM, D // PHM),
    )
    return adapter


def adapter_factors(adapter):
    mix, down_left, down_right, up_left, up_right = adapter
    eye = jnp.eye(PHM, dtype=jnp.float32)
    left = mix.transpose(2, 0, 1)[:, None] * down_right.T[None, :, :, None]
    right = (eye[None, :, :, None] * down_left[:, None, None, :]).reshape(PHM * PHM, D)
    wide = mix.transpose(1, 0, 2)[:, None] * up_left.T[None, :, :, None]
    tall = (eye[None, :, :, None] * up_right[:, None, None, :]).reshape(PHM * PHM, D)
    return (left.reshape(R, PHM * PHM), right, wide.reshape(R, PHM * PHM), tall)


def normal_parts(values):
    size = jnp.abs(values)
    shrink = 1.0 / (1.0 + (0.3275911 * math.sqrt(0.5)) * size)
    bell = jnp.exp(-0.5 * values * values)
    series = 0.5 * 1.061405429
    for term in (-1.453152027, 1.421413741, -0.284496736, 0.254829592):
        series = series * shrink + 0.5 * term
    tail = series * shrink * bell
    return jnp.where(values >= 0.0, 1.0 - tail, tail), bell * (1.0 / math.sqrt(2.0 * math.pi))


def contract(left, right, left_dim, right_dim):
    return lax.dot_general(
        left,
        right,
        (((left_dim,), (right_dim,)), ((), ())),
        preferred_element_type=jnp.float32,
    )


def bias_window(bias, window):
    for tile in range(WINDOW // TILE):
        base = WINDOW - TILE * tile
        row = jnp.broadcast_to(bias[:, base - TILE : base + TILE], (TILE, 2 * TILE))
        rolled = pltpu.roll(row, TILE, 1, stride=1, stride_axis=0)
        window[TILE * tile : TILE * (tile + 1), :] = rolled[:, :TILE]


def attend_head(
    query_rows, key_rows, value_rows, segment_keys_ref, segment_queries_ref, window, scores, exp_ref
):
    keys = key_rows.T
    values = jnp.concatenate([value_rows, jnp.ones((16, SEQ), jnp.bfloat16)], axis=0)
    outs, scales = [], []
    for q0 in range(0, SEQ, QUERY_TILE):
        queries = query_rows[:, q0 : q0 + QUERY_TILE]
        peak = jnp.full((8, QUERY_TILE), -jnp.inf, jnp.float32)
        for k0 in range(0, SEQ, KEY_TILE):
            raw = jnp.dot(keys[k0 : k0 + KEY_TILE], queries, preferred_element_type=jnp.float32)
            parts = []
            for l0 in range(0, QUERY_TILE, TILE):
                start = SEQ - TILE - (q0 + l0) + k0
                same_doc = (
                    segment_keys_ref[k0 : k0 + KEY_TILE, :]
                    == segment_queries_ref[:, q0 + l0 : q0 + l0 + TILE]
                )
                part = jnp.where(
                    same_doc,
                    raw[:, l0 : l0 + TILE] + window[start : start + KEY_TILE, :],
                    masked_score,
                )
                scores[k0 : k0 + KEY_TILE, l0 : l0 + TILE] = part
                parts.append(part)
            whole = jnp.concatenate(parts, axis=1)
            peak = jnp.maximum(peak, jnp.max(whole.reshape(KEY_TILE // 8, 8, QUERY_TILE), axis=0))
        peak = jnp.max(peak, axis=0, keepdims=True)
        total = jnp.zeros((HS + 16, QUERY_TILE), jnp.float32)
        for k0 in range(0, SEQ, KEY_TILE):
            exp_scores = jnp.exp(scores[k0 : k0 + KEY_TILE, :] - peak).astype(jnp.bfloat16)
            exp_ref[k0 : k0 + KEY_TILE, q0 : q0 + QUERY_TILE] = exp_scores
            total = total + jnp.dot(
                values[:, k0 : k0 + KEY_TILE], exp_scores, preferred_element_type=jnp.float32
            )
        scale = 1.0 / total[HS : HS + 1]
        scales.append(scale)
        outs.append((total[:HS] * scale).astype(jnp.bfloat16))
    return jnp.concatenate(outs, axis=1), jnp.concatenate(scales, axis=1)


def one_hot(place, shape, dim):
    hit = lax.broadcasted_iota(jnp.int32, shape, dim) == place
    return jnp.where(hit, 1.0, 0.0).astype(jnp.bfloat16)


def plan_kernel(dp_count, pair_rows, local_sizes, *refs):
    roles = len(local_sizes)
    owners_ref, slot_ref, spread_ref = refs[:3]
    order_refs, place_refs = refs[3 : roles + 3], refs[roles + 3 :]
    dp_pos = lax.axis_index("dp").astype(jnp.float32)

    def quotient(values):
        return jnp.floor((values + 0.5) * (1.0 / dp_count))

    def remainder(values):
        return values - dp_count * quotient(values)

    line = dp_count // 2

    def halve(values):
        return jnp.floor((values + 0.5) * 0.5)

    def around(values):
        return values - line * jnp.floor((values + 0.5) * (1.0 / line))

    whole = owners_ref[...].astype(jnp.float32)
    owners, low = [], 0
    for ref in order_refs:
        owners.append(whole[:, low : low + ref.shape[1]])
        low += ref.shape[1]

    def stats(who):
        counts = [
            jnp.sum(jnp.where(row == who, 1.0, 0.0), axis=1, keepdims=True) for row in owners
        ]
        starts = [jnp.sum(jnp.where(row < who, 1.0, 0.0), axis=1, keepdims=True) for row in owners]
        return counts, starts

    def hits(first, number, target):
        return quotient(first + number - 1.0 - target) - quotient(first - 1.0 - target)

    counts, starts = stats(jnp.full((1, 1), dp_pos))
    slot = lax.broadcasted_iota(jnp.int32, slot_ref.shape, 1).astype(jnp.float32)
    found = jnp.full(slot_ref.shape, -1.0)
    low = jnp.zeros((1, 1), jnp.float32)
    for role in range(roles):
        rank = slot - low
        target = remainder(starts[role] + rank)
        place = quotient(rank)
        for other in range(role):
            place = place + hits(starts[other], counts[other], target)
        found = jnp.where(
            (rank >= 0.0) & (rank < counts[role]),
            remainder(target - dp_pos) * pair_rows + place,
            found,
        )
        low = low + counts[role]
    slot_ref[...] = found.astype(jnp.int32)

    column = lax.broadcasted_iota(jnp.int32, (dp_count, 1), 0).astype(jnp.float32)
    counts, starts = stats(remainder(dp_pos - column))
    pair = lax.broadcasted_iota(jnp.int32, spread_ref.shape, 1).astype(jnp.float32)
    found = jnp.full(spread_ref.shape, -1.0)
    passed = jnp.zeros((dp_count, 1), jnp.float32)
    for role in range(roles):
        number = hits(starts[role], counts[role], dp_pos)
        first = starts[role] + remainder(dp_pos - starts[role])
        rank = pair - passed
        local = sum(local_sizes[:role]) + quotient(first) + rank
        found = jnp.where((rank >= 0.0) & (rank < number), local, found)
        passed = passed + number
    spread_ref[...] = found.astype(jnp.int32)

    counts, starts = stats(column)
    for role in range(roles):
        width = owners[role].shape[1]
        before = starts[role]
        for c0 in range(0, width, TILE):
            c1 = min(c0 + TILE, width)
            hot = jnp.where(owners[role][:, c0:c1] == column, 1.0, 0.0)
            shape = (c1 - c0, c1 - c0)
            above = lax.broadcasted_iota(jnp.int32, shape, 0) < lax.broadcasted_iota(
                jnp.int32, shape, 1
            )
            rank = jnp.dot(
                hot.astype(jnp.bfloat16),
                jnp.where(above, 1.0, 0.0).astype(jnp.bfloat16),
                preferred_element_type=jnp.float32,
            )
            number = jnp.sum(hot * (rank + before), axis=0, keepdims=True)
            before = before + jnp.sum(hot, axis=1, keepdims=True)
            target, row = remainder(number), quotient(number)
            side = jnp.abs(target - 2.0 * halve(target) - dp_pos + 2.0 * halve(dp_pos)) * line
            ahead = halve(target) - halve(dp_pos)
            order = (around(0.0 - ahead) + side) * local_sizes[role] + row
            place = (around(ahead) + side) * local_sizes[role] + row
            order_refs[role][:, c0:c1] = order.astype(jnp.int32)
            place_refs[role][:, c0:c1] = place.astype(jnp.int32)


def plan(owners, sizes, local_sizes, capacity, pair_rows):
    dp_count = lax.axis_size("dp")
    outs = pl.pallas_call(
        functools.partial(plan_kernel, dp_count, pair_rows, local_sizes),
        out_shape=[
            jax.ShapeDtypeStruct((1, capacity), jnp.int32),
            jax.ShapeDtypeStruct((dp_count, pair_rows), jnp.int32),
        ]
        + [jax.ShapeDtypeStruct((1, size), jnp.int32) for size in sizes] * 2,
        name="plan",
    )(owners[None, :])
    return outs[0], outs[1], outs[2 : 2 + len(sizes)], outs[2 + len(sizes) :]


def true_group(positions, group, tensor_count):
    flips = positions + (tensor_count - 1 - positions[0],)
    found = flips[0]
    for g in range(1, tensor_count):
        found = found + (flips[g] - flips[0]) * (
            lax.div(group + tensor_count - g, tensor_count)
            - lax.div(group + tensor_count - g - 1, tensor_count)
        )
    return found


def front_kernel(
    sizes,
    mine_ref,
    slot_place_ref,
    spread_place_ref,
    order_qkv_ref,
    order_out_ref,
    order_in_ref,
    order_down_ref,
    tokens_ref,
    small_ref,
    bucket_ref,
    segment_ref,
    cotangent_ref,
    left_ref,
    right_ref,
    wide_ref,
    tall_ref,
    w_qkv_out,
    w_out_ref,
    w_in_ref,
    w_down_ref,
    projected_out,
    attended_ref,
    scale_ref,
    normed_ref,
    exp_ref,
    activ_ref,
    slope_ref,
    normed_two_ref,
    mid_ref,
    layer_out_ref,
    ffn_grad_ref,
    left_grad_ref,
    right_grad_ref,
    wide_grad_ref,
    tall_grad_ref,
    w_qkv_ref,
    projected_ref,
    feed_weights,
    ffn_out,
    mid_rows,
    sent,
    received,
    spread,
    bias,
    segment_keys,
    buf_qkv,
    buf_out,
    buf_in,
    buf_down,
    buf_far,
    far_spread,
    stage_out,
    stage_in,
    stage_down,
    stage_far,
    window,
    scores,
    exp_stage,
    deal_send,
    deal_recv,
    far_send,
    far_recv,
    line_send,
    line_recv,
    side_send,
    side_recv,
    group_send,
    group_recv,
    local_sem,
    exp_sem,
    save_sem,
    feed_sem,
    out_sem,
):
    dp_count, pair_rows = sent.shape[0], sent.shape[1]
    tensor_count = w_qkv_ref.shape[0]
    heads = scale_ref.shape[0]
    low = jnp.bfloat16
    group_heads = heads // tensor_count
    head_rows = group_heads * HS
    dp_pos, tensor_pos = lax.axis_index("dp"), lax.axis_index("tensor")
    core_pos = tensor_pos + 1 - 2 * lax.rem(tensor_pos, 2)
    far_pos = lax.rem(tensor_pos + 2, tensor_count)
    core_peer, far_peer = (dp_pos, core_pos), (dp_pos, far_pos)

    def dp_peer(m):
        return (lax.rem(dp_pos + m, dp_count), tensor_pos)

    def each_peer(run):
        def step(m, carry):
            run(m)
            return carry

        lax.fori_loop(1, dp_count, step, 0)

    barrier = pltpu.get_barrier_semaphore()

    def greet(m):
        pl.semaphore_signal(barrier, inc=1, device_id=dp_peer(m), device_id_type=MESH)

    each_peer(greet)
    for peer in (core_peer, far_peer):
        pl.semaphore_signal(barrier, inc=1, device_id=peer, device_id_type=MESH)

    mine = mine_ref[...].astype(jnp.bfloat16)
    hot = one_hot(slot_place_ref[...], (dp_count * pair_rows, mine.shape[0]), 0)
    sent[...] = (
        jnp.dot(hot, mine, preferred_element_type=jnp.float32)
        .astype(jnp.bfloat16)
        .reshape(dp_count, pair_rows, D)
    )
    pl.semaphore_wait(barrier, dp_count + 1)

    def deal(m):
        return pltpu.make_async_remote_copy(
            sent.at[m],
            received.at[m],
            deal_send.at[m],
            deal_recv.at[m],
            device_id=dp_peer(m),
            device_id_type=MESH,
        )

    each_peer(lambda m: deal(m).start())
    received[0] = sent[0]

    for r0 in range(0, SEQ, 128):
        values = tokens_ref[r0 : r0 + 128, :].astype(jnp.float32)
        inverse = lax.rsqrt(jnp.mean(values * values, axis=1, keepdims=True) + norm_epsilon)
        normed_ref[r0 : r0 + 128, :] = (values * inverse * small_ref[:, 0:D]).astype(jnp.bfloat16)
    flat = small_ref[...][:, 2 * D + NADAPT :]
    entry = lax.broadcasted_iota(jnp.int32, (16, NB * H), 1)
    bucket = jnp.floor((entry.astype(jnp.float32) + 0.5) * (1.0 / H))
    head_of = entry.astype(jnp.float32) - H * bucket
    line_of = lax.broadcasted_iota(jnp.int32, (16, NB * H), 0).astype(jnp.float32)
    rest = jnp.where(head_of == line_of, jnp.broadcast_to(flat, (16, NB * H)), 0.0)
    entry = lax.broadcasted_iota(jnp.int32, (NB * H, 2 * SEQ), 0).astype(jnp.float32)
    bucket = jnp.floor((entry + 0.5) * (1.0 / H))
    hot = jnp.where(bucket == bucket_ref[...].astype(jnp.float32), 1.0, 0.0).astype(jnp.bfloat16)
    biases = jnp.zeros((rest.shape[0], 2 * SEQ), jnp.float32)
    for _ in range(3):
        part = rest.astype(jnp.bfloat16)
        rest = rest - part.astype(jnp.float32)
        biases = biases + jnp.dot(part, hot, preferred_element_type=jnp.float32)
    for head in range(heads):
        bias[head] = biases[head : head + 1, :]
    segment_keys[...] = jnp.broadcast_to(segment_ref[...], (TILE, SEQ)).T

    each_peer(lambda m: deal(m).wait())
    rows = spread.shape[0]
    place = jnp.concatenate([spread_place_ref[m : m + 1, :] for m in range(dp_count)], axis=1)
    hot = one_hot(place, (rows, dp_count * pair_rows), 0)
    spread[...] = jnp.dot(
        hot, received[...].reshape(dp_count * pair_rows, D), preferred_element_type=jnp.float32
    ).astype(jnp.bfloat16)

    bufs = (buf_qkv, buf_out, buf_in, buf_down, buf_far)
    orders = (order_qkv_ref, order_out_ref, order_in_ref, order_down_ref, order_down_ref)
    stages = (w_qkv_ref.at[0], stage_out, stage_in, stage_down, stage_far)
    finals = (w_qkv_ref, w_out_ref, w_in_ref, w_down_ref, w_down_ref)
    sizes = tuple(sizes) + (sizes[3],)
    offsets = [sum(buf.shape[1] for buf in bufs[:role]) for role in range(4)]
    line = dp_count // 2
    line_pos, side = lax.div(dp_pos, 2), lax.rem(dp_pos, 2)
    side_peer = (dp_pos + 1 - 2 * side, tensor_pos)

    def far_exchange():
        return pltpu.make_async_remote_copy(
            spread.at[pl.ds(offsets[3], far_spread.shape[0])],
            far_spread,
            far_send,
            far_recv,
            device_id=far_peer,
            device_id_type=MESH,
        )

    def block(role):
        if role == 4:
            return far_spread
        return spread.at[pl.ds(offsets[role], bufs[role].shape[1])]

    def along_line(role, m):
        return pltpu.make_async_remote_copy(
            block(role),
            bufs[role].at[m],
            line_send.at[role, m],
            line_recv.at[role, m],
            device_id=(lax.rem(line_pos + m, line) * 2 + side, tensor_pos),
            device_id_type=MESH,
        )

    def to_side(role, m):
        return pltpu.make_async_remote_copy(
            bufs[role].at[m],
            bufs[role].at[line + m],
            side_send.at[role, m],
            side_recv.at[role, m],
            device_id=side_peer,
            device_id_type=MESH,
        )

    def each_line(first, run):
        def step(m, carry):
            run(m)
            return carry

        lax.fori_loop(first, line, step, 0)

    def start_line(role):
        if role == 4:
            far_exchange().wait()
        each_line(1, lambda m: along_line(role, m).start())
        bufs[role][0] = block(role)[...]
        to_side(role, 0).start()

    def start_side(role):
        def step(m):
            along_line(role, m).wait()
            to_side(role, m).start()

        each_line(1, step)

    def order(role):
        each_line(0, lambda m: to_side(role, m).wait())
        count = bufs[role].shape[1]
        source = bufs[role][...].reshape(dp_count * count, D)
        step = 384 if sizes[role] > 576 else sizes[role]
        for r0 in range(0, sizes[role], step):
            r1 = min(r0 + step, sizes[role])
            hot = one_hot(orders[role][:, r0:r1], (dp_count * count, r1 - r0), 0)
            stages[role][r0:r1, :] = contract(hot, source, 0, 0).astype(jnp.bfloat16)

    def share(role, part):
        if role == 4:
            src, slot, peer = stages[role], 3, core_peer
        else:
            src, slot, peer = (
                (stages[role], 1, core_peer),
                (stages[role], 2, far_peer),
                (finals[role].at[2], 3, core_peer),
            )[part]
        return pltpu.make_async_remote_copy(
            src,
            finals[role].at[slot],
            group_send.at[role, part],
            group_recv.at[role, part],
            device_id=peer,
            device_id_type=MESH,
        )

    def keep(role):
        slot = 2 if role == 4 else 0
        return pltpu.make_async_copy(stages[role], finals[role].at[slot], local_sem.at[role])

    def start_share(role):
        order(role)
        share(role, 0).start()
        if role < 3:
            share(role, 1).start()
        if role > 0:
            keep(role).start()

    def forward(role):
        share(role, 1).wait_recv()
        share(role, 2).start()

    far_exchange().start()
    start_line(0)
    start_side(0)
    start_share(0)
    start_line(1)
    start_line(2)

    def save_group(which, group):
        source, target = ((projected_ref, projected_out), (w_qkv_ref, w_qkv_out))[which]
        return pltpu.make_async_copy(
            source.at[group], target.at[group], save_sem.at[which, group]
        )

    def true_head(group, head):
        return true_group((tensor_pos, core_pos, far_pos), group, tensor_count) * group_heads + head

    def head_step(i, carry):
        group, head = lax.div(i, group_heads), lax.rem(i, group_heads)

        @pl.when(i == 1)
        def _():
            start_side(1)

        @pl.when(i == 3)
        def _():
            start_share(1)

        @pl.when(i == 5)
        def _():
            start_side(2)
            start_line(3)
            start_line(4)

        @pl.when(i == 10)
        def _():
            start_share(2)

        @pl.when(i == group_heads)
        def _():
            share(0, 0).wait_recv()

        @pl.when(i == 2 * group_heads)
        def _():
            forward(0)

        @pl.when(i == 3 * group_heads)
        def _():
            share(0, 2).wait_recv()
            forward(1)

        @pl.when(i == 11)
        def _():
            start_side(3)

        @pl.when(head == 0)
        def _():
            projected_ref[group] = contract(w_qkv_ref[group], normed_ref[...], 1, 1).astype(
                jnp.bfloat16
            )
            save_group(0, group).start()
            save_group(1, group).start()

        def head_part(part):
            start = pl.multiple_of(part * head_rows + head * HS, HS)
            return projected_ref[group, pl.ds(start, HS), :]

        slot = lax.rem(i, 2)

        def save(head_index, slot):
            return pltpu.make_async_copy(
                exp_stage.at[slot], exp_ref.at[head_index], exp_sem.at[slot]
            )

        @pl.when(i >= 2)
        def _():
            save(i - 2, slot).wait()

        bias_window(bias[true_head(group, head)], window)
        attended, scale = attend_head(
            head_part(0),
            head_part(1),
            head_part(2),
            segment_keys,
            segment_ref,
            window,
            scores,
            exp_stage.at[slot],
        )
        attended_ref[pl.ds(pl.multiple_of(i * HS, HS), HS), :] = attended
        scale_ref[i] = scale
        save(i, slot).start()
        return carry

    lax.fori_loop(0, heads, head_step, 0)
    for i in (heads - 2, heads - 1):
        pltpu.make_async_copy(exp_stage.at[i % 2], exp_ref.at[i], exp_sem.at[i % 2]).wait()
    start_side(4)
    start_share(3)
    start_share(4)
    forward(2)

    def load_feed(group, slot, which):
        return pltpu.make_async_copy(
            (w_in_ref, w_down_ref)[which].at[group],
            feed_weights.at[slot, which],
            feed_sem.at[slot, which],
        )

    def load_out(group):
        return pltpu.make_async_copy(
            w_out_ref.at[group],
            feed_weights.at[1, 0, pl.ds(group * head_rows, head_rows)],
            out_sem.at[group],
        )

    keep(1).wait()
    share(1, 0).wait_recv()
    share(1, 2).wait_recv()
    for group in range(tensor_count):
        load_out(group).start()
    keep(2).wait()
    keep(3).wait()
    load_feed(0, 0, 0).start()
    load_feed(0, 0, 1).start()
    for group in range(tensor_count):
        load_out(group).wait()
    tiles = [slice(r0, r0 + 256) for r0 in range(0, SEQ, 256)]
    for rows in tiles:
        attn = jnp.dot(
            attended_ref[:, rows].T, feed_weights[1, 0], preferred_element_type=jnp.float32
        )
        mid = tokens_ref[rows, :].astype(jnp.float32) + attn
        mid_rows[rows, :] = mid
        mid_ref[rows, :] = mid.astype(low)
        inverse = lax.rsqrt(jnp.mean(mid * mid, axis=1, keepdims=True) + norm_epsilon)
        normed_two_ref[rows, :] = (mid * inverse * small_ref[:, D : 2 * D]).astype(low)
        ffn_out[rows, :] = jnp.zeros((256, D), jnp.float32)
    hidden_rows = w_in_ref.shape[1]

    def save_feed(group, which):
        columns = pl.ds(pl.multiple_of(group * hidden_rows, TILE), hidden_rows)
        return pltpu.make_async_copy(
            exp_stage.at[which, :, pl.ds(0, hidden_rows)],
            (activ_ref, slope_ref)[which].at[:, columns],
            exp_sem.at[which],
        )

    def feed_step(group, carry):
        slot = lax.rem(group, 2)
        for which in range(2):
            load_feed(group, slot, which).wait()

        @pl.when(group == 0)
        def _():
            share(2, 0).wait_recv()
            share(3, 0).wait_recv()

        @pl.when(group == 1)
        def _():
            keep(4).wait()

        @pl.when(group == 2)
        def _():
            share(2, 2).wait_recv()
            share(4, 0).wait_recv()

        @pl.when(group + 1 < tensor_count)
        def _():
            for which in range(2):
                load_feed(group + 1, 1 - slot, which).start()

        @pl.when(group > 0)
        def _():
            for which in range(2):
                save_feed(group - 1, which).wait()

        for rows in tiles:
            pre = contract(normed_two_ref[rows, :], feed_weights[slot, 0], 1, 1)
            cdf, density = normal_parts(pre)
            activ = (pre * cdf).astype(low)
            exp_stage[0, rows, 0:hidden_rows] = activ
            exp_stage[1, rows, 0:hidden_rows] = (cdf + pre * density).astype(low)
            ffn_out[rows, :] += jnp.dot(
                activ, feed_weights[slot, 1], preferred_element_type=jnp.float32
            )
        for which in range(2):
            save_feed(group, which).start()
        return carry

    lax.fori_loop(0, tensor_count, feed_step, 0)

    down = jnp.dot(
        left_ref[...], right_ref[...], precision=highest, preferred_element_type=jnp.float32
    ).astype(low)
    up = jnp.dot(
        wide_ref[...], tall_ref[...], precision=highest, preferred_element_type=jnp.float32
    ).astype(low)
    down_grad = jnp.zeros((R, D), jnp.float32)
    up_grad = jnp.zeros((R, D), jnp.float32)
    for rows in tiles:
        ffn = ffn_out[rows, :]
        ffn_low = ffn.astype(low)
        grad_low = cotangent_ref[rows, :]
        zed = contract(ffn_low, down, 1, 1)
        cdf, density = normal_parts(zed)
        hidden = (zed * cdf).astype(low)
        added = jnp.dot(hidden, up, preferred_element_type=jnp.float32)
        layer_out_ref[rows, :] = (mid_rows[rows, :] + ffn + added).astype(low)
        zed_grad = contract(grad_low, up, 1, 1) * (cdf + zed * density)
        zed_low = zed_grad.astype(low)
        ffn_grad_ref[rows, :] = (
            grad_low.astype(jnp.float32)
            + jnp.dot(zed_low, down, preferred_element_type=jnp.float32)
        ).astype(low)
        up_grad = up_grad + contract(hidden, grad_low, 0, 0)
        down_grad = down_grad + contract(zed_low, ffn_low, 0, 0)

    def exact(left, right, left_dim, right_dim):
        return lax.dot_general(
            left,
            right,
            (((left_dim,), (right_dim,)), ((), ())),
            precision=highest,
            preferred_element_type=jnp.float32,
        )

    left_grad_ref[...] = exact(down_grad, right_ref[...], 1, 1)
    right_grad_ref[...] = exact(left_ref[...], down_grad, 0, 0)
    wide_grad_ref[...] = exact(up_grad, tall_ref[...], 1, 1)
    tall_grad_ref[...] = exact(wide_ref[...], up_grad, 0, 0)

    for which in range(2):
        save_feed(tensor_count - 1, which).wait()
        for group in range(tensor_count):
            save_group(which, group).wait()
    for role in range(len(bufs)):
        share(role, 0).wait_send()
        if role < 3:
            share(role, 1).wait_send()
            share(role, 2).wait_send()


def front(
    mine,
    slot_place,
    spread_place,
    orders,
    local_sizes,
    tokens,
    small_row,
    bucket_place,
    segments,
    cotangent,
    factors,
):
    dp_count, tensor_count = lax.axis_size("dp"), lax.axis_size("tensor")
    sizes = [order.shape[1] for order in orders]
    pair_rows = spread_place.shape[1]
    low = jnp.bfloat16
    dma = pltpu.SemaphoreType.DMA
    roles = len(sizes)
    whole = pl.BlockSpec(memory_space=pltpu.VMEM)
    away = pl.BlockSpec(memory_space=pl.ANY)
    return pl.pallas_call(
        functools.partial(front_kernel, sizes),
        in_specs=[whole] * 16,
        out_specs=[away] * 5 + [whole] * 3 + [away] * 3 + [whole] * 8,
        out_shape=[jax.ShapeDtypeStruct((tensor_count, size, D), low) for size in sizes]
        + [
            jax.ShapeDtypeStruct((tensor_count, sizes[0], SEQ), low),
            jax.ShapeDtypeStruct((H * HS, SEQ), low),
            jax.ShapeDtypeStruct((H, 1, SEQ), jnp.float32),
            jax.ShapeDtypeStruct((SEQ, D), low),
            jax.ShapeDtypeStruct((H, SEQ, SEQ), low),
            jax.ShapeDtypeStruct((SEQ, FF), low),
            jax.ShapeDtypeStruct((SEQ, FF), low),
        ]
        + [jax.ShapeDtypeStruct((SEQ, D), low)] * 4
        + [jax.ShapeDtypeStruct(factor.shape, jnp.float32) for factor in factors],
        scratch_shapes=[
            pltpu.VMEM((tensor_count, sizes[0], D), low),
            pltpu.VMEM((tensor_count, sizes[0], SEQ), low),
            pltpu.VMEM((2, 2, sizes[2], D), low),
            pltpu.VMEM((SEQ, D), jnp.float32),
            pltpu.VMEM((SEQ, D), jnp.float32),
            pltpu.VMEM((dp_count, pair_rows, D), low),
            pltpu.VMEM((dp_count, pair_rows, D), low),
            pltpu.VMEM((sum(local_sizes), D), low),
            pltpu.VMEM((H, 1, 2 * SEQ), jnp.float32),
            pltpu.VMEM((SEQ, TILE), jnp.float32),
        ]
        + [pltpu.VMEM((dp_count, size, D), low) for size in local_sizes + local_sizes[3:]]
        + [pltpu.VMEM((local_sizes[3], D), low)]
        + [pltpu.VMEM((size, D), low) for size in sizes[1:] + sizes[3:]]
        + [
            pltpu.VMEM((WINDOW, TILE), jnp.float32),
            pltpu.VMEM((SEQ, QUERY_TILE), jnp.float32),
            pltpu.VMEM((2, SEQ, SEQ), low),
            dma((dp_count,)),
            dma((dp_count,)),
            dma,
            dma,
            dma((roles + 1, dp_count // 2)),
            dma((roles + 1, dp_count // 2)),
            dma((roles + 1, dp_count // 2)),
            dma((roles + 1, dp_count // 2)),
            dma((roles + 1, 3)),
            dma((roles + 1, 3)),
            dma((roles + 1,)),
            dma((2,)),
            dma((2, tensor_count)),
            dma((2, 2)),
            dma((tensor_count,)),
        ],
        compiler_params=pltpu.CompilerParams(
            collective_id=1, has_side_effects=True, vmem_limit_bytes=63 * 1024 * 1024
        ),
        cost_estimate=pl.CostEstimate(
            flops=10 * H * SEQ * SEQ * 256 + 4 * SEQ * FF * D,
            bytes_accessed=96 * 1024 * 1024,
            transcendentals=H * SEQ * SEQ + 2 * SEQ * FF,
        ),
        name="front",
    )(
        mine,
        slot_place,
        spread_place,
        *orders,
        tokens,
        small_row,
        bucket_place,
        segments.astype(jnp.float32)[None, :],
        cotangent,
        *factors,
    )


def attend_head_back(
    query_rows,
    key_rows,
    value_rows,
    exp_ref,
    attended,
    scale,
    attended_grad,
    window,
    score_grads,
    store,
):
    scaled = attended_grad.astype(jnp.float32) * scale
    delta = jnp.sum(scaled * attended.astype(jnp.float32), axis=0, keepdims=True)
    scaled_low = scaled.astype(jnp.bfloat16)
    delta_high = delta.astype(jnp.bfloat16).astype(jnp.float32)
    delta_rest = delta - delta_high
    place = lax.broadcasted_iota(jnp.int32, (16, SEQ), 0)
    extra = jnp.where(
        place == 0,
        jnp.broadcast_to(-delta_high, (16, SEQ)),
        jnp.where(place == 1, jnp.broadcast_to(-delta_rest, (16, SEQ)), 0.0),
    ).astype(jnp.bfloat16)
    grads = jnp.concatenate([scaled_low, extra], axis=0)
    values = jnp.concatenate([value_rows, jnp.ones((16, SEQ), jnp.bfloat16)], axis=0).T
    window[...] = jnp.zeros_like(window)
    for q0 in range(0, SEQ, BACK_QUERY_TILE):
        total = jnp.zeros((HS, BACK_QUERY_TILE), jnp.float32)
        for k0 in range(0, SEQ, BACK_KEY_TILE):
            centered = jnp.dot(
                values[k0 : k0 + BACK_KEY_TILE],
                grads[:, q0 : q0 + BACK_QUERY_TILE],
                preferred_element_type=jnp.float32,
            )
            score_grad = centered * exp_ref[
                k0 : k0 + BACK_KEY_TILE, q0 : q0 + BACK_QUERY_TILE
            ].astype(jnp.float32)
            for l0 in range(0, BACK_QUERY_TILE, TILE):
                start = SEQ - TILE - (q0 + l0) + k0
                window[start : start + BACK_KEY_TILE, :] += score_grad[:, l0 : l0 + TILE]
            score_low = score_grad.astype(jnp.bfloat16)
            score_grads[k0 : k0 + BACK_KEY_TILE, q0 : q0 + BACK_QUERY_TILE] = score_low
            total = total + jnp.dot(
                key_rows[:, k0 : k0 + BACK_KEY_TILE], score_low, preferred_element_type=jnp.float32
            )
        store(0, q0, total.astype(jnp.bfloat16))
    queries = query_rows.T
    scaled_rows = scaled_low.T
    for k0 in range(0, SEQ, BACK_KEY_TILE):
        key_grad = jnp.dot(
            score_grads[k0 : k0 + BACK_KEY_TILE, :], queries, preferred_element_type=jnp.float32
        )
        value_grad = jnp.dot(
            exp_ref[k0 : k0 + BACK_KEY_TILE, :], scaled_rows, preferred_element_type=jnp.float32
        )
        store(1, k0, key_grad.T.astype(jnp.bfloat16))
        store(2, k0, value_grad.T.astype(jnp.bfloat16))
    pieces = [jnp.zeros((1, TILE), jnp.float32)] * (2 * SEQ // TILE)
    for tile in range(WINDOW // TILE):
        base = WINDOW - TILE * tile
        block = window[TILE * tile : TILE * (tile + 1), :]
        folded = jnp.concatenate([jnp.zeros((TILE, TILE), jnp.float32), block], axis=1)
        rows = TILE // 2
        while rows >= 1:
            folded = folded[:rows] + pltpu.roll(folded[rows:], 2 * TILE - rows, 1)
            rows //= 2
        pieces[base // TILE - 1] += folded[:, :TILE]
        pieces[base // TILE] += folded[:, TILE:]
    return jnp.concatenate(pieces, axis=1)


SMALL_ROWS = 48
TABLE_ROW = 32


def back_kernel(
    sizes,
    ffn_grad_ref,
    normed_two_ref,
    mid_ref,
    cotangent_ref,
    w_out_ref,
    activ_ref,
    slope_ref,
    w_in_ref,
    w_down_ref,
    projected_ref,
    exp_ref,
    w_qkv_ref,
    tokens_ref,
    normed_one_ref,
    attended_ref,
    scale_ref,
    params_ref,
    small_ref,
    bucket_ref,
    place_qkv_ref,
    place_out_ref,
    place_in_ref,
    place_down_ref,
    spread_place_ref,
    slot_place_ref,
    owned_ref,
    input_grad_ref,
    small_total_ref,
    proj_grad_ref,
    bucket_hot,
    weights,
    proj,
    proj_grad,
    normed_grad,
    window,
    score_grads,
    exp_stage,
    row_grads,
    normed,
    attended_grad,
    odd_out,
    odd_in,
    odd_down,
    zero_qkv,
    zero_out,
    zero_in,
    zero_down,
    two_qkv,
    two_out,
    two_in,
    two_down,
    core_one_qkv,
    core_one_out,
    core_one_in,
    core_one_down,
    core_three_qkv,
    core_three_out,
    core_three_in,
    core_three_down,
    far_qkv,
    far_out,
    far_in,
    far_down,
    got_qkv,
    got_out,
    got_in,
    got_down,
    side_qkv,
    side_out,
    side_down,
    end_mine,
    end_far,
    spread,
    sent,
    received,
    small_own,
    small_tensor,
    small_dp,
    core_send,
    core_recv,
    far_send,
    far_recv,
    side_send,
    side_recv,
    line_send,
    line_recv,
    end_send,
    end_recv,
    back_send,
    back_recv,
    small_send,
    small_recv,
    load_sem,
    exp_sem,
    proj_sem,
    again_sem,
):
    dp_count, pair_rows = spread_place_ref.shape
    hidden_rows = w_in_ref.shape[1]
    tensor_count = w_qkv_ref.shape[0]
    heads = scale_ref.shape[0]
    group_heads = heads // tensor_count
    head_rows = group_heads * HS
    dp_pos, tensor_pos = lax.axis_index("dp"), lax.axis_index("tensor")
    core_pos = tensor_pos + 1 - 2 * lax.rem(tensor_pos, 2)
    far_pos = lax.rem(tensor_pos + 2, tensor_count)
    core_peer, far_peer = (dp_pos, core_pos), (dp_pos, far_pos)
    zeros = (zero_qkv, zero_out, zero_in, zero_down)
    twos = (two_qkv, two_out, two_in, two_down)
    core_ones = (core_one_qkv, core_one_out, core_one_in, core_one_down)
    core_threes = (core_three_qkv, core_three_out, core_three_in, core_three_down)
    fars = (far_qkv, far_out, far_in, far_down)
    gots = (got_qkv, got_out, got_in, got_down)
    side_got = (side_qkv, side_out, far_in, side_down)
    places = (place_qkv_ref, place_out_ref, place_in_ref, place_down_ref)
    offsets = [sum(got.shape[1] for got in gots[:role]) for role in range(len(gots))]
    low = jnp.bfloat16

    def up(m):
        return lax.rem(dp_pos + m, dp_count)

    def down(m):
        return lax.rem(dp_pos + dp_count - m, dp_count)

    def each_peer(run):
        def step(m, carry):
            run(m)
            return carry

        lax.fori_loop(1, dp_count, step, 0)

    def tensor_peer(m):
        return (dp_pos, lax.rem(tensor_pos + m, tensor_count))

    barrier = pltpu.get_barrier_semaphore()

    def greet(m):
        pl.semaphore_signal(barrier, inc=1, device_id=(up(m), tensor_pos), device_id_type=MESH)

    each_peer(greet)
    for m in range(1, tensor_count):
        pl.semaphore_signal(barrier, inc=1, device_id=tensor_peer(m), device_id_type=MESH)

    def load_exp(head, slot):
        return pltpu.make_async_copy(exp_ref.at[head], exp_stage.at[slot], exp_sem.at[slot])

    def load_proj(group):
        return pltpu.make_async_copy(projected_ref.at[group], proj, proj_sem.at[0])

    def save_proj(group):
        return pltpu.make_async_copy(proj_grad, proj_grad_ref.at[group], proj_sem.at[1])

    def reload(group, which):
        odd = group % 2
        source, target = (
            (proj_grad_ref.at[group], proj if odd else proj_grad),
            (w_qkv_ref.at[group], zero_qkv if odd else weights),
        )[which]
        return pltpu.make_async_copy(source, target, again_sem.at[odd, which])

    def load(which, group=0):
        columns = pl.ds(pl.multiple_of(group * hidden_rows, TILE), hidden_rows)
        source, target = (
            (lambda: activ_ref.at[:, columns], lambda: exp_stage.at[0, :, pl.ds(0, hidden_rows)]),
            (lambda: slope_ref.at[:, columns], lambda: exp_stage.at[1, :, pl.ds(0, hidden_rows)]),
            (lambda: w_in_ref.at[group], lambda: received.at[pl.ds(0, hidden_rows)]),
            (lambda: w_down_ref.at[group], lambda: sent.at[pl.ds(0, hidden_rows)]),
            (lambda: ffn_grad_ref, lambda: row_grads),
            (lambda: normed_two_ref, lambda: normed),
            (lambda: mid_ref, lambda: exp_stage.at[0, :, pl.ds(0, D)]),
            (lambda: cotangent_ref, lambda: exp_stage.at[1, :, pl.ds(0, D)]),
            (lambda: w_out_ref, lambda: sent.at[pl.ds(0, D)]),
            (lambda: normed_one_ref, lambda: normed),
            (lambda: tokens_ref, lambda: exp_stage.at[0, :, pl.ds(0, D)]),
        )[which]
        return pltpu.make_async_copy(source(), target(), load_sem.at[which])

    def core_copy(role, which):
        half = which // 2
        if role == 0:
            src = (odd_in, odd_down)[half].at[pl.ds(0, sizes[0])]
        else:
            src = (None, odd_out.at[half], odd_in, odd_down)[role]
        target = (core_ones if which == 1 else core_threes)[role].at[pl.ds(0, sizes[role])]
        return pltpu.make_async_remote_copy(
            src,
            target,
            core_send.at[role, half],
            core_recv.at[role, half],
            device_id=core_peer,
            device_id_type=MESH,
        )

    def far_copy(role):
        return pltpu.make_async_remote_copy(
            twos[role],
            fars[role],
            far_send.at[role],
            far_recv.at[role],
            device_id=far_peer,
            device_id_type=MESH,
        )

    line = dp_count // 2
    line_pos, side = lax.div(dp_pos, 2), lax.rem(dp_pos, 2)
    side_peer = (dp_pos + 1 - 2 * side, tensor_pos)

    def each_line(run):
        def step(m, carry):
            run(m)
            return carry

        lax.fori_loop(1, line, step, 0)

    def leaving(role, far):
        return core_ones[role] if role == 2 and not far else core_threes[role]

    def side_copy(role, far=0):
        count = gots[role].shape[1] * line
        return pltpu.make_async_remote_copy(
            leaving(role, far).at[pl.ds(count, count)],
            side_got[role].at[pl.ds(count * far, count)],
            side_send.at[role, far],
            side_recv.at[role, far],
            device_id=side_peer,
            device_id_type=MESH,
        )

    def line_copy(role, m, far=0):
        count = gots[role].shape[1]
        return pltpu.make_async_remote_copy(
            leaving(role, far).at[pl.ds(pl.multiple_of(m * count, 16), count)],
            gots[role].at[far * line + m],
            line_send.at[role, far * line + m],
            line_recv.at[role, far * line + m],
            device_id=(lax.rem(line_pos + m, line) * 2 + side, tensor_pos),
            device_id_type=MESH,
        )

    def end_copy():
        return pltpu.make_async_remote_copy(
            end_mine, end_far, end_send, end_recv, device_id=far_peer, device_id_type=MESH
        )

    def send_far(role):
        core_copy(role, 3).wait_recv()
        count = twos[role].shape[0]
        twos[role][...] = (
            twos[role][...].astype(jnp.float32)
            + core_threes[role][0:count, :].astype(jnp.float32)
        ).astype(low)
        far_copy(role).start()

    def scatter(role, far, total):
        count = gots[role].shape[1]
        for r0 in range(0, dp_count * count, 384):
            r1 = min(r0 + 384, dp_count * count)
            hot = one_hot(places[role][...] - r0, (r1 - r0, sizes[role]), 0)
            leaving(role, far)[r0:r1, :] = jnp.dot(
                hot, total, preferred_element_type=jnp.float32
            ).astype(low)
        side_copy(role, far).start()

    def send_deal(role):
        core_copy(role, 1).wait_recv()
        far_copy(role).wait_recv()
        total = (
            zeros[role][...].astype(jnp.float32)
            + core_ones[role][...].astype(jnp.float32)
            + fars[role][...].astype(jnp.float32)
        ).astype(low)
        scatter(role, 0, total)

    def send_half(role, far):
        core_copy(role, 3 if far else 1).wait_recv()
        count = sizes[role]
        mine = (twos if far else zeros)[role][...].astype(jnp.float32)
        core = (core_threes if far else core_ones)[role][0:count, :].astype(jnp.float32)
        scatter(role, far, (mine + core).astype(low))

    def pass_line(role, far=0):
        side_copy(role, far).wait()
        count = gots[role].shape[1] * line
        leaving(role, far)[0:count, :] = (
            leaving(role, far)[0:count, :].astype(jnp.float32)
            + side_got[role][count * far : count * (far + 1), :].astype(jnp.float32)
        ).astype(low)
        each_line(lambda m: line_copy(role, m, far).start())

    def line_sum(role, far=0):
        each_line(lambda m: line_copy(role, m, far).wait())
        total = leaving(role, far)[0 : gots[role].shape[1], :].astype(jnp.float32)
        for m in range(1, line):
            total = total + gots[role][far * line + m].astype(jnp.float32)
        return total

    def finish_deal(role):
        count = gots[role].shape[1]
        spread[offsets[role] : offsets[role] + count, :] = line_sum(role).astype(low)

    def finish_far():
        end_mine[...] = line_sum(2, 1).astype(low)
        end_copy().start()

    def finish_near():
        total = line_sum(2)
        end_copy().wait()
        count = gots[2].shape[1]
        spread[offsets[2] : offsets[2] + count, :] = (
            total + end_far[...].astype(jnp.float32)
        ).astype(low)

    for which in (4, 5):
        load(which).start()
    for which in range(4):
        load(which, tensor_count - 1).start()
    bucket_hot[...] = one_hot(bucket_ref[...], (NB, 2 * SEQ), 0)
    normed_grad[...] = jnp.zeros_like(normed_grad)
    small_own[0:TABLE_ROW, :] = small_ref[...]
    small_own[TABLE_ROW:SMALL_ROWS, :] = jnp.zeros((SMALL_ROWS - TABLE_ROW, TILE), jnp.float32)
    pl.semaphore_wait(barrier, dp_count + tensor_count - 2)
    for which in (4, 5):
        load(which).wait()
    row_tiles = [slice(r0, r0 + 256) for r0 in range(0, SEQ, 256)]
    pre_grad = score_grads

    def feed_step(i, carry):
        group = tensor_count - 1 - i

        def load_next(which):
            @pl.when(group > 0)
            def _():
                load(which, group - 1).start()

        load(3, group).wait()
        load(1, group).wait()
        for rows in row_tiles:
            grad = contract(row_grads[rows, :], sent[0:hidden_rows, :], 1, 1)
            grad = grad * exp_stage[1, rows, 0:hidden_rows].astype(jnp.float32)
            pre_grad[rows, 0:hidden_rows] = grad.astype(low)
        load_next(3)
        load_next(1)
        load(2, group).wait()
        for rows in row_tiles:
            normed_grad[rows, :] += jnp.dot(
                pre_grad[rows, 0:hidden_rows],
                received[0:hidden_rows, :],
                preferred_element_type=jnp.float32,
            )
        load_next(2)

        @pl.when(group == 2)
        def _():
            for role in (3, 2):
                core_copy(role, 3).wait_send()

        @pl.when(group == 0)
        def _():
            for role in (3, 2):
                core_copy(role, 1).wait_send()

        load(0, group).wait()
        for c0 in range(0, hidden_rows, 256):
            columns = slice(c0, c0 + 256)
            odd_down[columns, :] = jnp.dot(
                exp_stage[0, :, columns].T, row_grads[...], preferred_element_type=jnp.float32
            ).astype(low)
        load_next(0)

        @pl.when(group == 3)
        def _():
            core_copy(3, 3).start()

        @pl.when(group == 2)
        def _():
            two_down[...] = odd_down[...]
            send_far(3)

        @pl.when(group == 1)
        def _():
            core_copy(3, 1).start()

        @pl.when(group == 0)
        def _():
            zero_down[...] = odd_down[...]

        for c0 in range(0, hidden_rows, 256):
            columns = slice(c0, c0 + 256)
            odd_in[columns, :] = jnp.dot(
                pre_grad[:, columns].T, normed[...], preferred_element_type=jnp.float32
            ).astype(low)

        @pl.when(group == 3)
        def _():
            core_copy(2, 3).start()

        @pl.when(group == 2)
        def _():
            two_in[...] = odd_in[...]
            send_half(2, 1)

        @pl.when(group == 1)
        def _():
            core_copy(2, 1).start()

        @pl.when(group == 0)
        def _():
            zero_in[...] = odd_in[...]

        return carry

    lax.fori_loop(0, tensor_count, feed_step, 0)
    for which in (6, 7, 8, 9):
        load(which).start()
    send_half(2, 0)
    pass_line(2, 1)
    for which in (6, 7, 8):
        load(which).wait()
    gain_grad = jnp.zeros((1, D), jnp.float32)
    for r0 in range(0, SEQ, 128):
        rows = slice(r0, r0 + 128)
        mid = exp_stage[0, rows, 0:D].astype(jnp.float32)
        grads = normed_grad[rows, :]
        inverse = lax.rsqrt(jnp.mean(mid * mid, axis=1, keepdims=True) + norm_epsilon)
        scaled = mid * inverse
        gain_grad = gain_grad + jnp.sum(grads * scaled, axis=0, keepdims=True)
        grads = grads * params_ref[:, D : 2 * D]
        inner = jnp.mean(grads * scaled, axis=1, keepdims=True)
        row_grads[rows, :] = (
            exp_stage[1, rows, 0:D].astype(jnp.float32) + inverse * (grads - scaled * inner)
        ).astype(low)
    for part in range(D // TILE):
        line_at = D // TILE + part
        small_own[line_at : line_at + 1, :] = gain_grad[:, TILE * part : TILE * (part + 1)]
    normed_grad[...] = jnp.zeros_like(normed_grad)
    load_exp(heads - group_heads, 0).start()
    load_proj(tensor_count - 1).start()
    for group, target in enumerate((zero_out, odd_out.at[0], two_out, odd_out.at[1])):
        rows = slice(group * head_rows, (group + 1) * head_rows)
        target[...] = jnp.dot(
            attended_ref[rows, :], row_grads[...], preferred_element_type=jnp.float32
        ).astype(low)
    core_copy(1, 3).start()
    core_copy(1, 1).start()
    for r0 in range(0, D, 256):
        rows = slice(r0, r0 + 256)
        attended_grad[rows, :] = contract(sent[rows, :], row_grads[...], 1, 1).astype(low)
    load(9).wait()

    def head_step(i, carry):
        group = tensor_count - 1 - lax.div(i, group_heads)
        part_head = lax.rem(i, group_heads)
        head = group * group_heads + part_head
        slot = lax.rem(i, 2)

        @pl.when(i == 1)
        def _():
            send_deal(3)

        @pl.when(i == 2)
        def _():
            send_far(1)

        @pl.when(i == 3)
        def _():
            pass_line(2, 0)

        @pl.when(i == 5)
        def _():
            send_deal(1)

        @pl.when(i == 6)
        def _():
            send_far(0)
            pass_line(3)

        @pl.when(i == 8)
        def _():
            pass_line(1)

        @pl.when((part_head == 0) & (i > 0))
        def _():
            save_proj(group + 1).wait()

        @pl.when(part_head == 0)
        def _():
            load_proj(group).wait()

        @pl.when(i + 1 < heads)
        def _():
            later = i + 1
            later_group = tensor_count - 1 - lax.div(later, group_heads)
            later_head = later_group * group_heads + lax.rem(later, group_heads)
            load_exp(later_head, lax.rem(later, 2)).start()

        load_exp(head, slot).wait()

        def rows(part):
            return pl.ds(pl.multiple_of(part * head_rows + part_head * HS, HS), HS)

        def store(part, column, value):
            proj_grad[rows(part), column : column + value.shape[1]] = value

        here = pl.ds(pl.multiple_of(head * HS, HS), HS)
        offset_grad = attend_head_back(
            proj[rows(0), :],
            proj[rows(1), :],
            proj[rows(2), :],
            exp_stage.at[slot],
            attended_ref[here, :],
            scale_ref[head],
            attended_grad[here, :],
            window,
            score_grads,
            store,
        )
        place = (
            true_group((tensor_pos, core_pos, far_pos), group, tensor_count) * group_heads + part_head
        )
        high = offset_grad.astype(low)
        rest = (offset_grad - high.astype(jnp.float32)).astype(low)
        both = jnp.concatenate([high, rest] + [jnp.zeros_like(high)] * 6, axis=0)
        sums = contract(both, bucket_hot[...], 1, 1)
        row = lax.broadcasted_iota(jnp.int32, (SMALL_ROWS - TABLE_ROW, TILE), 0)
        found = jnp.concatenate(
            [sums[0:1] + sums[1:2], jnp.zeros((1, TILE - NB), jnp.float32)], axis=1
        )
        small_own[TABLE_ROW:SMALL_ROWS, :] += jnp.where(
            row == place,
            jnp.broadcast_to(found, (SMALL_ROWS - TABLE_ROW, TILE)),
            0.0,
        )

        @pl.when(part_head == group_heads - 1)
        def _():
            @pl.when(group > 0)
            def _():
                load_proj(group - 1).start()

            def weight_grad(target):
                for r0 in range(0, 3 * head_rows, head_rows):
                    target[r0 : r0 + head_rows, :] = jnp.dot(
                        proj_grad[r0 : r0 + head_rows, :],
                        normed[...],
                        preferred_element_type=jnp.float32,
                    ).astype(low)

            @pl.when(group == 3)
            def _():
                weight_grad(odd_down)
                core_copy(0, 3).start()

            @pl.when(group == 2)
            def _():
                weight_grad(two_qkv)

            @pl.when(group == 1)
            def _():
                weight_grad(odd_in)
                core_copy(0, 1).start()

            @pl.when(group == 0)
            def _():
                weight_grad(zero_qkv)

            save_proj(group).start()

        return carry

    lax.fori_loop(0, heads, head_step, 0)

    load(10).start()
    save_proj(0).wait()
    reload(0, 1).start()
    reload(1, 0).start()
    send_deal(0)
    reload(1, 1).start()
    for group in range(tensor_count):
        if group > 0:
            reload(group, 0).wait()
        reload(group, 1).wait()
        part, rows_in = (proj, zero_qkv) if group % 2 else (proj_grad, weights)
        for r0 in range(0, SEQ, 256):
            normed_grad[r0 : r0 + 256, :] += jnp.dot(
                part[:, r0 : r0 + 256].T, rows_in[...], preferred_element_type=jnp.float32
            )
        if group + 2 < tensor_count:
            reload(group + 2, 0).start()
            reload(group + 2, 1).start()
    pass_line(0)
    load(10).wait()

    gain_grad = jnp.zeros((1, D), jnp.float32)
    for r0 in range(0, SEQ, 128):
        values = exp_stage[0, r0 : r0 + 128, 0:D].astype(jnp.float32)
        grads = normed_grad[r0 : r0 + 128, :]
        inverse = lax.rsqrt(jnp.mean(values * values, axis=1, keepdims=True) + norm_epsilon)
        scaled = values * inverse
        gain_grad = gain_grad + jnp.sum(grads * scaled, axis=0, keepdims=True)
        grads = grads * params_ref[:, 0:D]
        inner = jnp.mean(grads * scaled, axis=1, keepdims=True)
        row_grads[r0 : r0 + 128, :] = (
            row_grads[r0 : r0 + 128, :].astype(jnp.float32) + inverse * (grads - scaled * inner)
        ).astype(low)
    for part in range(D // TILE):
        small_own[part : part + 1, :] = gain_grad[:, TILE * part : TILE * (part + 1)]

    save_rows = pltpu.make_async_copy(row_grads, input_grad_ref, exp_sem.at[1])
    save_rows.start()

    def small_copy(stage, m):
        if stage == 0:
            src, target, peer = small_own, small_tensor.at[tensor_pos], tensor_peer(m)
        else:
            src, target, peer = small_total_ref, small_dp.at[dp_pos], (up(m), tensor_pos)
        return pltpu.make_async_remote_copy(
            src,
            target,
            small_send.at[stage, m],
            small_recv.at[stage, m],
            device_id=peer,
            device_id_type=MESH,
        )

    for m in range(1, tensor_count):
        small_copy(0, m).start()
    small_tensor[tensor_pos] = small_own[...]
    for m in range(1, tensor_count):
        small_copy(0, m).wait()
    total = small_tensor[0]
    for m in range(1, tensor_count):
        total = total + small_tensor[m]
    small_total_ref[...] = total
    each_peer(lambda m: small_copy(1, m).start())
    finish_far()
    finish_near()
    finish_deal(3)
    small_dp[dp_pos] = small_total_ref[...]
    each_peer(lambda m: small_copy(1, m).wait())
    total = small_dp[0]
    for m in range(1, dp_count):
        total = total + small_dp[m]
    small_total_ref[...] = total
    finish_deal(1)
    finish_deal(0)

    place = jnp.concatenate([spread_place_ref[m : m + 1, :] for m in range(dp_count)], axis=1)
    hot = one_hot(place, (spread.shape[0], dp_count * pair_rows), 0)
    sent[0 : dp_count * pair_rows, :] = contract(hot, spread[...], 0, 0).astype(low)

    def back_copy(m):
        here = pl.ds(pl.multiple_of(m * pair_rows, 16), pair_rows)
        return pltpu.make_async_remote_copy(
            sent.at[here],
            received.at[here],
            back_send.at[m],
            back_recv.at[m],
            device_id=(down(m), tensor_pos),
            device_id_type=MESH,
        )

    each_peer(lambda m: back_copy(m).start())
    received[0:pair_rows, :] = sent[0:pair_rows, :]
    each_peer(lambda m: back_copy(m).wait())
    hot = one_hot(slot_place_ref[...], (dp_count * pair_rows, owned_ref.shape[0]), 0)
    owned_ref[...] = contract(hot, received[0 : dp_count * pair_rows, :], 0, 0)
    save_rows.wait()
    for role in range(len(gots)):
        if role < 2:
            core_copy(role, 1).wait_send()
            core_copy(role, 3).wait_send()
        if role != 2:
            far_copy(role).wait_send()


def back(
    feed_parts,
    projected,
    exp_scores,
    w_qkv,
    tokens,
    normed_one,
    attended,
    scale,
    small_row,
    small,
    bucket_place,
    places,
    local_sizes,
    spread_place,
    slot_place,
):
    dp_count, tensor_count = lax.axis_size("dp"), lax.axis_size("tensor")
    sizes = [place.shape[1] for place in places]
    capacity, pair_rows = slot_place.shape[1], spread_place.shape[1]
    low = jnp.bfloat16
    dma = pltpu.SemaphoreType.DMA
    roles = len(sizes)
    whole = pl.BlockSpec(memory_space=pltpu.VMEM)
    away = pl.BlockSpec(memory_space=pl.ANY)
    parts = [pltpu.VMEM((size, D), low) for size in sizes]
    padded = [
        pltpu.VMEM((max(dp_count * size, full), D), low) for size, full in zip(local_sizes, sizes)
    ]
    return pl.pallas_call(
        functools.partial(back_kernel, sizes),
        in_specs=[away] * 14 + [whole] * 11,
        out_specs=[whole, away, whole, away],
        out_shape=[
            jax.ShapeDtypeStruct((capacity, D), jnp.float32),
            jax.ShapeDtypeStruct((SEQ, D), low),
            jax.ShapeDtypeStruct((SMALL_ROWS, TILE), jnp.float32),
            jax.ShapeDtypeStruct((tensor_count, sizes[0], SEQ), low),
        ],
        scratch_shapes=[
            pltpu.VMEM((NB, 2 * SEQ), low),
            pltpu.VMEM((sizes[0], D), low),
            pltpu.VMEM((sizes[0], SEQ), low),
            pltpu.VMEM((sizes[0], SEQ), low),
            pltpu.VMEM((SEQ, D), jnp.float32),
            pltpu.VMEM((WINDOW, TILE), jnp.float32),
            pltpu.VMEM((SEQ, SEQ), low),
            pltpu.VMEM((2, SEQ, SEQ), low),
            pltpu.VMEM((SEQ, D), low),
            pltpu.VMEM((SEQ, D), low),
            pltpu.VMEM((D, SEQ), low),
            pltpu.VMEM((2, sizes[1], D), low),
            pltpu.VMEM((sizes[2], D), low),
            pltpu.VMEM((sizes[3], D), low),
        ]
        + parts
        + parts
        + parts[:2]
        + padded[2:3]
        + parts[3:]
        + padded
        + parts[:2]
        + [pltpu.VMEM((dp_count * local_sizes[2], D), low)]
        + parts[3:]
        + [
            pltpu.VMEM((dp_count if role == 2 else dp_count // 2, size, D), low)
            for role, size in enumerate(local_sizes)
        ]
        + [pltpu.VMEM((dp_count // 2 * local_sizes[role], D), low) for role in (0, 1, 3)]
        + [
            pltpu.VMEM((local_sizes[2], D), low),
            pltpu.VMEM((local_sizes[2], D), low),
            pltpu.VMEM((sum(local_sizes), D), low),
            pltpu.VMEM((max(dp_count * pair_rows, D), D), low),
            pltpu.VMEM((max(dp_count * pair_rows, D), D), low),
            pltpu.VMEM((SMALL_ROWS, TILE), jnp.float32),
            pltpu.VMEM((tensor_count, SMALL_ROWS, TILE), jnp.float32),
            pltpu.VMEM((dp_count, SMALL_ROWS, TILE), jnp.float32),
            dma((roles, 2)),
            dma((roles, 2)),
            dma((roles,)),
            dma((roles,)),
            dma((roles, 2)),
            dma((roles, 2)),
            dma((roles, dp_count)),
            dma((roles, dp_count)),
            dma,
            dma,
            dma((dp_count,)),
            dma((dp_count,)),
            dma((2, max(dp_count, tensor_count))),
            dma((2, max(dp_count, tensor_count))),
            dma((11,)),
            dma((2,)),
            dma((2,)),
            dma((2, 2)),
        ],
        compiler_params=pltpu.CompilerParams(
            collective_id=2, has_side_effects=True, vmem_limit_bytes=63 * 1024 * 1024
        ),
        cost_estimate=pl.CostEstimate(
            flops=16 * H * SEQ * SEQ * 256 + 8 * SEQ * FF * D,
            bytes_accessed=96 * 1024 * 1024,
            transcendentals=0,
        ),
        name="back",
    )(
        *feed_parts,
        projected,
        exp_scores,
        w_qkv,
        tokens,
        normed_one,
        attended,
        scale,
        small_row,
        small,
        bucket_place,
        *places,
        spread_place,
        slot_place,
    )


def adamw(weights, grads, first, second, step):
    first_new = beta_first * first + (1.0 - beta_first) * grads
    second_new = beta_second * second + (1.0 - beta_second) * grads * grads
    first_hat = first_new / (1.0 - beta_first**step)
    second_hat = second_new / (1.0 - beta_second**step)
    weights_new = weights - rate_per_step * step * (
        first_hat / (jnp.sqrt(second_hat) + adam_epsilon) + weight_decay * weights
    )
    return (weights_new, first_new, second_new)


def per_device(
    tokens,
    cotangent,
    segment_ids,
    buckets,
    owners,
    master,
    first_moment,
    second_moment,
    small_params,
    small_first,
    small_second,
    adapter_ema,
    step_count,
):
    dp_count = lax.axis_size("dp")
    tensor_count = lax.axis_size("tensor")
    capacity = master.shape[1]
    group_heads = H // tensor_count
    head_rows = group_heads * HS
    hidden_rows = FF // tensor_count
    tensor_pos = lax.axis_index("tensor")
    sizes = [3 * head_rows, head_rows, hidden_rows, hidden_rows]
    local_sizes = [-(-size // dp_count // 16) * 16 for size in sizes]
    pair_rows = -(-((capacity + len(sizes) * (dp_count - 1)) // dp_count) // 16) * 16
    slot_place, spread_place, orders, places = plan(
        owners, sizes, local_sizes, capacity, pair_rows
    )

    adapter = unpack(small_params)
    bucket_place = jnp.concatenate([jnp.full((1,), -1, jnp.int32), buckets[::-1]])[None, :]
    segments = lax.dynamic_slice_in_dim(segment_ids, tensor_pos * SEQ, SEQ, 0)
    factors, factors_pull = jax.vjp(adapter_factors, adapter)
    outs = front(
        master[0],
        slot_place,
        spread_place,
        orders,
        local_sizes,
        tokens,
        small_params[None, :],
        bucket_place,
        segments,
        cotangent,
        factors,
    )
    w_qkv, w_out, w_in, w_down, projected, attended, scale, normed_one, exp_scores = outs[:9]
    activ, slope, normed_two, mid, layer_out, ffn_grad = outs[9:15]
    factor_grads = tuple(outs[15:])
    (adapter_grad,) = factors_pull(factor_grads)
    small_local = jnp.concatenate(
        [jnp.zeros((2 * D,), jnp.float32)]
        + [piece.reshape(-1) for piece in adapter_grad]
        + [jnp.zeros((TABLE_ROW * TILE - 2 * D - NADAPT,), jnp.float32)]
    ).reshape(TABLE_ROW, TILE)
    owned_grad, input_grad, small_total, _ = back(
        (
            ffn_grad,
            normed_two,
            mid,
            cotangent,
            w_out.reshape(D, D),
            activ,
            slope,
            w_in,
            w_down,
        ),
        projected,
        exp_scores,
        w_qkv,
        tokens,
        normed_one,
        attended,
        scale,
        small_params[None, :],
        small_local,
        bucket_place,
        places,
        local_sizes,
        spread_place,
        slot_place,
    )
    small_total = jnp.concatenate(
        [
            small_total[:TABLE_ROW].reshape(-1)[: 2 * D + NADAPT],
            small_total[TABLE_ROW : TABLE_ROW + H, :NB].T.reshape(-1),
        ]
    )
    own_filled = (slot_place[0] >= 0).astype(jnp.float32)[:, None]
    step = step_count[0].astype(jnp.float32)
    owned_grad = owned_grad * own_filled
    new_master, new_first, new_second = adamw(
        master[0], owned_grad, first_moment[0], second_moment[0], step
    )
    new_master = new_master * own_filled
    new_first = new_first * own_filled
    new_second = new_second * own_filled
    small_new, small_first_new, small_second_new = adamw(
        small_params, small_total, small_first, small_second, step
    )
    ema_new = average_keep * adapter_ema + (1.0 - average_keep) * small_new[2 * D : 2 * D + NADAPT]
    return (
        layer_out,
        input_grad,
        owned_grad[None],
        new_first[None],
        new_second[None],
        new_master[None],
        new_master.astype(jnp.bfloat16)[None],
        small_total,
        small_first_new,
        small_second_new,
        small_new,
        ema_new,
    )


def solution(mesh):
    token_spec = P(("dp", "tensor"), None)
    owner_spec = P("tensor", "dp", None)
    return jax.shard_map(
        per_device,
        mesh=mesh,
        in_specs=(token_spec, token_spec, P("dp"), P(), P())
        + (owner_spec,) * 3
        + (P(),) * 5,
        out_specs=(token_spec,) * 2 + (owner_spec,) * 5 + (P(),) * 5,
        check_vma=False,
    )
```

```python
import functools
import math

import jax
import jax.numpy as jnp
from jax import lax
from jax.experimental import pallas as pl
from jax.experimental.pallas import tpu as pltpu
from jax.sharding import PartitionSpec as P

D = 768
H = 12
HS = 64
FF = 3072
NB = 32
R = 48
PHM = 4
SEQ = 1024
NADAPT = 1696

highest = lax.Precision.HIGHEST
norm_epsilon = 1e-06
beta_first = 0.5
beta_second = 0.5
adam_epsilon = 1e-08
rate_per_step = 0.01
weight_decay = 0.1
average_keep = 0.75
masked_score = -1000000000.0

TILE = 128
WINDOW = 2 * SEQ - TILE
QUERY_TILE = 512
KEY_TILE = 512
BACK_QUERY_TILE = 512
BACK_KEY_TILE = 1024
VMEM_LIMIT = 48 * 1024 * 1024
MESH = pl.DeviceIdType.MESH
SMALL_ROWS = 48
TABLE_ROW = 32


def exact(left, right, left_dim, right_dim):
    return lax.dot_general(
        left,
        right,
        (((left_dim,), (right_dim,)), ((), ())),
        precision=highest,
        preferred_element_type=jnp.float32,
    )


def grid(shape, dim, parts):
    rest = lax.broadcasted_iota(jnp.int32, shape, dim).astype(jnp.float32)
    found = []
    for part in parts:
        high = jnp.floor((rest + 0.5) * (1.0 / part))
        found.append(high)
        rest = rest - part * high
    return found + [rest]


def zero_one(hit):
    return jnp.where(hit, 1.0, 0.0)


def adapter_places():
    rank = R // PHM
    outer = PHM * PHM
    block, inner = grid((R, PHM * outer), 0, (rank,))
    _, first, second = grid((R, PHM * outer), 1, (outer, PHM))
    term, left_at, right_at = grid((PHM * outer, outer), 0, (outer, PHM))
    column, last = grid((PHM * outer, outer), 1, (PHM,))
    mix_down = (
        zero_one(second == block),
        zero_one((term == column) & (left_at == last)),
    )
    mix_up = (
        zero_one(first == block),
        zero_one((term == column) & (right_at == last)),
    )
    _, inner = grid((R, R), 0, (rank,))
    _, short = grid((R, R), 1, (rank,))
    term, _ = grid((R, outer), 0, (rank,))
    column, _ = grid((R, outer), 1, (PHM,))
    side = (zero_one(inner == short), zero_one(term == column))
    return mix_down, mix_up, side


def lay_out(row, places):
    keep, gather = places
    return exact(keep * row, gather, 1, 0)


def take_back(values, places):
    keep, gather = places
    return jnp.sum(keep * exact(values, gather, 1, 1), axis=0, keepdims=True)


def lay_long(row):
    part = D // PHM
    term, block = grid((PHM * PHM, D), 0, (PHM,))
    place, _ = grid((PHM * PHM, D), 1, (part,))
    total = jnp.zeros((PHM * PHM, D), jnp.float32)
    for i in range(PHM):
        tiled = jnp.concatenate([row[:, part * i : part * (i + 1)]] * PHM, axis=1)
        total = jnp.where((term == i) & (place == block), tiled, total)
    return total


def take_long(values):
    part = D // PHM
    _, block = grid((PHM * PHM, D), 0, (PHM,))
    place, _ = grid((PHM * PHM, D), 1, (part,))
    values = jnp.where(place == block, values, 0.0)
    pieces = []
    for i in range(PHM):
        row = jnp.sum(values[PHM * i : PHM * (i + 1), :], axis=0, keepdims=True)
        pieces.append(sum(row[:, part * a : part * (a + 1)] for a in range(PHM)))
    return jnp.concatenate(pieces, axis=1)


def normal_parts(values):
    size = jnp.abs(values)
    shrink = 1.0 / (1.0 + (0.3275911 * math.sqrt(0.5)) * size)
    bell = jnp.exp(-0.5 * values * values)
    series = 0.5 * 1.061405429
    for term in (-1.453152027, 1.421413741, -0.284496736, 0.254829592):
        series = series * shrink + 0.5 * term
    tail = series * shrink * bell
    return jnp.where(values >= 0.0, 1.0 - tail, tail), bell * (1.0 / math.sqrt(2.0 * math.pi))


def contract(left, right, left_dim, right_dim):
    return lax.dot_general(
        left,
        right,
        (((left_dim,), (right_dim,)), ((), ())),
        preferred_element_type=jnp.float32,
    )


def bias_window(bias, window):
    for tile in range(WINDOW // TILE):
        base = WINDOW - TILE * tile
        row = jnp.broadcast_to(bias[:, base - TILE : base + TILE], (TILE, 2 * TILE))
        rolled = pltpu.roll(row, TILE, 1, stride=1, stride_axis=0)
        window[TILE * tile : TILE * (tile + 1), :] = rolled[:, :TILE]


def attend_head(
    query_rows, key_rows, value_rows, segment_keys_ref, segment_queries_ref, window, scores, exp_ref
):
    keys = key_rows.T
    values = jnp.concatenate([value_rows, jnp.ones((16, SEQ), jnp.bfloat16)], axis=0)
    outs, scales = [], []
    for q0 in range(0, SEQ, QUERY_TILE):
        queries = query_rows[:, q0 : q0 + QUERY_TILE]
        peak = jnp.full((8, QUERY_TILE), -jnp.inf, jnp.float32)
        for k0 in range(0, SEQ, KEY_TILE):
            raw = jnp.dot(keys[k0 : k0 + KEY_TILE], queries, preferred_element_type=jnp.float32)
            parts = []
            for l0 in range(0, QUERY_TILE, TILE):
                start = SEQ - TILE - (q0 + l0) + k0
                same_doc = (
                    segment_keys_ref[k0 : k0 + KEY_TILE, :]
                    == segment_queries_ref[:, q0 + l0 : q0 + l0 + TILE]
                )
                part = jnp.where(
                    same_doc,
                    raw[:, l0 : l0 + TILE] + window[start : start + KEY_TILE, :],
                    masked_score,
                )
                scores[k0 : k0 + KEY_TILE, l0 : l0 + TILE] = part
                parts.append(part)
            whole = jnp.concatenate(parts, axis=1)
            peak = jnp.maximum(peak, jnp.max(whole.reshape(KEY_TILE // 8, 8, QUERY_TILE), axis=0))
        peak = jnp.max(peak, axis=0, keepdims=True)
        total = jnp.zeros((HS + 16, QUERY_TILE), jnp.float32)
        for k0 in range(0, SEQ, KEY_TILE):
            exp_scores = jnp.exp(scores[k0 : k0 + KEY_TILE, :] - peak).astype(jnp.bfloat16)
            exp_ref[k0 : k0 + KEY_TILE, q0 : q0 + QUERY_TILE] = exp_scores
            total = total + jnp.dot(
                values[:, k0 : k0 + KEY_TILE], exp_scores, preferred_element_type=jnp.float32
            )
        scale = 1.0 / total[HS : HS + 1]
        scales.append(scale)
        outs.append((total[:HS] * scale).astype(jnp.bfloat16))
    return jnp.concatenate(outs, axis=1), jnp.concatenate(scales, axis=1)


def one_hot(place, shape, dim):
    hit = lax.broadcasted_iota(jnp.int32, shape, dim) == place
    return jnp.where(hit, 1.0, 0.0).astype(jnp.bfloat16)


def plan_kernel(dp_count, pair_rows, local_sizes, *refs):
    roles = len(local_sizes)
    owners_ref, slot_ref, spread_ref = refs[:3]
    order_refs, place_refs = refs[3 : roles + 3], refs[roles + 3 :]
    dp_pos = lax.axis_index("dp").astype(jnp.float32)

    def quotient(values):
        return jnp.floor((values + 0.5) * (1.0 / dp_count))

    def remainder(values):
        return values - dp_count * quotient(values)

    line = dp_count // 2

    def halve(values):
        return jnp.floor((values + 0.5) * 0.5)

    def around(values):
        return values - line * jnp.floor((values + 0.5) * (1.0 / line))

    whole = owners_ref[...].astype(jnp.float32)
    whole = jnp.concatenate([whole[i : i + 1, :] for i in range(whole.shape[0])], axis=1)
    owners, low = [], 0
    for ref in order_refs:
        owners.append(whole[:, low : low + ref.shape[1]])
        low += ref.shape[1]

    def stats(who):
        counts = [
            jnp.sum(jnp.where(row == who, 1.0, 0.0), axis=1, keepdims=True) for row in owners
        ]
        starts = [jnp.sum(jnp.where(row < who, 1.0, 0.0), axis=1, keepdims=True) for row in owners]
        return counts, starts

    def hits(first, number, target):
        return quotient(first + number - 1.0 - target) - quotient(first - 1.0 - target)

    counts, starts = stats(jnp.full((1, 1), dp_pos))
    slot = lax.broadcasted_iota(jnp.int32, slot_ref.shape, 1).astype(jnp.float32)
    found = jnp.full(slot_ref.shape, -1.0)
    low = jnp.zeros((1, 1), jnp.float32)
    for role in range(roles):
        rank = slot - low
        target = remainder(starts[role] + rank)
        place = quotient(rank)
        for other in range(role):
            place = place + hits(starts[other], counts[other], target)
        found = jnp.where(
            (rank >= 0.0) & (rank < counts[role]),
            remainder(target - dp_pos) * pair_rows + place,
            found,
        )
        low = low + counts[role]
    slot_ref[...] = found.astype(jnp.int32)

    column = lax.broadcasted_iota(jnp.int32, (dp_count, 1), 0).astype(jnp.float32)
    counts, starts = stats(remainder(dp_pos - column))
    pair = lax.broadcasted_iota(jnp.int32, spread_ref.shape, 1).astype(jnp.float32)
    found = jnp.full(spread_ref.shape, -1.0)
    passed = jnp.zeros((dp_count, 1), jnp.float32)
    for role in range(roles):
        number = hits(starts[role], counts[role], dp_pos)
        first = starts[role] + remainder(dp_pos - starts[role])
        rank = pair - passed
        local = sum(local_sizes[:role]) + quotient(first) + rank
        found = jnp.where((rank >= 0.0) & (rank < number), local, found)
        passed = passed + number
    spread_ref[...] = found.astype(jnp.int32)

    counts, starts = stats(column)
    for role in range(roles):
        width = owners[role].shape[1]
        before = starts[role]
        for c0 in range(0, width, TILE):
            c1 = min(c0 + TILE, width)
            hot = jnp.where(owners[role][:, c0:c1] == column, 1.0, 0.0)
            shape = (c1 - c0, c1 - c0)
            above = lax.broadcasted_iota(jnp.int32, shape, 0) < lax.broadcasted_iota(
                jnp.int32, shape, 1
            )
            rank = jnp.dot(
                hot.astype(jnp.bfloat16),
                jnp.where(above, 1.0, 0.0).astype(jnp.bfloat16),
                preferred_element_type=jnp.float32,
            )
            number = jnp.sum(hot * (rank + before), axis=0, keepdims=True)
            before = before + jnp.sum(hot, axis=1, keepdims=True)
            target, row = remainder(number), quotient(number)
            side = jnp.abs(target - 2.0 * halve(target) - dp_pos + 2.0 * halve(dp_pos)) * line
            ahead = halve(target) - halve(dp_pos)
            order = (around(0.0 - ahead) + side) * local_sizes[role] + row
            place = (around(ahead) + side) * local_sizes[role] + row
            order_refs[role][:, c0:c1] = order.astype(jnp.int32)
            place_refs[role][:, c0:c1] = place.astype(jnp.int32)


def plan(owners, sizes, local_sizes, capacity, pair_rows):
    dp_count = lax.axis_size("dp")
    outs = pl.pallas_call(
        functools.partial(plan_kernel, dp_count, pair_rows, local_sizes),
        out_shape=[
            jax.ShapeDtypeStruct((1, capacity), jnp.int32),
            jax.ShapeDtypeStruct((dp_count, pair_rows), jnp.int32),
        ]
        + [jax.ShapeDtypeStruct((1, size), jnp.int32) for size in sizes] * 2,
        name="plan",
    )(owners.reshape(-1, TILE))
    return outs[0], outs[1], outs[2 : 2 + len(sizes)], outs[2 + len(sizes) :]


def true_group(positions, group, tensor_count):
    flips = positions + (tensor_count - 1 - positions[0],)
    found = flips[0]
    for g in range(1, tensor_count):
        found = found + (flips[g] - flips[0]) * (
            lax.div(group + tensor_count - g, tensor_count)
            - lax.div(group + tensor_count - g - 1, tensor_count)
        )
    return found


def front_kernel(
    sizes,
    mine_ref,
    slot_place_ref,
    spread_place_ref,
    order_qkv_ref,
    order_out_ref,
    order_in_ref,
    order_down_ref,
    tokens_ref,
    small_ref,
    bucket_ref,
    segment_ref,
    cotangent_ref,
    w_qkv_out,
    w_out_ref,
    w_in_ref,
    w_down_ref,
    projected_out,
    attended_ref,
    scale_ref,
    normed_ref,
    exp_ref,
    activ_ref,
    slope_ref,
    normed_two_ref,
    mid_ref,
    layer_out_ref,
    ffn_grad_ref,
    small_part_ref,
    w_qkv_ref,
    projected_ref,
    feed_weights,
    ffn_out,
    mid_rows,
    hot_qkv,
    hot_out,
    hot_in,
    hot_down,
    sent,
    received,
    spread,
    bias,
    segment_keys,
    buf_qkv,
    buf_out,
    buf_in,
    buf_down,
    buf_far,
    far_spread,
    stage_out,
    stage_in,
    stage_down,
    stage_far,
    window,
    scores,
    exp_stage,
    deal_send,
    deal_recv,
    far_send,
    far_recv,
    line_send,
    line_recv,
    side_send,
    side_recv,
    group_send,
    group_recv,
    local_sem,
    exp_sem,
    save_sem,
    feed_sem,
    out_sem,
):
    dp_count, pair_rows = sent.shape[0], sent.shape[1]
    tensor_count = w_qkv_ref.shape[0]
    heads = scale_ref.shape[0]
    low = jnp.bfloat16
    group_heads = heads // tensor_count
    head_rows = group_heads * HS
    dp_pos, tensor_pos = lax.axis_index("dp"), lax.axis_index("tensor")
    core_pos = tensor_pos + 1 - 2 * lax.rem(tensor_pos, 2)
    far_pos = lax.rem(tensor_pos + 2, tensor_count)
    core_peer, far_peer = (dp_pos, core_pos), (dp_pos, far_pos)

    def dp_peer(m):
        return (lax.rem(dp_pos + m, dp_count), tensor_pos)

    def each_peer(run):
        def step(m, carry):
            run(m)
            return carry

        lax.fori_loop(1, dp_count, step, 0)

    barrier = pltpu.get_barrier_semaphore()

    def greet(m):
        pl.semaphore_signal(barrier, inc=1, device_id=dp_peer(m), device_id_type=MESH)

    each_peer(greet)
    for peer in (core_peer, far_peer):
        pl.semaphore_signal(barrier, inc=1, device_id=peer, device_id_type=MESH)

    mine = mine_ref[...].astype(jnp.bfloat16)
    hot = one_hot(slot_place_ref[...], (dp_count * pair_rows, mine.shape[0]), 0)
    sent[...] = (
        jnp.dot(hot, mine, preferred_element_type=jnp.float32)
        .astype(jnp.bfloat16)
        .reshape(dp_count, pair_rows, D)
    )
    pl.semaphore_wait(barrier, dp_count + 1)

    def deal(m):
        return pltpu.make_async_remote_copy(
            sent.at[m],
            received.at[m],
            deal_send.at[m],
            deal_recv.at[m],
            device_id=dp_peer(m),
            device_id_type=MESH,
        )

    each_peer(lambda m: deal(m).start())
    received[0] = sent[0]

    for r0 in range(0, SEQ, 128):
        values = tokens_ref[r0 : r0 + 128, :].astype(jnp.float32)
        inverse = lax.rsqrt(jnp.mean(values * values, axis=1, keepdims=True) + norm_epsilon)
        normed_ref[r0 : r0 + 128, :] = (values * inverse * small_ref[:, 0:D]).astype(jnp.bfloat16)
    flat = small_ref[...][:, 2 * D + NADAPT :]
    entry = lax.broadcasted_iota(jnp.int32, (16, NB * H), 1)
    bucket = jnp.floor((entry.astype(jnp.float32) + 0.5) * (1.0 / H))
    head_of = entry.astype(jnp.float32) - H * bucket
    line_of = lax.broadcasted_iota(jnp.int32, (16, NB * H), 0).astype(jnp.float32)
    rest = jnp.where(head_of == line_of, jnp.broadcast_to(flat, (16, NB * H)), 0.0)
    entry = lax.broadcasted_iota(jnp.int32, (NB * H, 2 * SEQ), 0).astype(jnp.float32)
    bucket = jnp.floor((entry + 0.5) * (1.0 / H))
    hot = jnp.where(bucket == bucket_ref[...].astype(jnp.float32), 1.0, 0.0).astype(jnp.bfloat16)
    biases = jnp.zeros((rest.shape[0], 2 * SEQ), jnp.float32)
    for _ in range(3):
        part = rest.astype(jnp.bfloat16)
        rest = rest - part.astype(jnp.float32)
        biases = biases + jnp.dot(part, hot, preferred_element_type=jnp.float32)
    for head in range(heads):
        bias[head] = biases[head : head + 1, :]
    segment_keys[...] = jnp.broadcast_to(segment_ref[...], (TILE, SEQ)).T
    hots = (hot_qkv, hot_out, hot_in, hot_down, hot_down)
    for hot, place in zip(hots, (order_qkv_ref, order_out_ref, order_in_ref, order_down_ref)):
        hot[...] = one_hot(place[...], (hot.shape[1], hot.shape[0]), 0).T

    each_peer(lambda m: deal(m).wait())
    rows = spread.shape[0]
    place = jnp.concatenate([spread_place_ref[m : m + 1, :] for m in range(dp_count)], axis=1)
    hot = one_hot(place, (rows, dp_count * pair_rows), 0)
    spread[...] = jnp.dot(
        hot, received[...].reshape(dp_count * pair_rows, D), preferred_element_type=jnp.float32
    ).astype(jnp.bfloat16)

    bufs = (buf_qkv, buf_out, buf_in, buf_down, buf_far)
    stages = (w_qkv_ref.at[0], stage_out, stage_in, stage_down, stage_far)
    finals = (w_qkv_ref, w_out_ref, w_in_ref, w_down_ref, w_down_ref)
    sizes = tuple(sizes) + (sizes[3],)
    offsets = [sum(buf.shape[1] for buf in bufs[:role]) for role in range(4)]
    line = dp_count // 2
    line_pos, side = lax.div(dp_pos, 2), lax.rem(dp_pos, 2)
    side_peer = (dp_pos + 1 - 2 * side, tensor_pos)

    def far_exchange():
        return pltpu.make_async_remote_copy(
            spread.at[pl.ds(offsets[3], far_spread.shape[0])],
            far_spread,
            far_send,
            far_recv,
            device_id=far_peer,
            device_id_type=MESH,
        )

    def block(role):
        if role == 4:
            return far_spread
        return spread.at[pl.ds(offsets[role], bufs[role].shape[1])]

    def along_line(role, m):
        return pltpu.make_async_remote_copy(
            block(role),
            bufs[role].at[m],
            line_send.at[role, m],
            line_recv.at[role, m],
            device_id=(lax.rem(line_pos + m, line) * 2 + side, tensor_pos),
            device_id_type=MESH,
        )

    def to_side(role, m):
        return pltpu.make_async_remote_copy(
            bufs[role].at[m],
            bufs[role].at[line + m],
            side_send.at[role, m],
            side_recv.at[role, m],
            device_id=side_peer,
            device_id_type=MESH,
        )

    def each_line(first, run):
        def step(m, carry):
            run(m)
            return carry

        lax.fori_loop(first, line, step, 0)

    def start_line(role):
        if role == 4:
            far_exchange().wait()
        each_line(1, lambda m: along_line(role, m).start())
        bufs[role][0] = block(role)[...]
        to_side(role, 0).start()

    def start_side(role):
        def step(m):
            along_line(role, m).wait()
            to_side(role, m).start()

        each_line(1, step)

    def order(role):
        each_line(0, lambda m: to_side(role, m).wait())
        count = bufs[role].shape[1]
        source = bufs[role][...].reshape(dp_count * count, D)
        step = 384 if sizes[role] > 576 else sizes[role]
        for r0 in range(0, sizes[role], step):
            r1 = min(r0 + step, sizes[role])
            stages[role][r0:r1, :] = jnp.dot(
                hots[role][r0:r1, :], source, preferred_element_type=jnp.float32
            ).astype(jnp.bfloat16)

    def share(role, part):
        if role == 4:
            src, slot, peer = stages[role], 3, core_peer
        else:
            src, slot, peer = (
                (stages[role], 1, core_peer),
                (stages[role], 2, far_peer),
                (finals[role].at[2], 3, core_peer),
            )[part]
        return pltpu.make_async_remote_copy(
            src,
            finals[role].at[slot],
            group_send.at[role, part],
            group_recv.at[role, part],
            device_id=peer,
            device_id_type=MESH,
        )

    def keep(role):
        slot = 2 if role == 4 else 0
        return pltpu.make_async_copy(stages[role], finals[role].at[slot], local_sem.at[role])

    def start_share(role):
        order(role)
        share(role, 0).start()
        if role < 3:
            share(role, 1).start()
        if role > 0:
            keep(role).start()

    def forward(role):
        share(role, 1).wait_recv()
        share(role, 2).start()

    far_exchange().start()
    start_line(0)
    start_side(0)
    start_share(0)
    start_line(1)
    start_line(2)

    def save_group(which, group):
        source, target = ((projected_ref, projected_out), (w_qkv_ref, w_qkv_out))[which]
        return pltpu.make_async_copy(
            source.at[group], target.at[group], save_sem.at[which, group]
        )

    def true_head(group, head):
        return true_group((tensor_pos, core_pos, far_pos), group, tensor_count) * group_heads + head

    def head_step(i, carry):
        group, head = lax.div(i, group_heads), lax.rem(i, group_heads)

        @pl.when(i == 1)
        def _():
            start_side(1)

        @pl.when(i == 3)
        def _():
            start_share(1)

        @pl.when(i == 5)
        def _():
            start_side(2)
            start_line(3)
            start_line(4)

        @pl.when(i == 10)
        def _():
            start_share(2)

        @pl.when(i == group_heads)
        def _():
            share(0, 0).wait_recv()

        @pl.when(i == 2 * group_heads)
        def _():
            forward(0)

        @pl.when(i == 3 * group_heads)
        def _():
            share(0, 2).wait_recv()
            forward(1)

        @pl.when(i == 11)
        def _():
            start_side(3)

        @pl.when(head == 0)
        def _():
            projected_ref[group] = contract(w_qkv_ref[group], normed_ref[...], 1, 1).astype(
                jnp.bfloat16
            )
            save_group(0, group).start()
            save_group(1, group).start()

        def head_part(part):
            start = pl.multiple_of(part * head_rows + head * HS, HS)
            return projected_ref[group, pl.ds(start, HS), :]

        slot = lax.rem(i, 2)

        def save(head_index, slot):
            return pltpu.make_async_copy(
                exp_stage.at[slot], exp_ref.at[head_index], exp_sem.at[slot]
            )

        @pl.when(i >= 2)
        def _():
            save(i - 2, slot).wait()

        bias_window(bias[true_head(group, head)], window)
        attended, scale = attend_head(
            head_part(0),
            head_part(1),
            head_part(2),
            segment_keys,
            segment_ref,
            window,
            scores,
            exp_stage.at[slot],
        )
        attended_ref[pl.ds(pl.multiple_of(i * HS, HS), HS), :] = attended
        scale_ref[i] = scale
        save(i, slot).start()
        return carry

    lax.fori_loop(0, heads, head_step, 0)
    for i in (heads - 2, heads - 1):
        pltpu.make_async_copy(exp_stage.at[i % 2], exp_ref.at[i], exp_sem.at[i % 2]).wait()
    start_side(4)
    start_share(3)
    start_share(4)
    forward(2)

    def load_feed(group, slot, which):
        return pltpu.make_async_copy(
            (w_in_ref, w_down_ref)[which].at[group],
            feed_weights.at[slot, which],
            feed_sem.at[slot, which],
        )

    def load_out(group):
        return pltpu.make_async_copy(
            w_out_ref.at[group],
            feed_weights.at[1, 0, pl.ds(group * head_rows, head_rows)],
            out_sem.at[group],
        )

    keep(1).wait()
    share(1, 0).wait_recv()
    share(1, 2).wait_recv()
    for group in range(tensor_count):
        load_out(group).start()
    keep(2).wait()
    keep(3).wait()
    load_feed(0, 0, 0).start()
    load_feed(0, 0, 1).start()
    for group in range(tensor_count):
        load_out(group).wait()
    tiles = [slice(r0, r0 + 256) for r0 in range(0, SEQ, 256)]
    for rows in tiles:
        attn = jnp.dot(
            attended_ref[:, rows].T, feed_weights[1, 0], preferred_element_type=jnp.float32
        )
        mid = tokens_ref[rows, :].astype(jnp.float32) + attn
        mid_rows[rows, :] = mid
        mid_ref[rows, :] = mid.astype(low)
        inverse = lax.rsqrt(jnp.mean(mid * mid, axis=1, keepdims=True) + norm_epsilon)
        normed_two_ref[rows, :] = (mid * inverse * small_ref[:, D : 2 * D]).astype(low)
        ffn_out[rows, :] = jnp.zeros((256, D), jnp.float32)
    hidden_rows = w_in_ref.shape[1]

    def save_feed(group, which):
        columns = pl.ds(pl.multiple_of(group * hidden_rows, TILE), hidden_rows)
        return pltpu.make_async_copy(
            exp_stage.at[which, :, pl.ds(0, hidden_rows)],
            (activ_ref, slope_ref)[which].at[:, columns],
            exp_sem.at[which],
        )

    def feed_step(group, carry):
        slot = lax.rem(group, 2)
        for which in range(2):
            load_feed(group, slot, which).wait()

        @pl.when(group == 0)
        def _():
            share(2, 0).wait_recv()
            share(3, 0).wait_recv()

        @pl.when(group == 1)
        def _():
            keep(4).wait()

        @pl.when(group == 2)
        def _():
            share(2, 2).wait_recv()
            share(4, 0).wait_recv()

        @pl.when(group + 1 < tensor_count)
        def _():
            for which in range(2):
                load_feed(group + 1, 1 - slot, which).start()

        @pl.when(group > 0)
        def _():
            for which in range(2):
                save_feed(group - 1, which).wait()

        for rows in tiles:
            pre = contract(normed_two_ref[rows, :], feed_weights[slot, 0], 1, 1)
            cdf, density = normal_parts(pre)
            activ = (pre * cdf).astype(low)
            exp_stage[0, rows, 0:hidden_rows] = activ
            exp_stage[1, rows, 0:hidden_rows] = (cdf + pre * density).astype(low)
            ffn_out[rows, :] += jnp.dot(
                activ, feed_weights[slot, 1], preferred_element_type=jnp.float32
            )
        for which in range(2):
            save_feed(group, which).start()
        return carry

    lax.fori_loop(0, tensor_count, feed_step, 0)

    row = small_ref[...]
    starts = [2 * D]
    for width in (PHM**3, D, R, R, D):
        starts.append(starts[-1] + width)
    mix, down_long, down_short, up_short, up_long = [
        row[:, low_at:high_at] for low_at, high_at in zip(starts[:-1], starts[1:])
    ]
    mix_down, mix_up, short_place = adapter_places()
    mixes = (lay_out(mix, mix_down), lay_out(mix, mix_up))
    shorts = (lay_out(down_short, short_place), lay_out(up_short, short_place))
    left, wide = mixes[0] * shorts[0], mixes[1] * shorts[1]
    right, tall = lay_long(down_long), lay_long(up_long)
    down = exact(left, right, 1, 0).astype(low)
    up = exact(wide, tall, 1, 0).astype(low)
    down_grad = jnp.zeros((R, D), jnp.float32)
    up_grad = jnp.zeros((R, D), jnp.float32)
    for rows in tiles:
        ffn = ffn_out[rows, :]
        ffn_low = ffn.astype(low)
        grad_low = cotangent_ref[rows, :]
        zed = contract(ffn_low, down, 1, 1)
        cdf, density = normal_parts(zed)
        hidden = (zed * cdf).astype(low)
        added = jnp.dot(hidden, up, preferred_element_type=jnp.float32)
        layer_out_ref[rows, :] = (mid_rows[rows, :] + ffn + added).astype(low)
        zed_grad = contract(grad_low, up, 1, 1) * (cdf + zed * density)
        zed_low = zed_grad.astype(low)
        ffn_grad_ref[rows, :] = (
            grad_low.astype(jnp.float32)
            + jnp.dot(zed_low, down, preferred_element_type=jnp.float32)
        ).astype(low)
        up_grad = up_grad + contract(hidden, grad_low, 0, 0)
        down_grad = down_grad + contract(zed_low, ffn_low, 0, 0)

    left_grad = exact(down_grad, right, 1, 1)
    wide_grad = exact(up_grad, tall, 1, 1)
    grads = [
        take_back(left_grad * shorts[0], mix_down) + take_back(wide_grad * shorts[1], mix_up),
        take_long(exact(left, down_grad, 0, 0)),
        take_back(left_grad * mixes[0], short_place),
        take_back(wide_grad * mixes[1], short_place),
        take_long(exact(wide, up_grad, 0, 0)),
    ]
    lines = -(-NADAPT // TILE)
    grads.append(jnp.zeros((1, lines * TILE - NADAPT), jnp.float32))
    grads = jnp.concatenate(grads, axis=1)
    small_part_ref[...] = jnp.zeros(small_part_ref.shape, jnp.float32)
    for part in range(lines):
        line_at = 2 * D // TILE + part
        small_part_ref[line_at : line_at + 1, :] = grads[:, TILE * part : TILE * (part + 1)]

    for which in range(2):
        save_feed(tensor_count - 1, which).wait()
        for group in range(tensor_count):
            save_group(which, group).wait()
    for role in range(len(bufs)):
        share(role, 0).wait_send()
        if role < 3:
            share(role, 1).wait_send()
            share(role, 2).wait_send()


def front(
    mine,
    slot_place,
    spread_place,
    orders,
    local_sizes,
    tokens,
    small_row,
    bucket_place,
    segments,
    cotangent,
):
    dp_count, tensor_count = lax.axis_size("dp"), lax.axis_size("tensor")
    sizes = [order.shape[1] for order in orders]
    pair_rows = spread_place.shape[1]
    low = jnp.bfloat16
    dma = pltpu.SemaphoreType.DMA
    roles = len(sizes)
    whole = pl.BlockSpec(memory_space=pltpu.VMEM)
    away = pl.BlockSpec(memory_space=pl.ANY)
    return pl.pallas_call(
        functools.partial(front_kernel, sizes),
        in_specs=[whole] * 12,
        out_specs=[away] * 5 + [whole] * 3 + [away] * 3 + [whole] * 5,
        out_shape=[jax.ShapeDtypeStruct((tensor_count, size, D), low) for size in sizes]
        + [
            jax.ShapeDtypeStruct((tensor_count, sizes[0], SEQ), low),
            jax.ShapeDtypeStruct((H * HS, SEQ), low),
            jax.ShapeDtypeStruct((H, 1, SEQ), jnp.float32),
            jax.ShapeDtypeStruct((SEQ, D), low),
            jax.ShapeDtypeStruct((H, SEQ, SEQ), low),
            jax.ShapeDtypeStruct((SEQ, FF), low),
            jax.ShapeDtypeStruct((SEQ, FF), low),
        ]
        + [jax.ShapeDtypeStruct((SEQ, D), low)] * 4
        + [jax.ShapeDtypeStruct((TABLE_ROW, TILE), jnp.float32)],
        scratch_shapes=[
            pltpu.VMEM((tensor_count, sizes[0], D), low),
            pltpu.VMEM((tensor_count, sizes[0], SEQ), low),
            pltpu.VMEM((2, 2, sizes[2], D), low),
            pltpu.VMEM((SEQ, D), jnp.float32),
            pltpu.VMEM((SEQ, D), jnp.float32),
        ]
        + [
            pltpu.VMEM((size, dp_count * local), low)
            for size, local in zip(sizes, local_sizes)
        ]
        + [
            pltpu.VMEM((dp_count, pair_rows, D), low),
            pltpu.VMEM((dp_count, pair_rows, D), low),
            pltpu.VMEM((sum(local_sizes), D), low),
            pltpu.VMEM((H, 1, 2 * SEQ), jnp.float32),
            pltpu.VMEM((SEQ, TILE), jnp.float32),
        ]
        + [pltpu.VMEM((dp_count, size, D), low) for size in local_sizes + local_sizes[3:]]
        + [pltpu.VMEM((local_sizes[3], D), low)]
        + [pltpu.VMEM((size, D), low) for size in sizes[1:] + sizes[3:]]
        + [
            pltpu.VMEM((WINDOW, TILE), jnp.float32),
            pltpu.VMEM((SEQ, QUERY_TILE), jnp.float32),
            pltpu.VMEM((2, SEQ, SEQ), low),
            dma((dp_count,)),
            dma((dp_count,)),
            dma,
            dma,
            dma((roles + 1, dp_count // 2)),
            dma((roles + 1, dp_count // 2)),
            dma((roles + 1, dp_count // 2)),
            dma((roles + 1, dp_count // 2)),
            dma((roles + 1, 3)),
            dma((roles + 1, 3)),
            dma((roles + 1,)),
            dma((2,)),
            dma((2, tensor_count)),
            dma((2, 2)),
            dma((tensor_count,)),
        ],
        compiler_params=pltpu.CompilerParams(
            collective_id=1, has_side_effects=True, vmem_limit_bytes=63 * 1024 * 1024
        ),
        cost_estimate=pl.CostEstimate(
            flops=10 * H * SEQ * SEQ * 256 + 4 * SEQ * FF * D,
            bytes_accessed=96 * 1024 * 1024,
            transcendentals=H * SEQ * SEQ + 2 * SEQ * FF,
        ),
        name="front",
    )(
        mine,
        slot_place,
        spread_place,
        *orders,
        tokens,
        small_row,
        bucket_place,
        segments.astype(jnp.float32)[None, :],
        cotangent,
    )


def attend_head_back(
    query_rows,
    key_rows,
    value_rows,
    exp_ref,
    attended,
    scale,
    attended_grad,
    window,
    score_grads,
    store,
):
    scaled = attended_grad.astype(jnp.float32) * scale
    delta = jnp.sum(scaled * attended.astype(jnp.float32), axis=0, keepdims=True)
    scaled_low = scaled.astype(jnp.bfloat16)
    delta_high = delta.astype(jnp.bfloat16).astype(jnp.float32)
    delta_rest = delta - delta_high
    place = lax.broadcasted_iota(jnp.int32, (16, SEQ), 0)
    extra = jnp.where(
        place == 0,
        jnp.broadcast_to(-delta_high, (16, SEQ)),
        jnp.where(place == 1, jnp.broadcast_to(-delta_rest, (16, SEQ)), 0.0),
    ).astype(jnp.bfloat16)
    grads = jnp.concatenate([scaled_low, extra], axis=0)
    values = jnp.concatenate([value_rows, jnp.ones((16, SEQ), jnp.bfloat16)], axis=0).T
    window[...] = jnp.zeros_like(window)
    for q0 in range(0, SEQ, BACK_QUERY_TILE):
        total = jnp.zeros((HS, BACK_QUERY_TILE), jnp.float32)
        for k0 in range(0, SEQ, BACK_KEY_TILE):
            centered = jnp.dot(
                values[k0 : k0 + BACK_KEY_TILE],
                grads[:, q0 : q0 + BACK_QUERY_TILE],
                preferred_element_type=jnp.float32,
            )
            score_grad = centered * exp_ref[
                k0 : k0 + BACK_KEY_TILE, q0 : q0 + BACK_QUERY_TILE
            ].astype(jnp.float32)
            for l0 in range(0, BACK_QUERY_TILE, TILE):
                start = SEQ - TILE - (q0 + l0) + k0
                window[start : start + BACK_KEY_TILE, :] += score_grad[:, l0 : l0 + TILE]
            score_low = score_grad.astype(jnp.bfloat16)
            score_grads[k0 : k0 + BACK_KEY_TILE, q0 : q0 + BACK_QUERY_TILE] = score_low
            total = total + jnp.dot(
                key_rows[:, k0 : k0 + BACK_KEY_TILE], score_low, preferred_element_type=jnp.float32
            )
        store(0, q0, total.astype(jnp.bfloat16))
    queries = query_rows.T
    scaled_rows = scaled_low.T
    for k0 in range(0, SEQ, BACK_KEY_TILE):
        key_grad = jnp.dot(
            score_grads[k0 : k0 + BACK_KEY_TILE, :], queries, preferred_element_type=jnp.float32
        )
        value_grad = jnp.dot(
            exp_ref[k0 : k0 + BACK_KEY_TILE, :], scaled_rows, preferred_element_type=jnp.float32
        )
        store(1, k0, key_grad.T.astype(jnp.bfloat16))
        store(2, k0, value_grad.T.astype(jnp.bfloat16))
    pieces = [jnp.zeros((1, TILE), jnp.float32)] * (2 * SEQ // TILE)
    for tile in range(WINDOW // TILE):
        base = WINDOW - TILE * tile
        block = window[TILE * tile : TILE * (tile + 1), :]
        folded = jnp.concatenate([jnp.zeros((TILE, TILE), jnp.float32), block], axis=1)
        rows = TILE // 2
        while rows >= 1:
            folded = folded[:rows] + pltpu.roll(folded[rows:], 2 * TILE - rows, 1)
            rows //= 2
        pieces[base // TILE - 1] += folded[:, :TILE]
        pieces[base // TILE] += folded[:, TILE:]
    return jnp.concatenate(pieces, axis=1)


def back_kernel(
    sizes,
    ffn_grad_ref,
    normed_two_ref,
    mid_ref,
    cotangent_ref,
    w_out_ref,
    activ_ref,
    slope_ref,
    w_in_ref,
    w_down_ref,
    projected_ref,
    exp_ref,
    w_qkv_ref,
    tokens_ref,
    normed_one_ref,
    attended_ref,
    scale_ref,
    params_ref,
    small_ref,
    bucket_ref,
    place_qkv_ref,
    place_out_ref,
    place_in_ref,
    place_down_ref,
    spread_place_ref,
    slot_place_ref,
    owned_ref,
    input_grad_ref,
    small_total_ref,
    proj_grad_ref,
    bucket_hot,
    weights,
    proj,
    proj_grad,
    normed_grad,
    window,
    score_grads,
    exp_stage,
    row_grads,
    normed,
    attended_grad,
    odd_out,
    odd_in,
    odd_down,
    zero_qkv,
    zero_out,
    zero_in,
    zero_down,
    two_qkv,
    two_out,
    two_in,
    two_down,
    core_one_qkv,
    core_one_out,
    core_one_in,
    core_one_down,
    core_three_qkv,
    core_three_out,
    core_three_in,
    core_three_down,
    far_qkv,
    far_out,
    far_in,
    far_down,
    got_qkv,
    got_out,
    got_in,
    got_down,
    side_qkv,
    side_out,
    side_down,
    end_mine,
    end_far,
    spread,
    sent,
    received,
    small_own,
    small_tensor,
    small_dp,
    core_send,
    core_recv,
    far_send,
    far_recv,
    side_send,
    side_recv,
    line_send,
    line_recv,
    end_send,
    end_recv,
    back_send,
    back_recv,
    small_send,
    small_recv,
    load_sem,
    exp_sem,
    proj_sem,
    again_sem,
):
    dp_count, pair_rows = spread_place_ref.shape
    hidden_rows = w_in_ref.shape[1]
    tensor_count = w_qkv_ref.shape[0]
    heads = scale_ref.shape[0]
    group_heads = heads // tensor_count
    head_rows = group_heads * HS
    dp_pos, tensor_pos = lax.axis_index("dp"), lax.axis_index("tensor")
    core_pos = tensor_pos + 1 - 2 * lax.rem(tensor_pos, 2)
    far_pos = lax.rem(tensor_pos + 2, tensor_count)
    core_peer, far_peer = (dp_pos, core_pos), (dp_pos, far_pos)
    zeros = (zero_qkv, zero_out, zero_in, zero_down)
    twos = (two_qkv, two_out, two_in, two_down)
    core_ones = (core_one_qkv, core_one_out, core_one_in, core_one_down)
    core_threes = (core_three_qkv, core_three_out, core_three_in, core_three_down)
    fars = (far_qkv, far_out, far_in, far_down)
    gots = (got_qkv, got_out, got_in, got_down)
    side_got = (side_qkv, side_out, far_in, side_down)
    places = (place_qkv_ref, place_out_ref, place_in_ref, place_down_ref)
    offsets = [sum(got.shape[1] for got in gots[:role]) for role in range(len(gots))]
    low = jnp.bfloat16

    def up(m):
        return lax.rem(dp_pos + m, dp_count)

    def down(m):
        return lax.rem(dp_pos + dp_count - m, dp_count)

    def each_peer(run):
        def step(m, carry):
            run(m)
            return carry

        lax.fori_loop(1, dp_count, step, 0)

    def tensor_peer(m):
        return (dp_pos, lax.rem(tensor_pos + m, tensor_count))

    barrier = pltpu.get_barrier_semaphore()

    def greet(m):
        pl.semaphore_signal(barrier, inc=1, device_id=(up(m), tensor_pos), device_id_type=MESH)

    each_peer(greet)
    for m in range(1, tensor_count):
        pl.semaphore_signal(barrier, inc=1, device_id=tensor_peer(m), device_id_type=MESH)

    def load_exp(head, slot):
        return pltpu.make_async_copy(exp_ref.at[head], exp_stage.at[slot], exp_sem.at[slot])

    def load_proj(group):
        return pltpu.make_async_copy(projected_ref.at[group], proj, proj_sem.at[0])

    def save_proj(group):
        return pltpu.make_async_copy(proj_grad, proj_grad_ref.at[group], proj_sem.at[1])

    def reload(group, which):
        odd = group % 2
        source, target = (
            (proj_grad_ref.at[group], proj if odd else proj_grad),
            (w_qkv_ref.at[group], zero_qkv if odd else weights),
        )[which]
        return pltpu.make_async_copy(source, target, again_sem.at[odd, which])

    def load(which, group=0):
        columns = pl.ds(pl.multiple_of(group * hidden_rows, TILE), hidden_rows)
        source, target = (
            (lambda: activ_ref.at[:, columns], lambda: exp_stage.at[0, :, pl.ds(0, hidden_rows)]),
            (lambda: slope_ref.at[:, columns], lambda: exp_stage.at[1, :, pl.ds(0, hidden_rows)]),
            (lambda: w_in_ref.at[group], lambda: received.at[pl.ds(0, hidden_rows)]),
            (lambda: w_down_ref.at[group], lambda: sent.at[pl.ds(0, hidden_rows)]),
            (lambda: ffn_grad_ref, lambda: row_grads),
            (lambda: normed_two_ref, lambda: normed),
            (lambda: mid_ref, lambda: exp_stage.at[0, :, pl.ds(0, D)]),
            (lambda: cotangent_ref, lambda: exp_stage.at[1, :, pl.ds(0, D)]),
            (lambda: w_out_ref, lambda: sent.at[pl.ds(0, D)]),
            (lambda: normed_one_ref, lambda: normed),
            (lambda: tokens_ref, lambda: exp_stage.at[0, :, pl.ds(0, D)]),
        )[which]
        return pltpu.make_async_copy(source(), target(), load_sem.at[which])

    def core_copy(role, which):
        half = which // 2
        if role == 0:
            src = (odd_in, odd_down)[half].at[pl.ds(0, sizes[0])]
        else:
            src = (None, odd_out.at[half], odd_in, odd_down)[role]
        target = (core_ones if which == 1 else core_threes)[role].at[pl.ds(0, sizes[role])]
        return pltpu.make_async_remote_copy(
            src,
            target,
            core_send.at[role, half],
            core_recv.at[role, half],
            device_id=core_peer,
            device_id_type=MESH,
        )

    def far_copy(role):
        return pltpu.make_async_remote_copy(
            twos[role],
            fars[role],
            far_send.at[role],
            far_recv.at[role],
            device_id=far_peer,
            device_id_type=MESH,
        )

    line = dp_count // 2
    line_pos, side = lax.div(dp_pos, 2), lax.rem(dp_pos, 2)
    side_peer = (dp_pos + 1 - 2 * side, tensor_pos)

    def each_line(run):
        def step(m, carry):
            run(m)
            return carry

        lax.fori_loop(1, line, step, 0)

    def leaving(role, far):
        return core_ones[role] if role == 2 and not far else core_threes[role]

    def side_copy(role, far=0):
        count = gots[role].shape[1] * line
        return pltpu.make_async_remote_copy(
            leaving(role, far).at[pl.ds(count, count)],
            side_got[role].at[pl.ds(count * far, count)],
            side_send.at[role, far],
            side_recv.at[role, far],
            device_id=side_peer,
            device_id_type=MESH,
        )

    def line_copy(role, m, far=0):
        count = gots[role].shape[1]
        return pltpu.make_async_remote_copy(
            leaving(role, far).at[pl.ds(pl.multiple_of(m * count, 16), count)],
            gots[role].at[far * line + m],
            line_send.at[role, far * line + m],
            line_recv.at[role, far * line + m],
            device_id=(lax.rem(line_pos + m, line) * 2 + side, tensor_pos),
            device_id_type=MESH,
        )

    def end_copy():
        return pltpu.make_async_remote_copy(
            end_mine, end_far, end_send, end_recv, device_id=far_peer, device_id_type=MESH
        )

    def send_far(role):
        core_copy(role, 3).wait_recv()
        count = twos[role].shape[0]
        twos[role][...] = (
            twos[role][...].astype(jnp.float32)
            + core_threes[role][0:count, :].astype(jnp.float32)
        ).astype(low)
        far_copy(role).start()

    def scatter(role, far, total):
        count = gots[role].shape[1]
        for r0 in range(0, dp_count * count, 384):
            r1 = min(r0 + 384, dp_count * count)
            hot = one_hot(places[role][...] - r0, (r1 - r0, sizes[role]), 0)
            leaving(role, far)[r0:r1, :] = jnp.dot(
                hot, total, preferred_element_type=jnp.float32
            ).astype(low)
        side_copy(role, far).start()

    def send_deal(role):
        core_copy(role, 1).wait_recv()
        far_copy(role).wait_recv()
        total = (
            zeros[role][...].astype(jnp.float32)
            + core_ones[role][...].astype(jnp.float32)
            + fars[role][...].astype(jnp.float32)
        ).astype(low)
        scatter(role, 0, total)

    def send_half(role, far):
        core_copy(role, 3 if far else 1).wait_recv()
        count = sizes[role]
        mine = (twos if far else zeros)[role][...].astype(jnp.float32)
        core = (core_threes if far else core_ones)[role][0:count, :].astype(jnp.float32)
        scatter(role, far, (mine + core).astype(low))

    def pass_line(role, far=0):
        side_copy(role, far).wait()
        count = gots[role].shape[1] * line
        leaving(role, far)[0:count, :] = (
            leaving(role, far)[0:count, :].astype(jnp.float32)
            + side_got[role][count * far : count * (far + 1), :].astype(jnp.float32)
        ).astype(low)
        each_line(lambda m: line_copy(role, m, far).start())

    def line_sum(role, far=0):
        each_line(lambda m: line_copy(role, m, far).wait())
        total = leaving(role, far)[0 : gots[role].shape[1], :].astype(jnp.float32)
        for m in range(1, line):
            total = total + gots[role][far * line + m].astype(jnp.float32)
        return total

    def finish_deal(role):
        count = gots[role].shape[1]
        spread[offsets[role] : offsets[role] + count, :] = line_sum(role).astype(low)

    def finish_far():
        end_mine[...] = line_sum(2, 1).astype(low)
        end_copy().start()

    def finish_near():
        total = line_sum(2)
        end_copy().wait()
        count = gots[2].shape[1]
        spread[offsets[2] : offsets[2] + count, :] = (
            total + end_far[...].astype(jnp.float32)
        ).astype(low)

    for which in (4, 5):
        load(which).start()
    for which in range(4):
        load(which, tensor_count - 1).start()
    bucket_hot[...] = one_hot(bucket_ref[...], (NB, 2 * SEQ), 0)
    normed_grad[...] = jnp.zeros_like(normed_grad)
    small_own[0:TABLE_ROW, :] = small_ref[...]
    small_own[TABLE_ROW:SMALL_ROWS, :] = jnp.zeros((SMALL_ROWS - TABLE_ROW, TILE), jnp.float32)
    pl.semaphore_wait(barrier, dp_count + tensor_count - 2)
    for which in (4, 5):
        load(which).wait()
    row_tiles = [slice(r0, r0 + 256) for r0 in range(0, SEQ, 256)]
    pre_grad = score_grads

    def feed_step(i, carry):
        group = tensor_count - 1 - i

        def load_next(which):
            @pl.when(group > 0)
            def _():
                load(which, group - 1).start()

        load(3, group).wait()
        load(1, group).wait()
        for rows in row_tiles:
            grad = contract(row_grads[rows, :], sent[0:hidden_rows, :], 1, 1)
            grad = grad * exp_stage[1, rows, 0:hidden_rows].astype(jnp.float32)
            pre_grad[rows, 0:hidden_rows] = grad.astype(low)
        load_next(3)
        load_next(1)
        load(2, group).wait()
        for rows in row_tiles:
            normed_grad[rows, :] += jnp.dot(
                pre_grad[rows, 0:hidden_rows],
                received[0:hidden_rows, :],
                preferred_element_type=jnp.float32,
            )
        load_next(2)

        @pl.when(group == 2)
        def _():
            for role in (3, 2):
                core_copy(role, 3).wait_send()

        @pl.when(group == 0)
        def _():
            for role in (3, 2):
                core_copy(role, 1).wait_send()

        load(0, group).wait()
        for c0 in range(0, hidden_rows, 256):
            columns = slice(c0, c0 + 256)
            odd_down[columns, :] = jnp.dot(
                exp_stage[0, :, columns].T, row_grads[...], preferred_element_type=jnp.float32
            ).astype(low)
        load_next(0)

        @pl.when(group == 3)
        def _():
            core_copy(3, 3).start()

        @pl.when(group == 2)
        def _():
            two_down[...] = odd_down[...]
            send_far(3)

        @pl.when(group == 1)
        def _():
            core_copy(3, 1).start()

        @pl.when(group == 0)
        def _():
            zero_down[...] = odd_down[...]

        for c0 in range(0, hidden_rows, 256):
            columns = slice(c0, c0 + 256)
            odd_in[columns, :] = jnp.dot(
                pre_grad[:, columns].T, normed[...], preferred_element_type=jnp.float32
            ).astype(low)

        @pl.when(group == 3)
        def _():
            core_copy(2, 3).start()

        @pl.when(group == 2)
        def _():
            two_in[...] = odd_in[...]
            send_half(2, 1)

        @pl.when(group == 1)
        def _():
            core_copy(2, 1).start()

        @pl.when(group == 0)
        def _():
            zero_in[...] = odd_in[...]

        return carry

    lax.fori_loop(0, tensor_count, feed_step, 0)
    for which in (6, 7, 8, 9):
        load(which).start()
    send_half(2, 0)
    pass_line(2, 1)
    for which in (6, 7, 8):
        load(which).wait()
    gain_grad = jnp.zeros((1, D), jnp.float32)
    for r0 in range(0, SEQ, 128):
        rows = slice(r0, r0 + 128)
        mid = exp_stage[0, rows, 0:D].astype(jnp.float32)
        grads = normed_grad[rows, :]
        inverse = lax.rsqrt(jnp.mean(mid * mid, axis=1, keepdims=True) + norm_epsilon)
        scaled = mid * inverse
        gain_grad = gain_grad + jnp.sum(grads * scaled, axis=0, keepdims=True)
        grads = grads * params_ref[:, D : 2 * D]
        inner = jnp.mean(grads * scaled, axis=1, keepdims=True)
        row_grads[rows, :] = (
            exp_stage[1, rows, 0:D].astype(jnp.float32) + inverse * (grads - scaled * inner)
        ).astype(low)
    for part in range(D // TILE):
        line_at = D // TILE + part
        small_own[line_at : line_at + 1, :] = gain_grad[:, TILE * part : TILE * (part + 1)]
    normed_grad[...] = jnp.zeros_like(normed_grad)
    load_exp(heads - group_heads, 0).start()
    load_proj(tensor_count - 1).start()
    for group, target in enumerate((zero_out, odd_out.at[0], two_out, odd_out.at[1])):
        rows = slice(group * head_rows, (group + 1) * head_rows)
        target[...] = jnp.dot(
            attended_ref[rows, :], row_grads[...], preferred_element_type=jnp.float32
        ).astype(low)
    core_copy(1, 3).start()
    core_copy(1, 1).start()
    for r0 in range(0, D, 256):
        rows = slice(r0, r0 + 256)
        attended_grad[rows, :] = contract(sent[rows, :], row_grads[...], 1, 1).astype(low)
    load(9).wait()

    def head_step(i, carry):
        group = tensor_count - 1 - lax.div(i, group_heads)
        part_head = lax.rem(i, group_heads)
        head = group * group_heads + part_head
        slot = lax.rem(i, 2)

        @pl.when(i == 1)
        def _():
            send_deal(3)

        @pl.when(i == 2)
        def _():
            send_far(1)

        @pl.when(i == 3)
        def _():
            pass_line(2, 0)

        @pl.when(i == 5)
        def _():
            send_deal(1)

        @pl.when(i == 6)
        def _():
            send_far(0)
            pass_line(3)

        @pl.when(i == 8)
        def _():
            pass_line(1)

        @pl.when((part_head == 0) & (i > 0))
        def _():
            save_proj(group + 1).wait()

        @pl.when(part_head == 0)
        def _():
            load_proj(group).wait()

        @pl.when(i + 1 < heads)
        def _():
            later = i + 1
            later_group = tensor_count - 1 - lax.div(later, group_heads)
            later_head = later_group * group_heads + lax.rem(later, group_heads)
            load_exp(later_head, lax.rem(later, 2)).start()

        load_exp(head, slot).wait()

        def rows(part):
            return pl.ds(pl.multiple_of(part * head_rows + part_head * HS, HS), HS)

        def store(part, column, value):
            proj_grad[rows(part), column : column + value.shape[1]] = value

        here = pl.ds(pl.multiple_of(head * HS, HS), HS)
        offset_grad = attend_head_back(
            proj[rows(0), :],
            proj[rows(1), :],
            proj[rows(2), :],
            exp_stage.at[slot],
            attended_ref[here, :],
            scale_ref[head],
            attended_grad[here, :],
            window,
            score_grads,
            store,
        )
        place = (
            true_group((tensor_pos, core_pos, far_pos), group, tensor_count) * group_heads + part_head
        )
        high = offset_grad.astype(low)
        rest = (offset_grad - high.astype(jnp.float32)).astype(low)
        both = jnp.concatenate([high, rest] + [jnp.zeros_like(high)] * 6, axis=0)
        sums = contract(both, bucket_hot[...], 1, 1)
        row = lax.broadcasted_iota(jnp.int32, (SMALL_ROWS - TABLE_ROW, TILE), 0)
        found = jnp.concatenate(
            [sums[0:1] + sums[1:2], jnp.zeros((1, TILE - NB), jnp.float32)], axis=1
        )
        small_own[TABLE_ROW:SMALL_ROWS, :] += jnp.where(
            row == place,
            jnp.broadcast_to(found, (SMALL_ROWS - TABLE_ROW, TILE)),
            0.0,
        )

        @pl.when(part_head == group_heads - 1)
        def _():
            @pl.when(group > 0)
            def _():
                load_proj(group - 1).start()

            def weight_grad(target):
                for r0 in range(0, 3 * head_rows, head_rows):
                    target[r0 : r0 + head_rows, :] = jnp.dot(
                        proj_grad[r0 : r0 + head_rows, :],
                        normed[...],
                        preferred_element_type=jnp.float32,
                    ).astype(low)

            @pl.when(group == 3)
            def _():
                weight_grad(odd_down)
                core_copy(0, 3).start()

            @pl.when(group == 2)
            def _():
                weight_grad(two_qkv)

            @pl.when(group == 1)
            def _():
                weight_grad(odd_in)
                core_copy(0, 1).start()

            @pl.when(group == 0)
            def _():
                weight_grad(zero_qkv)

            save_proj(group).start()

        return carry

    lax.fori_loop(0, heads, head_step, 0)

    load(10).start()
    save_proj(0).wait()
    reload(0, 1).start()
    reload(1, 0).start()
    send_deal(0)
    reload(1, 1).start()
    for group in range(tensor_count):
        if group > 0:
            reload(group, 0).wait()
        reload(group, 1).wait()
        part, rows_in = (proj, zero_qkv) if group % 2 else (proj_grad, weights)
        for r0 in range(0, SEQ, 256):
            normed_grad[r0 : r0 + 256, :] += jnp.dot(
                part[:, r0 : r0 + 256].T, rows_in[...], preferred_element_type=jnp.float32
            )
        if group + 2 < tensor_count:
            reload(group + 2, 0).start()
            reload(group + 2, 1).start()
    pass_line(0)
    load(10).wait()

    gain_grad = jnp.zeros((1, D), jnp.float32)
    for r0 in range(0, SEQ, 128):
        values = exp_stage[0, r0 : r0 + 128, 0:D].astype(jnp.float32)
        grads = normed_grad[r0 : r0 + 128, :]
        inverse = lax.rsqrt(jnp.mean(values * values, axis=1, keepdims=True) + norm_epsilon)
        scaled = values * inverse
        gain_grad = gain_grad + jnp.sum(grads * scaled, axis=0, keepdims=True)
        grads = grads * params_ref[:, 0:D]
        inner = jnp.mean(grads * scaled, axis=1, keepdims=True)
        row_grads[r0 : r0 + 128, :] = (
            row_grads[r0 : r0 + 128, :].astype(jnp.float32) + inverse * (grads - scaled * inner)
        ).astype(low)
    for part in range(D // TILE):
        small_own[part : part + 1, :] = gain_grad[:, TILE * part : TILE * (part + 1)]

    save_rows = pltpu.make_async_copy(row_grads, input_grad_ref, exp_sem.at[1])
    save_rows.start()

    def small_copy(stage, m):
        if stage == 0:
            src, target, peer = small_own, small_tensor.at[tensor_pos], tensor_peer(m)
        else:
            src, target, peer = small_total_ref, small_dp.at[dp_pos], (up(m), tensor_pos)
        return pltpu.make_async_remote_copy(
            src,
            target,
            small_send.at[stage, m],
            small_recv.at[stage, m],
            device_id=peer,
            device_id_type=MESH,
        )

    for m in range(1, tensor_count):
        small_copy(0, m).start()
    small_tensor[tensor_pos] = small_own[...]
    for m in range(1, tensor_count):
        small_copy(0, m).wait()
    total = small_tensor[0]
    for m in range(1, tensor_count):
        total = total + small_tensor[m]
    small_total_ref[...] = total
    each_peer(lambda m: small_copy(1, m).start())
    finish_far()
    finish_near()
    finish_deal(3)
    small_dp[dp_pos] = small_total_ref[...]
    each_peer(lambda m: small_copy(1, m).wait())
    total = small_dp[0]
    for m in range(1, dp_count):
        total = total + small_dp[m]
    small_total_ref[...] = total
    finish_deal(1)
    finish_deal(0)

    place = jnp.concatenate([spread_place_ref[m : m + 1, :] for m in range(dp_count)], axis=1)
    hot = one_hot(place, (spread.shape[0], dp_count * pair_rows), 0)
    sent[0 : dp_count * pair_rows, :] = contract(hot, spread[...], 0, 0).astype(low)

    def back_copy(m):
        here = pl.ds(pl.multiple_of(m * pair_rows, 16), pair_rows)
        return pltpu.make_async_remote_copy(
            sent.at[here],
            received.at[here],
            back_send.at[m],
            back_recv.at[m],
            device_id=(down(m), tensor_pos),
            device_id_type=MESH,
        )

    each_peer(lambda m: back_copy(m).start())
    received[0:pair_rows, :] = sent[0:pair_rows, :]
    each_peer(lambda m: back_copy(m).wait())
    hot = one_hot(slot_place_ref[...], (dp_count * pair_rows, owned_ref.shape[0]), 0)
    owned_ref[...] = contract(hot, received[0 : dp_count * pair_rows, :], 0, 0)
    save_rows.wait()
    for role in range(len(gots)):
        if role < 2:
            core_copy(role, 1).wait_send()
            core_copy(role, 3).wait_send()
        if role != 2:
            far_copy(role).wait_send()


def back(
    feed_parts,
    projected,
    exp_scores,
    w_qkv,
    tokens,
    normed_one,
    attended,
    scale,
    small_row,
    small,
    bucket_place,
    places,
    local_sizes,
    spread_place,
    slot_place,
):
    dp_count, tensor_count = lax.axis_size("dp"), lax.axis_size("tensor")
    sizes = [place.shape[1] for place in places]
    capacity, pair_rows = slot_place.shape[1], spread_place.shape[1]
    low = jnp.bfloat16
    dma = pltpu.SemaphoreType.DMA
    roles = len(sizes)
    whole = pl.BlockSpec(memory_space=pltpu.VMEM)
    away = pl.BlockSpec(memory_space=pl.ANY)
    parts = [pltpu.VMEM((size, D), low) for size in sizes]
    padded = [
        pltpu.VMEM((max(dp_count * size, full), D), low) for size, full in zip(local_sizes, sizes)
    ]
    return pl.pallas_call(
        functools.partial(back_kernel, sizes),
        in_specs=[away] * 14 + [whole] * 11,
        out_specs=[whole, away, whole, away],
        out_shape=[
            jax.ShapeDtypeStruct((capacity, D), jnp.float32),
            jax.ShapeDtypeStruct((SEQ, D), low),
            jax.ShapeDtypeStruct((SMALL_ROWS, TILE), jnp.float32),
            jax.ShapeDtypeStruct((tensor_count, sizes[0], SEQ), low),
        ],
        scratch_shapes=[
            pltpu.VMEM((NB, 2 * SEQ), low),
            pltpu.VMEM((sizes[0], D), low),
            pltpu.VMEM((sizes[0], SEQ), low),
            pltpu.VMEM((sizes[0], SEQ), low),
            pltpu.VMEM((SEQ, D), jnp.float32),
            pltpu.VMEM((WINDOW, TILE), jnp.float32),
            pltpu.VMEM((SEQ, SEQ), low),
            pltpu.VMEM((2, SEQ, SEQ), low),
            pltpu.VMEM((SEQ, D), low),
            pltpu.VMEM((SEQ, D), low),
            pltpu.VMEM((D, SEQ), low),
            pltpu.VMEM((2, sizes[1], D), low),
            pltpu.VMEM((sizes[2], D), low),
            pltpu.VMEM((sizes[3], D), low),
        ]
        + parts
        + parts
        + parts[:2]
        + padded[2:3]
        + parts[3:]
        + padded
        + parts[:2]
        + [pltpu.VMEM((dp_count * local_sizes[2], D), low)]
        + parts[3:]
        + [
            pltpu.VMEM((dp_count if role == 2 else dp_count // 2, size, D), low)
            for role, size in enumerate(local_sizes)
        ]
        + [pltpu.VMEM((dp_count // 2 * local_sizes[role], D), low) for role in (0, 1, 3)]
        + [
            pltpu.VMEM((local_sizes[2], D), low),
            pltpu.VMEM((local_sizes[2], D), low),
            pltpu.VMEM((sum(local_sizes), D), low),
            pltpu.VMEM((max(dp_count * pair_rows, D), D), low),
            pltpu.VMEM((max(dp_count * pair_rows, D), D), low),
            pltpu.VMEM((SMALL_ROWS, TILE), jnp.float32),
            pltpu.VMEM((tensor_count, SMALL_ROWS, TILE), jnp.float32),
            pltpu.VMEM((dp_count, SMALL_ROWS, TILE), jnp.float32),
            dma((roles, 2)),
            dma((roles, 2)),
            dma((roles,)),
            dma((roles,)),
            dma((roles, 2)),
            dma((roles, 2)),
            dma((roles, dp_count)),
            dma((roles, dp_count)),
            dma,
            dma,
            dma((dp_count,)),
            dma((dp_count,)),
            dma((2, max(dp_count, tensor_count))),
            dma((2, max(dp_count, tensor_count))),
            dma((11,)),
            dma((2,)),
            dma((2,)),
            dma((2, 2)),
        ],
        compiler_params=pltpu.CompilerParams(
            collective_id=2, has_side_effects=True, vmem_limit_bytes=63 * 1024 * 1024
        ),
        cost_estimate=pl.CostEstimate(
            flops=16 * H * SEQ * SEQ * 256 + 8 * SEQ * FF * D,
            bytes_accessed=96 * 1024 * 1024,
            transcendentals=0,
        ),
        name="back",
    )(
        *feed_parts,
        projected,
        exp_scores,
        w_qkv,
        tokens,
        normed_one,
        attended,
        scale,
        small_row,
        small,
        bucket_place,
        *places,
        spread_place,
        slot_place,
    )


def adamw(weights, grads, first, second, step):
    first_new = beta_first * first + (1.0 - beta_first) * grads
    second_new = beta_second * second + (1.0 - beta_second) * grads * grads
    first_hat = first_new / (1.0 - beta_first**step)
    second_hat = second_new / (1.0 - beta_second**step)
    weights_new = weights - rate_per_step * step * (
        first_hat / (jnp.sqrt(second_hat) + adam_epsilon) + weight_decay * weights
    )
    return (weights_new, first_new, second_new)


def per_device(
    tokens,
    cotangent,
    segment_ids,
    buckets,
    owners,
    master,
    first_moment,
    second_moment,
    small_params,
    small_first,
    small_second,
    adapter_ema,
    step_count,
):
    dp_count = lax.axis_size("dp")
    tensor_count = lax.axis_size("tensor")
    capacity = master.shape[1]
    group_heads = H // tensor_count
    head_rows = group_heads * HS
    hidden_rows = FF // tensor_count
    tensor_pos = lax.axis_index("tensor")
    sizes = [3 * head_rows, head_rows, hidden_rows, hidden_rows]
    local_sizes = [-(-size // dp_count // 16) * 16 for size in sizes]
    pair_rows = -(-((capacity + len(sizes) * (dp_count - 1)) // dp_count) // 16) * 16
    slot_place, spread_place, orders, places = plan(
        owners, sizes, local_sizes, capacity, pair_rows
    )

    bucket_place = jnp.concatenate([jnp.full((1,), -1, jnp.int32), buckets[::-1]])[None, :]
    segments = lax.dynamic_slice_in_dim(segment_ids, tensor_pos * SEQ, SEQ, 0)
    outs = front(
        master[0],
        slot_place,
        spread_place,
        orders,
        local_sizes,
        tokens,
        small_params[None, :],
        bucket_place,
        segments,
        cotangent,
    )
    w_qkv, w_out, w_in, w_down, projected, attended, scale, normed_one, exp_scores = outs[:9]
    activ, slope, normed_two, mid, layer_out, ffn_grad, small_local = outs[9:]
    owned_grad, input_grad, small_total, _ = back(
        (
            ffn_grad,
            normed_two,
            mid,
            cotangent,
            w_out.reshape(D, D),
            activ,
            slope,
            w_in,
            w_down,
        ),
        projected,
        exp_scores,
        w_qkv,
        tokens,
        normed_one,
        attended,
        scale,
        small_params[None, :],
        small_local,
        bucket_place,
        places,
        local_sizes,
        spread_place,
        slot_place,
    )
    small_total = jnp.concatenate(
        [
            small_total[:TABLE_ROW].reshape(-1)[: 2 * D + NADAPT],
            small_total[TABLE_ROW : TABLE_ROW + H, :NB].T.reshape(-1),
        ]
    )
    own_filled = (slot_place[0] >= 0).astype(jnp.float32)[:, None]
    step = step_count[0].astype(jnp.float32)
    owned_grad = owned_grad * own_filled
    new_master, new_first, new_second = adamw(
        master[0], owned_grad, first_moment[0], second_moment[0], step
    )
    new_master = new_master * own_filled
    new_first = new_first * own_filled
    new_second = new_second * own_filled
    small_new, small_first_new, small_second_new = adamw(
        small_params, small_total, small_first, small_second, step
    )
    ema_new = average_keep * adapter_ema + (1.0 - average_keep) * small_new[2 * D : 2 * D + NADAPT]
    return (
        layer_out,
        input_grad,
        owned_grad[None],
        new_first[None],
        new_second[None],
        new_master[None],
        new_master.astype(jnp.bfloat16)[None],
        small_total,
        small_first_new,
        small_second_new,
        small_new,
        ema_new,
    )


def solution(mesh):
    token_spec = P(("dp", "tensor"), None)
    owner_spec = P("tensor", "dp", None)
    return jax.shard_map(
        per_device,
        mesh=mesh,
        in_specs=(token_spec, token_spec, P("dp"), P(), P())
        + (owner_spec,) * 3
        + (P(),) * 5,
        out_specs=(token_spec,) * 2 + (owner_spec,) * 5 + (P(),) * 5,
        check_vma=False,
    )
```

```python
import functools
import math

import jax
import jax.numpy as jnp
from jax import lax
from jax.experimental import pallas as pl
from jax.experimental.pallas import tpu as pltpu
from jax.sharding import PartitionSpec as P

D = 768
H = 12
HS = 64
FF = 3072
NB = 32
R = 48
PHM = 4
SEQ = 1024
NADAPT = 1696

highest = lax.Precision.HIGHEST
norm_epsilon = 1e-06
beta_first = 0.5
beta_second = 0.5
adam_epsilon = 1e-08
rate_per_step = 0.01
weight_decay = 0.1
average_keep = 0.75
masked_score = -1000000000.0

TILE = 128
WINDOW = 2 * SEQ - TILE
QUERY_TILE = 512
KEY_TILE = 512
BACK_QUERY_TILE = 512
BACK_KEY_TILE = 1024
VMEM_LIMIT = 48 * 1024 * 1024
MESH = pl.DeviceIdType.MESH
SMALL_ROWS = 48
TABLE_ROW = 32


def exact(left, right, left_dim, right_dim):
    return lax.dot_general(
        left,
        right,
        (((left_dim,), (right_dim,)), ((), ())),
        precision=highest,
        preferred_element_type=jnp.float32,
    )


def grid(shape, dim, parts):
    rest = lax.broadcasted_iota(jnp.int32, shape, dim).astype(jnp.float32)
    found = []
    for part in parts:
        high = jnp.floor((rest + 0.5) * (1.0 / part))
        found.append(high)
        rest = rest - part * high
    return found + [rest]


def zero_one(hit):
    return jnp.where(hit, 1.0, 0.0)


def adapter_places():
    rank = R // PHM
    outer = PHM * PHM
    block, inner = grid((R, PHM * outer), 0, (rank,))
    _, first, second = grid((R, PHM * outer), 1, (outer, PHM))
    term, left_at, right_at = grid((PHM * outer, outer), 0, (outer, PHM))
    column, last = grid((PHM * outer, outer), 1, (PHM,))
    mix_down = (
        zero_one(second == block),
        zero_one((term == column) & (left_at == last)),
    )
    mix_up = (
        zero_one(first == block),
        zero_one((term == column) & (right_at == last)),
    )
    _, inner = grid((R, R), 0, (rank,))
    _, short = grid((R, R), 1, (rank,))
    term, _ = grid((R, outer), 0, (rank,))
    column, _ = grid((R, outer), 1, (PHM,))
    side = (zero_one(inner == short), zero_one(term == column))
    return mix_down, mix_up, side


def lay_out(row, places):
    keep, gather = places
    return exact(keep * row, gather, 1, 0)


def take_back(values, places):
    keep, gather = places
    return jnp.sum(keep * exact(values, gather, 1, 1), axis=0, keepdims=True)


def lay_long(row):
    part = D // PHM
    term, block = grid((PHM * PHM, D), 0, (PHM,))
    place, _ = grid((PHM * PHM, D), 1, (part,))
    total = jnp.zeros((PHM * PHM, D), jnp.float32)
    for i in range(PHM):
        tiled = jnp.concatenate([row[:, part * i : part * (i + 1)]] * PHM, axis=1)
        total = jnp.where((term == i) & (place == block), tiled, total)
    return total


def take_long(values):
    part = D // PHM
    _, block = grid((PHM * PHM, D), 0, (PHM,))
    place, _ = grid((PHM * PHM, D), 1, (part,))
    values = jnp.where(place == block, values, 0.0)
    pieces = []
    for i in range(PHM):
        row = jnp.sum(values[PHM * i : PHM * (i + 1), :], axis=0, keepdims=True)
        pieces.append(sum(row[:, part * a : part * (a + 1)] for a in range(PHM)))
    return jnp.concatenate(pieces, axis=1)


def normal_parts(values):
    size = jnp.abs(values)
    shrink = 1.0 / (1.0 + (0.3275911 * math.sqrt(0.5)) * size)
    bell = jnp.exp(-0.5 * values * values)
    series = 0.5 * 1.061405429
    for term in (-1.453152027, 1.421413741, -0.284496736, 0.254829592):
        series = series * shrink + 0.5 * term
    tail = series * shrink * bell
    return jnp.where(values >= 0.0, 1.0 - tail, tail), bell * (1.0 / math.sqrt(2.0 * math.pi))


def contract(left, right, left_dim, right_dim):
    return lax.dot_general(
        left,
        right,
        (((left_dim,), (right_dim,)), ((), ())),
        preferred_element_type=jnp.float32,
    )


def bias_window(bias, window):
    for tile in range(WINDOW // TILE):
        base = WINDOW - TILE * tile
        row = jnp.broadcast_to(bias[:, base - TILE : base + TILE], (TILE, 2 * TILE))
        rolled = pltpu.roll(row, TILE, 1, stride=1, stride_axis=0)
        window[TILE * tile : TILE * (tile + 1), :] = rolled[:, :TILE]


def attend_head(
    query_rows, key_rows, value_rows, segment_keys_ref, segment_queries_ref, window, scores, exp_ref
):
    keys = key_rows.T
    values = jnp.concatenate([value_rows, jnp.ones((16, SEQ), jnp.bfloat16)], axis=0)
    outs, scales = [], []
    for q0 in range(0, SEQ, QUERY_TILE):
        queries = query_rows[:, q0 : q0 + QUERY_TILE]
        peak = jnp.full((8, QUERY_TILE), -jnp.inf, jnp.float32)
        for k0 in range(0, SEQ, KEY_TILE):
            raw = jnp.dot(keys[k0 : k0 + KEY_TILE], queries, preferred_element_type=jnp.float32)
            parts = []
            for l0 in range(0, QUERY_TILE, TILE):
                start = SEQ - TILE - (q0 + l0) + k0
                same_doc = (
                    segment_keys_ref[k0 : k0 + KEY_TILE, :]
                    == segment_queries_ref[:, q0 + l0 : q0 + l0 + TILE]
                )
                part = jnp.where(
                    same_doc,
                    raw[:, l0 : l0 + TILE] + window[start : start + KEY_TILE, :],
                    masked_score,
                )
                scores[k0 : k0 + KEY_TILE, l0 : l0 + TILE] = part
                parts.append(part)
            whole = jnp.concatenate(parts, axis=1)
            peak = jnp.maximum(peak, jnp.max(whole.reshape(KEY_TILE // 8, 8, QUERY_TILE), axis=0))
        peak = jnp.max(peak, axis=0, keepdims=True)
        total = jnp.zeros((HS + 16, QUERY_TILE), jnp.float32)
        for k0 in range(0, SEQ, KEY_TILE):
            exp_scores = jnp.exp(scores[k0 : k0 + KEY_TILE, :] - peak).astype(jnp.bfloat16)
            exp_ref[k0 : k0 + KEY_TILE, q0 : q0 + QUERY_TILE] = exp_scores
            total = total + jnp.dot(
                values[:, k0 : k0 + KEY_TILE], exp_scores, preferred_element_type=jnp.float32
            )
        scale = 1.0 / total[HS : HS + 1]
        scales.append(scale)
        outs.append((total[:HS] * scale).astype(jnp.bfloat16))
    return jnp.concatenate(outs, axis=1), jnp.concatenate(scales, axis=1)


def one_hot(place, shape, dim):
    hit = lax.broadcasted_iota(jnp.int32, shape, dim) == place
    return jnp.where(hit, 1.0, 0.0).astype(jnp.bfloat16)


def plan_kernel(dp_count, pair_rows, local_sizes, *refs):
    roles = len(local_sizes)
    owners_ref, slot_ref, spread_ref = refs[:3]
    order_refs, place_refs = refs[3 : roles + 3], refs[roles + 3 :]
    dp_pos = lax.axis_index("dp").astype(jnp.float32)

    def quotient(values):
        return jnp.floor((values + 0.5) * (1.0 / dp_count))

    def remainder(values):
        return values - dp_count * quotient(values)

    line = dp_count // 2

    def halve(values):
        return jnp.floor((values + 0.5) * 0.5)

    def around(values):
        return values - line * jnp.floor((values + 0.5) * (1.0 / line))

    whole = owners_ref[...].astype(jnp.float32)
    whole = jnp.concatenate([whole[i : i + 1, :] for i in range(whole.shape[0])], axis=1)
    owners, low = [], 0
    for ref in order_refs:
        owners.append(whole[:, low : low + ref.shape[1]])
        low += ref.shape[1]

    def stats(who):
        counts = [
            jnp.sum(jnp.where(row == who, 1.0, 0.0), axis=1, keepdims=True) for row in owners
        ]
        starts = [jnp.sum(jnp.where(row < who, 1.0, 0.0), axis=1, keepdims=True) for row in owners]
        return counts, starts

    def hits(first, number, target):
        return quotient(first + number - 1.0 - target) - quotient(first - 1.0 - target)

    counts, starts = stats(jnp.full((1, 1), dp_pos))
    slot = lax.broadcasted_iota(jnp.int32, slot_ref.shape, 1).astype(jnp.float32)
    found = jnp.full(slot_ref.shape, -1.0)
    low = jnp.zeros((1, 1), jnp.float32)
    for role in range(roles):
        rank = slot - low
        target = remainder(starts[role] + rank)
        place = quotient(rank)
        for other in range(role):
            place = place + hits(starts[other], counts[other], target)
        found = jnp.where(
            (rank >= 0.0) & (rank < counts[role]),
            remainder(target - dp_pos) * pair_rows + place,
            found,
        )
        low = low + counts[role]
    slot_ref[...] = found.astype(jnp.int32)

    column = lax.broadcasted_iota(jnp.int32, (dp_count, 1), 0).astype(jnp.float32)
    counts, starts = stats(remainder(dp_pos - column))
    pair = lax.broadcasted_iota(jnp.int32, spread_ref.shape, 1).astype(jnp.float32)
    found = jnp.full(spread_ref.shape, -1.0)
    passed = jnp.zeros((dp_count, 1), jnp.float32)
    for role in range(roles):
        number = hits(starts[role], counts[role], dp_pos)
        first = starts[role] + remainder(dp_pos - starts[role])
        rank = pair - passed
        local = sum(local_sizes[:role]) + quotient(first) + rank
        found = jnp.where((rank >= 0.0) & (rank < number), local, found)
        passed = passed + number
    spread_ref[...] = found.astype(jnp.int32)

    counts, starts = stats(column)
    for role in range(roles):
        width = owners[role].shape[1]
        before = starts[role]
        for c0 in range(0, width, TILE):
            c1 = min(c0 + TILE, width)
            hot = jnp.where(owners[role][:, c0:c1] == column, 1.0, 0.0)
            shape = (c1 - c0, c1 - c0)
            above = lax.broadcasted_iota(jnp.int32, shape, 0) < lax.broadcasted_iota(
                jnp.int32, shape, 1
            )
            rank = jnp.dot(
                hot.astype(jnp.bfloat16),
                jnp.where(above, 1.0, 0.0).astype(jnp.bfloat16),
                preferred_element_type=jnp.float32,
            )
            number = jnp.sum(hot * (rank + before), axis=0, keepdims=True)
            before = before + jnp.sum(hot, axis=1, keepdims=True)
            target, row = remainder(number), quotient(number)
            side = jnp.abs(target - 2.0 * halve(target) - dp_pos + 2.0 * halve(dp_pos)) * line
            ahead = halve(target) - halve(dp_pos)
            order = (around(0.0 - ahead) + side) * local_sizes[role] + row
            place = (around(ahead) + side) * local_sizes[role] + row
            order_refs[role][:, c0:c1] = order.astype(jnp.int32)
            place_refs[role][:, c0:c1] = place.astype(jnp.int32)


def plan(owners, sizes, local_sizes, capacity, pair_rows):
    dp_count = lax.axis_size("dp")
    outs = pl.pallas_call(
        functools.partial(plan_kernel, dp_count, pair_rows, local_sizes),
        out_shape=[
            jax.ShapeDtypeStruct((1, capacity), jnp.int32),
            jax.ShapeDtypeStruct((dp_count, pair_rows), jnp.int32),
        ]
        + [jax.ShapeDtypeStruct((1, size), jnp.int32) for size in sizes] * 2,
        name="plan",
    )(owners.reshape(-1, TILE))
    return outs[0], outs[1], outs[2 : 2 + len(sizes)], outs[2 + len(sizes) :]


def true_group(positions, group, tensor_count):
    flips = positions + (tensor_count - 1 - positions[0],)
    found = flips[0]
    for g in range(1, tensor_count):
        found = found + (flips[g] - flips[0]) * (
            lax.div(group + tensor_count - g, tensor_count)
            - lax.div(group + tensor_count - g - 1, tensor_count)
        )
    return found


def front_kernel(
    sizes,
    mine_ref,
    slot_place_ref,
    spread_place_ref,
    order_qkv_ref,
    order_out_ref,
    order_in_ref,
    order_down_ref,
    tokens_ref,
    small_ref,
    bucket_ref,
    segment_ref,
    cotangent_ref,
    w_qkv_out,
    w_out_ref,
    w_in_ref,
    w_down_ref,
    projected_out,
    attended_ref,
    scale_ref,
    normed_ref,
    exp_ref,
    activ_ref,
    slope_ref,
    normed_two_ref,
    mid_ref,
    layer_out_ref,
    ffn_grad_ref,
    small_part_ref,
    w_qkv_ref,
    projected_ref,
    feed_weights,
    ffn_out,
    mid_rows,
    hot_qkv,
    hot_out,
    hot_in,
    hot_down,
    sent,
    received,
    spread,
    bias,
    segment_keys,
    buf_qkv,
    buf_out,
    buf_in,
    buf_down,
    buf_far,
    far_spread,
    stage_out,
    stage_in,
    stage_down,
    stage_far,
    window,
    scores,
    exp_stage,
    deal_send,
    deal_recv,
    far_send,
    far_recv,
    line_send,
    line_recv,
    side_send,
    side_recv,
    group_send,
    group_recv,
    local_sem,
    exp_sem,
    save_sem,
    feed_sem,
    out_sem,
):
    dp_count, pair_rows = sent.shape[0], sent.shape[1]
    tensor_count = w_qkv_ref.shape[0]
    heads = scale_ref.shape[0]
    low = jnp.bfloat16
    group_heads = heads // tensor_count
    head_rows = group_heads * HS
    dp_pos, tensor_pos = lax.axis_index("dp"), lax.axis_index("tensor")
    core_pos = tensor_pos + 1 - 2 * lax.rem(tensor_pos, 2)
    far_pos = lax.rem(tensor_pos + 2, tensor_count)
    core_peer, far_peer = (dp_pos, core_pos), (dp_pos, far_pos)

    def dp_peer(m):
        return (lax.rem(dp_pos + m, dp_count), tensor_pos)

    def each_peer(run):
        def step(m, carry):
            run(m)
            return carry

        lax.fori_loop(1, dp_count, step, 0)

    barrier = pltpu.get_barrier_semaphore()

    def greet(m):
        pl.semaphore_signal(barrier, inc=1, device_id=dp_peer(m), device_id_type=MESH)

    each_peer(greet)
    for peer in (core_peer, far_peer):
        pl.semaphore_signal(barrier, inc=1, device_id=peer, device_id_type=MESH)

    mine = mine_ref[...].astype(jnp.bfloat16)
    hot = one_hot(slot_place_ref[...], (dp_count * pair_rows, mine.shape[0]), 0)
    sent[...] = (
        jnp.dot(hot, mine, preferred_element_type=jnp.float32)
        .astype(jnp.bfloat16)
        .reshape(dp_count, pair_rows, D)
    )
    pl.semaphore_wait(barrier, dp_count + 1)

    def deal(m):
        return pltpu.make_async_remote_copy(
            sent.at[m],
            received.at[m],
            deal_send.at[m],
            deal_recv.at[m],
            device_id=dp_peer(m),
            device_id_type=MESH,
        )

    each_peer(lambda m: deal(m).start())
    received[0] = sent[0]

    for r0 in range(0, SEQ, 128):
        values = tokens_ref[r0 : r0 + 128, :].astype(jnp.float32)
        inverse = lax.rsqrt(jnp.mean(values * values, axis=1, keepdims=True) + norm_epsilon)
        normed_ref[r0 : r0 + 128, :] = (values * inverse * small_ref[:, 0:D]).astype(jnp.bfloat16)
    flat = small_ref[...][:, 2 * D + NADAPT :]
    entry = lax.broadcasted_iota(jnp.int32, (16, NB * H), 1)
    bucket = jnp.floor((entry.astype(jnp.float32) + 0.5) * (1.0 / H))
    head_of = entry.astype(jnp.float32) - H * bucket
    line_of = lax.broadcasted_iota(jnp.int32, (16, NB * H), 0).astype(jnp.float32)
    rest = jnp.where(head_of == line_of, jnp.broadcast_to(flat, (16, NB * H)), 0.0)
    entry = lax.broadcasted_iota(jnp.int32, (NB * H, 2 * SEQ), 0).astype(jnp.float32)
    bucket = jnp.floor((entry + 0.5) * (1.0 / H))
    hot = jnp.where(bucket == bucket_ref[...].astype(jnp.float32), 1.0, 0.0).astype(jnp.bfloat16)
    biases = jnp.zeros((rest.shape[0], 2 * SEQ), jnp.float32)
    for _ in range(3):
        part = rest.astype(jnp.bfloat16)
        rest = rest - part.astype(jnp.float32)
        biases = biases + jnp.dot(part, hot, preferred_element_type=jnp.float32)
    for head in range(heads):
        bias[head] = biases[head : head + 1, :]
    segment_keys[...] = jnp.broadcast_to(segment_ref[...], (TILE, SEQ)).T
    hots = (hot_qkv, hot_out, hot_in, hot_down, hot_down)
    for hot, place in zip(hots, (order_qkv_ref, order_out_ref, order_in_ref, order_down_ref)):
        hot[...] = one_hot(place[...], (hot.shape[1], hot.shape[0]), 0).T

    row = small_ref[...]
    starts = [2 * D]
    for width in (PHM**3, D, R, R, D):
        starts.append(starts[-1] + width)
    mix, down_long, down_short, up_short, up_long = [
        row[:, low_at:high_at] for low_at, high_at in zip(starts[:-1], starts[1:])
    ]
    mix_down, mix_up, short_place = adapter_places()
    mixes = (lay_out(mix, mix_down), lay_out(mix, mix_up))
    shorts = (lay_out(down_short, short_place), lay_out(up_short, short_place))
    left, wide = mixes[0] * shorts[0], mixes[1] * shorts[1]
    right, tall = lay_long(down_long), lay_long(up_long)
    down = exact(left, right, 1, 0).astype(low)
    up = exact(wide, tall, 1, 0).astype(low)

    each_peer(lambda m: deal(m).wait())
    rows = spread.shape[0]
    place = jnp.concatenate([spread_place_ref[m : m + 1, :] for m in range(dp_count)], axis=1)
    hot = one_hot(place, (rows, dp_count * pair_rows), 0)
    spread[...] = jnp.dot(
        hot, received[...].reshape(dp_count * pair_rows, D), preferred_element_type=jnp.float32
    ).astype(jnp.bfloat16)

    bufs = (buf_qkv, buf_out, buf_in, buf_down, buf_far)
    stages = (w_qkv_ref.at[0], stage_out, stage_in, stage_down, stage_far)
    finals = (w_qkv_ref, w_out_ref, w_in_ref, w_down_ref, w_down_ref)
    sizes = tuple(sizes) + (sizes[3],)
    offsets = [sum(buf.shape[1] for buf in bufs[:role]) for role in range(4)]
    line = dp_count // 2
    line_pos, side = lax.div(dp_pos, 2), lax.rem(dp_pos, 2)
    side_peer = (dp_pos + 1 - 2 * side, tensor_pos)

    def far_exchange():
        return pltpu.make_async_remote_copy(
            spread.at[pl.ds(offsets[3], far_spread.shape[0])],
            far_spread,
            far_send,
            far_recv,
            device_id=far_peer,
            device_id_type=MESH,
        )

    def block(role):
        if role == 4:
            return far_spread
        return spread.at[pl.ds(offsets[role], bufs[role].shape[1])]

    def along_line(role, m):
        return pltpu.make_async_remote_copy(
            block(role),
            bufs[role].at[m],
            line_send.at[role, m],
            line_recv.at[role, m],
            device_id=(lax.rem(line_pos + m, line) * 2 + side, tensor_pos),
            device_id_type=MESH,
        )

    def to_side(role, m):
        return pltpu.make_async_remote_copy(
            bufs[role].at[m],
            bufs[role].at[line + m],
            side_send.at[role, m],
            side_recv.at[role, m],
            device_id=side_peer,
            device_id_type=MESH,
        )

    def each_line(first, run):
        def step(m, carry):
            run(m)
            return carry

        lax.fori_loop(first, line, step, 0)

    def start_line(role):
        if role == 4:
            far_exchange().wait()
        each_line(1, lambda m: along_line(role, m).start())
        bufs[role][0] = block(role)[...]
        to_side(role, 0).start()

    def start_side(role):
        def step(m):
            along_line(role, m).wait()
            to_side(role, m).start()

        each_line(1, step)

    def order(role):
        each_line(0, lambda m: to_side(role, m).wait())
        count = bufs[role].shape[1]
        source = bufs[role][...].reshape(dp_count * count, D)
        step = 384 if sizes[role] > 576 else sizes[role]
        for r0 in range(0, sizes[role], step):
            r1 = min(r0 + step, sizes[role])
            stages[role][r0:r1, :] = jnp.dot(
                hots[role][r0:r1, :], source, preferred_element_type=jnp.float32
            ).astype(jnp.bfloat16)

    def share(role, part):
        if role == 4:
            src, slot, peer = stages[role], 3, core_peer
        else:
            src, slot, peer = (
                (stages[role], 1, core_peer),
                (stages[role], 2, far_peer),
                (finals[role].at[2], 3, core_peer),
            )[part]
        return pltpu.make_async_remote_copy(
            src,
            finals[role].at[slot],
            group_send.at[role, part],
            group_recv.at[role, part],
            device_id=peer,
            device_id_type=MESH,
        )

    def keep(role):
        slot = 2 if role == 4 else 0
        return pltpu.make_async_copy(stages[role], finals[role].at[slot], local_sem.at[role])

    def start_share(role):
        order(role)
        share(role, 0).start()
        if role < 3:
            share(role, 1).start()
        if role > 0:
            keep(role).start()

    def forward(role):
        share(role, 1).wait_recv()
        share(role, 2).start()

    far_exchange().start()
    start_line(0)
    start_side(0)
    start_share(0)
    start_line(1)
    start_line(2)

    def save_group(which, group):
        source, target = ((projected_ref, projected_out), (w_qkv_ref, w_qkv_out))[which]
        return pltpu.make_async_copy(
            source.at[group], target.at[group], save_sem.at[which, group]
        )

    def true_head(group, head):
        return true_group((tensor_pos, core_pos, far_pos), group, tensor_count) * group_heads + head

    def head_step(i, carry):
        group, head = lax.div(i, group_heads), lax.rem(i, group_heads)

        @pl.when(i == 1)
        def _():
            start_side(1)

        @pl.when(i == 3)
        def _():
            start_share(1)

        @pl.when(i == 5)
        def _():
            start_side(2)
            start_line(3)
            start_line(4)

        @pl.when(i == 10)
        def _():
            start_share(2)

        @pl.when(i == group_heads)
        def _():
            share(0, 0).wait_recv()

        @pl.when(i == 2 * group_heads)
        def _():
            forward(0)

        @pl.when(i == 3 * group_heads)
        def _():
            share(0, 2).wait_recv()
            forward(1)

        @pl.when(i == 11)
        def _():
            start_side(3)

        @pl.when(head == 0)
        def _():
            projected_ref[group] = contract(w_qkv_ref[group], normed_ref[...], 1, 1).astype(
                jnp.bfloat16
            )
            save_group(0, group).start()
            save_group(1, group).start()

        def head_part(part):
            start = pl.multiple_of(part * head_rows + head * HS, HS)
            return projected_ref[group, pl.ds(start, HS), :]

        slot = lax.rem(i, 2)

        def save(head_index, slot):
            return pltpu.make_async_copy(
                exp_stage.at[slot], exp_ref.at[head_index], exp_sem.at[slot]
            )

        @pl.when(i >= 2)
        def _():
            save(i - 2, slot).wait()

        bias_window(bias[true_head(group, head)], window)
        attended, scale = attend_head(
            head_part(0),
            head_part(1),
            head_part(2),
            segment_keys,
            segment_ref,
            window,
            scores,
            exp_stage.at[slot],
        )
        attended_ref[pl.ds(pl.multiple_of(i * HS, HS), HS), :] = attended
        scale_ref[i] = scale
        save(i, slot).start()
        return carry

    lax.fori_loop(0, heads, head_step, 0)
    for i in (heads - 2, heads - 1):
        pltpu.make_async_copy(exp_stage.at[i % 2], exp_ref.at[i], exp_sem.at[i % 2]).wait()
    start_side(4)

    def load_feed(group, slot, which):
        return pltpu.make_async_copy(
            (w_in_ref, w_down_ref)[which].at[group],
            feed_weights.at[slot, which],
            feed_sem.at[slot, which],
        )

    def load_out(group):
        return pltpu.make_async_copy(
            w_out_ref.at[group],
            feed_weights.at[1, 0, pl.ds(group * head_rows, head_rows)],
            out_sem.at[group],
        )

    keep(1).wait()
    share(1, 0).wait_recv()
    share(1, 2).wait_recv()
    for group in range(tensor_count):
        load_out(group).start()
    keep(2).wait()
    load_feed(0, 0, 0).start()
    for group in range(tensor_count):
        load_out(group).wait()
    tiles = [slice(r0, r0 + 256) for r0 in range(0, SEQ, 256)]
    for rows in tiles:
        attn = jnp.dot(
            attended_ref[:, rows].T, feed_weights[1, 0], preferred_element_type=jnp.float32
        )
        mid = tokens_ref[rows, :].astype(jnp.float32) + attn
        mid_rows[rows, :] = mid
        mid_ref[rows, :] = mid.astype(low)
        inverse = lax.rsqrt(jnp.mean(mid * mid, axis=1, keepdims=True) + norm_epsilon)
        normed_two_ref[rows, :] = (mid * inverse * small_ref[:, D : 2 * D]).astype(low)
        ffn_out[rows, :] = jnp.zeros((256, D), jnp.float32)
    hidden_rows = w_in_ref.shape[1]

    def save_feed(group, which):
        columns = pl.ds(pl.multiple_of(group * hidden_rows, TILE), hidden_rows)
        return pltpu.make_async_copy(
            exp_stage.at[which, :, pl.ds(0, hidden_rows)],
            (activ_ref, slope_ref)[which].at[:, columns],
            exp_sem.at[which],
        )

    def feed_step(group, carry):
        slot = lax.rem(group, 2)
        load_feed(group, slot, 0).wait()

        @pl.when(group > 0)
        def _():
            for which in range(2):
                save_feed(group - 1, which).wait()

        for rows in tiles:
            pre = contract(normed_two_ref[rows, :], feed_weights[slot, 0], 1, 1)
            cdf, density = normal_parts(pre)
            exp_stage[0, rows, 0:hidden_rows] = (pre * cdf).astype(low)
            exp_stage[1, rows, 0:hidden_rows] = (cdf + pre * density).astype(low)
        for which in range(2):
            save_feed(group, which).start()

        @pl.when(group == 0)
        def _():
            share(2, 0).wait_recv()

        @pl.when(group == 1)
        def _():
            start_share(3)
            start_share(4)
            forward(2)

        @pl.when(group == 2)
        def _():
            share(2, 2).wait_recv()

        @pl.when(group + 1 < tensor_count)
        def _():
            load_feed(group + 1, 1 - slot, 0).start()

        return carry

    lax.fori_loop(0, tensor_count, feed_step, 0)

    def load_activ(group, slot):
        columns = pl.ds(pl.multiple_of(group * hidden_rows, TILE), hidden_rows)
        return pltpu.make_async_copy(
            activ_ref.at[:, columns],
            exp_stage.at[slot, :, pl.ds(0, hidden_rows)],
            exp_sem.at[slot],
        )

    keep(3).wait()
    load_feed(0, 0, 1).start()
    share(3, 0).wait_recv()
    load_feed(1, 1, 1).start()
    for which in range(2):
        save_feed(tensor_count - 1, which).wait()
    load_activ(0, 0).start()
    load_activ(1, 1).start()

    def down_step(group, carry):
        slot = lax.rem(group, 2)
        load_feed(group, slot, 1).wait()
        load_activ(group, slot).wait()
        for rows in tiles:
            ffn_out[rows, :] += jnp.dot(
                exp_stage[slot, rows, 0:hidden_rows],
                feed_weights[slot, 1],
                preferred_element_type=jnp.float32,
            )

        @pl.when(group == 0)
        def _():
            keep(4).wait()

        @pl.when(group == 1)
        def _():
            share(4, 0).wait_recv()

        @pl.when(group + 2 < tensor_count)
        def _():
            load_feed(group + 2, slot, 1).start()
            load_activ(group + 2, slot).start()

        return carry

    lax.fori_loop(0, tensor_count, down_step, 0)

    down_grad = jnp.zeros((R, D), jnp.float32)
    up_grad = jnp.zeros((R, D), jnp.float32)
    for rows in tiles:
        ffn = ffn_out[rows, :]
        ffn_low = ffn.astype(low)
        grad_low = cotangent_ref[rows, :]
        zed = contract(ffn_low, down, 1, 1)
        cdf, density = normal_parts(zed)
        hidden = (zed * cdf).astype(low)
        added = jnp.dot(hidden, up, preferred_element_type=jnp.float32)
        layer_out_ref[rows, :] = (mid_rows[rows, :] + ffn + added).astype(low)
        zed_grad = contract(grad_low, up, 1, 1) * (cdf + zed * density)
        zed_low = zed_grad.astype(low)
        ffn_grad_ref[rows, :] = (
            grad_low.astype(jnp.float32)
            + jnp.dot(zed_low, down, preferred_element_type=jnp.float32)
        ).astype(low)
        up_grad = up_grad + contract(hidden, grad_low, 0, 0)
        down_grad = down_grad + contract(zed_low, ffn_low, 0, 0)

    left_grad = exact(down_grad, right, 1, 1)
    wide_grad = exact(up_grad, tall, 1, 1)
    grads = [
        take_back(left_grad * shorts[0], mix_down) + take_back(wide_grad * shorts[1], mix_up),
        take_long(exact(left, down_grad, 0, 0)),
        take_back(left_grad * mixes[0], short_place),
        take_back(wide_grad * mixes[1], short_place),
        take_long(exact(wide, up_grad, 0, 0)),
    ]
    lines = -(-NADAPT // TILE)
    grads.append(jnp.zeros((1, lines * TILE - NADAPT), jnp.float32))
    grads = jnp.concatenate(grads, axis=1)
    small_part_ref[...] = jnp.zeros(small_part_ref.shape, jnp.float32)
    for part in range(lines):
        line_at = 2 * D // TILE + part
        small_part_ref[line_at : line_at + 1, :] = grads[:, TILE * part : TILE * (part + 1)]

    for which in range(2):
        for group in range(tensor_count):
            save_group(which, group).wait()
    for role in range(len(bufs)):
        share(role, 0).wait_send()
        if role < 3:
            share(role, 1).wait_send()
            share(role, 2).wait_send()


def front(
    mine,
    slot_place,
    spread_place,
    orders,
    local_sizes,
    tokens,
    small_row,
    bucket_place,
    segments,
    cotangent,
):
    dp_count, tensor_count = lax.axis_size("dp"), lax.axis_size("tensor")
    sizes = [order.shape[1] for order in orders]
    pair_rows = spread_place.shape[1]
    low = jnp.bfloat16
    dma = pltpu.SemaphoreType.DMA
    roles = len(sizes)
    whole = pl.BlockSpec(memory_space=pltpu.VMEM)
    away = pl.BlockSpec(memory_space=pl.ANY)
    return pl.pallas_call(
        functools.partial(front_kernel, sizes),
        in_specs=[whole] * 12,
        out_specs=[away] * 5 + [whole] * 3 + [away] * 3 + [whole] * 5,
        out_shape=[jax.ShapeDtypeStruct((tensor_count, size, D), low) for size in sizes]
        + [
            jax.ShapeDtypeStruct((tensor_count, sizes[0], SEQ), low),
            jax.ShapeDtypeStruct((H * HS, SEQ), low),
            jax.ShapeDtypeStruct((H, 1, SEQ), jnp.float32),
            jax.ShapeDtypeStruct((SEQ, D), low),
            jax.ShapeDtypeStruct((H, SEQ, SEQ), low),
            jax.ShapeDtypeStruct((SEQ, FF), low),
            jax.ShapeDtypeStruct((SEQ, FF), low),
        ]
        + [jax.ShapeDtypeStruct((SEQ, D), low)] * 4
        + [jax.ShapeDtypeStruct((TABLE_ROW, TILE), jnp.float32)],
        scratch_shapes=[
            pltpu.VMEM((tensor_count, sizes[0], D), low),
            pltpu.VMEM((tensor_count, sizes[0], SEQ), low),
            pltpu.VMEM((2, 2, sizes[2], D), low),
            pltpu.VMEM((SEQ, D), jnp.float32),
            pltpu.VMEM((SEQ, D), jnp.float32),
        ]
        + [
            pltpu.VMEM((size, dp_count * local), low)
            for size, local in zip(sizes, local_sizes)
        ]
        + [
            pltpu.VMEM((dp_count, pair_rows, D), low),
            pltpu.VMEM((dp_count, pair_rows, D), low),
            pltpu.VMEM((sum(local_sizes), D), low),
            pltpu.VMEM((H, 1, 2 * SEQ), jnp.float32),
            pltpu.VMEM((SEQ, TILE), jnp.float32),
        ]
        + [pltpu.VMEM((dp_count, size, D), low) for size in local_sizes + local_sizes[3:]]
        + [pltpu.VMEM((local_sizes[3], D), low)]
        + [pltpu.VMEM((size, D), low) for size in sizes[1:] + sizes[3:]]
        + [
            pltpu.VMEM((WINDOW, TILE), jnp.float32),
            pltpu.VMEM((SEQ, QUERY_TILE), jnp.float32),
            pltpu.VMEM((2, SEQ, SEQ), low),
            dma((dp_count,)),
            dma((dp_count,)),
            dma,
            dma,
            dma((roles + 1, dp_count // 2)),
            dma((roles + 1, dp_count // 2)),
            dma((roles + 1, dp_count // 2)),
            dma((roles + 1, dp_count // 2)),
            dma((roles + 1, 3)),
            dma((roles + 1, 3)),
            dma((roles + 1,)),
            dma((2,)),
            dma((2, tensor_count)),
            dma((2, 2)),
            dma((tensor_count,)),
        ],
        compiler_params=pltpu.CompilerParams(
            collective_id=1, has_side_effects=True, vmem_limit_bytes=63 * 1024 * 1024
        ),
        cost_estimate=pl.CostEstimate(
            flops=10 * H * SEQ * SEQ * 256 + 4 * SEQ * FF * D,
            bytes_accessed=96 * 1024 * 1024,
            transcendentals=H * SEQ * SEQ + 2 * SEQ * FF,
        ),
        name="front",
    )(
        mine,
        slot_place,
        spread_place,
        *orders,
        tokens,
        small_row,
        bucket_place,
        segments.astype(jnp.float32)[None, :],
        cotangent,
    )


def attend_head_back(
    query_rows,
    key_rows,
    value_rows,
    exp_ref,
    attended,
    scale,
    attended_grad,
    window,
    score_grads,
    store,
):
    scaled = attended_grad.astype(jnp.float32) * scale
    delta = jnp.sum(scaled * attended.astype(jnp.float32), axis=0, keepdims=True)
    scaled_low = scaled.astype(jnp.bfloat16)
    delta_high = delta.astype(jnp.bfloat16).astype(jnp.float32)
    delta_rest = delta - delta_high
    place = lax.broadcasted_iota(jnp.int32, (16, SEQ), 0)
    extra = jnp.where(
        place == 0,
        jnp.broadcast_to(-delta_high, (16, SEQ)),
        jnp.where(place == 1, jnp.broadcast_to(-delta_rest, (16, SEQ)), 0.0),
    ).astype(jnp.bfloat16)
    grads = jnp.concatenate([scaled_low, extra], axis=0)
    values = jnp.concatenate([value_rows, jnp.ones((16, SEQ), jnp.bfloat16)], axis=0).T
    window[...] = jnp.zeros_like(window)
    for q0 in range(0, SEQ, BACK_QUERY_TILE):
        total = jnp.zeros((HS, BACK_QUERY_TILE), jnp.float32)
        for k0 in range(0, SEQ, BACK_KEY_TILE):
            centered = jnp.dot(
                values[k0 : k0 + BACK_KEY_TILE],
                grads[:, q0 : q0 + BACK_QUERY_TILE],
                preferred_element_type=jnp.float32,
            )
            score_grad = centered * exp_ref[
                k0 : k0 + BACK_KEY_TILE, q0 : q0 + BACK_QUERY_TILE
            ].astype(jnp.float32)
            for l0 in range(0, BACK_QUERY_TILE, TILE):
                start = SEQ - TILE - (q0 + l0) + k0
                window[start : start + BACK_KEY_TILE, :] += score_grad[:, l0 : l0 + TILE]
            score_low = score_grad.astype(jnp.bfloat16)
            score_grads[k0 : k0 + BACK_KEY_TILE, q0 : q0 + BACK_QUERY_TILE] = score_low
            total = total + jnp.dot(
                key_rows[:, k0 : k0 + BACK_KEY_TILE], score_low, preferred_element_type=jnp.float32
            )
        store(0, q0, total.astype(jnp.bfloat16))
    queries = query_rows.T
    scaled_rows = scaled_low.T
    for k0 in range(0, SEQ, BACK_KEY_TILE):
        key_grad = jnp.dot(
            score_grads[k0 : k0 + BACK_KEY_TILE, :], queries, preferred_element_type=jnp.float32
        )
        value_grad = jnp.dot(
            exp_ref[k0 : k0 + BACK_KEY_TILE, :], scaled_rows, preferred_element_type=jnp.float32
        )
        store(1, k0, key_grad.T.astype(jnp.bfloat16))
        store(2, k0, value_grad.T.astype(jnp.bfloat16))
    pieces = [jnp.zeros((1, TILE), jnp.float32)] * (2 * SEQ // TILE)
    for tile in range(WINDOW // TILE):
        base = WINDOW - TILE * tile
        block = window[TILE * tile : TILE * (tile + 1), :]
        folded = jnp.concatenate([jnp.zeros((TILE, TILE), jnp.float32), block], axis=1)
        rows = TILE // 2
        while rows >= 1:
            folded = folded[:rows] + pltpu.roll(folded[rows:], 2 * TILE - rows, 1)
            rows //= 2
        pieces[base // TILE - 1] += folded[:, :TILE]
        pieces[base // TILE] += folded[:, TILE:]
    return jnp.concatenate(pieces, axis=1)


def back_kernel(
    sizes,
    ffn_grad_ref,
    normed_two_ref,
    mid_ref,
    cotangent_ref,
    w_out_ref,
    activ_ref,
    slope_ref,
    w_in_ref,
    w_down_ref,
    projected_ref,
    exp_ref,
    w_qkv_ref,
    tokens_ref,
    normed_one_ref,
    attended_ref,
    scale_ref,
    params_ref,
    small_ref,
    bucket_ref,
    place_qkv_ref,
    place_out_ref,
    place_in_ref,
    place_down_ref,
    spread_place_ref,
    slot_place_ref,
    owned_ref,
    input_grad_ref,
    small_total_ref,
    proj_grad_ref,
    bucket_hot,
    weights,
    proj,
    proj_grad,
    normed_grad,
    window,
    score_grads,
    exp_stage,
    row_grads,
    normed,
    attended_grad,
    odd_out,
    odd_in,
    odd_down,
    zero_qkv,
    zero_out,
    zero_in,
    zero_down,
    two_qkv,
    two_out,
    two_in,
    two_down,
    core_one_qkv,
    core_one_out,
    core_one_in,
    core_one_down,
    core_three_qkv,
    core_three_out,
    core_three_in,
    core_three_down,
    far_qkv,
    far_out,
    far_in,
    far_down,
    got_qkv,
    got_out,
    got_in,
    got_down,
    side_qkv,
    side_out,
    side_down,
    end_mine,
    end_far,
    spread,
    sent,
    received,
    small_own,
    small_tensor,
    small_dp,
    core_send,
    core_recv,
    far_send,
    far_recv,
    side_send,
    side_recv,
    line_send,
    line_recv,
    end_send,
    end_recv,
    back_send,
    back_recv,
    small_send,
    small_recv,
    load_sem,
    exp_sem,
    proj_sem,
    again_sem,
):
    dp_count, pair_rows = spread_place_ref.shape
    hidden_rows = w_in_ref.shape[1]
    tensor_count = w_qkv_ref.shape[0]
    heads = scale_ref.shape[0]
    group_heads = heads // tensor_count
    head_rows = group_heads * HS
    dp_pos, tensor_pos = lax.axis_index("dp"), lax.axis_index("tensor")
    core_pos = tensor_pos + 1 - 2 * lax.rem(tensor_pos, 2)
    far_pos = lax.rem(tensor_pos + 2, tensor_count)
    core_peer, far_peer = (dp_pos, core_pos), (dp_pos, far_pos)
    zeros = (zero_qkv, zero_out, zero_in, zero_down)
    twos = (two_qkv, two_out, two_in, two_down)
    core_ones = (core_one_qkv, core_one_out, core_one_in, core_one_down)
    core_threes = (core_three_qkv, core_three_out, core_three_in, core_three_down)
    fars = (far_qkv, far_out, far_in, far_down)
    gots = (got_qkv, got_out, got_in, got_down)
    side_got = (side_qkv, side_out, far_in, side_down)
    places = (place_qkv_ref, place_out_ref, place_in_ref, place_down_ref)
    offsets = [sum(got.shape[1] for got in gots[:role]) for role in range(len(gots))]
    low = jnp.bfloat16

    def up(m):
        return lax.rem(dp_pos + m, dp_count)

    def down(m):
        return lax.rem(dp_pos + dp_count - m, dp_count)

    def each_peer(run):
        def step(m, carry):
            run(m)
            return carry

        lax.fori_loop(1, dp_count, step, 0)

    def tensor_peer(m):
        return (dp_pos, lax.rem(tensor_pos + m, tensor_count))

    barrier = pltpu.get_barrier_semaphore()

    def greet(m):
        pl.semaphore_signal(barrier, inc=1, device_id=(up(m), tensor_pos), device_id_type=MESH)

    each_peer(greet)
    for m in range(1, tensor_count):
        pl.semaphore_signal(barrier, inc=1, device_id=tensor_peer(m), device_id_type=MESH)

    def load_exp(head, slot):
        return pltpu.make_async_copy(exp_ref.at[head], exp_stage.at[slot], exp_sem.at[slot])

    def load_proj(group):
        return pltpu.make_async_copy(projected_ref.at[group], proj, proj_sem.at[0])

    def save_proj(group):
        return pltpu.make_async_copy(proj_grad, proj_grad_ref.at[group], proj_sem.at[1])

    def reload(group, which):
        odd = group % 2
        source, target = (
            (proj_grad_ref.at[group], proj if odd else proj_grad),
            (w_qkv_ref.at[group], zero_qkv if odd else weights),
        )[which]
        return pltpu.make_async_copy(source, target, again_sem.at[odd, which])

    def load(which, group=0):
        columns = pl.ds(pl.multiple_of(group * hidden_rows, TILE), hidden_rows)
        source, target = (
            (lambda: activ_ref.at[:, columns], lambda: exp_stage.at[0, :, pl.ds(0, hidden_rows)]),
            (lambda: slope_ref.at[:, columns], lambda: exp_stage.at[1, :, pl.ds(0, hidden_rows)]),
            (lambda: w_in_ref.at[group], lambda: received.at[pl.ds(0, hidden_rows)]),
            (lambda: w_down_ref.at[group], lambda: sent.at[pl.ds(0, hidden_rows)]),
            (lambda: ffn_grad_ref, lambda: row_grads),
            (lambda: normed_two_ref, lambda: normed),
            (lambda: mid_ref, lambda: exp_stage.at[0, :, pl.ds(0, D)]),
            (lambda: cotangent_ref, lambda: exp_stage.at[1, :, pl.ds(0, D)]),
            (lambda: w_out_ref, lambda: sent.at[pl.ds(0, D)]),
            (lambda: normed_one_ref, lambda: normed),
            (lambda: tokens_ref, lambda: exp_stage.at[0, :, pl.ds(0, D)]),
        )[which]
        return pltpu.make_async_copy(source(), target(), load_sem.at[which])

    def core_copy(role, which):
        half = which // 2
        if role == 0:
            src = (odd_in, odd_down)[half].at[pl.ds(0, sizes[0])]
        else:
            src = (None, odd_out.at[half], odd_in, odd_down)[role]
        target = (core_ones if which == 1 else core_threes)[role].at[pl.ds(0, sizes[role])]
        return pltpu.make_async_remote_copy(
            src,
            target,
            core_send.at[role, half],
            core_recv.at[role, half],
            device_id=core_peer,
            device_id_type=MESH,
        )

    def far_copy(role):
        return pltpu.make_async_remote_copy(
            twos[role],
            fars[role],
            far_send.at[role],
            far_recv.at[role],
            device_id=far_peer,
            device_id_type=MESH,
        )

    line = dp_count // 2
    line_pos, side = lax.div(dp_pos, 2), lax.rem(dp_pos, 2)
    side_peer = (dp_pos + 1 - 2 * side, tensor_pos)

    def each_line(run):
        def step(m, carry):
            run(m)
            return carry

        lax.fori_loop(1, line, step, 0)

    def leaving(role, far):
        return core_ones[role] if role == 2 and not far else core_threes[role]

    def side_copy(role, far=0):
        count = gots[role].shape[1] * line
        return pltpu.make_async_remote_copy(
            leaving(role, far).at[pl.ds(count, count)],
            side_got[role].at[pl.ds(count * far, count)],
            side_send.at[role, far],
            side_recv.at[role, far],
            device_id=side_peer,
            device_id_type=MESH,
        )

    def line_copy(role, m, far=0):
        count = gots[role].shape[1]
        return pltpu.make_async_remote_copy(
            leaving(role, far).at[pl.ds(pl.multiple_of(m * count, 16), count)],
            gots[role].at[far * line + m],
            line_send.at[role, far * line + m],
            line_recv.at[role, far * line + m],
            device_id=(lax.rem(line_pos + m, line) * 2 + side, tensor_pos),
            device_id_type=MESH,
        )

    def end_copy():
        return pltpu.make_async_remote_copy(
            end_mine, end_far, end_send, end_recv, device_id=far_peer, device_id_type=MESH
        )

    def send_far(role):
        core_copy(role, 3).wait_recv()
        count = twos[role].shape[0]
        twos[role][...] = (
            twos[role][...].astype(jnp.float32)
            + core_threes[role][0:count, :].astype(jnp.float32)
        ).astype(low)
        far_copy(role).start()

    def scatter(role, far, total):
        count = gots[role].shape[1]
        for r0 in range(0, dp_count * count, 384):
            r1 = min(r0 + 384, dp_count * count)
            hot = one_hot(places[role][...] - r0, (r1 - r0, sizes[role]), 0)
            leaving(role, far)[r0:r1, :] = jnp.dot(
                hot, total, preferred_element_type=jnp.float32
            ).astype(low)
        side_copy(role, far).start()

    def send_deal(role):
        core_copy(role, 1).wait_recv()
        far_copy(role).wait_recv()
        total = (
            zeros[role][...].astype(jnp.float32)
            + core_ones[role][...].astype(jnp.float32)
            + fars[role][...].astype(jnp.float32)
        ).astype(low)
        scatter(role, 0, total)

    def send_half(role, far):
        core_copy(role, 3 if far else 1).wait_recv()
        count = sizes[role]
        mine = (twos if far else zeros)[role][...].astype(jnp.float32)
        core = (core_threes if far else core_ones)[role][0:count, :].astype(jnp.float32)
        scatter(role, far, (mine + core).astype(low))

    def pass_line(role, far=0):
        side_copy(role, far).wait()
        count = gots[role].shape[1] * line
        leaving(role, far)[0:count, :] = (
            leaving(role, far)[0:count, :].astype(jnp.float32)
            + side_got[role][count * far : count * (far + 1), :].astype(jnp.float32)
        ).astype(low)
        each_line(lambda m: line_copy(role, m, far).start())

    def line_sum(role, far=0):
        each_line(lambda m: line_copy(role, m, far).wait())
        total = leaving(role, far)[0 : gots[role].shape[1], :].astype(jnp.float32)
        for m in range(1, line):
            total = total + gots[role][far * line + m].astype(jnp.float32)
        return total

    def finish_deal(role):
        count = gots[role].shape[1]
        spread[offsets[role] : offsets[role] + count, :] = line_sum(role).astype(low)

    def finish_far():
        end_mine[...] = line_sum(2, 1).astype(low)
        end_copy().start()

    def finish_near():
        total = line_sum(2)
        end_copy().wait()
        count = gots[2].shape[1]
        spread[offsets[2] : offsets[2] + count, :] = (
            total + end_far[...].astype(jnp.float32)
        ).astype(low)

    for which in (4, 5):
        load(which).start()
    for which in range(4):
        load(which, tensor_count - 1).start()
    bucket_hot[...] = one_hot(bucket_ref[...], (NB, 2 * SEQ), 0)
    normed_grad[...] = jnp.zeros_like(normed_grad)
    small_own[0:TABLE_ROW, :] = small_ref[...]
    small_own[TABLE_ROW:SMALL_ROWS, :] = jnp.zeros((SMALL_ROWS - TABLE_ROW, TILE), jnp.float32)
    pl.semaphore_wait(barrier, dp_count + tensor_count - 2)
    for which in (4, 5):
        load(which).wait()
    row_tiles = [slice(r0, r0 + 256) for r0 in range(0, SEQ, 256)]
    pre_grad = score_grads

    def feed_step(i, carry):
        group = tensor_count - 1 - i

        def load_next(which):
            @pl.when(group > 0)
            def _():
                load(which, group - 1).start()

        load(3, group).wait()
        load(1, group).wait()
        for rows in row_tiles:
            grad = contract(row_grads[rows, :], sent[0:hidden_rows, :], 1, 1)
            grad = grad * exp_stage[1, rows, 0:hidden_rows].astype(jnp.float32)
            pre_grad[rows, 0:hidden_rows] = grad.astype(low)
        load_next(3)
        load_next(1)
        load(2, group).wait()
        for rows in row_tiles:
            normed_grad[rows, :] += jnp.dot(
                pre_grad[rows, 0:hidden_rows],
                received[0:hidden_rows, :],
                preferred_element_type=jnp.float32,
            )
        load_next(2)

        @pl.when(group == 2)
        def _():
            for role in (3, 2):
                core_copy(role, 3).wait_send()

        @pl.when(group == 0)
        def _():
            for role in (3, 2):
                core_copy(role, 1).wait_send()

        load(0, group).wait()
        for c0 in range(0, hidden_rows, 256):
            columns = slice(c0, c0 + 256)
            odd_down[columns, :] = jnp.dot(
                exp_stage[0, :, columns].T, row_grads[...], preferred_element_type=jnp.float32
            ).astype(low)
        load_next(0)

        @pl.when(group == 3)
        def _():
            core_copy(3, 3).start()

        @pl.when(group == 2)
        def _():
            two_down[...] = odd_down[...]
            send_far(3)

        @pl.when(group == 1)
        def _():
            core_copy(3, 1).start()

        @pl.when(group == 0)
        def _():
            zero_down[...] = odd_down[...]

        for c0 in range(0, hidden_rows, 256):
            columns = slice(c0, c0 + 256)
            odd_in[columns, :] = jnp.dot(
                pre_grad[:, columns].T, normed[...], preferred_element_type=jnp.float32
            ).astype(low)

        @pl.when(group == 3)
        def _():
            core_copy(2, 3).start()

        @pl.when(group == 2)
        def _():
            two_in[...] = odd_in[...]
            send_half(2, 1)

        @pl.when(group == 1)
        def _():
            core_copy(2, 1).start()

        @pl.when(group == 0)
        def _():
            zero_in[...] = odd_in[...]

        return carry

    lax.fori_loop(0, tensor_count, feed_step, 0)
    for which in (6, 7, 8, 9):
        load(which).start()
    send_half(2, 0)
    pass_line(2, 1)
    for which in (6, 7, 8):
        load(which).wait()
    gain_grad = jnp.zeros((1, D), jnp.float32)
    for r0 in range(0, SEQ, 128):
        rows = slice(r0, r0 + 128)
        mid = exp_stage[0, rows, 0:D].astype(jnp.float32)
        grads = normed_grad[rows, :]
        inverse = lax.rsqrt(jnp.mean(mid * mid, axis=1, keepdims=True) + norm_epsilon)
        scaled = mid * inverse
        gain_grad = gain_grad + jnp.sum(grads * scaled, axis=0, keepdims=True)
        grads = grads * params_ref[:, D : 2 * D]
        inner = jnp.mean(grads * scaled, axis=1, keepdims=True)
        row_grads[rows, :] = (
            exp_stage[1, rows, 0:D].astype(jnp.float32) + inverse * (grads - scaled * inner)
        ).astype(low)
    for part in range(D // TILE):
        line_at = D // TILE + part
        small_own[line_at : line_at + 1, :] = gain_grad[:, TILE * part : TILE * (part + 1)]
    normed_grad[...] = jnp.zeros_like(normed_grad)
    load_exp(heads - group_heads, 0).start()
    load_proj(tensor_count - 1).start()
    for group, target in enumerate((zero_out, odd_out.at[0], two_out, odd_out.at[1])):
        rows = slice(group * head_rows, (group + 1) * head_rows)
        target[...] = jnp.dot(
            attended_ref[rows, :], row_grads[...], preferred_element_type=jnp.float32
        ).astype(low)
    core_copy(1, 3).start()
    core_copy(1, 1).start()
    for r0 in range(0, D, 256):
        rows = slice(r0, r0 + 256)
        attended_grad[rows, :] = contract(sent[rows, :], row_grads[...], 1, 1).astype(low)
    load(9).wait()

    def head_step(i, carry):
        group = tensor_count - 1 - lax.div(i, group_heads)
        part_head = lax.rem(i, group_heads)
        head = group * group_heads + part_head
        slot = lax.rem(i, 2)

        @pl.when(i == 1)
        def _():
            send_deal(3)

        @pl.when(i == 2)
        def _():
            send_far(1)

        @pl.when(i == 3)
        def _():
            pass_line(2, 0)

        @pl.when(i == 5)
        def _():
            send_deal(1)

        @pl.when(i == 6)
        def _():
            send_far(0)
            pass_line(3)

        @pl.when(i == 8)
        def _():
            pass_line(1)

        @pl.when((part_head == 0) & (i > 0))
        def _():
            save_proj(group + 1).wait()

        @pl.when(part_head == 0)
        def _():
            load_proj(group).wait()

        @pl.when(i + 1 < heads)
        def _():
            later = i + 1
            later_group = tensor_count - 1 - lax.div(later, group_heads)
            later_head = later_group * group_heads + lax.rem(later, group_heads)
            load_exp(later_head, lax.rem(later, 2)).start()

        load_exp(head, slot).wait()

        def rows(part):
            return pl.ds(pl.multiple_of(part * head_rows + part_head * HS, HS), HS)

        def store(part, column, value):
            proj_grad[rows(part), column : column + value.shape[1]] = value

        here = pl.ds(pl.multiple_of(head * HS, HS), HS)
        offset_grad = attend_head_back(
            proj[rows(0), :],
            proj[rows(1), :],
            proj[rows(2), :],
            exp_stage.at[slot],
            attended_ref[here, :],
            scale_ref[head],
            attended_grad[here, :],
            window,
            score_grads,
            store,
        )
        place = (
            true_group((tensor_pos, core_pos, far_pos), group, tensor_count) * group_heads + part_head
        )
        high = offset_grad.astype(low)
        rest = (offset_grad - high.astype(jnp.float32)).astype(low)
        both = jnp.concatenate([high, rest] + [jnp.zeros_like(high)] * 6, axis=0)
        sums = contract(both, bucket_hot[...], 1, 1)
        row = lax.broadcasted_iota(jnp.int32, (SMALL_ROWS - TABLE_ROW, TILE), 0)
        found = jnp.concatenate(
            [sums[0:1] + sums[1:2], jnp.zeros((1, TILE - NB), jnp.float32)], axis=1
        )
        small_own[TABLE_ROW:SMALL_ROWS, :] += jnp.where(
            row == place,
            jnp.broadcast_to(found, (SMALL_ROWS - TABLE_ROW, TILE)),
            0.0,
        )

        @pl.when(part_head == group_heads - 1)
        def _():
            @pl.when(group > 0)
            def _():
                load_proj(group - 1).start()

            def weight_grad(target):
                for r0 in range(0, 3 * head_rows, head_rows):
                    target[r0 : r0 + head_rows, :] = jnp.dot(
                        proj_grad[r0 : r0 + head_rows, :],
                        normed[...],
                        preferred_element_type=jnp.float32,
                    ).astype(low)

            @pl.when(group == 3)
            def _():
                weight_grad(odd_down)
                core_copy(0, 3).start()

            @pl.when(group == 2)
            def _():
                weight_grad(two_qkv)

            @pl.when(group == 1)
            def _():
                weight_grad(odd_in)
                core_copy(0, 1).start()

            @pl.when(group == 0)
            def _():
                weight_grad(zero_qkv)

            save_proj(group).start()

        return carry

    lax.fori_loop(0, heads, head_step, 0)

    load(10).start()
    save_proj(0).wait()
    reload(0, 1).start()
    reload(1, 0).start()
    send_deal(0)
    reload(1, 1).start()
    for group in range(tensor_count):
        if group > 0:
            reload(group, 0).wait()
        reload(group, 1).wait()
        part, rows_in = (proj, zero_qkv) if group % 2 else (proj_grad, weights)
        for r0 in range(0, SEQ, 256):
            normed_grad[r0 : r0 + 256, :] += jnp.dot(
                part[:, r0 : r0 + 256].T, rows_in[...], preferred_element_type=jnp.float32
            )
        if group + 2 < tensor_count:
            reload(group + 2, 0).start()
            reload(group + 2, 1).start()
    pass_line(0)
    load(10).wait()

    gain_grad = jnp.zeros((1, D), jnp.float32)
    for r0 in range(0, SEQ, 128):
        values = exp_stage[0, r0 : r0 + 128, 0:D].astype(jnp.float32)
        grads = normed_grad[r0 : r0 + 128, :]
        inverse = lax.rsqrt(jnp.mean(values * values, axis=1, keepdims=True) + norm_epsilon)
        scaled = values * inverse
        gain_grad = gain_grad + jnp.sum(grads * scaled, axis=0, keepdims=True)
        grads = grads * params_ref[:, 0:D]
        inner = jnp.mean(grads * scaled, axis=1, keepdims=True)
        row_grads[r0 : r0 + 128, :] = (
            row_grads[r0 : r0 + 128, :].astype(jnp.float32) + inverse * (grads - scaled * inner)
        ).astype(low)
    for part in range(D // TILE):
        small_own[part : part + 1, :] = gain_grad[:, TILE * part : TILE * (part + 1)]

    save_rows = pltpu.make_async_copy(row_grads, input_grad_ref, exp_sem.at[1])
    save_rows.start()

    def small_copy(stage, m):
        if stage == 0:
            src, target, peer = small_own, small_tensor.at[tensor_pos], tensor_peer(m)
        else:
            src, target, peer = small_total_ref, small_dp.at[dp_pos], (up(m), tensor_pos)
        return pltpu.make_async_remote_copy(
            src,
            target,
            small_send.at[stage, m],
            small_recv.at[stage, m],
            device_id=peer,
            device_id_type=MESH,
        )

    for m in range(1, tensor_count):
        small_copy(0, m).start()
    small_tensor[tensor_pos] = small_own[...]
    for m in range(1, tensor_count):
        small_copy(0, m).wait()
    total = small_tensor[0]
    for m in range(1, tensor_count):
        total = total + small_tensor[m]
    small_total_ref[...] = total
    each_peer(lambda m: small_copy(1, m).start())
    finish_far()
    finish_near()
    finish_deal(3)
    small_dp[dp_pos] = small_total_ref[...]
    each_peer(lambda m: small_copy(1, m).wait())
    total = small_dp[0]
    for m in range(1, dp_count):
        total = total + small_dp[m]
    small_total_ref[...] = total
    finish_deal(1)
    finish_deal(0)

    place = jnp.concatenate([spread_place_ref[m : m + 1, :] for m in range(dp_count)], axis=1)
    hot = one_hot(place, (spread.shape[0], dp_count * pair_rows), 0)
    sent[0 : dp_count * pair_rows, :] = contract(hot, spread[...], 0, 0).astype(low)

    def back_copy(m):
        here = pl.ds(pl.multiple_of(m * pair_rows, 16), pair_rows)
        return pltpu.make_async_remote_copy(
            sent.at[here],
            received.at[here],
            back_send.at[m],
            back_recv.at[m],
            device_id=(down(m), tensor_pos),
            device_id_type=MESH,
        )

    each_peer(lambda m: back_copy(m).start())
    received[0:pair_rows, :] = sent[0:pair_rows, :]
    each_peer(lambda m: back_copy(m).wait())
    hot = one_hot(slot_place_ref[...], (dp_count * pair_rows, owned_ref.shape[0]), 0)
    owned_ref[...] = contract(hot, received[0 : dp_count * pair_rows, :], 0, 0)
    save_rows.wait()
    for role in range(len(gots)):
        if role < 2:
            core_copy(role, 1).wait_send()
            core_copy(role, 3).wait_send()
        if role != 2:
            far_copy(role).wait_send()


def back(
    feed_parts,
    projected,
    exp_scores,
    w_qkv,
    tokens,
    normed_one,
    attended,
    scale,
    small_row,
    small,
    bucket_place,
    places,
    local_sizes,
    spread_place,
    slot_place,
):
    dp_count, tensor_count = lax.axis_size("dp"), lax.axis_size("tensor")
    sizes = [place.shape[1] for place in places]
    capacity, pair_rows = slot_place.shape[1], spread_place.shape[1]
    low = jnp.bfloat16
    dma = pltpu.SemaphoreType.DMA
    roles = len(sizes)
    whole = pl.BlockSpec(memory_space=pltpu.VMEM)
    away = pl.BlockSpec(memory_space=pl.ANY)
    parts = [pltpu.VMEM((size, D), low) for size in sizes]
    padded = [
        pltpu.VMEM((max(dp_count * size, full), D), low) for size, full in zip(local_sizes, sizes)
    ]
    return pl.pallas_call(
        functools.partial(back_kernel, sizes),
        in_specs=[away] * 14 + [whole] * 11,
        out_specs=[whole, away, whole, away],
        out_shape=[
            jax.ShapeDtypeStruct((capacity, D), jnp.float32),
            jax.ShapeDtypeStruct((SEQ, D), low),
            jax.ShapeDtypeStruct((SMALL_ROWS, TILE), jnp.float32),
            jax.ShapeDtypeStruct((tensor_count, sizes[0], SEQ), low),
        ],
        scratch_shapes=[
            pltpu.VMEM((NB, 2 * SEQ), low),
            pltpu.VMEM((sizes[0], D), low),
            pltpu.VMEM((sizes[0], SEQ), low),
            pltpu.VMEM((sizes[0], SEQ), low),
            pltpu.VMEM((SEQ, D), jnp.float32),
            pltpu.VMEM((WINDOW, TILE), jnp.float32),
            pltpu.VMEM((SEQ, SEQ), low),
            pltpu.VMEM((2, SEQ, SEQ), low),
            pltpu.VMEM((SEQ, D), low),
            pltpu.VMEM((SEQ, D), low),
            pltpu.VMEM((D, SEQ), low),
            pltpu.VMEM((2, sizes[1], D), low),
            pltpu.VMEM((sizes[2], D), low),
            pltpu.VMEM((sizes[3], D), low),
        ]
        + parts
        + parts
        + parts[:2]
        + padded[2:3]
        + parts[3:]
        + padded
        + parts[:2]
        + [pltpu.VMEM((dp_count * local_sizes[2], D), low)]
        + parts[3:]
        + [
            pltpu.VMEM((dp_count if role == 2 else dp_count // 2, size, D), low)
            for role, size in enumerate(local_sizes)
        ]
        + [pltpu.VMEM((dp_count // 2 * local_sizes[role], D), low) for role in (0, 1, 3)]
        + [
            pltpu.VMEM((local_sizes[2], D), low),
            pltpu.VMEM((local_sizes[2], D), low),
            pltpu.VMEM((sum(local_sizes), D), low),
            pltpu.VMEM((max(dp_count * pair_rows, D), D), low),
            pltpu.VMEM((max(dp_count * pair_rows, D), D), low),
            pltpu.VMEM((SMALL_ROWS, TILE), jnp.float32),
            pltpu.VMEM((tensor_count, SMALL_ROWS, TILE), jnp.float32),
            pltpu.VMEM((dp_count, SMALL_ROWS, TILE), jnp.float32),
            dma((roles, 2)),
            dma((roles, 2)),
            dma((roles,)),
            dma((roles,)),
            dma((roles, 2)),
            dma((roles, 2)),
            dma((roles, dp_count)),
            dma((roles, dp_count)),
            dma,
            dma,
            dma((dp_count,)),
            dma((dp_count,)),
            dma((2, max(dp_count, tensor_count))),
            dma((2, max(dp_count, tensor_count))),
            dma((11,)),
            dma((2,)),
            dma((2,)),
            dma((2, 2)),
        ],
        compiler_params=pltpu.CompilerParams(
            collective_id=2, has_side_effects=True, vmem_limit_bytes=63 * 1024 * 1024
        ),
        cost_estimate=pl.CostEstimate(
            flops=16 * H * SEQ * SEQ * 256 + 8 * SEQ * FF * D,
            bytes_accessed=96 * 1024 * 1024,
            transcendentals=0,
        ),
        name="back",
    )(
        *feed_parts,
        projected,
        exp_scores,
        w_qkv,
        tokens,
        normed_one,
        attended,
        scale,
        small_row,
        small,
        bucket_place,
        *places,
        spread_place,
        slot_place,
    )


def adamw(weights, grads, first, second, step):
    first_new = beta_first * first + (1.0 - beta_first) * grads
    second_new = beta_second * second + (1.0 - beta_second) * grads * grads
    first_hat = first_new / (1.0 - beta_first**step)
    second_hat = second_new / (1.0 - beta_second**step)
    weights_new = weights - rate_per_step * step * (
        first_hat / (jnp.sqrt(second_hat) + adam_epsilon) + weight_decay * weights
    )
    return (weights_new, first_new, second_new)


def per_device(
    tokens,
    cotangent,
    segment_ids,
    buckets,
    owners,
    master,
    first_moment,
    second_moment,
    small_params,
    small_first,
    small_second,
    adapter_ema,
    step_count,
):
    dp_count = lax.axis_size("dp")
    tensor_count = lax.axis_size("tensor")
    capacity = master.shape[1]
    group_heads = H // tensor_count
    head_rows = group_heads * HS
    hidden_rows = FF // tensor_count
    tensor_pos = lax.axis_index("tensor")
    sizes = [3 * head_rows, head_rows, hidden_rows, hidden_rows]
    local_sizes = [-(-size // dp_count // 16) * 16 for size in sizes]
    pair_rows = -(-((capacity + len(sizes) * (dp_count - 1)) // dp_count) // 16) * 16
    slot_place, spread_place, orders, places = plan(
        owners, sizes, local_sizes, capacity, pair_rows
    )

    bucket_place = jnp.concatenate([jnp.full((1,), -1, jnp.int32), buckets[::-1]])[None, :]
    segments = lax.dynamic_slice_in_dim(segment_ids, tensor_pos * SEQ, SEQ, 0)
    outs = front(
        master[0],
        slot_place,
        spread_place,
        orders,
        local_sizes,
        tokens,
        small_params[None, :],
        bucket_place,
        segments,
        cotangent,
    )
    w_qkv, w_out, w_in, w_down, projected, attended, scale, normed_one, exp_scores = outs[:9]
    activ, slope, normed_two, mid, layer_out, ffn_grad, small_local = outs[9:]
    owned_grad, input_grad, small_total, _ = back(
        (
            ffn_grad,
            normed_two,
            mid,
            cotangent,
            w_out.reshape(D, D),
            activ,
            slope,
            w_in,
            w_down,
        ),
        projected,
        exp_scores,
        w_qkv,
        tokens,
        normed_one,
        attended,
        scale,
        small_params[None, :],
        small_local,
        bucket_place,
        places,
        local_sizes,
        spread_place,
        slot_place,
    )
    small_total = jnp.concatenate(
        [
            small_total[:TABLE_ROW].reshape(-1)[: 2 * D + NADAPT],
            small_total[TABLE_ROW : TABLE_ROW + H, :NB].T.reshape(-1),
        ]
    )
    own_filled = (slot_place[0] >= 0).astype(jnp.float32)[:, None]
    step = step_count[0].astype(jnp.float32)
    owned_grad = owned_grad * own_filled
    new_master, new_first, new_second = adamw(
        master[0], owned_grad, first_moment[0], second_moment[0], step
    )
    new_master = new_master * own_filled
    new_first = new_first * own_filled
    new_second = new_second * own_filled
    small_new, small_first_new, small_second_new = adamw(
        small_params, small_total, small_first, small_second, step
    )
    ema_new = average_keep * adapter_ema + (1.0 - average_keep) * small_new[2 * D : 2 * D + NADAPT]
    return (
        layer_out,
        input_grad,
        owned_grad[None],
        new_first[None],
        new_second[None],
        new_master[None],
        new_master.astype(jnp.bfloat16)[None],
        small_total,
        small_first_new,
        small_second_new,
        small_new,
        ema_new,
    )


def solution(mesh):
    token_spec = P(("dp", "tensor"), None)
    owner_spec = P("tensor", "dp", None)
    return jax.shard_map(
        per_device,
        mesh=mesh,
        in_specs=(token_spec, token_spec, P("dp"), P(), P())
        + (owner_spec,) * 3
        + (P(),) * 5,
        out_specs=(token_spec,) * 2 + (owner_spec,) * 5 + (P(),) * 5,
        check_vma=False,
    )
```

```python
import functools
import math

import jax
import jax.numpy as jnp
from jax import lax
from jax.experimental import pallas as pl
from jax.experimental.pallas import tpu as pltpu
from jax.sharding import PartitionSpec as P

D = 768
H = 12
HS = 64
FF = 3072
NB = 32
R = 48
PHM = 4
SEQ = 1024
NADAPT = 1696

highest = lax.Precision.HIGHEST
norm_epsilon = 1e-06
beta_first = 0.5
beta_second = 0.5
adam_epsilon = 1e-08
rate_per_step = 0.01
weight_decay = 0.1
average_keep = 0.75
masked_score = -1000000000.0

TILE = 128
WINDOW = 2 * SEQ - TILE
QUERY_TILE = 1024
KEY_TILE = 1024
BACK_QUERY_TILE = 512
BACK_KEY_TILE = 1024
VMEM_LIMIT = 48 * 1024 * 1024
MESH = pl.DeviceIdType.MESH
SMALL_ROWS = 48
TABLE_ROW = 32


def exact(left, right, left_dim, right_dim):
    return lax.dot_general(
        left,
        right,
        (((left_dim,), (right_dim,)), ((), ())),
        precision=highest,
        preferred_element_type=jnp.float32,
    )


def grid(shape, dim, parts):
    rest = lax.broadcasted_iota(jnp.int32, shape, dim).astype(jnp.float32)
    found = []
    for part in parts:
        high = jnp.floor((rest + 0.5) * (1.0 / part))
        found.append(high)
        rest = rest - part * high
    return found + [rest]


def zero_one(hit):
    return jnp.where(hit, 1.0, 0.0)


def adapter_places():
    rank = R // PHM
    outer = PHM * PHM
    block, inner = grid((R, PHM * outer), 0, (rank,))
    _, first, second = grid((R, PHM * outer), 1, (outer, PHM))
    term, left_at, right_at = grid((PHM * outer, outer), 0, (outer, PHM))
    column, last = grid((PHM * outer, outer), 1, (PHM,))
    mix_down = (
        zero_one(second == block),
        zero_one((term == column) & (left_at == last)),
    )
    mix_up = (
        zero_one(first == block),
        zero_one((term == column) & (right_at == last)),
    )
    _, inner = grid((R, R), 0, (rank,))
    _, short = grid((R, R), 1, (rank,))
    term, _ = grid((R, outer), 0, (rank,))
    column, _ = grid((R, outer), 1, (PHM,))
    side = (zero_one(inner == short), zero_one(term == column))
    return mix_down, mix_up, side


def lay_out(row, places):
    keep, gather = places
    return exact(keep * row, gather, 1, 0)


def take_back(values, places):
    keep, gather = places
    return jnp.sum(keep * exact(values, gather, 1, 1), axis=0, keepdims=True)


def lay_long(row):
    part = D // PHM
    term, block = grid((PHM * PHM, D), 0, (PHM,))
    place, _ = grid((PHM * PHM, D), 1, (part,))
    total = jnp.zeros((PHM * PHM, D), jnp.float32)
    for i in range(PHM):
        tiled = jnp.concatenate([row[:, part * i : part * (i + 1)]] * PHM, axis=1)
        total = jnp.where((term == i) & (place == block), tiled, total)
    return total


def take_long(values):
    part = D // PHM
    _, block = grid((PHM * PHM, D), 0, (PHM,))
    place, _ = grid((PHM * PHM, D), 1, (part,))
    values = jnp.where(place == block, values, 0.0)
    pieces = []
    for i in range(PHM):
        row = jnp.sum(values[PHM * i : PHM * (i + 1), :], axis=0, keepdims=True)
        pieces.append(sum(row[:, part * a : part * (a + 1)] for a in range(PHM)))
    return jnp.concatenate(pieces, axis=1)


def normal_parts(values):
    size = jnp.abs(values)
    shrink = 1.0 / (1.0 + (0.3275911 * math.sqrt(0.5)) * size)
    bell = jnp.exp(-0.5 * values * values)
    series = 0.5 * 1.061405429
    for term in (-1.453152027, 1.421413741, -0.284496736, 0.254829592):
        series = series * shrink + 0.5 * term
    tail = series * shrink * bell
    return jnp.where(values >= 0.0, 1.0 - tail, tail), bell * (1.0 / math.sqrt(2.0 * math.pi))


def contract(left, right, left_dim, right_dim):
    return lax.dot_general(
        left,
        right,
        (((left_dim,), (right_dim,)), ((), ())),
        preferred_element_type=jnp.float32,
    )


def bias_window(bias, window):
    for tile in range(WINDOW // TILE):
        base = WINDOW - TILE * tile
        row = jnp.broadcast_to(bias[:, base - TILE : base + TILE], (TILE, 2 * TILE))
        rolled = pltpu.roll(row, TILE, 1, stride=1, stride_axis=0)
        window[TILE * tile : TILE * (tile + 1), :] = rolled[:, :TILE]


def attend_head(
    query_rows, key_rows, value_rows, segment_keys_ref, segment_queries_ref, window, scores, exp_ref
):
    keys = key_rows.T
    values = jnp.concatenate([value_rows, jnp.ones((16, SEQ), jnp.bfloat16)], axis=0)
    outs, scales = [], []
    for q0 in range(0, SEQ, QUERY_TILE):
        queries = query_rows[:, q0 : q0 + QUERY_TILE]
        peak = jnp.full((8, QUERY_TILE), -jnp.inf, jnp.float32)
        for k0 in range(0, SEQ, KEY_TILE):
            raw = jnp.dot(keys[k0 : k0 + KEY_TILE], queries, preferred_element_type=jnp.float32)
            parts = []
            for l0 in range(0, QUERY_TILE, TILE):
                start = SEQ - TILE - (q0 + l0) + k0
                same_doc = (
                    segment_keys_ref[k0 : k0 + KEY_TILE, :]
                    == segment_queries_ref[:, q0 + l0 : q0 + l0 + TILE]
                )
                part = jnp.where(
                    same_doc,
                    raw[:, l0 : l0 + TILE] + window[start : start + KEY_TILE, :],
                    masked_score,
                )
                scores[k0 : k0 + KEY_TILE, l0 : l0 + TILE] = part
                parts.append(part)
            whole = jnp.concatenate(parts, axis=1)
            peak = jnp.maximum(peak, jnp.max(whole.reshape(KEY_TILE // 8, 8, QUERY_TILE), axis=0))
        peak = jnp.max(peak, axis=0, keepdims=True)
        total = jnp.zeros((HS + 16, QUERY_TILE), jnp.float32)
        for k0 in range(0, SEQ, KEY_TILE):
            exp_scores = jnp.exp(scores[k0 : k0 + KEY_TILE, :] - peak).astype(jnp.bfloat16)
            exp_ref[k0 : k0 + KEY_TILE, q0 : q0 + QUERY_TILE] = exp_scores
            total = total + jnp.dot(
                values[:, k0 : k0 + KEY_TILE], exp_scores, preferred_element_type=jnp.float32
            )
        scale = 1.0 / total[HS : HS + 1]
        scales.append(scale)
        outs.append((total[:HS] * scale).astype(jnp.bfloat16))
    return jnp.concatenate(outs, axis=1), jnp.concatenate(scales, axis=1)


def one_hot(place, shape, dim):
    hit = lax.broadcasted_iota(jnp.int32, shape, dim) == place
    return jnp.where(hit, 1.0, 0.0).astype(jnp.bfloat16)


def plan_kernel(dp_count, pair_rows, local_sizes, *refs):
    roles = len(local_sizes)
    owners_ref, slot_ref, spread_ref = refs[:3]
    order_refs, place_refs = refs[3 : roles + 3], refs[roles + 3 :]
    dp_pos = lax.axis_index("dp").astype(jnp.float32)

    def quotient(values):
        return jnp.floor((values + 0.5) * (1.0 / dp_count))

    def remainder(values):
        return values - dp_count * quotient(values)

    line = dp_count // 2

    def halve(values):
        return jnp.floor((values + 0.5) * 0.5)

    def around(values):
        return values - line * jnp.floor((values + 0.5) * (1.0 / line))

    whole = owners_ref[...].astype(jnp.float32)
    whole = jnp.concatenate([whole[i : i + 1, :] for i in range(whole.shape[0])], axis=1)
    owners, low = [], 0
    for ref in order_refs:
        owners.append(whole[:, low : low + ref.shape[1]])
        low += ref.shape[1]

    def stats(who):
        counts = [
            jnp.sum(jnp.where(row == who, 1.0, 0.0), axis=1, keepdims=True) for row in owners
        ]
        starts = [jnp.sum(jnp.where(row < who, 1.0, 0.0), axis=1, keepdims=True) for row in owners]
        return counts, starts

    def hits(first, number, target):
        return quotient(first + number - 1.0 - target) - quotient(first - 1.0 - target)

    counts, starts = stats(jnp.full((1, 1), dp_pos))
    slot = lax.broadcasted_iota(jnp.int32, slot_ref.shape, 1).astype(jnp.float32)
    found = jnp.full(slot_ref.shape, -1.0)
    low = jnp.zeros((1, 1), jnp.float32)
    for role in range(roles):
        rank = slot - low
        target = remainder(starts[role] + rank)
        place = quotient(rank)
        for other in range(role):
            place = place + hits(starts[other], counts[other], target)
        found = jnp.where(
            (rank >= 0.0) & (rank < counts[role]),
            remainder(target - dp_pos) * pair_rows + place,
            found,
        )
        low = low + counts[role]
    slot_ref[...] = found.astype(jnp.int32)

    column = lax.broadcasted_iota(jnp.int32, (dp_count, 1), 0).astype(jnp.float32)
    counts, starts = stats(remainder(dp_pos - column))
    pair = lax.broadcasted_iota(jnp.int32, spread_ref.shape, 1).astype(jnp.float32)
    found = jnp.full(spread_ref.shape, -1.0)
    passed = jnp.zeros((dp_count, 1), jnp.float32)
    for role in range(roles):
        number = hits(starts[role], counts[role], dp_pos)
        first = starts[role] + remainder(dp_pos - starts[role])
        rank = pair - passed
        local = sum(local_sizes[:role]) + quotient(first) + rank
        found = jnp.where((rank >= 0.0) & (rank < number), local, found)
        passed = passed + number
    spread_ref[...] = found.astype(jnp.int32)

    counts, starts = stats(column)
    for role in range(roles):
        width = owners[role].shape[1]
        before = starts[role]
        for c0 in range(0, width, TILE):
            c1 = min(c0 + TILE, width)
            hot = jnp.where(owners[role][:, c0:c1] == column, 1.0, 0.0)
            shape = (c1 - c0, c1 - c0)
            above = lax.broadcasted_iota(jnp.int32, shape, 0) < lax.broadcasted_iota(
                jnp.int32, shape, 1
            )
            rank = jnp.dot(
                hot.astype(jnp.bfloat16),
                jnp.where(above, 1.0, 0.0).astype(jnp.bfloat16),
                preferred_element_type=jnp.float32,
            )
            number = jnp.sum(hot * (rank + before), axis=0, keepdims=True)
            before = before + jnp.sum(hot, axis=1, keepdims=True)
            target, row = remainder(number), quotient(number)
            side = jnp.abs(target - 2.0 * halve(target) - dp_pos + 2.0 * halve(dp_pos)) * line
            ahead = halve(target) - halve(dp_pos)
            order = (around(0.0 - ahead) + side) * local_sizes[role] + row
            place = (around(ahead) + side) * local_sizes[role] + row
            order_refs[role][:, c0:c1] = order.astype(jnp.int32)
            place_refs[role][:, c0:c1] = place.astype(jnp.int32)


def plan(owners, sizes, local_sizes, capacity, pair_rows):
    dp_count = lax.axis_size("dp")
    outs = pl.pallas_call(
        functools.partial(plan_kernel, dp_count, pair_rows, local_sizes),
        out_shape=[
            jax.ShapeDtypeStruct((1, capacity), jnp.int32),
            jax.ShapeDtypeStruct((dp_count, pair_rows), jnp.int32),
        ]
        + [jax.ShapeDtypeStruct((1, size), jnp.int32) for size in sizes] * 2,
        name="plan",
    )(owners.reshape(-1, TILE))
    return outs[0], outs[1], outs[2 : 2 + len(sizes)], outs[2 + len(sizes) :]


def true_group(positions, group, tensor_count):
    flips = positions + (tensor_count - 1 - positions[0],)
    found = flips[0]
    for g in range(1, tensor_count):
        found = found + (flips[g] - flips[0]) * (
            lax.div(group + tensor_count - g, tensor_count)
            - lax.div(group + tensor_count - g - 1, tensor_count)
        )
    return found


def front_kernel(
    sizes,
    mine_ref,
    slot_place_ref,
    spread_place_ref,
    order_qkv_ref,
    order_out_ref,
    order_in_ref,
    order_down_ref,
    tokens_ref,
    small_ref,
    bucket_ref,
    segment_ref,
    cotangent_ref,
    w_qkv_out,
    w_out_ref,
    w_in_ref,
    w_down_ref,
    projected_out,
    attended_ref,
    scale_ref,
    normed_ref,
    exp_ref,
    activ_ref,
    slope_ref,
    normed_two_ref,
    mid_ref,
    layer_out_ref,
    ffn_grad_ref,
    small_part_ref,
    w_qkv_ref,
    projected_ref,
    feed_weights,
    ffn_out,
    mid_rows,
    hot_qkv,
    hot_out,
    hot_in,
    hot_down,
    sent,
    received,
    spread,
    bias,
    segment_keys,
    buf_qkv,
    buf_out,
    buf_in,
    buf_down,
    buf_far,
    far_spread,
    stage_out,
    stage_in,
    stage_down,
    stage_far,
    window,
    scores,
    exp_stage,
    deal_send,
    deal_recv,
    far_send,
    far_recv,
    line_send,
    line_recv,
    side_send,
    side_recv,
    group_send,
    group_recv,
    local_sem,
    exp_sem,
    save_sem,
    feed_sem,
    out_sem,
):
    dp_count, pair_rows = sent.shape[0], sent.shape[1]
    tensor_count = w_qkv_ref.shape[0]
    heads = scale_ref.shape[0]
    low = jnp.bfloat16
    group_heads = heads // tensor_count
    head_rows = group_heads * HS
    dp_pos, tensor_pos = lax.axis_index("dp"), lax.axis_index("tensor")
    core_pos = tensor_pos + 1 - 2 * lax.rem(tensor_pos, 2)
    far_pos = lax.rem(tensor_pos + 2, tensor_count)
    core_peer, far_peer = (dp_pos, core_pos), (dp_pos, far_pos)

    def dp_peer(m):
        return (lax.rem(dp_pos + m, dp_count), tensor_pos)

    def each_peer(run):
        def step(m, carry):
            run(m)
            return carry

        lax.fori_loop(1, dp_count, step, 0)

    barrier = pltpu.get_barrier_semaphore()

    def greet(m):
        pl.semaphore_signal(barrier, inc=1, device_id=dp_peer(m), device_id_type=MESH)

    each_peer(greet)
    for peer in (core_peer, far_peer):
        pl.semaphore_signal(barrier, inc=1, device_id=peer, device_id_type=MESH)

    mine = mine_ref[...].astype(jnp.bfloat16)
    hot = one_hot(slot_place_ref[...], (dp_count * pair_rows, mine.shape[0]), 0)
    sent[...] = (
        jnp.dot(hot, mine, preferred_element_type=jnp.float32)
        .astype(jnp.bfloat16)
        .reshape(dp_count, pair_rows, D)
    )
    pl.semaphore_wait(barrier, dp_count + 1)

    def deal(m):
        return pltpu.make_async_remote_copy(
            sent.at[m],
            received.at[m],
            deal_send.at[m],
            deal_recv.at[m],
            device_id=dp_peer(m),
            device_id_type=MESH,
        )

    each_peer(lambda m: deal(m).start())
    received[0] = sent[0]

    for r0 in range(0, SEQ, 128):
        values = tokens_ref[r0 : r0 + 128, :].astype(jnp.float32)
        inverse = lax.rsqrt(jnp.mean(values * values, axis=1, keepdims=True) + norm_epsilon)
        normed_ref[r0 : r0 + 128, :] = (values * inverse * small_ref[:, 0:D]).astype(jnp.bfloat16)
    flat = small_ref[...][:, 2 * D + NADAPT :]
    entry = lax.broadcasted_iota(jnp.int32, (16, NB * H), 1)
    bucket = jnp.floor((entry.astype(jnp.float32) + 0.5) * (1.0 / H))
    head_of = entry.astype(jnp.float32) - H * bucket
    line_of = lax.broadcasted_iota(jnp.int32, (16, NB * H), 0).astype(jnp.float32)
    rest = jnp.where(head_of == line_of, jnp.broadcast_to(flat, (16, NB * H)), 0.0)
    entry = lax.broadcasted_iota(jnp.int32, (NB * H, 2 * SEQ), 0).astype(jnp.float32)
    bucket = jnp.floor((entry + 0.5) * (1.0 / H))
    hot = jnp.where(bucket == bucket_ref[...].astype(jnp.float32), 1.0, 0.0).astype(jnp.bfloat16)
    biases = jnp.zeros((rest.shape[0], 2 * SEQ), jnp.float32)
    for _ in range(3):
        part = rest.astype(jnp.bfloat16)
        rest = rest - part.astype(jnp.float32)
        biases = biases + jnp.dot(part, hot, preferred_element_type=jnp.float32)
    for head in range(heads):
        bias[head] = biases[head : head + 1, :]
    segment_keys[...] = jnp.broadcast_to(segment_ref[...], (TILE, SEQ)).T
    hots = (hot_qkv, hot_out, hot_in, hot_down, hot_down)
    for hot, place in zip(hots, (order_qkv_ref, order_out_ref, order_in_ref, order_down_ref)):
        hot[...] = one_hot(place[...], (hot.shape[1], hot.shape[0]), 0).T

    row = small_ref[...]
    starts = [2 * D]
    for width in (PHM**3, D, R, R, D):
        starts.append(starts[-1] + width)
    mix, down_long, down_short, up_short, up_long = [
        row[:, low_at:high_at] for low_at, high_at in zip(starts[:-1], starts[1:])
    ]
    mix_down, mix_up, short_place = adapter_places()
    mixes = (lay_out(mix, mix_down), lay_out(mix, mix_up))
    shorts = (lay_out(down_short, short_place), lay_out(up_short, short_place))
    left, wide = mixes[0] * shorts[0], mixes[1] * shorts[1]
    right, tall = lay_long(down_long), lay_long(up_long)
    down = exact(left, right, 1, 0).astype(low)
    up = exact(wide, tall, 1, 0).astype(low)

    each_peer(lambda m: deal(m).wait())
    rows = spread.shape[0]
    place = jnp.concatenate([spread_place_ref[m : m + 1, :] for m in range(dp_count)], axis=1)
    hot = one_hot(place, (rows, dp_count * pair_rows), 0)
    spread[...] = jnp.dot(
        hot, received[...].reshape(dp_count * pair_rows, D), preferred_element_type=jnp.float32
    ).astype(jnp.bfloat16)

    bufs = (buf_qkv, buf_out, buf_in, buf_down, buf_far)
    stages = (w_qkv_ref.at[0], stage_out, stage_in, stage_down, stage_far)
    finals = (w_qkv_ref, w_out_ref, w_in_ref, w_down_ref, w_down_ref)
    sizes = tuple(sizes) + (sizes[3],)
    offsets = [sum(buf.shape[1] for buf in bufs[:role]) for role in range(4)]
    line = dp_count // 2
    line_pos, side = lax.div(dp_pos, 2), lax.rem(dp_pos, 2)
    side_peer = (dp_pos + 1 - 2 * side, tensor_pos)

    def far_exchange():
        return pltpu.make_async_remote_copy(
            spread.at[pl.ds(offsets[3], far_spread.shape[0])],
            far_spread,
            far_send,
            far_recv,
            device_id=far_peer,
            device_id_type=MESH,
        )

    def block(role):
        if role == 4:
            return far_spread
        return spread.at[pl.ds(offsets[role], bufs[role].shape[1])]

    def along_line(role, m):
        return pltpu.make_async_remote_copy(
            block(role),
            bufs[role].at[m],
            line_send.at[role, m],
            line_recv.at[role, m],
            device_id=(lax.rem(line_pos + m, line) * 2 + side, tensor_pos),
            device_id_type=MESH,
        )

    def to_side(role, m):
        return pltpu.make_async_remote_copy(
            bufs[role].at[m],
            bufs[role].at[line + m],
            side_send.at[role, m],
            side_recv.at[role, m],
            device_id=side_peer,
            device_id_type=MESH,
        )

    def each_line(first, run):
        def step(m, carry):
            run(m)
            return carry

        lax.fori_loop(first, line, step, 0)

    def start_line(role):
        if role == 4:
            far_exchange().wait()
        each_line(1, lambda m: along_line(role, m).start())
        bufs[role][0] = block(role)[...]
        to_side(role, 0).start()

    def start_side(role):
        def step(m):
            along_line(role, m).wait()
            to_side(role, m).start()

        each_line(1, step)

    def order(role):
        each_line(0, lambda m: to_side(role, m).wait())
        count = bufs[role].shape[1]
        source = bufs[role][...].reshape(dp_count * count, D)
        step = 384 if sizes[role] > 576 else sizes[role]
        for r0 in range(0, sizes[role], step):
            r1 = min(r0 + step, sizes[role])
            stages[role][r0:r1, :] = jnp.dot(
                hots[role][r0:r1, :], source, preferred_element_type=jnp.float32
            ).astype(jnp.bfloat16)

    def share(role, part):
        if role == 4:
            src, slot, peer = stages[role], 3, core_peer
        else:
            src, slot, peer = (
                (stages[role], 1, core_peer),
                (stages[role], 2, far_peer),
                (finals[role].at[2], 3, core_peer),
            )[part]
        return pltpu.make_async_remote_copy(
            src,
            finals[role].at[slot],
            group_send.at[role, part],
            group_recv.at[role, part],
            device_id=peer,
            device_id_type=MESH,
        )

    def keep(role):
        slot = 2 if role == 4 else 0
        return pltpu.make_async_copy(stages[role], finals[role].at[slot], local_sem.at[role])

    def start_share(role):
        order(role)
        share(role, 0).start()
        if role < 3:
            share(role, 1).start()
        if role > 0:
            keep(role).start()

    def forward(role):
        share(role, 1).wait_recv()
        share(role, 2).start()

    far_exchange().start()
    start_line(0)
    start_side(0)
    start_share(0)
    start_line(1)
    start_line(2)

    def save_group(which, group):
        source, target = ((projected_ref, projected_out), (w_qkv_ref, w_qkv_out))[which]
        return pltpu.make_async_copy(
            source.at[group], target.at[group], save_sem.at[which, group]
        )

    def true_head(group, head):
        return true_group((tensor_pos, core_pos, far_pos), group, tensor_count) * group_heads + head

    def head_step(i, carry):
        group, head = lax.div(i, group_heads), lax.rem(i, group_heads)

        @pl.when(i == 1)
        def _():
            start_side(1)

        @pl.when(i == 3)
        def _():
            start_share(1)

        @pl.when(i == 5)
        def _():
            start_side(2)
            start_line(3)
            start_line(4)

        @pl.when(i == 10)
        def _():
            start_share(2)

        @pl.when(i == group_heads)
        def _():
            share(0, 0).wait_recv()

        @pl.when(i == 2 * group_heads)
        def _():
            forward(0)

        @pl.when(i == 3 * group_heads)
        def _():
            share(0, 2).wait_recv()
            forward(1)

        @pl.when(i == 11)
        def _():
            start_side(3)

        @pl.when(head == 0)
        def _():
            projected_ref[group] = contract(w_qkv_ref[group], normed_ref[...], 1, 1).astype(
                jnp.bfloat16
            )
            save_group(0, group).start()
            save_group(1, group).start()

        def head_part(part):
            start = pl.multiple_of(part * head_rows + head * HS, HS)
            return projected_ref[group, pl.ds(start, HS), :]

        slot = lax.rem(i, 2)

        def save(head_index, slot):
            return pltpu.make_async_copy(
                exp_stage.at[slot], exp_ref.at[head_index], exp_sem.at[slot]
            )

        @pl.when(i >= 2)
        def _():
            save(i - 2, slot).wait()

        bias_window(bias[true_head(group, head)], window)
        attended, scale = attend_head(
            head_part(0),
            head_part(1),
            head_part(2),
            segment_keys,
            segment_ref,
            window,
            scores,
            exp_stage.at[slot],
        )
        attended_ref[pl.ds(pl.multiple_of(i * HS, HS), HS), :] = attended
        scale_ref[i] = scale
        save(i, slot).start()
        return carry

    lax.fori_loop(0, heads, head_step, 0)
    for i in (heads - 2, heads - 1):
        pltpu.make_async_copy(exp_stage.at[i % 2], exp_ref.at[i], exp_sem.at[i % 2]).wait()
    start_side(4)

    def load_feed(group, slot, which):
        return pltpu.make_async_copy(
            (w_in_ref, w_down_ref)[which].at[group],
            feed_weights.at[slot, which],
            feed_sem.at[slot, which],
        )

    def load_out(group):
        return pltpu.make_async_copy(
            w_out_ref.at[group],
            feed_weights.at[1, 0, pl.ds(group * head_rows, head_rows)],
            out_sem.at[group],
        )

    keep(1).wait()
    share(1, 0).wait_recv()
    share(1, 2).wait_recv()
    for group in range(tensor_count):
        load_out(group).start()
    keep(2).wait()
    load_feed(0, 0, 0).start()
    for group in range(tensor_count):
        load_out(group).wait()
    tiles = [slice(r0, r0 + 256) for r0 in range(0, SEQ, 256)]
    for rows in tiles:
        attn = jnp.dot(
            attended_ref[:, rows].T, feed_weights[1, 0], preferred_element_type=jnp.float32
        )
        mid = tokens_ref[rows, :].astype(jnp.float32) + attn
        mid_rows[rows, :] = mid
        mid_ref[rows, :] = mid.astype(low)
        inverse = lax.rsqrt(jnp.mean(mid * mid, axis=1, keepdims=True) + norm_epsilon)
        normed_two_ref[rows, :] = (mid * inverse * small_ref[:, D : 2 * D]).astype(low)
        ffn_out[rows, :] = jnp.zeros((256, D), jnp.float32)
    hidden_rows = w_in_ref.shape[1]

    def save_feed(group, which):
        columns = pl.ds(pl.multiple_of(group * hidden_rows, TILE), hidden_rows)
        return pltpu.make_async_copy(
            exp_stage.at[which, :, pl.ds(0, hidden_rows)],
            (activ_ref, slope_ref)[which].at[:, columns],
            exp_sem.at[which],
        )

    def feed_step(group, carry):
        slot = lax.rem(group, 2)
        load_feed(group, slot, 0).wait()

        @pl.when(group > 0)
        def _():
            for which in range(2):
                save_feed(group - 1, which).wait()

        for rows in tiles:
            pre = contract(normed_two_ref[rows, :], feed_weights[slot, 0], 1, 1)
            cdf, density = normal_parts(pre)
            exp_stage[0, rows, 0:hidden_rows] = (pre * cdf).astype(low)
            exp_stage[1, rows, 0:hidden_rows] = (cdf + pre * density).astype(low)
        for which in range(2):
            save_feed(group, which).start()

        @pl.when(group == 0)
        def _():
            share(2, 0).wait_recv()

        @pl.when(group == 1)
        def _():
            start_share(3)
            start_share(4)
            forward(2)

        @pl.when(group == 2)
        def _():
            share(2, 2).wait_recv()

        @pl.when(group + 1 < tensor_count)
        def _():
            load_feed(group + 1, 1 - slot, 0).start()

        return carry

    lax.fori_loop(0, tensor_count, feed_step, 0)

    def load_activ(group, slot):
        columns = pl.ds(pl.multiple_of(group * hidden_rows, TILE), hidden_rows)
        return pltpu.make_async_copy(
            activ_ref.at[:, columns],
            exp_stage.at[slot, :, pl.ds(0, hidden_rows)],
            exp_sem.at[slot],
        )

    keep(3).wait()
    load_feed(0, 0, 1).start()
    share(3, 0).wait_recv()
    load_feed(1, 1, 1).start()
    for which in range(2):
        save_feed(tensor_count - 1, which).wait()
    load_activ(0, 0).start()
    load_activ(1, 1).start()

    def down_step(group, carry):
        slot = lax.rem(group, 2)
        load_feed(group, slot, 1).wait()
        load_activ(group, slot).wait()
        for rows in tiles:
            ffn_out[rows, :] += jnp.dot(
                exp_stage[slot, rows, 0:hidden_rows],
                feed_weights[slot, 1],
                preferred_element_type=jnp.float32,
            )

        @pl.when(group == 0)
        def _():
            keep(4).wait()

        @pl.when(group == 1)
        def _():
            share(4, 0).wait_recv()

        @pl.when(group + 2 < tensor_count)
        def _():
            load_feed(group + 2, slot, 1).start()
            load_activ(group + 2, slot).start()

        return carry

    lax.fori_loop(0, tensor_count, down_step, 0)

    down_grad = jnp.zeros((R, D), jnp.float32)
    up_grad = jnp.zeros((R, D), jnp.float32)
    for rows in tiles:
        ffn = ffn_out[rows, :]
        ffn_low = ffn.astype(low)
        grad_low = cotangent_ref[rows, :]
        zed = contract(ffn_low, down, 1, 1)
        cdf, density = normal_parts(zed)
        hidden = (zed * cdf).astype(low)
        added = jnp.dot(hidden, up, preferred_element_type=jnp.float32)
        layer_out_ref[rows, :] = (mid_rows[rows, :] + ffn + added).astype(low)
        zed_grad = contract(grad_low, up, 1, 1) * (cdf + zed * density)
        zed_low = zed_grad.astype(low)
        ffn_grad_ref[rows, :] = (
            grad_low.astype(jnp.float32)
            + jnp.dot(zed_low, down, preferred_element_type=jnp.float32)
        ).astype(low)
        up_grad = up_grad + contract(hidden, grad_low, 0, 0)
        down_grad = down_grad + contract(zed_low, ffn_low, 0, 0)

    left_grad = exact(down_grad, right, 1, 1)
    wide_grad = exact(up_grad, tall, 1, 1)
    grads = [
        take_back(left_grad * shorts[0], mix_down) + take_back(wide_grad * shorts[1], mix_up),
        take_long(exact(left, down_grad, 0, 0)),
        take_back(left_grad * mixes[0], short_place),
        take_back(wide_grad * mixes[1], short_place),
        take_long(exact(wide, up_grad, 0, 0)),
    ]
    lines = -(-NADAPT // TILE)
    grads.append(jnp.zeros((1, lines * TILE - NADAPT), jnp.float32))
    grads = jnp.concatenate(grads, axis=1)
    small_part_ref[...] = jnp.zeros(small_part_ref.shape, jnp.float32)
    for part in range(lines):
        line_at = 2 * D // TILE + part
        small_part_ref[line_at : line_at + 1, :] = grads[:, TILE * part : TILE * (part + 1)]

    for which in range(2):
        for group in range(tensor_count):
            save_group(which, group).wait()
    for role in range(len(bufs)):
        share(role, 0).wait_send()
        if role < 3:
            share(role, 1).wait_send()
            share(role, 2).wait_send()


def front(
    mine,
    slot_place,
    spread_place,
    orders,
    local_sizes,
    tokens,
    small_row,
    bucket_place,
    segments,
    cotangent,
):
    dp_count, tensor_count = lax.axis_size("dp"), lax.axis_size("tensor")
    sizes = [order.shape[1] for order in orders]
    pair_rows = spread_place.shape[1]
    low = jnp.bfloat16
    dma = pltpu.SemaphoreType.DMA
    roles = len(sizes)
    whole = pl.BlockSpec(memory_space=pltpu.VMEM)
    away = pl.BlockSpec(memory_space=pl.ANY)
    return pl.pallas_call(
        functools.partial(front_kernel, sizes),
        in_specs=[whole] * 12,
        out_specs=[away] * 5 + [whole] * 3 + [away] * 3 + [whole] * 5,
        out_shape=[jax.ShapeDtypeStruct((tensor_count, size, D), low) for size in sizes]
        + [
            jax.ShapeDtypeStruct((tensor_count, sizes[0], SEQ), low),
            jax.ShapeDtypeStruct((H * HS, SEQ), low),
            jax.ShapeDtypeStruct((H, 1, SEQ), jnp.float32),
            jax.ShapeDtypeStruct((SEQ, D), low),
            jax.ShapeDtypeStruct((H, SEQ, SEQ), low),
            jax.ShapeDtypeStruct((SEQ, FF), low),
            jax.ShapeDtypeStruct((SEQ, FF), low),
        ]
        + [jax.ShapeDtypeStruct((SEQ, D), low)] * 4
        + [jax.ShapeDtypeStruct((TABLE_ROW, TILE), jnp.float32)],
        scratch_shapes=[
            pltpu.VMEM((tensor_count, sizes[0], D), low),
            pltpu.VMEM((tensor_count, sizes[0], SEQ), low),
            pltpu.VMEM((2, 2, sizes[2], D), low),
            pltpu.VMEM((SEQ, D), jnp.float32),
            pltpu.VMEM((SEQ, D), jnp.float32),
        ]
        + [
            pltpu.VMEM((size, dp_count * local), low)
            for size, local in zip(sizes, local_sizes)
        ]
        + [
            pltpu.VMEM((dp_count, pair_rows, D), low),
            pltpu.VMEM((dp_count, pair_rows, D), low),
            pltpu.VMEM((sum(local_sizes), D), low),
            pltpu.VMEM((H, 1, 2 * SEQ), jnp.float32),
            pltpu.VMEM((SEQ, TILE), jnp.float32),
        ]
        + [pltpu.VMEM((dp_count, size, D), low) for size in local_sizes + local_sizes[3:]]
        + [pltpu.VMEM((local_sizes[3], D), low)]
        + [pltpu.VMEM((size, D), low) for size in sizes[1:] + sizes[3:]]
        + [
            pltpu.VMEM((WINDOW, TILE), jnp.float32),
            pltpu.VMEM((SEQ, QUERY_TILE), jnp.float32),
            pltpu.VMEM((2, SEQ, SEQ), low),
            dma((dp_count,)),
            dma((dp_count,)),
            dma,
            dma,
            dma((roles + 1, dp_count // 2)),
            dma((roles + 1, dp_count // 2)),
            dma((roles + 1, dp_count // 2)),
            dma((roles + 1, dp_count // 2)),
            dma((roles + 1, 3)),
            dma((roles + 1, 3)),
            dma((roles + 1,)),
            dma((2,)),
            dma((2, tensor_count)),
            dma((2, 2)),
            dma((tensor_count,)),
        ],
        compiler_params=pltpu.CompilerParams(
            collective_id=1, has_side_effects=True, vmem_limit_bytes=63 * 1024 * 1024
        ),
        cost_estimate=pl.CostEstimate(
            flops=10 * H * SEQ * SEQ * 256 + 4 * SEQ * FF * D,
            bytes_accessed=96 * 1024 * 1024,
            transcendentals=H * SEQ * SEQ + 2 * SEQ * FF,
        ),
        name="front",
    )(
        mine,
        slot_place,
        spread_place,
        *orders,
        tokens,
        small_row,
        bucket_place,
        segments.astype(jnp.float32)[None, :],
        cotangent,
    )


def attend_head_back(
    query_rows,
    key_rows,
    value_rows,
    exp_ref,
    attended,
    scale,
    attended_grad,
    window,
    score_grads,
    store,
):
    scaled = attended_grad.astype(jnp.float32) * scale
    delta = jnp.sum(scaled * attended.astype(jnp.float32), axis=0, keepdims=True)
    scaled_low = scaled.astype(jnp.bfloat16)
    delta_high = delta.astype(jnp.bfloat16).astype(jnp.float32)
    delta_rest = delta - delta_high
    place = lax.broadcasted_iota(jnp.int32, (16, SEQ), 0)
    extra = jnp.where(
        place == 0,
        jnp.broadcast_to(-delta_high, (16, SEQ)),
        jnp.where(place == 1, jnp.broadcast_to(-delta_rest, (16, SEQ)), 0.0),
    ).astype(jnp.bfloat16)
    grads = jnp.concatenate([scaled_low, extra], axis=0)
    values = jnp.concatenate([value_rows, jnp.ones((16, SEQ), jnp.bfloat16)], axis=0).T
    window[...] = jnp.zeros_like(window)
    for q0 in range(0, SEQ, BACK_QUERY_TILE):
        total = jnp.zeros((HS, BACK_QUERY_TILE), jnp.float32)
        for k0 in range(0, SEQ, BACK_KEY_TILE):
            centered = jnp.dot(
                values[k0 : k0 + BACK_KEY_TILE],
                grads[:, q0 : q0 + BACK_QUERY_TILE],
                preferred_element_type=jnp.float32,
            )
            score_grad = centered * exp_ref[
                k0 : k0 + BACK_KEY_TILE, q0 : q0 + BACK_QUERY_TILE
            ].astype(jnp.float32)
            for l0 in range(0, BACK_QUERY_TILE, TILE):
                start = SEQ - TILE - (q0 + l0) + k0
                window[start : start + BACK_KEY_TILE, :] += score_grad[:, l0 : l0 + TILE]
            score_low = score_grad.astype(jnp.bfloat16)
            score_grads[k0 : k0 + BACK_KEY_TILE, q0 : q0 + BACK_QUERY_TILE] = score_low
            total = total + jnp.dot(
                key_rows[:, k0 : k0 + BACK_KEY_TILE], score_low, preferred_element_type=jnp.float32
            )
        store(0, q0, total.astype(jnp.bfloat16))
    queries = query_rows.T
    scaled_rows = scaled_low.T
    for k0 in range(0, SEQ, BACK_KEY_TILE):
        key_grad = jnp.dot(
            score_grads[k0 : k0 + BACK_KEY_TILE, :], queries, preferred_element_type=jnp.float32
        )
        value_grad = jnp.dot(
            exp_ref[k0 : k0 + BACK_KEY_TILE, :], scaled_rows, preferred_element_type=jnp.float32
        )
        store(1, k0, key_grad.T.astype(jnp.bfloat16))
        store(2, k0, value_grad.T.astype(jnp.bfloat16))
    pieces = [jnp.zeros((1, TILE), jnp.float32)] * (2 * SEQ // TILE)
    for tile in range(WINDOW // TILE):
        base = WINDOW - TILE * tile
        block = window[TILE * tile : TILE * (tile + 1), :]
        folded = jnp.concatenate([jnp.zeros((TILE, TILE), jnp.float32), block], axis=1)
        rows = TILE // 2
        while rows >= 1:
            folded = folded[:rows] + pltpu.roll(folded[rows:], 2 * TILE - rows, 1)
            rows //= 2
        pieces[base // TILE - 1] += folded[:, :TILE]
        pieces[base // TILE] += folded[:, TILE:]
    return jnp.concatenate(pieces, axis=1)


def back_kernel(
    sizes,
    ffn_grad_ref,
    normed_two_ref,
    mid_ref,
    cotangent_ref,
    w_out_ref,
    activ_ref,
    slope_ref,
    w_in_ref,
    w_down_ref,
    projected_ref,
    exp_ref,
    w_qkv_ref,
    tokens_ref,
    normed_one_ref,
    attended_ref,
    scale_ref,
    params_ref,
    small_ref,
    bucket_ref,
    place_qkv_ref,
    place_out_ref,
    place_in_ref,
    place_down_ref,
    spread_place_ref,
    slot_place_ref,
    owned_ref,
    input_grad_ref,
    small_total_ref,
    proj_grad_ref,
    bucket_hot,
    weights,
    proj,
    proj_grad,
    normed_grad,
    window,
    score_grads,
    exp_stage,
    row_grads,
    normed,
    attended_grad,
    odd_out,
    odd_in,
    odd_down,
    zero_qkv,
    zero_out,
    zero_in,
    zero_down,
    two_qkv,
    two_out,
    two_in,
    two_down,
    core_one_qkv,
    core_one_out,
    core_one_in,
    core_one_down,
    core_three_qkv,
    core_three_out,
    core_three_in,
    core_three_down,
    far_qkv,
    far_out,
    far_in,
    far_down,
    got_qkv,
    got_out,
    got_in,
    got_down,
    side_qkv,
    side_out,
    side_down,
    end_mine,
    end_far,
    spread,
    sent,
    received,
    small_own,
    small_tensor,
    small_dp,
    core_send,
    core_recv,
    far_send,
    far_recv,
    side_send,
    side_recv,
    line_send,
    line_recv,
    end_send,
    end_recv,
    back_send,
    back_recv,
    small_send,
    small_recv,
    load_sem,
    exp_sem,
    proj_sem,
    again_sem,
):
    dp_count, pair_rows = spread_place_ref.shape
    hidden_rows = w_in_ref.shape[1]
    tensor_count = w_qkv_ref.shape[0]
    heads = scale_ref.shape[0]
    group_heads = heads // tensor_count
    head_rows = group_heads * HS
    dp_pos, tensor_pos = lax.axis_index("dp"), lax.axis_index("tensor")
    core_pos = tensor_pos + 1 - 2 * lax.rem(tensor_pos, 2)
    far_pos = lax.rem(tensor_pos + 2, tensor_count)
    core_peer, far_peer = (dp_pos, core_pos), (dp_pos, far_pos)
    zeros = (zero_qkv, zero_out, zero_in, zero_down)
    twos = (two_qkv, two_out, two_in, two_down)
    core_ones = (core_one_qkv, core_one_out, core_one_in, core_one_down)
    core_threes = (core_three_qkv, core_three_out, core_three_in, core_three_down)
    fars = (far_qkv, far_out, far_in, far_down)
    gots = (got_qkv, got_out, got_in, got_down)
    side_got = (side_qkv, side_out, far_in, side_down)
    places = (place_qkv_ref, place_out_ref, place_in_ref, place_down_ref)
    offsets = [sum(got.shape[1] for got in gots[:role]) for role in range(len(gots))]
    low = jnp.bfloat16

    def up(m):
        return lax.rem(dp_pos + m, dp_count)

    def down(m):
        return lax.rem(dp_pos + dp_count - m, dp_count)

    def each_peer(run):
        def step(m, carry):
            run(m)
            return carry

        lax.fori_loop(1, dp_count, step, 0)

    def tensor_peer(m):
        return (dp_pos, lax.rem(tensor_pos + m, tensor_count))

    barrier = pltpu.get_barrier_semaphore()

    def greet(m):
        pl.semaphore_signal(barrier, inc=1, device_id=(up(m), tensor_pos), device_id_type=MESH)

    each_peer(greet)
    for m in range(1, tensor_count):
        pl.semaphore_signal(barrier, inc=1, device_id=tensor_peer(m), device_id_type=MESH)

    def load_exp(head, slot):
        return pltpu.make_async_copy(exp_ref.at[head], exp_stage.at[slot], exp_sem.at[slot])

    def load_proj(group):
        return pltpu.make_async_copy(projected_ref.at[group], proj, proj_sem.at[0])

    def save_proj(group):
        return pltpu.make_async_copy(proj_grad, proj_grad_ref.at[group], proj_sem.at[1])

    def reload(group, which):
        odd = group % 2
        source, target = (
            (proj_grad_ref.at[group], proj if odd else proj_grad),
            (w_qkv_ref.at[group], zero_qkv if odd else weights),
        )[which]
        return pltpu.make_async_copy(source, target, again_sem.at[odd, which])

    def load(which, group=0):
        columns = pl.ds(pl.multiple_of(group * hidden_rows, TILE), hidden_rows)
        source, target = (
            (lambda: activ_ref.at[:, columns], lambda: exp_stage.at[0, :, pl.ds(0, hidden_rows)]),
            (lambda: slope_ref.at[:, columns], lambda: exp_stage.at[1, :, pl.ds(0, hidden_rows)]),
            (lambda: w_in_ref.at[group], lambda: received.at[pl.ds(0, hidden_rows)]),
            (lambda: w_down_ref.at[group], lambda: sent.at[pl.ds(0, hidden_rows)]),
            (lambda: ffn_grad_ref, lambda: row_grads),
            (lambda: normed_two_ref, lambda: normed),
            (lambda: mid_ref, lambda: exp_stage.at[0, :, pl.ds(0, D)]),
            (lambda: cotangent_ref, lambda: exp_stage.at[1, :, pl.ds(0, D)]),
            (lambda: w_out_ref, lambda: sent.at[pl.ds(0, D)]),
            (lambda: normed_one_ref, lambda: normed),
            (lambda: tokens_ref, lambda: exp_stage.at[0, :, pl.ds(0, D)]),
        )[which]
        return pltpu.make_async_copy(source(), target(), load_sem.at[which])

    def core_copy(role, which):
        half = which // 2
        if role == 0:
            src = (odd_in, odd_down)[half].at[pl.ds(0, sizes[0])]
        else:
            src = (None, odd_out.at[half], odd_in, odd_down)[role]
        target = (core_ones if which == 1 else core_threes)[role].at[pl.ds(0, sizes[role])]
        return pltpu.make_async_remote_copy(
            src,
            target,
            core_send.at[role, half],
            core_recv.at[role, half],
            device_id=core_peer,
            device_id_type=MESH,
        )

    def far_copy(role):
        return pltpu.make_async_remote_copy(
            twos[role],
            fars[role],
            far_send.at[role],
            far_recv.at[role],
            device_id=far_peer,
            device_id_type=MESH,
        )

    line = dp_count // 2
    line_pos, side = lax.div(dp_pos, 2), lax.rem(dp_pos, 2)
    side_peer = (dp_pos + 1 - 2 * side, tensor_pos)

    def each_line(run):
        def step(m, carry):
            run(m)
            return carry

        lax.fori_loop(1, line, step, 0)

    def leaving(role, far):
        return core_ones[role] if role == 2 and not far else core_threes[role]

    def side_copy(role, far=0):
        count = gots[role].shape[1] * line
        return pltpu.make_async_remote_copy(
            leaving(role, far).at[pl.ds(count, count)],
            side_got[role].at[pl.ds(count * far, count)],
            side_send.at[role, far],
            side_recv.at[role, far],
            device_id=side_peer,
            device_id_type=MESH,
        )

    def line_copy(role, m, far=0):
        count = gots[role].shape[1]
        return pltpu.make_async_remote_copy(
            leaving(role, far).at[pl.ds(pl.multiple_of(m * count, 16), count)],
            gots[role].at[far * line + m],
            line_send.at[role, far * line + m],
            line_recv.at[role, far * line + m],
            device_id=(lax.rem(line_pos + m, line) * 2 + side, tensor_pos),
            device_id_type=MESH,
        )

    def end_copy():
        return pltpu.make_async_remote_copy(
            end_mine, end_far, end_send, end_recv, device_id=far_peer, device_id_type=MESH
        )

    def send_far(role):
        core_copy(role, 3).wait_recv()
        count = twos[role].shape[0]
        twos[role][...] = (
            twos[role][...].astype(jnp.float32)
            + core_threes[role][0:count, :].astype(jnp.float32)
        ).astype(low)
        far_copy(role).start()

    def scatter(role, far, total):
        count = gots[role].shape[1]
        for r0 in range(0, dp_count * count, 384):
            r1 = min(r0 + 384, dp_count * count)
            hot = one_hot(places[role][...] - r0, (r1 - r0, sizes[role]), 0)
            leaving(role, far)[r0:r1, :] = jnp.dot(
                hot, total, preferred_element_type=jnp.float32
            ).astype(low)
        side_copy(role, far).start()

    def send_deal(role):
        core_copy(role, 1).wait_recv()
        far_copy(role).wait_recv()
        total = (
            zeros[role][...].astype(jnp.float32)
            + core_ones[role][...].astype(jnp.float32)
            + fars[role][...].astype(jnp.float32)
        ).astype(low)
        scatter(role, 0, total)

    def send_half(role, far):
        core_copy(role, 3 if far else 1).wait_recv()
        count = sizes[role]
        mine = (twos if far else zeros)[role][...].astype(jnp.float32)
        core = (core_threes if far else core_ones)[role][0:count, :].astype(jnp.float32)
        scatter(role, far, (mine + core).astype(low))

    def pass_line(role, far=0):
        side_copy(role, far).wait()
        count = gots[role].shape[1] * line
        leaving(role, far)[0:count, :] = (
            leaving(role, far)[0:count, :].astype(jnp.float32)
            + side_got[role][count * far : count * (far + 1), :].astype(jnp.float32)
        ).astype(low)
        each_line(lambda m: line_copy(role, m, far).start())

    def line_sum(role, far=0):
        each_line(lambda m: line_copy(role, m, far).wait())
        total = leaving(role, far)[0 : gots[role].shape[1], :].astype(jnp.float32)
        for m in range(1, line):
            total = total + gots[role][far * line + m].astype(jnp.float32)
        return total

    def finish_deal(role):
        count = gots[role].shape[1]
        spread[offsets[role] : offsets[role] + count, :] = line_sum(role).astype(low)

    def finish_far():
        end_mine[...] = line_sum(2, 1).astype(low)
        end_copy().start()

    def finish_near():
        total = line_sum(2)
        end_copy().wait()
        count = gots[2].shape[1]
        spread[offsets[2] : offsets[2] + count, :] = (
            total + end_far[...].astype(jnp.float32)
        ).astype(low)

    for which in (4, 5):
        load(which).start()
    for which in range(4):
        load(which, tensor_count - 1).start()
    bucket_hot[...] = one_hot(bucket_ref[...], (NB, 2 * SEQ), 0)
    normed_grad[...] = jnp.zeros_like(normed_grad)
    small_own[0:TABLE_ROW, :] = small_ref[...]
    small_own[TABLE_ROW:SMALL_ROWS, :] = jnp.zeros((SMALL_ROWS - TABLE_ROW, TILE), jnp.float32)
    pl.semaphore_wait(barrier, dp_count + tensor_count - 2)
    for which in (4, 5):
        load(which).wait()
    row_tiles = [slice(r0, r0 + 256) for r0 in range(0, SEQ, 256)]
    pre_grad = score_grads

    def feed_step(i, carry):
        group = tensor_count - 1 - i

        def load_next(which):
            @pl.when(group > 0)
            def _():
                load(which, group - 1).start()

        load(3, group).wait()
        load(1, group).wait()
        for rows in row_tiles:
            grad = contract(row_grads[rows, :], sent[0:hidden_rows, :], 1, 1)
            grad = grad * exp_stage[1, rows, 0:hidden_rows].astype(jnp.float32)
            pre_grad[rows, 0:hidden_rows] = grad.astype(low)
        load_next(3)
        load_next(1)
        load(2, group).wait()
        for rows in row_tiles:
            normed_grad[rows, :] += jnp.dot(
                pre_grad[rows, 0:hidden_rows],
                received[0:hidden_rows, :],
                preferred_element_type=jnp.float32,
            )
        load_next(2)

        @pl.when(group == 2)
        def _():
            for role in (3, 2):
                core_copy(role, 3).wait_send()

        @pl.when(group == 0)
        def _():
            for role in (3, 2):
                core_copy(role, 1).wait_send()

        load(0, group).wait()
        for c0 in range(0, hidden_rows, 256):
            columns = slice(c0, c0 + 256)
            odd_down[columns, :] = jnp.dot(
                exp_stage[0, :, columns].T, row_grads[...], preferred_element_type=jnp.float32
            ).astype(low)
        load_next(0)

        @pl.when(group == 3)
        def _():
            core_copy(3, 3).start()

        @pl.when(group == 2)
        def _():
            two_down[...] = odd_down[...]
            send_far(3)

        @pl.when(group == 1)
        def _():
            core_copy(3, 1).start()

        @pl.when(group == 0)
        def _():
            zero_down[...] = odd_down[...]

        for c0 in range(0, hidden_rows, 256):
            columns = slice(c0, c0 + 256)
            odd_in[columns, :] = jnp.dot(
                pre_grad[:, columns].T, normed[...], preferred_element_type=jnp.float32
            ).astype(low)

        @pl.when(group == 3)
        def _():
            core_copy(2, 3).start()

        @pl.when(group == 2)
        def _():
            two_in[...] = odd_in[...]
            send_half(2, 1)

        @pl.when(group == 1)
        def _():
            core_copy(2, 1).start()

        @pl.when(group == 0)
        def _():
            zero_in[...] = odd_in[...]

        return carry

    lax.fori_loop(0, tensor_count, feed_step, 0)
    for which in (6, 7, 8, 9):
        load(which).start()
    send_half(2, 0)
    pass_line(2, 1)
    for which in (6, 7, 8):
        load(which).wait()
    gain_grad = jnp.zeros((1, D), jnp.float32)
    for r0 in range(0, SEQ, 128):
        rows = slice(r0, r0 + 128)
        mid = exp_stage[0, rows, 0:D].astype(jnp.float32)
        grads = normed_grad[rows, :]
        inverse = lax.rsqrt(jnp.mean(mid * mid, axis=1, keepdims=True) + norm_epsilon)
        scaled = mid * inverse
        gain_grad = gain_grad + jnp.sum(grads * scaled, axis=0, keepdims=True)
        grads = grads * params_ref[:, D : 2 * D]
        inner = jnp.mean(grads * scaled, axis=1, keepdims=True)
        row_grads[rows, :] = (
            exp_stage[1, rows, 0:D].astype(jnp.float32) + inverse * (grads - scaled * inner)
        ).astype(low)
    for part in range(D // TILE):
        line_at = D // TILE + part
        small_own[line_at : line_at + 1, :] = gain_grad[:, TILE * part : TILE * (part + 1)]
    normed_grad[...] = jnp.zeros_like(normed_grad)
    load_exp(heads - group_heads, 0).start()
    load_proj(tensor_count - 1).start()
    for group, target in enumerate((zero_out, odd_out.at[0], two_out, odd_out.at[1])):
        rows = slice(group * head_rows, (group + 1) * head_rows)
        target[...] = jnp.dot(
            attended_ref[rows, :], row_grads[...], preferred_element_type=jnp.float32
        ).astype(low)
    core_copy(1, 3).start()
    core_copy(1, 1).start()
    for r0 in range(0, D, 256):
        rows = slice(r0, r0 + 256)
        attended_grad[rows, :] = contract(sent[rows, :], row_grads[...], 1, 1).astype(low)
    load(9).wait()

    def head_step(i, carry):
        group = tensor_count - 1 - lax.div(i, group_heads)
        part_head = lax.rem(i, group_heads)
        head = group * group_heads + part_head
        slot = lax.rem(i, 2)

        @pl.when(i == 1)
        def _():
            send_deal(3)

        @pl.when(i == 2)
        def _():
            send_far(1)

        @pl.when(i == 3)
        def _():
            pass_line(2, 0)

        @pl.when(i == 5)
        def _():
            send_deal(1)

        @pl.when(i == 6)
        def _():
            send_far(0)
            pass_line(3)

        @pl.when(i == 8)
        def _():
            pass_line(1)

        @pl.when((part_head == 0) & (i > 0))
        def _():
            save_proj(group + 1).wait()

        @pl.when(part_head == 0)
        def _():
            load_proj(group).wait()

        @pl.when(i + 1 < heads)
        def _():
            later = i + 1
            later_group = tensor_count - 1 - lax.div(later, group_heads)
            later_head = later_group * group_heads + lax.rem(later, group_heads)
            load_exp(later_head, lax.rem(later, 2)).start()

        load_exp(head, slot).wait()

        def rows(part):
            return pl.ds(pl.multiple_of(part * head_rows + part_head * HS, HS), HS)

        def store(part, column, value):
            proj_grad[rows(part), column : column + value.shape[1]] = value

        here = pl.ds(pl.multiple_of(head * HS, HS), HS)
        offset_grad = attend_head_back(
            proj[rows(0), :],
            proj[rows(1), :],
            proj[rows(2), :],
            exp_stage.at[slot],
            attended_ref[here, :],
            scale_ref[head],
            attended_grad[here, :],
            window,
            score_grads,
            store,
        )
        place = (
            true_group((tensor_pos, core_pos, far_pos), group, tensor_count) * group_heads + part_head
        )
        high = offset_grad.astype(low)
        rest = (offset_grad - high.astype(jnp.float32)).astype(low)
        both = jnp.concatenate([high, rest] + [jnp.zeros_like(high)] * 6, axis=0)
        sums = contract(both, bucket_hot[...], 1, 1)
        row = lax.broadcasted_iota(jnp.int32, (SMALL_ROWS - TABLE_ROW, TILE), 0)
        found = jnp.concatenate(
            [sums[0:1] + sums[1:2], jnp.zeros((1, TILE - NB), jnp.float32)], axis=1
        )
        small_own[TABLE_ROW:SMALL_ROWS, :] += jnp.where(
            row == place,
            jnp.broadcast_to(found, (SMALL_ROWS - TABLE_ROW, TILE)),
            0.0,
        )

        @pl.when(part_head == group_heads - 1)
        def _():
            @pl.when(group > 0)
            def _():
                load_proj(group - 1).start()

            def weight_grad(target):
                for r0 in range(0, 3 * head_rows, head_rows):
                    target[r0 : r0 + head_rows, :] = jnp.dot(
                        proj_grad[r0 : r0 + head_rows, :],
                        normed[...],
                        preferred_element_type=jnp.float32,
                    ).astype(low)

            @pl.when(group == 3)
            def _():
                weight_grad(odd_down)
                core_copy(0, 3).start()

            @pl.when(group == 2)
            def _():
                weight_grad(two_qkv)

            @pl.when(group == 1)
            def _():
                weight_grad(odd_in)
                core_copy(0, 1).start()

            @pl.when(group == 0)
            def _():
                weight_grad(zero_qkv)

            save_proj(group).start()

        return carry

    lax.fori_loop(0, heads, head_step, 0)

    load(10).start()
    save_proj(0).wait()
    reload(0, 1).start()
    reload(1, 0).start()
    send_deal(0)
    reload(1, 1).start()
    for group in range(tensor_count):
        if group > 0:
            reload(group, 0).wait()
        reload(group, 1).wait()
        part, rows_in = (proj, zero_qkv) if group % 2 else (proj_grad, weights)
        for r0 in range(0, SEQ, 256):
            normed_grad[r0 : r0 + 256, :] += jnp.dot(
                part[:, r0 : r0 + 256].T, rows_in[...], preferred_element_type=jnp.float32
            )
        if group + 2 < tensor_count:
            reload(group + 2, 0).start()
            reload(group + 2, 1).start()
    pass_line(0)
    load(10).wait()

    gain_grad = jnp.zeros((1, D), jnp.float32)
    for r0 in range(0, SEQ, 128):
        values = exp_stage[0, r0 : r0 + 128, 0:D].astype(jnp.float32)
        grads = normed_grad[r0 : r0 + 128, :]
        inverse = lax.rsqrt(jnp.mean(values * values, axis=1, keepdims=True) + norm_epsilon)
        scaled = values * inverse
        gain_grad = gain_grad + jnp.sum(grads * scaled, axis=0, keepdims=True)
        grads = grads * params_ref[:, 0:D]
        inner = jnp.mean(grads * scaled, axis=1, keepdims=True)
        row_grads[r0 : r0 + 128, :] = (
            row_grads[r0 : r0 + 128, :].astype(jnp.float32) + inverse * (grads - scaled * inner)
        ).astype(low)
    for part in range(D // TILE):
        small_own[part : part + 1, :] = gain_grad[:, TILE * part : TILE * (part + 1)]

    save_rows = pltpu.make_async_copy(row_grads, input_grad_ref, exp_sem.at[1])
    save_rows.start()

    def small_copy(stage, m):
        if stage == 0:
            src, target, peer = small_own, small_tensor.at[tensor_pos], tensor_peer(m)
        else:
            src, target, peer = small_total_ref, small_dp.at[dp_pos], (up(m), tensor_pos)
        return pltpu.make_async_remote_copy(
            src,
            target,
            small_send.at[stage, m],
            small_recv.at[stage, m],
            device_id=peer,
            device_id_type=MESH,
        )

    for m in range(1, tensor_count):
        small_copy(0, m).start()
    small_tensor[tensor_pos] = small_own[...]
    for m in range(1, tensor_count):
        small_copy(0, m).wait()
    total = small_tensor[0]
    for m in range(1, tensor_count):
        total = total + small_tensor[m]
    small_total_ref[...] = total
    each_peer(lambda m: small_copy(1, m).start())
    finish_far()
    finish_near()
    finish_deal(3)
    small_dp[dp_pos] = small_total_ref[...]
    each_peer(lambda m: small_copy(1, m).wait())
    total = small_dp[0]
    for m in range(1, dp_count):
        total = total + small_dp[m]
    small_total_ref[...] = total
    finish_deal(1)
    finish_deal(0)

    place = jnp.concatenate([spread_place_ref[m : m + 1, :] for m in range(dp_count)], axis=1)
    hot = one_hot(place, (spread.shape[0], dp_count * pair_rows), 0)
    sent[0 : dp_count * pair_rows, :] = contract(hot, spread[...], 0, 0).astype(low)

    def back_copy(m):
        here = pl.ds(pl.multiple_of(m * pair_rows, 16), pair_rows)
        return pltpu.make_async_remote_copy(
            sent.at[here],
            received.at[here],
            back_send.at[m],
            back_recv.at[m],
            device_id=(down(m), tensor_pos),
            device_id_type=MESH,
        )

    each_peer(lambda m: back_copy(m).start())
    received[0:pair_rows, :] = sent[0:pair_rows, :]
    each_peer(lambda m: back_copy(m).wait())
    hot = one_hot(slot_place_ref[...], (dp_count * pair_rows, owned_ref.shape[0]), 0)
    owned_ref[...] = contract(hot, received[0 : dp_count * pair_rows, :], 0, 0)
    save_rows.wait()
    for role in range(len(gots)):
        if role < 2:
            core_copy(role, 1).wait_send()
            core_copy(role, 3).wait_send()
        if role != 2:
            far_copy(role).wait_send()


def back(
    feed_parts,
    projected,
    exp_scores,
    w_qkv,
    tokens,
    normed_one,
    attended,
    scale,
    small_row,
    small,
    bucket_place,
    places,
    local_sizes,
    spread_place,
    slot_place,
):
    dp_count, tensor_count = lax.axis_size("dp"), lax.axis_size("tensor")
    sizes = [place.shape[1] for place in places]
    capacity, pair_rows = slot_place.shape[1], spread_place.shape[1]
    low = jnp.bfloat16
    dma = pltpu.SemaphoreType.DMA
    roles = len(sizes)
    whole = pl.BlockSpec(memory_space=pltpu.VMEM)
    away = pl.BlockSpec(memory_space=pl.ANY)
    parts = [pltpu.VMEM((size, D), low) for size in sizes]
    padded = [
        pltpu.VMEM((max(dp_count * size, full), D), low) for size, full in zip(local_sizes, sizes)
    ]
    return pl.pallas_call(
        functools.partial(back_kernel, sizes),
        in_specs=[away] * 14 + [whole] * 11,
        out_specs=[whole, away, whole, away],
        out_shape=[
            jax.ShapeDtypeStruct((capacity, D), jnp.float32),
            jax.ShapeDtypeStruct((SEQ, D), low),
            jax.ShapeDtypeStruct((SMALL_ROWS, TILE), jnp.float32),
            jax.ShapeDtypeStruct((tensor_count, sizes[0], SEQ), low),
        ],
        scratch_shapes=[
            pltpu.VMEM((NB, 2 * SEQ), low),
            pltpu.VMEM((sizes[0], D), low),
            pltpu.VMEM((sizes[0], SEQ), low),
            pltpu.VMEM((sizes[0], SEQ), low),
            pltpu.VMEM((SEQ, D), jnp.float32),
            pltpu.VMEM((WINDOW, TILE), jnp.float32),
            pltpu.VMEM((SEQ, SEQ), low),
            pltpu.VMEM((2, SEQ, SEQ), low),
            pltpu.VMEM((SEQ, D), low),
            pltpu.VMEM((SEQ, D), low),
            pltpu.VMEM((D, SEQ), low),
            pltpu.VMEM((2, sizes[1], D), low),
            pltpu.VMEM((sizes[2], D), low),
            pltpu.VMEM((sizes[3], D), low),
        ]
        + parts
        + parts
        + parts[:2]
        + padded[2:3]
        + parts[3:]
        + padded
        + parts[:2]
        + [pltpu.VMEM((dp_count * local_sizes[2], D), low)]
        + parts[3:]
        + [
            pltpu.VMEM((dp_count if role == 2 else dp_count // 2, size, D), low)
            for role, size in enumerate(local_sizes)
        ]
        + [pltpu.VMEM((dp_count // 2 * local_sizes[role], D), low) for role in (0, 1, 3)]
        + [
            pltpu.VMEM((local_sizes[2], D), low),
            pltpu.VMEM((local_sizes[2], D), low),
            pltpu.VMEM((sum(local_sizes), D), low),
            pltpu.VMEM((max(dp_count * pair_rows, D), D), low),
            pltpu.VMEM((max(dp_count * pair_rows, D), D), low),
            pltpu.VMEM((SMALL_ROWS, TILE), jnp.float32),
            pltpu.VMEM((tensor_count, SMALL_ROWS, TILE), jnp.float32),
            pltpu.VMEM((dp_count, SMALL_ROWS, TILE), jnp.float32),
            dma((roles, 2)),
            dma((roles, 2)),
            dma((roles,)),
            dma((roles,)),
            dma((roles, 2)),
            dma((roles, 2)),
            dma((roles, dp_count)),
            dma((roles, dp_count)),
            dma,
            dma,
            dma((dp_count,)),
            dma((dp_count,)),
            dma((2, max(dp_count, tensor_count))),
            dma((2, max(dp_count, tensor_count))),
            dma((11,)),
            dma((2,)),
            dma((2,)),
            dma((2, 2)),
        ],
        compiler_params=pltpu.CompilerParams(
            collective_id=2, has_side_effects=True, vmem_limit_bytes=63 * 1024 * 1024
        ),
        cost_estimate=pl.CostEstimate(
            flops=16 * H * SEQ * SEQ * 256 + 8 * SEQ * FF * D,
            bytes_accessed=96 * 1024 * 1024,
            transcendentals=0,
        ),
        name="back",
    )(
        *feed_parts,
        projected,
        exp_scores,
        w_qkv,
        tokens,
        normed_one,
        attended,
        scale,
        small_row,
        small,
        bucket_place,
        *places,
        spread_place,
        slot_place,
    )


def adamw(weights, grads, first, second, step):
    first_new = beta_first * first + (1.0 - beta_first) * grads
    second_new = beta_second * second + (1.0 - beta_second) * grads * grads
    first_hat = first_new / (1.0 - beta_first**step)
    second_hat = second_new / (1.0 - beta_second**step)
    weights_new = weights - rate_per_step * step * (
        first_hat / (jnp.sqrt(second_hat) + adam_epsilon) + weight_decay * weights
    )
    return (weights_new, first_new, second_new)


def per_device(
    tokens,
    cotangent,
    segment_ids,
    buckets,
    owners,
    master,
    first_moment,
    second_moment,
    small_params,
    small_first,
    small_second,
    adapter_ema,
    step_count,
):
    dp_count = lax.axis_size("dp")
    tensor_count = lax.axis_size("tensor")
    capacity = master.shape[1]
    group_heads = H // tensor_count
    head_rows = group_heads * HS
    hidden_rows = FF // tensor_count
    tensor_pos = lax.axis_index("tensor")
    sizes = [3 * head_rows, head_rows, hidden_rows, hidden_rows]
    local_sizes = [-(-size // dp_count // 16) * 16 for size in sizes]
    pair_rows = -(-((capacity + len(sizes) * (dp_count - 1)) // dp_count) // 16) * 16
    slot_place, spread_place, orders, places = plan(
        owners, sizes, local_sizes, capacity, pair_rows
    )

    bucket_place = jnp.concatenate([jnp.full((1,), -1, jnp.int32), buckets[::-1]])[None, :]
    segments = lax.dynamic_slice_in_dim(segment_ids, tensor_pos * SEQ, SEQ, 0)
    outs = front(
        master[0],
        slot_place,
        spread_place,
        orders,
        local_sizes,
        tokens,
        small_params[None, :],
        bucket_place,
        segments,
        cotangent,
    )
    w_qkv, w_out, w_in, w_down, projected, attended, scale, normed_one, exp_scores = outs[:9]
    activ, slope, normed_two, mid, layer_out, ffn_grad, small_local = outs[9:]
    owned_grad, input_grad, small_total, _ = back(
        (
            ffn_grad,
            normed_two,
            mid,
            cotangent,
            w_out.reshape(D, D),
            activ,
            slope,
            w_in,
            w_down,
        ),
        projected,
        exp_scores,
        w_qkv,
        tokens,
        normed_one,
        attended,
        scale,
        small_params[None, :],
        small_local,
        bucket_place,
        places,
        local_sizes,
        spread_place,
        slot_place,
    )
    small_total = jnp.concatenate(
        [
            small_total[:TABLE_ROW].reshape(-1)[: 2 * D + NADAPT],
            small_total[TABLE_ROW : TABLE_ROW + H, :NB].T.reshape(-1),
        ]
    )
    own_filled = (slot_place[0] >= 0).astype(jnp.float32)[:, None]
    step = step_count[0].astype(jnp.float32)
    owned_grad = owned_grad * own_filled
    new_master, new_first, new_second = adamw(
        master[0], owned_grad, first_moment[0], second_moment[0], step
    )
    new_master = new_master * own_filled
    new_first = new_first * own_filled
    new_second = new_second * own_filled
    small_new, small_first_new, small_second_new = adamw(
        small_params, small_total, small_first, small_second, step
    )
    ema_new = average_keep * adapter_ema + (1.0 - average_keep) * small_new[2 * D : 2 * D + NADAPT]
    return (
        layer_out,
        input_grad,
        owned_grad[None],
        new_first[None],
        new_second[None],
        new_master[None],
        new_master.astype(jnp.bfloat16)[None],
        small_total,
        small_first_new,
        small_second_new,
        small_new,
        ema_new,
    )


def solution(mesh):
    token_spec = P(("dp", "tensor"), None)
    owner_spec = P("tensor", "dp", None)
    return jax.shard_map(
        per_device,
        mesh=mesh,
        in_specs=(token_spec, token_spec, P("dp"), P(), P())
        + (owner_spec,) * 3
        + (P(),) * 5,
        out_specs=(token_spec,) * 2 + (owner_spec,) * 5 + (P(),) * 5,
        check_vma=False,
    )
```
